128 devices in a mesh: dp: 32 (over z, y, core), pipe: 4 (over x).
Axes of the slice: x: 4, y: 4, z: 4, core: 2. Of those that a mesh axis runs over, the one named last changes fastest.
Arguments:
- features: bfloat16 [25088, 2048], P('dp'), may hold values from -6 to 6
- out_cotangent: bfloat16 [25088, 2048], P('dp'), may hold values from -6 to 6
- seg_valid: int32 [64, 8], P('dp'), may hold values 0 or 1
- seg_video: int32 [64, 8], P('dp'), may hold values from 0 to 1, never falling along the last dimension, each value on 1 to 5 neighbouring positions
- frames: bfloat16 [256, 5, 3, 224, 224], P(('dp', 'pipe')), may hold values from -8 to 8
- stem_cotangent: bfloat16 [256, 64, 56, 56], P(('dp', 'pipe')), may hold values from -6 to 6
- stem_weight: bfloat16 [64, 3, 7, 7], replicated, may hold values from -0.5 to 0.5
- stem_diff_weight: bfloat16 [64, 12, 7, 7], replicated, may hold values from -0.25 to 0.25
- stem_gain: float32 [64], replicated, may hold values from 0.5 to 1.5
- stem_bias: float32 [64], replicated, may hold values from -1.5 to 1.5
- reduce_weight: bfloat16 [2048, 512], replicated, may hold values from -0.125 to 0.125
- reduce_gain: float32 [512], replicated, may hold values from 0.5 to 1.5
- reduce_bias: float32 [512], replicated, may hold values from -1.5 to 1.5
- spatial_weight: bfloat16 [4608, 512], replicated, may hold values from -0.09375 to 0.09375
- spatial_gain: float32 [512], replicated, may hold values from 0.5 to 1.5
- spatial_bias: float32 [512], replicated, may hold values from -1.5 to 1.5
- expand_weight: bfloat16 [512, 2048], replicated, may hold values from -0.25 to 0.25
- expand_gain: float32 [2048], replicated, may hold values from 0.5 to 1.5
- expand_bias: float32 [2048], replicated, may hold values from -1.5 to 1.5
- motion_weight: bfloat16 [2048, 512], replicated, may hold values from -0.125 to 0.125
- motion_gain: float32 [512], replicated, may hold values from 0.5 to 1.5
- depth_weight: float32 [2, 3, 3, 512], replicated, may hold values from -2 to 2
- excite_weight: bfloat16 [512, 2048], replicated, may hold values from -0.25 to 0.25
- excite_gain: float32 [2048], replicated, may hold values from 0.5 to 1.5
- excite_bias: float32 [2048], replicated, may hold values from -1.5 to 1.5
Outputs:
- result: bfloat16 [25088, 2048], P('dp', 'pipe')
- features_grad: bfloat16 [25088, 2048], P('dp', 'pipe')
- stem_weight_grad: float32 [64, 3, 7, 7], replicated
- stem_diff_grad: float32 [64, 12, 7, 7], replicated
- stem_gain_grad: float32 [64], replicated
- stem_bias_grad: float32 [64], replicated
- reduce_weight_grad: float32 [2048, 512], P('dp')
- reduce_gain_grad: float32 [512], replicated
- reduce_bias_grad: float32 [512], replicated
- spatial_weight_grad: float32 [4608, 512], P('dp')
- spatial_gain_grad: float32 [512], replicated
- spatial_bias_grad: float32 [512], replicated
- expand_weight_grad: float32 [512, 2048], P('dp')
- expand_gain_grad: float32 [2048], replicated
- expand_bias_grad: float32 [2048], replicated
- motion_weight_grad: float32 [2048, 512], P('dp')
- motion_gain_grad: float32 [512], replicated
- depth_weight_grad: float32 [2, 3, 3, 512], replicated
- excite_weight_grad: float32 [512, 2048], P('dp')
- excite_gain_grad: float32 [2048], replicated
- excite_bias_grad: float32 [2048], replicated
The draws below stay inside these ranges and needn't reach their ends.
Inputs may be any that keep to these rules, and one draw needn't show every extreme that they name: `seg_video`: never falls along a slot; each of the two videos has at least 3 of the slot's segments.
All inputs are finite; a program needn't handle non-finite values. No bound on the sum of `seg_valid` on one device may be relied on, other than what follows from the above.
Results may differ from the reference program's by a relative error of at most 0.018.
Values may be sent and summed in bfloat16 or wider, within the bound.
No kernel may reach another device: no remote copies, remote signals or barrier semaphores. Data moves between devices by JAX's collectives and lax.ppermute only.
A program may use at most 832 MiB of HBM per device.

```python
import math
import jax
import jax.numpy as jnp
import numpy as np
from jax import lax

C = 2048
MID = 512
STEMC = 64
SIDE = 224
FEAT = 7
SEG = 8
MICRO = 2
SLOT_MB = 1
STEM_SEG = 1
SLOTS = 64
ROWS = 25088
STEM_N = 256
N_DP = 32
N_PIPE = 4


def draw_frames(key, part):
    key = jax.random.fold_in(key, 11)
    shape = (STEM_N, 5, 3, SIDE, SIDE)
    position = jnp.arange(STEM_N, dtype=jnp.float32) / float(max(STEM_N - 1, 1))
    scale = 0.6 * jnp.power(3.0, position)
    values = jnp.clip(jax.random.normal(key, shape, jnp.float32), -4.0, 4.0)
    return (values * scale[:, None, None, None, None]).astype(jnp.bfloat16)


def set_ends(drawn, key, least, high):
    spot = [jax.random.randint(jax.random.fold_in(key, axis), (), 0, length) for axis, length in enumerate(drawn.shape)]
    longest = drawn.shape.index(max(drawn.shape))
    neighbour = spot[:longest] + [(spot[longest] + 1) % drawn.shape[longest]] + spot[longest + 1:]
    return drawn.at[tuple(spot)].set(least).at[tuple(neighbour)].set(high)


def block_levels(own_key, shape, cuts, least, largest):
    def one(dim, blocks):
        draws = jax.random.uniform(jax.random.fold_in(jax.random.fold_in(own_key, 6), dim), (blocks,), jnp.float32, least / len(cuts), largest / len(cuts))
        return jnp.repeat(jnp.exp(draws), shape[dim] // blocks).reshape((-1,) + (1,) * (len(shape) - dim - 1))

    level = one(*cuts[0])
    for cut in cuts[1:]:
        level = level * one(*cut)
    return level


def profile(amount, total, limit, slope):
    loads = [(1 << 20) // math.isqrt(grade ** slope) + 1 for grade in range(2, amount + 1)]
    rest, given = total - limit - (amount - 1), [1] * (amount - 1)
    while rest > 0:
        candidates = [i for i in range(amount - 1) if given[i] < limit]
        whole, left = sum([loads[i] for i in candidates]), rest
        for i in candidates:
            extra = min(limit - given[i], max(1, left * loads[i] // whole), rest)
            given[i] = given[i] + extra
            rest = rest - extra
    return np.array([limit] + given)


def ragged(stream_key, number_of, total, reach, slope):
    if number_of == 2:
        one = jax.random.randint(stream_key, (), max(1, total - reach), min(reach, total - 1) + 1)
        return jnp.stack([one, total - one])
    lengths = jnp.asarray(profile(number_of, total, reach, slope), jnp.int32)
    twos = (number_of - 1) // 2
    giver, sink = lengths[1:1 + 2 * twos:2], lengths[2:2 + 2 * twos:2]
    room = jnp.minimum(giver - 1, reach - sink)
    shifted = jax.random.randint(jax.random.fold_in(stream_key, 1), (twos,), 0, 1 << 20) % (room + 1)
    lengths = lengths.at[1:1 + 2 * twos:2].set(giver - shifted).at[2:2 + 2 * twos:2].set(sink + shifted)
    return lengths[jax.random.permutation(jax.random.fold_in(stream_key, 2), number_of)]


def bell_draw(rng, extent, scale, reach, cuts=(), held_as=jnp.bfloat16):
    level = block_levels(rng, extent, cuts, -0.22, 0.18) if cuts else 1.0
    values = jax.random.normal(rng, extent, jnp.float32) * scale * level
    return jnp.minimum(jnp.maximum(values, -reach), reach).astype(held_as)


def setup_inputs(seed: int = 0) -> dict:
    keys = jax.random.split(jax.random.key(seed), 26)
    features = bell_draw(keys[0], (ROWS, C), 1.0, 6.0, ((0, 32),))
    out_cotangent = bell_draw(keys[1], (ROWS, C), 1.0, 6.0, ((0, 32),))
    seg_valid = set_ends((jax.random.randint(keys[2], (SLOTS, SEG), 0, 8) < 7).astype(jnp.int32), jax.random.fold_in(keys[2], 1), 0, 1)
    seg_video = jax.vmap(lambda own: jnp.searchsorted(jnp.cumsum(ragged(own, 2, SEG, 5, 0)), jnp.arange(SEG), side="right"))(jax.random.split(keys[3], SLOTS)).reshape((SLOTS, SEG)).astype(jnp.int32)
    frames = draw_frames(jax.random.fold_in(keys[25], 71), 0)
    stem_cotangent = bell_draw(keys[5], (STEM_N, STEMC, SIDE // 4, SIDE // 4), 1.0, 6.0, ((0, 128),))
    stem_weight = bell_draw(keys[6], (STEMC, 3, 7, 7), 147 ** -0.5, 0.5)
    stem_diff_weight = bell_draw(keys[7], (STEMC, 12, 7, 7), 588 ** -0.5, 0.25)
    stem_gain = jnp.clip(1.0 + 0.1 * jax.random.normal(keys[8], (STEMC,), jnp.float32), 0.5, 1.5)
    stem_bias = bell_draw(keys[9], (STEMC,), 0.3, 1.5, (), jnp.float32)
    reduce_weight = bell_draw(keys[10], (C, MID), C ** -0.5, 0.125)
    reduce_gain = jnp.clip(1.0 + 0.1 * jax.random.normal(keys[11], (MID,), jnp.float32), 0.5, 1.5)
    reduce_bias = bell_draw(keys[12], (MID,), 0.3, 1.5, (), jnp.float32)
    spatial_weight = bell_draw(keys[13], (9 * MID, MID), (9 * MID) ** -0.5, 0.09375)
    spatial_gain = jnp.clip(1.0 + 0.1 * jax.random.normal(keys[14], (MID,), jnp.float32), 0.5, 1.5)
    spatial_bias = bell_draw(keys[15], (MID,), 0.3, 1.5, (), jnp.float32)
    expand_weight = bell_draw(keys[16], (MID, C), MID ** -0.5, 0.25)
    expand_gain = jnp.clip(1.0 + 0.1 * jax.random.normal(keys[17], (C,), jnp.float32), 0.5, 1.5)
    expand_bias = bell_draw(keys[18], (C,), 0.3, 1.5, (), jnp.float32)
    motion_weight = bell_draw(keys[19], (C, MID), C ** -0.5, 0.125)
    motion_gain = jnp.clip(1.0 + 0.1 * jax.random.normal(keys[20], (MID,), jnp.float32), 0.5, 1.5)
    depth_weight = bell_draw(keys[21], (2, 3, 3, MID), 9 ** -0.5, 2.0, (), jnp.float32)
    excite_weight = bell_draw(keys[22], (MID, C), MID ** -0.5, 0.25)
    excite_gain = jnp.clip(1.0 + 0.1 * jax.random.normal(keys[23], (C,), jnp.float32), 0.5, 1.5)
    excite_bias = bell_draw(keys[24], (C,), 0.3, 1.5, (), jnp.float32)
    return dict(features=features, out_cotangent=out_cotangent, seg_valid=seg_valid, seg_video=seg_video, frames=frames, stem_cotangent=stem_cotangent, stem_weight=stem_weight, stem_diff_weight=stem_diff_weight, stem_gain=stem_gain, stem_bias=stem_bias, reduce_weight=reduce_weight, reduce_gain=reduce_gain, reduce_bias=reduce_bias, spatial_weight=spatial_weight, spatial_gain=spatial_gain, spatial_bias=spatial_bias, expand_weight=expand_weight, expand_gain=expand_gain, expand_bias=expand_bias, motion_weight=motion_weight, motion_gain=motion_gain, depth_weight=depth_weight, excite_weight=excite_weight, excite_gain=excite_gain, excite_bias=excite_bias)


EPS = 1e-05
HIGH = lax.Precision.HIGHEST
PLANE = ('NCHW', 'OIHW', 'NCHW')
FIELD = ('NHWC', 'HWIO', 'NHWC')

@jax.custom_vjp
def low(v):
    return lax.optimization_barrier(v.astype(jnp.bfloat16)).astype(jnp.float32)

@jax.custom_vjp
def low_back(v):
    return v

def low_keep(v):
    return (low(v), None)

def low_pass(kept, grad):
    return (grad,)

def back_keep(v):
    return (v, None)

def back_low(kept, grad):
    return (low(grad),)
low.defvjp(low_keep, low_pass)
low_back.defvjp(back_keep, back_low)

def silu_of(values):
    return values * jax.nn.sigmoid(values)

def norm_over(values, axes, gain, bias):
    average = lax.optimization_barrier(jnp.mean(values, axis=axes, keepdims=True))
    square = lax.optimization_barrier(jnp.mean(values * values, axis=axes, keepdims=True))
    return (values - average) * lax.rsqrt(square - average * average + EPS) * gain + bias

def keep_pairs(valid_rows, video_rows):
    valid_float = valid_rows.astype(jnp.float32)
    same_video = (video_rows[:, 1:] == video_rows[:, :-1]).astype(jnp.float32)
    pair_keep = valid_float[:, 1:] * valid_float[:, :-1] * same_video
    return jnp.concatenate([pair_keep, jnp.zeros_like(pair_keep[:, :1])], axis=1)

def depth_apply(grid_in, kernel):
    padded = jnp.pad(grid_in, ((0, 0), (1, 1), (1, 1), (0, 0)))
    summed = jnp.zeros_like(grid_in)
    for row_off in range(3):
        for col_off in range(3):
            summed = summed + padded[:, row_off:row_off + FEAT, col_off:col_off + FEAT, :] * kernel[row_off, col_off]
    return summed

def motion_mix(reduced, keeping, depth_kernels):
    following = jnp.concatenate([reduced[:, 1:], jnp.zeros_like(reduced[:, :1])], axis=1)
    change = (following - reduced) * keeping[:, :, None, None, None]
    flat_grid = change.reshape(-1, FEAT, FEAT, change.shape[-1])
    average = jnp.full((3, 3, 1), 1.0 / 9.0, jnp.float32)
    mixed = depth_apply(flat_grid, depth_kernels[0]) + depth_apply(depth_apply(flat_grid, average), depth_kernels[1])
    return mixed.reshape(reduced.shape)

def stem_conv(centre_in, pooled_in, weight_a, weight_b):
    direct = lax.conv_general_dilated(centre_in, weight_a, (2, 2), ((3, 3), (3, 3)), dimension_numbers=PLANE, precision=HIGH)
    coarse = lax.conv_general_dilated(pooled_in, weight_b, (2, 2), ((3, 3), (3, 3)), dimension_numbers=PLANE, precision=HIGH)
    return direct + jnp.repeat(jnp.repeat(coarse, 2, axis=2), 2, axis=3)

def project(values, weight):
    return jnp.einsum('...c,ck->...k', values, weight, precision=HIGH)

def forward(params, feats, centre, pooled, keeping):
    stem_weight, stem_diff_weight, stem_gain, stem_bias, reduce_weight, reduce_gain, reduce_bias, spatial_weight, spatial_gain, spatial_bias, expand_weight, expand_gain, expand_bias, motion_weight, motion_gain, depth_weight, excite_weight, excite_gain, excite_bias = params
    half_side = SIDE // 2
    groups = N_DP * N_PIPE
    stem_raw = low_back(stem_conv(centre, low(pooled), stem_weight, stem_diff_weight))
    grouped = stem_raw.reshape(groups, MICRO, STEM_SEG, STEMC, half_side, half_side)
    stem_act = silu_of(norm_over(grouped, (0, 2, 4, 5), stem_gain[:, None, None], stem_bias[:, None, None]))
    stem_out = lax.optimization_barrier(jnp.mean(stem_act.reshape(groups, MICRO, STEM_SEG, STEMC, half_side // 2, 2, half_side // 2, 2), axis=(5, 7)))
    axes_norm = (0, 2, 3, 4, 5)
    pre_reduce = low_back(project(feats, reduce_weight))
    hidden_one = low(low_back(silu_of(norm_over(pre_reduce, axes_norm, reduce_gain, reduce_bias))))
    pre_spatial = lax.conv_general_dilated(hidden_one.reshape(-1, FEAT, FEAT, MID), spatial_weight.reshape(3, 3, MID, MID), (1, 1), ((1, 1), (1, 1)), dimension_numbers=FIELD, precision=HIGH)
    pre_spatial = low_back(pre_spatial.reshape(pre_reduce.shape))
    hidden_two = low(low_back(silu_of(norm_over(pre_spatial, axes_norm, spatial_gain, spatial_bias))))
    pre_expand = low_back(project(hidden_two, expand_weight))
    branch = low(low_back(norm_over(pre_expand, axes_norm, expand_gain, expand_bias)))
    pre_motion = low_back(project(feats, motion_weight))
    reduced = norm_over(pre_motion, axes_norm, motion_gain, jnp.float32(0.0))
    mixed = motion_mix(reduced.reshape(-1, SEG, FEAT, FEAT, MID), keeping.reshape(-1, SEG), depth_weight).reshape(reduced.shape)
    pre_excite = low_back(project(low(mixed), excite_weight))
    gate_value = jax.nn.sigmoid(norm_over(pre_excite, axes_norm, excite_gain, excite_bias))
    combined = branch + feats * gate_value
    return (stem_out, silu_of(combined))

def reference(features, out_cotangent, seg_valid, seg_video, frames, stem_cotangent, stem_weight, stem_diff_weight, stem_gain, stem_bias, reduce_weight, reduce_gain, reduce_bias, spatial_weight, spatial_gain, spatial_bias, expand_weight, expand_gain, expand_bias, motion_weight, motion_gain, depth_weight, excite_weight, excite_gain, excite_bias):
    params = tuple((item.astype(jnp.float32) for item in (stem_weight, stem_diff_weight, stem_gain, stem_bias, reduce_weight, reduce_gain, reduce_bias, spatial_weight, spatial_gain, spatial_bias, expand_weight, expand_gain, expand_bias, motion_weight, motion_gain, depth_weight, excite_weight, excite_gain, excite_bias)))
    feats = features.astype(jnp.float32).reshape(N_DP, MICRO, SLOT_MB, SEG, FEAT, FEAT, C)
    keeping = keep_pairs(seg_valid, seg_video)
    frames_float = frames.astype(jnp.float32)
    count_frames = frames.shape[0]
    centre = frames_float[:, 2]
    moved = (frames_float[:, 1:] - frames_float[:, :-1]).reshape(count_frames, 12, SIDE, SIDE)
    pooled = lax.optimization_barrier(jnp.mean(moved.reshape(count_frames, 12, SIDE // 2, 2, SIDE // 2, 2), axis=(3, 5)))

    def run_net(params_in, feats_in):
        return forward(params_in, feats_in, centre, pooled, keeping)
    outputs, pull_back = jax.vjp(run_net, params, feats)
    stem_seed = stem_cotangent.astype(jnp.float32).reshape(outputs[0].shape)
    main_seed = out_cotangent.astype(jnp.float32).reshape(outputs[1].shape)
    grad_params, grad_feats = pull_back((stem_seed, main_seed))
    result = outputs[1].reshape(-1, C).astype(jnp.bfloat16)
    features_grad = grad_feats.reshape(-1, C).astype(jnp.bfloat16)
    return (result, features_grad, grad_params[0], grad_params[1], grad_params[2], grad_params[3], grad_params[4], grad_params[5], grad_params[6], grad_params[7], grad_params[8], grad_params[9], grad_params[10], grad_params[11], grad_params[12], grad_params[13], grad_params[14], grad_params[15], grad_params[16], grad_params[17], grad_params[18])
```

```python
import functools

import jax
import jax.numpy as jnp
import numpy as np
from jax import lax
from jax.experimental import pallas as pl
from jax.experimental.pallas import tpu as pltpu
from jax.sharding import Mesh
from jax.sharding import PartitionSpec as P

C = 2048
MID = 512
STEMC = 64
SIDE = 224
FEAT = 7
SEG = 8
MICRO = 2
ROWS_MB = SEG * FEAT * FEAT
ROWS = MICRO * ROWS_MB
EPS = 1e-05
BF = jnp.bfloat16
F32 = jnp.float32
HIGH = lax.Precision.HIGHEST
NN = (((1,), (0,)), ((), ()))
NT = (((1,), (1,)), ((), ()))
TN = (((0,), (0,)), ((), ()))
GROUPS = 7
TILE = 256
VMEM = pl.BlockSpec(memory_space=pltpu.VMEM)


def dot(left, right, dims=NN, precision=None):
    return lax.dot_general(left, right, dims, precision=precision, preferred_element_type=F32)


def params(mib=50):
    return pltpu.CompilerParams(vmem_limit_bytes=mib * 2**20)


def cost(flops, nbytes):
    return pl.CostEstimate(flops=int(flops), bytes_accessed=int(nbytes), transcendentals=0)


def shape(dims, dtype=F32):
    return jax.ShapeDtypeStruct(dims, dtype)


def ring_sum(values, axis):
    size = lax.axis_size(axis)
    if size == 1:
        return values
    got = [
        lax.ppermute(values, axis, [(i, (i + step) % size) for i in range(size)])
        for step in range(1, size)
    ]
    if size == 2:
        return values + got[0]
    return (values + got[1]) + (got[0] + got[2])


def core_sum(values):
    pair = lax.all_gather(values, "c")
    return pair[0] + pair[1]


def sum_dp(values):
    return ring_sum(ring_sum(core_sum(values), "y"), "z")


def scatter_ring(blocks, axis):
    size = lax.axis_size(axis)
    me = lax.axis_index(axis)
    total = lax.dynamic_index_in_dim(blocks, me, 0, False).astype(F32)
    for step in range(1, size):
        outgoing = lax.dynamic_index_in_dim(blocks, (me + step) % size, 0, False)
        got = lax.ppermute(outgoing, axis, [(i, (i + step) % size) for i in range(size)])
        total = total + got.astype(F32)
    return total


def scatter_dp(blocks):
    for axis in ("c", "y", "z"):
        blocks = scatter_ring(blocks.astype(BF), axis)
    return lax.all_gather(blocks.astype(BF), "x").astype(F32)


def by_owner(partial, rows):
    count = partial.shape[0] // rows
    sizes = (lax.axis_size("z"), lax.axis_size("y"), lax.axis_size("c"))
    tiles = partial.shape[1] // 128
    cut = partial.reshape(*sizes, rows, tiles, 128)
    return cut.transpose(2, 1, 0, 4, 3, 5).reshape(
        sizes[2], sizes[1], sizes[0], tiles * rows, 128
    )


def stem_tables():
    half, quarter = SIDE // 2, SIDE // 4
    pool = np.zeros((SIDE, 128), np.float32)
    for column in range(SIDE):
        pool[column, column // 2] = 0.25
    fine = np.zeros((2, SIDE, 9 * 128), np.float32)
    coarse = np.zeros((2 * 128, 7 * 128), np.float32)
    for seg in range(2):
        for spot in range(quarter):
            for tap in range(9):
                column = 4 * spot + tap - 3
                if 0 <= column < SIDE:
                    fine[seg, column, tap * 128 + seg * 64 + spot] = 1
            for tap in range(7):
                column = 2 * spot + tap - 3
                if 0 <= column < half:
                    coarse[seg * 128 + column, tap * 128 + seg * 64 + spot] = 1
    sel_fine = np.zeros((8, 152, 432), np.float32)
    for up in range(2):
        for row in range(2):
            for col in range(2):
                for chan in range(3):
                    for dy in range(7):
                        for dx in range(7):
                            sel_fine[
                                up * 4 + row * 2 + col,
                                chan * 49 + dy * 7 + dx,
                                chan * 144 + (2 * col + dx) * 16 + 4 * up + 2 * row + dy,
                            ] = 1
    sel_coarse = np.zeros((4, 56, 128), np.float32)
    for up in range(4):
        for dy in range(7):
            for dx in range(7):
                sel_coarse[up, dy * 7 + dx, dx * 16 + 2 * up + dy] = 1
    lanes = np.zeros((8, 128), np.float32)
    lanes[0, :64] = 1
    lanes[1, 64:] = 1
    return [
        jnp.asarray(table, dtype)
        for table, dtype in (
            (pool, BF),
            (fine, BF),
            (coarse, BF),
            (sel_fine, BF),
            (sel_coarse, BF),
            (lanes, F32),
        )
    ]


def fine_patches(fine_ref, group):
    parts = []
    for pair in range(4):
        start = pl.multiple_of(32 * group + 8 * pair, 8)
        parts.append(
            jnp.concatenate(
                [
                    fine_ref[chan, pl.ds(start, 16), tap * 128 : (tap + 1) * 128]
                    for chan in range(3)
                    for tap in range(9)
                ],
                axis=0,
            )
        )
    return jnp.concatenate(parts, axis=1).astype(BF)


def coarse_patches(coarse_ref, group):
    parts = []
    blank = jnp.zeros((16, 128), F32)
    for quad in range(2):
        start = pl.multiple_of(16 * group + 8 * quad, 8)
        pieces = []
        for chan in range(12):
            for tap in range(7):
                pieces.append(coarse_ref[chan, pl.ds(start, 16), tap * 128 : (tap + 1) * 128])
            pieces.append(blank)
        parts.append(jnp.concatenate(pieces, axis=0))
    return jnp.concatenate(parts, axis=1).astype(BF)


def stem_forward(
    frames, weight, diff_weight, pool, fine_tab, coarse_tab, sel_fine, sel_coarse, lanes,
    raw_out, fine_out, coarse_out, sums_out,
    rows_ref, pooled_ref, wide_fine, wide_coarse, acc_ref,
):
    step = pl.program_id(0)

    @pl.when(step == 0)
    def prepare():
        for seg in range(2):

            @pl.loop(0, 3)
            def pool_channel(chan):
                before = dot(frames[seg, 0, chan], pool[...])
                for k in range(4):
                    after = dot(frames[seg, k + 1, chan], pool[...])
                    rows_ref[...] = after - before
                    before = after
                    small = rows_ref[pl.ds(0, SIDE // 2, 2), :] + rows_ref[pl.ds(1, SIDE // 2, 2), :]
                    pooled_ref[k * 3 + chan, :, seg * 128 : (seg + 1) * 128] = small.astype(BF)

        @pl.loop(0, 12)
        def spread_coarse(chan):
            coarse_out[chan, 0:8, :] = jnp.zeros((8, 7 * 128), F32)
            coarse_out[chan, 112:120, :] = jnp.zeros((8, 7 * 128), F32)
            coarse_out[chan, 3:115, :] = dot(pooled_ref[chan], coarse_tab[...])

        @pl.loop(0, 3)
        def spread_fine(chan):
            fine_out[chan, 0:8, :] = jnp.zeros((8, 9 * 128), F32)
            fine_out[chan, 224:232, :] = jnp.zeros((8, 9 * 128), F32)
            fine_out[chan, 3:227, :] = dot(frames[0, 2, chan], fine_tab[0]) + dot(
                frames[1, 2, chan], fine_tab[1]
            )

        for block in range(8):
            wide_fine[block * 64 : (block + 1) * 64, :] = dot(weight[...], sel_fine[block]).astype(BF)
        for up in range(4):
            for chan in range(12):
                wide_coarse[up * 64 : (up + 1) * 64, chan * 128 : (chan + 1) * 128] = dot(
                    diff_weight[chan], sel_coarse[up]
                ).astype(BF)
        acc_ref[...] = jnp.zeros_like(acc_ref)

    fine_sum = dot(wide_fine[...], fine_patches(fine_out, step))
    coarse_sum = dot(wide_coarse[...], coarse_patches(coarse_out, step))
    plain = acc_ref[0:64, :]
    square = acc_ref[64:128, :]
    for pair in range(4):
        for up in range(2):
            top = (2 * (pair % 2) + up) * 64
            left = (pair // 2) * 128
            lift = coarse_sum[top : top + 64, left : left + 128]
            for spot in range(4):
                row = (up * 4 + spot) * 64
                value = fine_sum[row : row + 64, pair * 128 : (pair + 1) * 128] + lift
                raw_out[0, row : row + 64, pair * 128 : (pair + 1) * 128] = value
                plain = plain + value
                square = square + value * value
    acc_ref[0:64, :] = plain
    acc_ref[64:128, :] = square

    @pl.when(step == GROUPS - 1)
    def finish():
        sums_out[...] = dot(lanes[...], acc_ref[...], NT, HIGH)


def stem_scales(totals, lanes, count):
    spread = dot(totals, lanes, TN, HIGH) * (1.0 / count)
    return spread[0:64, :], spread[64:128, :]


def stem_middle(
    raw, cotangent, totals, gain, bias, lanes, back_out, sums_out, cot_ref, coef_ref, acc_ref, *, count
):
    step = pl.program_id(0)

    @pl.when(step == 0)
    def prepare():
        average, square = stem_scales(totals[...], lanes[...], count)
        coef_ref[0] = average
        coef_ref[1] = lax.rsqrt(square - average * average + EPS)
        acc_ref[...] = jnp.zeros_like(acc_ref)

    blank = jnp.zeros((8, 64), F32)
    average = coef_ref[0]
    scale = coef_ref[1]
    plain = acc_ref[0:64, :]
    cross = acc_ref[64:128, :]
    for pair in range(4):
        for up in range(2):
            line = 8 * step + 2 * pair + up
            tall = jnp.concatenate(
                [cotangent[0, line].astype(F32), blank, cotangent[1, line].astype(F32), blank], axis=0
            )
            seed = jnp.transpose(tall) * 0.25
            for spot in range(4):
                row = (up * 4 + spot) * 64
                value = raw[0, row : row + 64, pair * 128 : (pair + 1) * 128]
                hat = (value - average) * scale
                act = hat * gain[...] + bias[...]
                sigma = jax.nn.sigmoid(act)
                back = seed * (sigma * (1.0 + act * (1.0 - sigma)))
                back_out[0, row : row + 64, pair * 128 : (pair + 1) * 128] = back
                plain = plain + back
                cross = cross + back * hat
    acc_ref[0:64, :] = plain
    acc_ref[64:128, :] = cross

    @pl.when(step == GROUPS - 1)
    def finish():
        sums_out[...] = dot(lanes[...], acc_ref[...], NT, HIGH)


def stem_backward(
    raw, back, fine_in, coarse_in, totals, back_totals, gain, sel_fine, sel_coarse, lanes,
    fine_grad, coarse_grad,
    coef_ref, draw_ref, small_ref, fine_acc, coarse_acc, *, count
):
    step = pl.program_id(0)

    @pl.when(step == 0)
    def prepare():
        average, square = stem_scales(totals[...], lanes[...], count)
        scale = lax.rsqrt(square - average * average + EPS)
        first, second = stem_scales(back_totals[...], lanes[...], count)
        coef_ref[0] = gain[...] * scale
        coef_ref[1] = -gain[...] * scale * scale * second
        coef_ref[2] = gain[...] * scale * (average * scale * second - first)
        fine_acc[...] = jnp.zeros_like(fine_acc)
        coarse_acc[...] = jnp.zeros_like(coarse_acc)

    for pair in range(4):
        for up in range(2):
            summed = None
            for spot in range(4):
                row = (up * 4 + spot) * 64
                cols = slice(pair * 128, (pair + 1) * 128)
                draw = (
                    back[0, row : row + 64, cols] * coef_ref[0]
                    + raw[0, row : row + 64, cols] * coef_ref[1]
                    + coef_ref[2]
                ).astype(BF)
                draw_ref[row : row + 64, cols] = draw
                wide = draw.astype(F32)
                summed = wide if summed is None else summed + wide
            top = (2 * (pair % 2) + up) * 64
            left = (pair // 2) * 128
            small_ref[top : top + 64, left : left + 128] = summed.astype(BF)
    fine_acc[...] += dot(draw_ref[...], fine_patches(fine_in, step), NT)
    coarse_acc[...] += dot(small_ref[...], coarse_patches(coarse_in, step), NT)

    @pl.when(step == GROUPS - 1)
    def finish():
        total = jnp.zeros((152, 64), F32)
        for block in range(8):
            total = total + dot(
                sel_fine[block].astype(F32), fine_acc[block * 64 : (block + 1) * 64, :], NT, HIGH
            )
        fine_grad[...] = total
        for duo in range(6):
            piece = jnp.zeros((56, 128), F32)
            for up in range(4):
                stacked = jnp.concatenate(
                    [
                        coarse_acc[up * 64 : (up + 1) * 64, chan * 128 : (chan + 1) * 128]
                        for chan in (2 * duo, 2 * duo + 1)
                    ],
                    axis=0,
                )
                piece = piece + dot(sel_coarse[up].astype(F32), stacked, NT, HIGH)
            coarse_grad[duo] = piece


def whole(*dims):
    return pl.BlockSpec(dims, lambda step, *rest: (0,) * len(dims))


def group_block():
    return pl.BlockSpec((1, 512, 512), lambda step: (step, 0, 0))


def stem_part(frames, stem_cotangent, stem_weight, stem_diff_weight, stem_gain, stem_bias):
    pool, fine_tab, coarse_tab, sel_fine, sel_coarse, lanes = stem_tables()
    count = float(
        lax.axis_size("z") * lax.axis_size("y") * lax.axis_size("c") * lax.axis_size("x")
    ) * (SIDE // 2) ** 2
    weight = jnp.pad(stem_weight.reshape(STEMC, 147), ((0, 0), (0, 5)))
    diff_weight = jnp.pad(
        stem_diff_weight.reshape(STEMC, 12, 49).transpose(1, 0, 2), ((0, 0), (0, 0), (0, 7))
    )
    raw, fine, coarse, sums = pl.pallas_call(
        stem_forward,
        grid=(GROUPS,),
        in_specs=[
            whole(2, 5, 3, SIDE, SIDE),
            whole(STEMC, 152),
            whole(12, STEMC, 56),
            whole(SIDE, 128),
            whole(2, SIDE, 1152),
            whole(256, 896),
            whole(8, 152, 432),
            whole(4, 56, 128),
            whole(8, 128),
        ],
        out_specs=[
            group_block(),
            whole(3, 232, 1152),
            whole(12, 120, 896),
            whole(8, 128),
        ],
        out_shape=[
            shape((GROUPS, 512, 512)),
            shape((3, 232, 1152)),
            shape((12, 120, 896)),
            shape((8, 128)),
        ],
        scratch_shapes=[
            pltpu.VMEM((SIDE, 128), F32),
            pltpu.VMEM((12, SIDE // 2, 256), BF),
            pltpu.VMEM((512, 432), BF),
            pltpu.VMEM((256, 1536), BF),
            pltpu.VMEM((128, 128), F32),
        ],
        compiler_params=params(),
        cost_estimate=cost(8e9, 2e7),
        name="stem_forward",
    )(frames, weight, diff_weight, pool, fine_tab, coarse_tab, sel_fine, sel_coarse, lanes)
    totals = ring_sum(sum_dp(sums), "x")
    gain = jnp.broadcast_to(stem_gain[:, None], (STEMC, 128))
    bias = jnp.broadcast_to(stem_bias[:, None], (STEMC, 128))
    cot = stem_cotangent.transpose(0, 2, 3, 1)
    back, back_sums = pl.pallas_call(
        functools.partial(stem_middle, count=count),
        grid=(GROUPS,),
        in_specs=[
            group_block(),
            whole(2, 56, 56, 64),
            whole(8, 128),
            whole(STEMC, 128),
            whole(STEMC, 128),
            whole(8, 128),
        ],
        out_specs=[group_block(), whole(8, 128)],
        out_shape=[shape((GROUPS, 512, 512)), shape((8, 128))],
        scratch_shapes=[
            pltpu.VMEM((8, 128), F32),
            pltpu.VMEM((2, 64, 128), F32),
            pltpu.VMEM((128, 128), F32),
        ],
        compiler_params=params(),
        cost_estimate=cost(8e9, 1.5e7),
        name="stem_middle",
    )(raw, cot, totals, gain, bias, lanes)
    back_totals = ring_sum(sum_dp(back_sums), "x")
    fine_grad, coarse_grad = pl.pallas_call(
        functools.partial(stem_backward, count=count),
        grid=(GROUPS,),
        in_specs=[
            group_block(),
            group_block(),
            whole(3, 232, 1152),
            whole(12, 120, 896),
            whole(8, 128),
            whole(8, 128),
            whole(STEMC, 128),
            whole(8, 152, 432),
            whole(4, 56, 128),
            whole(8, 128),
        ],
        out_specs=[whole(152, 64), whole(6, 56, 128)],
        out_shape=[shape((152, 64)), shape((6, 56, 128))],
        scratch_shapes=[
            pltpu.VMEM((3, 64, 128), F32),
            pltpu.VMEM((512, 512), BF),
            pltpu.VMEM((256, 256), BF),
            pltpu.VMEM((512, 432), F32),
            pltpu.VMEM((256, 1536), F32),
        ],
        compiler_params=params(),
        cost_estimate=cost(8e9, 2.5e7),
        name="stem_backward",
    )(raw, back, fine, coarse, totals, back_totals, gain, sel_fine, sel_coarse, lanes)
    packed = jnp.concatenate(
        [jnp.pad(fine_grad, ((0, 0), (0, 64))), coarse_grad.reshape(336, 128)], axis=0
    )
    packed = ring_sum(sum_dp(packed), "x")
    fine_sum = packed[:147, :64].reshape(3, 7, 7, STEMC).transpose(3, 0, 1, 2)
    coarse_sum = (
        packed[152:]
        .reshape(6, 56, 2, STEMC)[:, :49]
        .transpose(3, 0, 2, 1)
        .reshape(STEMC, 12, 7, 7)
    )
    both = back_totals[0] + back_totals[1]
    return fine_sum, coarse_sum, both[64:], both[:64]


def put_moments(out_ref, values, first=0):
    lines = []
    for micro in range(MICRO):
        part = values[micro * ROWS_MB : (micro + 1) * ROWS_MB]
        lines.append(jnp.sum(part, axis=0, keepdims=True))
        lines.append(jnp.sum(part * part, axis=0, keepdims=True))
    lines.append(jnp.zeros((4, values.shape[1]), F32))
    out_ref[...] = jnp.concatenate(lines, axis=0)


def moments(totals, micro, count):
    average = totals[2 * micro : 2 * micro + 1] * (1.0 / count)
    square = totals[2 * micro + 1 : 2 * micro + 2] * (1.0 / count)
    return average, lax.rsqrt(square - average * average + EPS)


def affine_of(totals, micro, count, gain, bias=None):
    average, scale = moments(totals, micro, count)
    slope = gain * scale
    shift = -average * slope
    return slope, shift if bias is None else shift + bias


def back_affine(totals, sums, micro, count, gain):
    average, scale = moments(totals, micro, count)
    first = sums[2 * micro : 2 * micro + 1] * (1.0 / count)
    second = sums[2 * micro + 1 : 2 * micro + 2] * (1.0 / count)
    on_grad = gain * scale
    on_value = -on_grad * scale * second
    return on_grad, on_value, -on_grad * first - on_value * average


def silu_slope(values):
    sigma = jax.nn.sigmoid(values)
    return sigma * (1.0 + values * (1.0 - sigma))


def first_matmuls(features, reduce_w, motion_w, reduce_out, motion_out, reduce_sum, motion_sum):
    value = dot(features[...], reduce_w[...])
    reduce_out[...] = value
    put_moments(reduce_sum, value)
    value = dot(features[...], motion_w[...])
    motion_out[...] = value
    put_moments(motion_sum, value)


def tap_mask(places, row_off, col_off):
    down = places[:, 0:128]
    right = places[:, 128:256]
    kept = None
    for value, off in ((down, row_off), (right, col_off)):
        if off:
            good = (value >= 1.0) if off < 0 else (value <= FEAT - 2.0)
            kept = good if kept is None else kept & good
    return None if kept is None else jnp.where(kept, 1.0, 0.0)


def tap_source(buffer, places, row_off, col_off, sign):
    move = sign * (7 * row_off + col_off)
    mask = tap_mask(places, sign * row_off, sign * col_off)
    value = buffer[8 + move : 8 + move + ROWS, :]
    if mask is not None:
        value = value * jnp.concatenate([mask] * (value.shape[1] // 128), axis=1)
    return value


def spatial_forward(
    pre_reduce, totals, gain, bias, places, weight, hidden_out, pre_out, sums_out, buffer, *, count
):
    buffer[0:8, :] = jnp.zeros((8, MID), F32)
    buffer[8 + ROWS : 16 + ROWS, :] = jnp.zeros((8, MID), F32)
    for micro in range(MICRO):
        rows = slice(micro * ROWS_MB, (micro + 1) * ROWS_MB)
        slope, shift = affine_of(totals[...], micro, count, gain[...], bias[...])
        value = pre_reduce[rows, :] * slope + shift
        buffer[8 + micro * ROWS_MB : 8 + (micro + 1) * ROWS_MB, :] = (
            (value * jax.nn.sigmoid(value)).astype(BF).astype(F32)
        )
    hidden_out[...] = buffer[8 : 8 + ROWS, :].astype(BF)
    for tap in range(9):
        row_off, col_off = tap // 3 - 1, tap % 3 - 1
        source = tap_source(buffer, places, row_off, col_off, 1).astype(BF)
        value = dot(source, weight[tap * MID : (tap + 1) * MID, :])
        if tap == 0:
            pre_out[...] = value
        else:
            pre_out[...] += value
    put_moments(sums_out, pre_out[...])


def expand_forward(pre_spatial, totals, gain, bias, weight, hidden_out, pre_out, sums_out, *, count):
    @pl.when(pl.program_id(0) == 0)
    def prepare():
        parts = []
        for micro in range(MICRO):
            slope, shift = affine_of(totals[...], micro, count, gain[...], bias[...])
            value = pre_spatial[micro * ROWS_MB : (micro + 1) * ROWS_MB, :] * slope + shift
            parts.append(value * jax.nn.sigmoid(value))
        hidden_out[...] = jnp.concatenate(parts, axis=0).astype(BF)

    value = dot(hidden_out[...], weight[...])
    pre_out[...] = value
    put_moments(sums_out, value)


def shifted(buffer, move):
    return buffer[64 + move : 64 + move + ROWS, :]


def column_shifts(buffer, places):
    left = shifted(buffer, -1) * tap_mask(places, 0, -1)
    right = shifted(buffer, 1) * tap_mask(places, 0, 1)
    return left, shifted(buffer, 0), right


def box_of(value, buffer, places):
    buffer[64 : 64 + ROWS, :] = value
    left, middle, right = column_shifts(buffer, places)
    buffer[64 : 64 + ROWS, :] = left + middle + right
    return (
        shifted(buffer, -7) * tap_mask(places, -1, 0)
        + shifted(buffer, 0)
        + shifted(buffer, 7) * tap_mask(places, 1, 0)
    ) * (1.0 / 9.0)


def change_of(pre_motion, coefs, keep, buffer, cols):
    for micro in range(MICRO):
        slope, shift = coefs[micro]
        buffer[64 + micro * ROWS_MB : 64 + (micro + 1) * ROWS_MB, :] = (
            pre_motion[micro * ROWS_MB : (micro + 1) * ROWS_MB, cols] * slope + shift
        )
    return (shifted(buffer, 49) - shifted(buffer, 0)) * keep[...]


def clear_margins(buffer):
    buffer[0:64, :] = jnp.zeros((64, 128), F32)
    buffer[64 + ROWS : 128 + ROWS, :] = jnp.zeros((64, 128), F32)


def motion_forward(
    pre_motion, totals, gain, keep, places, depth, weight, mixed_out, pre_out, sums_out, buffer, *, count
):
    @pl.when(pl.program_id(0) == 0)
    def prepare():
        clear_margins(buffer)

        @pl.loop(0, MID // 128)
        def one(tile):
            cols = pl.ds(pl.multiple_of(tile * 128, 128), 128)
            coefs = [
                affine_of(totals[:, cols], micro, count, gain[:, cols]) for micro in range(MICRO)
            ]
            change = change_of(pre_motion, coefs, keep, buffer, cols)
            buffer[64 : 64 + ROWS, :] = change
            near = column_shifts(buffer, places)
            average = box_of(change, buffer, places)
            buffer[64 : 64 + ROWS, :] = average
            wide = column_shifts(buffer, places)
            lines = []
            for row in range(3):
                line = None
                for col in range(3):
                    for scale, source in ((0, near), (1, wide)):
                        at = scale * 9 + row * 3 + col
                        term = source[col] * depth[at : at + 1, cols]
                        line = term if line is None else line + term
                lines.append(line)
            buffer[64 : 64 + ROWS, :] = lines[0]
            value = lines[1] + shifted(buffer, -7) * tap_mask(places, -1, 0)
            buffer[64 : 64 + ROWS, :] = lines[2]
            value = value + shifted(buffer, 7) * tap_mask(places, 1, 0)
            mixed_out[:, cols] = value.astype(BF)

    value = dot(mixed_out[...], weight[...])
    pre_out[...] = value
    put_moments(sums_out, value)


def gate_kernel(
    own, pre_expand, pre_excite, features, cotangent, expand_tot, excite_tot,
    expand_gain, expand_bias, excite_gain, excite_bias,
    result_out, direct_out, comb_out, gate_out, sums_out, *, count
):
    step = pl.program_id(0)
    for micro in range(MICRO):
        e_mean, e_scale = moments(expand_tot[...], micro, count)
        x_mean, x_scale = moments(excite_tot[...], micro, count)
        e_slope = expand_gain[...] * e_scale
        e_shift = expand_bias[...] - e_mean * e_slope
        x_slope = excite_gain[...] * x_scale
        x_shift = excite_bias[...] - x_mean * x_slope
        sums = [jnp.zeros((8, TILE), F32)] * 4
        for piece in range(7):
            at = micro * 7 + piece
            rows = slice(at * 56, (at + 1) * 56)
            pair = slice((at // 2) * 112, (at // 2 + 1) * 112)
            half = slice((at % 2) * 56, (at % 2 + 1) * 56)
            feats = features[pair, :].astype(F32)[half]
            seed = cotangent[pair, :].astype(F32)[half]
            pre_e = pre_expand[rows, :]
            pre_x = pre_excite[rows, :]
            branch = (pre_e * e_slope + e_shift).astype(BF).astype(F32)
            gate = jax.nn.sigmoid(pre_x * x_slope + x_shift)
            lifted = feats * gate
            combined = branch + lifted
            sigma = jax.nn.sigmoid(combined)
            output = combined * sigma
            grad = seed * (sigma + output * (1.0 - sigma))
            rounded = grad.astype(BF).astype(F32)
            grad_gate = grad * lifted * (1.0 - gate)
            comb_out[rows, :] = rounded
            gate_out[rows, :] = grad_gate

            @pl.when(step < MID // TILE)
            def store_own():
                result_out[rows, :] = output
                direct_out[rows, :] = grad * gate

            for spot, value in enumerate(
                (
                    rounded,
                    rounded * (pre_e - e_mean),
                    grad_gate,
                    grad_gate * (pre_x - x_mean),
                )
            ):
                sums[spot] = sums[spot] + jnp.sum(value.reshape(7, 8, TILE), axis=0)
        finals = [jnp.sum(value, axis=0, keepdims=True) for value in sums]
        sums_out[2 * micro : 2 * micro + 1, :] = finals[0]
        sums_out[2 * micro + 1 : 2 * micro + 2, :] = finals[1] * e_scale
        sums_out[4 + 2 * micro : 5 + 2 * micro, :] = finals[2]
        sums_out[5 + 2 * micro : 6 + 2 * micro, :] = finals[3] * x_scale


def put_grad_moments(out_ref, grad, value, totals, count):
    lines = []
    for micro in range(MICRO):
        rows = slice(micro * ROWS_MB, (micro + 1) * ROWS_MB)
        average, scale = moments(totals, micro, count)
        lines.append(jnp.sum(grad[rows], axis=0, keepdims=True))
        lines.append(jnp.sum(grad[rows] * (value[rows] - average), axis=0, keepdims=True) * scale)
    lines.append(jnp.zeros((4, grad.shape[1]), F32))
    out_ref[...] = jnp.concatenate(lines, axis=0)


def back_values(grad, value, totals, sums, gain, count):
    parts = []
    for micro in range(MICRO):
        rows = slice(micro * ROWS_MB, (micro + 1) * ROWS_MB)
        on_grad, on_value, constant = back_affine(totals, sums, micro, count, gain)
        parts.append(grad[rows] * on_grad + value[rows] * on_value + constant)
    return jnp.concatenate(parts, axis=0).astype(BF)


def activation_back(grad, value, totals, gain, bias, count):
    parts = []
    for micro in range(MICRO):
        rows = slice(micro * ROWS_MB, (micro + 1) * ROWS_MB)
        slope, shift = affine_of(totals, micro, count, gain, bias)
        parts.append(grad[rows] * silu_slope(value[rows] * slope + shift))
    return jnp.concatenate(parts, axis=0)


def expand_backward(
    own, grad, pre_expand, totals, sums, gain, weight, pre_spatial, s_totals, s_gain, s_bias,
    own_out, grad_out, sums_out, acc, *, count
):
    step = pl.program_id(0)
    value = back_values(
        grad[...], pre_expand[...], totals[...], sums[0:4, :], gain[...], count
    )

    @pl.when(step < MID // TILE)
    def store_own():
        own_out[...] = value

    part = dot(value, weight[...], NT)

    @pl.when(step == 0)
    def begin():
        acc[...] = part

    @pl.when(step > 0)
    def add():
        acc[...] += part

    @pl.when(step == C // TILE - 1)
    def finish():
        hidden = acc[...].astype(BF).astype(F32)
        back = activation_back(hidden, pre_spatial[...], s_totals[...], s_gain[...], s_bias[...], count)
        grad_out[...] = back
        put_grad_moments(sums_out, back, pre_spatial[...], s_totals[...], count)


def excite_backward(
    own, grad, pre_excite, totals, sums, gain, weight, pre_motion, m_totals, m_gain, keep, places, depth,
    own_out, grad_out, sums_out, depth_out, acc, buffer, *, count
):
    step = pl.program_id(0)
    value = back_values(
        grad[...], pre_excite[...], totals[...], sums[4:8, :], gain[...], count
    )

    @pl.when(step < MID // TILE)
    def store_own():
        own_out[...] = value

    part = dot(value, weight[...], NT)

    @pl.when(step == 0)
    def begin():
        acc[...] = part

    @pl.when(step > 0)
    def add():
        acc[...] += part

    @pl.when(step == C // TILE - 1)
    def finish():
        clear_margins(buffer)

        @pl.loop(0, MID // 128)
        def one(tile):
            cols = pl.ds(pl.multiple_of(tile * 128, 128), 128)
            coefs = [
                affine_of(m_totals[:, cols], micro, count, m_gain[:, cols]) for micro in range(MICRO)
            ]
            change = change_of(pre_motion, coefs, keep, buffer, cols)
            buffer[64 : 64 + ROWS, :] = change
            near = column_shifts(buffer, places)
            average = box_of(change, buffer, places)
            buffer[64 : 64 + ROWS, :] = average
            wide = column_shifts(buffer, places)
            grad_mixed = acc[:, cols]
            buffer[64 : 64 + ROWS, :] = grad_mixed
            lines = (
                shifted(buffer, 7) * tap_mask(places, 1, 0),
                grad_mixed,
                shifted(buffer, -7) * tap_mask(places, -1, 0),
            )
            pulled = []
            for scale, source in ((0, near), (1, wide)):
                terms = []
                for col in range(3):
                    term = None
                    for row in range(3):
                        at = scale * 9 + row * 3 + col
                        piece = lines[row] * depth[at : at + 1, cols]
                        term = piece if term is None else term + piece
                        depth_out[at : at + 1, cols] = jnp.sum(
                            lines[row] * source[col], axis=0, keepdims=True
                        )
                    terms.append(term)
                buffer[64 : 64 + ROWS, :] = terms[0]
                total = terms[1] + shifted(buffer, 1) * tap_mask(places, 0, 1)
                buffer[64 : 64 + ROWS, :] = terms[2]
                pulled.append(total + shifted(buffer, -1) * tap_mask(places, 0, -1))
            grad_change = (pulled[0] + box_of(pulled[1], buffer, places)) * keep[...]
            buffer[64 : 64 + ROWS, :] = grad_change
            grad_out[:, cols] = shifted(buffer, -49) - grad_change

        depth_out[18:24, :] = jnp.zeros((6, MID), F32)
        put_grad_moments(sums_out, grad_out[...], pre_motion[...], m_totals[...], count)


def spatial_backward(
    own, grad, pre_spatial, totals, sums, gain, places, weight, pre_reduce, r_totals, r_gain, r_bias,
    taps_out, grad_out, sums_out, buffer, source_ref, acc, *, count
):
    buffer[0:8, :] = jnp.zeros((8, MID), F32)
    buffer[8 + ROWS : 16 + ROWS, :] = jnp.zeros((8, MID), F32)
    buffer[8 : 8 + ROWS, :] = back_values(
        grad[...], pre_spatial[...], totals[...], sums[...], gain[...], count
    ).astype(F32)
    mine = pl.ds(pl.multiple_of(own[0] * 128, 128), 128)
    for tap in range(9):
        row_off, col_off = tap // 3 - 1, tap % 3 - 1
        source_ref[...] = tap_source(buffer, places, row_off, col_off, -1).astype(BF)
        taps_out[:, tap * 128 : (tap + 1) * 128] = source_ref[:, mine]
        value = dot(source_ref[...], weight[tap * MID : (tap + 1) * MID, :], NT)
        if tap == 0:
            acc[...] = value
        else:
            acc[...] += value
    hidden = acc[...].astype(BF).astype(F32)
    back = activation_back(hidden, pre_reduce[...], r_totals[...], r_gain[...], r_bias[...], count)
    grad_out[...] = back
    put_grad_moments(sums_out, back, pre_reduce[...], r_totals[...], count)


def motion_backward(
    own, grad, pre_motion, totals, sums, gain, weight, direct, own_out, part_out, value_ref, *, count
):
    value_ref[...] = back_values(
        grad[...], pre_motion[...], totals[...], sums[...], gain[...], count
    )
    own_out[...] = value_ref[:, pl.ds(pl.multiple_of(own[0] * 128, 128), 128)]
    part_out[...] = direct[...] + dot(value_ref[...], weight[...], NT)


def reduce_backward(
    own, grad, pre_reduce, totals, sums, gain, weight, part, own_out, grad_out, value_ref, *, count
):
    value_ref[...] = back_values(
        grad[...], pre_reduce[...], totals[...], sums[...], gain[...], count
    )
    own_out[...] = value_ref[:, pl.ds(pl.multiple_of(own[0] * 128, 128), 128)]
    grad_out[...] = (part[...] + dot(value_ref[...], weight[...], NT)).astype(BF)


def with_own(kernel, own, grid, in_specs, out_specs, out_shape, scratch, args, flops, nbytes, name, mib=50):
    return pl.pallas_call(
        kernel,
        grid_spec=pltpu.PrefetchScalarGridSpec(
            num_scalar_prefetch=1,
            grid=grid,
            in_specs=in_specs,
            out_specs=out_specs,
            scratch_shapes=scratch,
        ),
        out_shape=out_shape,
        compiler_params=params(mib),
        cost_estimate=cost(flops, nbytes),
        name=name,
    )(own, *args)


def place_table():
    rows = np.arange(ROWS)
    down = (rows % 49) // 7
    right = rows % 7
    return jnp.asarray(
        np.concatenate(
            [np.repeat(down[:, None], 128, 1), np.repeat(right[:, None], 128, 1)], axis=1
        ),
        F32,
    )


def keep_pairs(valid_rows, video_rows):
    valid_float = valid_rows.astype(F32)
    same_video = (video_rows[:, 1:] == video_rows[:, :-1]).astype(F32)
    pair_keep = valid_float[:, 1:] * valid_float[:, :-1] * same_video
    return jnp.concatenate([pair_keep, jnp.zeros_like(pair_keep[:, :1])], axis=1)


def on_device(
    features,
    out_cotangent,
    seg_valid,
    seg_video,
    frames,
    stem_cotangent,
    stem_weight,
    stem_diff_weight,
    stem_gain,
    stem_bias,
    reduce_weight,
    reduce_gain,
    reduce_bias,
    spatial_weight,
    spatial_gain,
    spatial_bias,
    expand_weight,
    expand_gain,
    expand_bias,
    motion_weight,
    motion_gain,
    depth_weight,
    excite_weight,
    excite_gain,
    excite_bias,
):
    count = float(lax.axis_size("z") * lax.axis_size("y") * lax.axis_size("c") * ROWS_MB)
    own = jnp.reshape(lax.axis_index("x"), (1,)).astype(jnp.int32)
    places = place_table()
    keep = jnp.broadcast_to(
        jnp.repeat(keep_pairs(seg_valid, seg_video).reshape(-1), FEAT * FEAT)[:, None], (ROWS, 128)
    )
    line = lambda vector: vector.reshape(1, -1)
    reduce_gain, reduce_bias = line(reduce_gain), line(reduce_bias)
    spatial_gain, spatial_bias = line(spatial_gain), line(spatial_bias)
    expand_gain, expand_bias = line(expand_gain), line(expand_bias)
    excite_gain, excite_bias = line(excite_gain), line(excite_bias)
    motion_gain = line(motion_gain)
    depth = jnp.pad(depth_weight.reshape(18, MID), ((0, 6), (0, 0)))

    column = lambda rows, width: pl.BlockSpec((rows, width), lambda step, *rest: (0, step))
    pre_reduce, pre_motion, reduce_sum, motion_sum = pl.pallas_call(
        first_matmuls,
        grid=(2,),
        in_specs=[whole(ROWS, C), column(C, 256), column(C, 256)],
        out_specs=[column(ROWS, 256), column(ROWS, 256), column(8, 256), column(8, 256)],
        out_shape=[shape((ROWS, MID)), shape((ROWS, MID)), shape((8, MID)), shape((8, MID))],
        compiler_params=params(),
        cost_estimate=cost(3.3e9, 1e7),
        name="first_matmuls",
    )(features, reduce_weight, motion_weight)
    first_tot = sum_dp(jnp.concatenate([reduce_sum[:4], motion_sum[:4]], axis=0))
    reduce_tot, motion_tot = first_tot[:4], first_tot[4:]

    hidden_one, pre_spatial, spatial_sum = pl.pallas_call(
        functools.partial(spatial_forward, count=count),
        in_specs=[VMEM] * 6,
        out_specs=[VMEM] * 3,
        out_shape=[shape((ROWS, MID), BF), shape((ROWS, MID)), shape((8, MID))],
        scratch_shapes=[pltpu.VMEM((ROWS + 16, MID), F32)],
        compiler_params=params(),
        cost_estimate=cost(3.7e9, 8e6),
        name="spatial_forward",
    )(pre_reduce, reduce_tot, reduce_gain, reduce_bias, places, spatial_weight)
    spatial_tot = sum_dp(spatial_sum)

    mixed, pre_excite, excite_sum = pl.pallas_call(
        functools.partial(motion_forward, count=count),
        grid=(4,),
        in_specs=[
            whole(ROWS, MID), whole(4, MID), whole(1, MID), whole(ROWS, 128), whole(ROWS, 256),
            whole(24, MID), column(MID, 512),
        ],
        out_specs=[whole(ROWS, MID), column(ROWS, 512), column(8, 512)],
        out_shape=[shape((ROWS, MID), BF), shape((ROWS, C)), shape((8, C))],
        scratch_shapes=[pltpu.VMEM((ROWS + 128, 128), F32)],
        compiler_params=params(),
        cost_estimate=cost(4e9, 1.2e7),
        name="motion_forward",
    )(pre_motion, motion_tot, motion_gain, keep, places, depth, excite_weight)
    excite_tot = sum_dp(excite_sum)

    hidden_two, pre_expand, expand_sum = pl.pallas_call(
        functools.partial(expand_forward, count=count),
        grid=(4,),
        in_specs=[
            whole(ROWS, MID), whole(8, MID), whole(1, MID), whole(1, MID), column(MID, 512),
        ],
        out_specs=[whole(ROWS, MID), column(ROWS, 512), column(8, 512)],
        out_shape=[shape((ROWS, MID), BF), shape((ROWS, C)), shape((8, C))],
        compiler_params=params(),
        cost_estimate=cost(1.7e9, 1e7),
        name="expand_forward",
    )(pre_spatial, spatial_tot, spatial_gain, spatial_bias, expand_weight)
    expand_tot = sum_dp(expand_sum)

    tiles = C // TILE
    mine = MID // TILE

    def rotated(rows):
        return pl.BlockSpec(
            (rows, TILE), lambda step, own_ref: (0, lax.rem(step + own_ref[0] * mine, tiles))
        )

    def kept(rows):
        return pl.BlockSpec((rows, TILE), lambda step, own_ref: (0, jnp.minimum(step, mine - 1)))

    result, direct, grad_comb, grad_gate, gate_sum = with_own(
        functools.partial(gate_kernel, count=count),
        own,
        (tiles,),
        [rotated(ROWS)] * 4 + [rotated(8), rotated(8)] + [rotated(1)] * 4,
        [kept(ROWS), kept(ROWS), rotated(ROWS), rotated(ROWS), rotated(8)],
        [shape((ROWS, MID)), shape((ROWS, MID)), shape((ROWS, C)), shape((ROWS, C)), shape((8, C))],
        [],
        (
            pre_expand, pre_excite, features, out_cotangent, expand_tot, excite_tot,
            expand_gain, expand_bias, excite_gain, excite_bias,
        ),
        3e9,
        3e7,
        "gate",
    )
    gate_tot = sum_dp(gate_sum)

    expand_own, grad_spatial, spatial_back = with_own(
        functools.partial(expand_backward, count=count),
        own,
        (tiles,),
        [
            rotated(ROWS), rotated(ROWS), rotated(8), rotated(8), rotated(1), rotated(MID),
            whole(ROWS, MID), whole(8, MID), whole(1, MID), whole(1, MID),
        ],
        [kept(ROWS), whole(ROWS, MID), whole(8, MID)],
        [shape((ROWS, MID), BF), shape((ROWS, MID)), shape((8, MID))],
        [pltpu.VMEM((ROWS, MID), F32)],
        (
            grad_comb, pre_expand, expand_tot, gate_tot, expand_gain, expand_weight,
            pre_spatial, spatial_tot, spatial_gain, spatial_bias,
        ),
        2e9,
        2e7,
        "expand_backward",
    )
    spatial_back_tot = sum_dp(spatial_back)

    excite_own, grad_reduced, motion_back, depth_part = with_own(
        functools.partial(excite_backward, count=count),
        own,
        (tiles,),
        [
            rotated(ROWS), rotated(ROWS), rotated(8), rotated(8), rotated(1), rotated(MID),
            whole(ROWS, MID), whole(4, MID), whole(1, MID), whole(ROWS, 128), whole(ROWS, 256),
            whole(24, MID),
        ],
        [kept(ROWS), whole(ROWS, MID), whole(8, MID), whole(24, MID)],
        [shape((ROWS, MID), BF), shape((ROWS, MID)), shape((8, MID)), shape((24, MID))],
        [pltpu.VMEM((ROWS, MID), F32), pltpu.VMEM((ROWS + 128, 128), F32)],
        (
            grad_gate, pre_excite, excite_tot, gate_tot, excite_gain, excite_weight,
            pre_motion, motion_tot, motion_gain, keep, places, depth,
        ),
        4e9,
        2e7,
        "excite_backward",
    )
    motion_back_all = sum_dp(jnp.concatenate([motion_back, depth_part], axis=0))
    motion_back_tot = motion_back_all[:8]
    depth_grad = motion_back_all[8:26].reshape(2, 3, 3, MID)

    taps, grad_reduce, reduce_back = with_own(
        functools.partial(spatial_backward, count=count),
        own,
        (1,),
        [
            whole(ROWS, MID), whole(ROWS, MID), whole(8, MID), whole(8, MID), whole(1, MID),
            whole(ROWS, 256), whole(9 * MID, MID), whole(ROWS, MID), whole(4, MID),
            whole(1, MID), whole(1, MID),
        ],
        [whole(ROWS, 9 * 128), whole(ROWS, MID), whole(8, MID)],
        [shape((ROWS, 9 * 128), BF), shape((ROWS, MID)), shape((8, MID))],
        [
            pltpu.VMEM((ROWS + 16, MID), F32),
            pltpu.VMEM((ROWS, MID), BF),
            pltpu.VMEM((ROWS, MID), F32),
        ],
        (
            grad_spatial, pre_spatial, spatial_tot, spatial_back_tot, spatial_gain, places,
            spatial_weight, pre_reduce, reduce_tot, reduce_gain, reduce_bias,
        ),
        4e9,
        1.2e7,
        "spatial_backward",
    )
    reduce_back_tot = sum_dp(reduce_back)

    own_rows = pl.BlockSpec((MID, MID), lambda step, own_ref: (own_ref[0], 0))
    motion_own, part = with_own(
        functools.partial(motion_backward, count=count),
        own,
        (1,),
        [
            whole(ROWS, MID), whole(ROWS, MID), whole(4, MID), whole(8, MID), whole(1, MID),
            own_rows, whole(ROWS, MID),
        ],
        [whole(ROWS, 128), whole(ROWS, MID)],
        [shape((ROWS, 128), BF), shape((ROWS, MID))],
        [pltpu.VMEM((ROWS, MID), BF)],
        (grad_reduced, pre_motion, motion_tot, motion_back_tot, motion_gain, motion_weight, direct),
        5e8,
        8e6,
        "motion_backward",
    )
    reduce_own, features_grad = with_own(
        functools.partial(reduce_backward, count=count),
        own,
        (1,),
        [
            whole(ROWS, MID), whole(ROWS, MID), whole(4, MID), whole(8, MID), whole(1, MID),
            own_rows, whole(ROWS, MID),
        ],
        [whole(ROWS, 128), whole(ROWS, MID)],
        [shape((ROWS, 128), BF), shape((ROWS, MID), BF)],
        [pltpu.VMEM((ROWS, MID), BF)],
        (grad_reduce, pre_reduce, reduce_tot, reduce_back_tot, reduce_gain, reduce_weight, part),
        5e8,
        8e6,
        "reduce_backward",
    )

    owners = lax.axis_size("z") * lax.axis_size("y") * lax.axis_size("c")
    across = lambda left, right: dot(left, right, TN).astype(BF)
    expand_part = across(hidden_two, expand_own)
    excite_part = across(mixed, excite_own)
    spatial_part = (
        across(hidden_one, taps).reshape(MID, 9, 128).transpose(1, 0, 2).reshape(9 * MID, 128)
    )
    motion_part = across(features, motion_own)
    reduce_part = across(features, reduce_own)

    early = scatter_dp(
        jnp.concatenate(
            [by_owner(expand_part, MID // owners), by_owner(excite_part, MID // owners)], axis=3
        )
    )
    middle = scatter_dp(
        jnp.concatenate(
            [by_owner(spatial_part, 9 * MID // owners), by_owner(motion_part, C // owners)], axis=3
        )
    )
    late = scatter_dp(by_owner(reduce_part, C // owners))

    def wide_rows(gathered):
        rows = MID // owners
        return gathered.reshape(-1, 4, rows, 128).transpose(2, 0, 1, 3).reshape(rows, C)

    def narrow_rows(gathered):
        return gathered.transpose(1, 0, 2).reshape(gathered.shape[1], MID)

    first = 4 * (MID // owners)
    expand_grad = wide_rows(early[:, :first])
    excite_grad = wide_rows(early[:, first:])
    cut = 9 * MID // owners
    spatial_grad = narrow_rows(middle[:, :cut])
    motion_grad = narrow_rows(middle[:, cut:])
    reduce_grad = narrow_rows(late)

    stem_weight_grad, stem_diff_grad, stem_gain_grad, stem_bias_grad = stem_part(
        frames, stem_cotangent, stem_weight, stem_diff_weight, stem_gain, stem_bias
    )
    gain_of = lambda totals, at=0: totals[at + 1] + totals[at + 3]
    bias_of = lambda totals, at=0: totals[at] + totals[at + 2]
    return (
        result.astype(BF),
        features_grad,
        stem_weight_grad,
        stem_diff_grad,
        stem_gain_grad,
        stem_bias_grad,
        reduce_grad,
        gain_of(reduce_back_tot),
        bias_of(reduce_back_tot),
        spatial_grad,
        gain_of(spatial_back_tot),
        bias_of(spatial_back_tot),
        expand_grad,
        gain_of(gate_tot),
        bias_of(gate_tot),
        motion_grad,
        gain_of(motion_back_tot),
        depth_grad,
        excite_grad,
        gain_of(gate_tot, 4),
        bias_of(gate_tot, 4),
    )


def solution(mesh):
    grid = Mesh(mesh.devices.reshape(4, 4, 2, 4), ("z", "y", "c", "x"))
    clips = ("z", "y", "c")
    everyone = ("z", "y", "c", "x")
    split = P(clips, None)
    copied = P()
    return jax.shard_map(
        on_device,
        mesh=grid,
        in_specs=(split,) * 4
        + (P(everyone, None, None, None, None), P(everyone, None, None, None))
        + (copied,) * 19,
        out_specs=(P(clips, "x"), P(clips, "x"))
        + (copied,) * 4
        + (split, copied, copied) * 3
        + (split, copied, copied)
        + (split, copied, copied),
        check_vma=False,
    )
```

```python
import functools

import jax
import jax.numpy as jnp
import numpy as np
from jax import lax
from jax.experimental import pallas as pl
from jax.experimental.pallas import tpu as pltpu
from jax.sharding import Mesh
from jax.sharding import PartitionSpec as P

C = 2048
MID = 512
STEMC = 64
SIDE = 224
FEAT = 7
SEG = 8
MICRO = 2
ROWS = SEG * FEAT * FEAT
EPS = 1e-05
BF = jnp.bfloat16
F32 = jnp.float32
HIGH = lax.Precision.HIGHEST
NN = (((1,), (0,)), ((), ()))
NT = (((1,), (1,)), ((), ()))
TN = (((0,), (0,)), ((), ()))
GROUPS = 7
TILE = 256
VMEM = pl.BlockSpec(memory_space=pltpu.VMEM)
PIECES = ((0, 112), (112, 112), (224, 112), (336, 56))


def sigmoid(values):
    return 0.5 + 0.5 * jnp.tanh(0.5 * values)


def dot(left, right, dims=NN, precision=None):
    return lax.dot_general(left, right, dims, precision=precision, preferred_element_type=F32)


def params(mib=50):
    return pltpu.CompilerParams(vmem_limit_bytes=mib * 2**20)


def cost(flops, nbytes):
    return pl.CostEstimate(flops=int(flops), bytes_accessed=int(nbytes), transcendentals=0)


def shape(dims, dtype=F32):
    return jax.ShapeDtypeStruct(dims, dtype)


def ring_sum(values, axis):
    size = lax.axis_size(axis)
    if size == 1:
        return values
    got = [
        lax.ppermute(values, axis, [(i, (i + step) % size) for i in range(size)])
        for step in range(1, size)
    ]
    if size == 2:
        return values + got[0]
    return (values + got[1]) + (got[0] + got[2])


def core_sum(values):
    pair = lax.all_gather(values, "c")
    return pair[0] + pair[1]


def sum_dp(values):
    return ring_sum(ring_sum(core_sum(values), "y"), "z")


def scatter_ring(blocks, axis, dim, kind):
    size = lax.axis_size(axis)
    me = lax.axis_index(axis)
    total = lax.dynamic_index_in_dim(blocks, me, dim, False).astype(F32)
    for step in range(1, size):
        outgoing = lax.dynamic_index_in_dim(blocks, (me + step) % size, dim, False)
        got = lax.ppermute(outgoing, axis, [(i, (i + step) % size) for i in range(size)])
        total = total + got.astype(F32)
    return total.astype(kind)


def scatter_dp(partial):
    sizes = [lax.axis_size(axis) for axis in ("z", "y", "c")]
    rows = partial.shape[0] // (sizes[0] * sizes[1] * sizes[2])
    blocks = partial.reshape(*sizes, rows, partial.shape[1])
    for axis, dim in (("c", 2), ("y", 1), ("z", 0)):
        blocks = scatter_ring(blocks, axis, dim, partial.dtype)
    return blocks


def from_peer(values, flip):
    size = lax.axis_size("x")
    return lax.ppermute(values, "x", [(i, i ^ flip) for i in range(size)])


def gather_x(block):
    return [block] + [from_peer(block, flip) for flip in (1, 2, 3)]


def merge_sum(*pieces):
    wide = jnp.concatenate(pieces, axis=1)
    total = sum_dp(wide)
    ends = np.cumsum([piece.shape[1] for piece in pieces])
    return [total[:, end - piece.shape[1] : end] for end, piece in zip(ends, pieces)]


def stem_tables():
    half, quarter = SIDE // 2, SIDE // 4
    pool = np.zeros((SIDE, 128), np.float32)
    for column in range(SIDE):
        pool[column, column // 2] = 0.25
    fine = np.zeros((2, SIDE, 9 * 128), np.float32)
    coarse = np.zeros((2 * 128, 7 * 128), np.float32)
    for seg in range(2):
        for spot in range(quarter):
            for tap in range(9):
                column = 4 * spot + tap - 3
                if 0 <= column < SIDE:
                    fine[seg, column, tap * 128 + seg * 64 + spot] = 1
            for tap in range(7):
                column = 2 * spot + tap - 3
                if 0 <= column < half:
                    coarse[seg * 128 + column, tap * 128 + seg * 64 + spot] = 1
    sel_fine = np.zeros((8, 168, 432), np.float32)
    for up in range(2):
        for row in range(2):
            for col in range(2):
                for chan in range(3):
                    for dy in range(7):
                        for dx in range(7):
                            sel_fine[
                                up * 4 + row * 2 + col,
                                chan * 56 + dy * 8 + dx,
                                chan * 144 + (2 * col + dx) * 16 + 4 * up + 2 * row + dy,
                            ] = 1
    sel_coarse = np.zeros((4, 56, 128), np.float32)
    for up in range(4):
        for dy in range(7):
            for dx in range(7):
                sel_coarse[up, dy * 8 + dx, dx * 16 + 2 * up + dy] = 1
    lanes = np.zeros((8, 128), np.float32)
    lanes[0, :64] = 1
    lanes[1, 64:] = 1
    return [
        jnp.asarray(table, dtype)
        for table, dtype in (
            (pool, BF),
            (fine, BF),
            (coarse, BF),
            (sel_fine, BF),
            (sel_coarse, BF),
            (lanes, F32),
        )
    ]


def fine_patches(fine_ref, group):
    parts = []
    for pair in range(4):
        start = pl.multiple_of(32 * group + 8 * pair, 8)
        parts.append(
            jnp.concatenate(
                [
                    fine_ref[chan, pl.ds(start, 16), tap * 128 : (tap + 1) * 128]
                    for chan in range(3)
                    for tap in range(9)
                ],
                axis=0,
            )
        )
    return jnp.concatenate(parts, axis=1).astype(BF)


def coarse_patches(coarse_ref, group):
    parts = []
    blank = jnp.zeros((16, 128), F32)
    for quad in range(2):
        start = pl.multiple_of(16 * group + 8 * quad, 8)
        pieces = []
        for chan in range(12):
            for tap in range(7):
                pieces.append(coarse_ref[chan, pl.ds(start, 16), tap * 128 : (tap + 1) * 128])
            pieces.append(blank)
        parts.append(jnp.concatenate(pieces, axis=0))
    return jnp.concatenate(parts, axis=1).astype(BF)


def stem_forward(
    frames, weight, diff_weight, pool, fine_tab, coarse_tab, sel_fine, sel_coarse, lanes, after,
    raw_out, fine_out, coarse_out, sums_out,
    rows_ref, pooled_ref, wide_fine, wide_coarse, acc_ref, flat_ref,
):
    step = pl.program_id(0)

    @pl.when(step == 0)
    def prepare():
        for seg in range(2):

            @pl.loop(0, 3)
            def pool_channel(chan):
                before = dot(frames[seg, 0, chan], pool[...])
                for k in range(4):
                    after = dot(frames[seg, k + 1, chan], pool[...])
                    rows_ref[...] = after - before
                    before = after
                    small = rows_ref[pl.ds(0, SIDE // 2, 2), :] + rows_ref[pl.ds(1, SIDE // 2, 2), :]
                    pooled_ref[k * 3 + chan, :, seg * 128 : (seg + 1) * 128] = small.astype(BF)

        @pl.loop(0, 12)
        def spread_coarse(chan):
            coarse_out[chan, 0:8, :] = jnp.zeros((8, 7 * 128), F32)
            coarse_out[chan, 112:120, :] = jnp.zeros((8, 7 * 128), F32)
            coarse_out[chan, 3:115, :] = dot(pooled_ref[chan], coarse_tab[...])

        @pl.loop(0, 3)
        def spread_fine(chan):
            fine_out[chan, 0:8, :] = jnp.zeros((8, 9 * 128), F32)
            fine_out[chan, 224:232, :] = jnp.zeros((8, 9 * 128), F32)
            fine_out[chan, 3:227, :] = dot(frames[0, 2, chan], fine_tab[0]) + dot(
                frames[1, 2, chan], fine_tab[1]
            )

        flat_ref[...] = jnp.zeros_like(flat_ref)
        for chan in range(3):
            for row in range(7):
                at = chan * 56 + row * 8
                flat_ref[at : at + 7, :] = weight[chan, row].astype(F32)
        for chan in range(12):
            for row in range(7):
                at = 168 + chan * 56 + row * 8
                flat_ref[at : at + 7, :] = diff_weight[chan, row].astype(F32)
        narrow = jnp.transpose(flat_ref[0:168, :]).astype(BF)
        for block in range(8):
            wide_fine[block * 64 : (block + 1) * 64, :] = dot(narrow, sel_fine[block]).astype(BF)
        for chan in range(12):
            narrow = jnp.transpose(flat_ref[168 + chan * 56 : 224 + chan * 56, :]).astype(BF)
            for up in range(4):
                wide_coarse[up * 64 : (up + 1) * 64, chan * 128 : (chan + 1) * 128] = dot(
                    narrow, sel_coarse[up]
                ).astype(BF)
        acc_ref[...] = jnp.zeros_like(acc_ref)

    fine_sum = dot(wide_fine[...], fine_patches(fine_out, step))
    coarse_sum = dot(wide_coarse[...], coarse_patches(coarse_out, step))
    plain = acc_ref[0:64, :]
    square = acc_ref[64:128, :]
    for pair in range(4):
        for up in range(2):
            top = (2 * (pair % 2) + up) * 64
            left = (pair // 2) * 128
            lift = coarse_sum[top : top + 64, left : left + 128]
            for spot in range(4):
                row = (up * 4 + spot) * 64
                value = fine_sum[row : row + 64, pair * 128 : (pair + 1) * 128] + lift
                raw_out[0, row : row + 64, pair * 128 : (pair + 1) * 128] = value
                plain = plain + value
                square = square + value * value
    acc_ref[0:64, :] = plain
    acc_ref[64:128, :] = square

    @pl.when(step == GROUPS - 1)
    def finish():
        sums_out[...] = dot(lanes[...], acc_ref[...], NT, HIGH)


def stem_scales(totals, lanes, count):
    spread = dot(totals, lanes, TN, HIGH) * (1.0 / count)
    return spread[0:64, :], spread[64:128, :]


def stem_middle(
    raw, cotangent, totals, gain, bias, lanes, back_out, sums_out, cot_ref, coef_ref, acc_ref, *, count
):
    step = pl.program_id(0)

    @pl.when(step == 0)
    def prepare():
        average, square = stem_scales(totals[...], lanes[...], count)
        coef_ref[0] = average
        coef_ref[1] = lax.rsqrt(square - average * average + EPS)
        acc_ref[...] = jnp.zeros_like(acc_ref)

    blank = jnp.zeros((8, 64), F32)
    average = coef_ref[0]
    scale = coef_ref[1]
    plain = acc_ref[0:64, :]
    cross = acc_ref[64:128, :]
    for pair in range(4):
        for up in range(2):
            line = 8 * step + 2 * pair + up
            tall = jnp.concatenate(
                [cotangent[0, line].astype(F32), blank, cotangent[1, line].astype(F32), blank], axis=0
            )
            seed = jnp.transpose(tall) * 0.25
            for spot in range(4):
                row = (up * 4 + spot) * 64
                value = raw[0, row : row + 64, pair * 128 : (pair + 1) * 128]
                hat = (value - average) * scale
                act = hat * gain[...] + bias[...]
                sigma = sigmoid(act)
                back = seed * (sigma * (1.0 + act * (1.0 - sigma)))
                back_out[0, row : row + 64, pair * 128 : (pair + 1) * 128] = back
                plain = plain + back
                cross = cross + back * hat
    acc_ref[0:64, :] = plain
    acc_ref[64:128, :] = cross

    @pl.when(step == GROUPS - 1)
    def finish():
        sums_out[...] = dot(lanes[...], acc_ref[...], NT, HIGH)


def stem_backward(
    raw, back, fine_in, coarse_in, totals, back_totals, gain, sel_fine, sel_coarse, lanes,
    packed,
    coef_ref, draw_ref, small_ref, fine_acc, coarse_acc, *, count
):
    step = pl.program_id(0)

    @pl.when(step == 0)
    def prepare():
        average, square = stem_scales(totals[...], lanes[...], count)
        scale = lax.rsqrt(square - average * average + EPS)
        first, second = stem_scales(back_totals[...], lanes[...], count)
        coef_ref[0] = gain[...] * scale
        coef_ref[1] = -gain[...] * scale * scale * second
        coef_ref[2] = gain[...] * scale * (average * scale * second - first)
        fine_acc[...] = jnp.zeros_like(fine_acc)
        coarse_acc[...] = jnp.zeros_like(coarse_acc)

    for pair in range(4):
        for up in range(2):
            summed = None
            for spot in range(4):
                row = (up * 4 + spot) * 64
                cols = slice(pair * 128, (pair + 1) * 128)
                draw = (
                    back[0, row : row + 64, cols] * coef_ref[0]
                    + raw[0, row : row + 64, cols] * coef_ref[1]
                    + coef_ref[2]
                ).astype(BF)
                draw_ref[row : row + 64, cols] = draw
                wide = draw.astype(F32)
                summed = wide if summed is None else summed + wide
            top = (2 * (pair % 2) + up) * 64
            left = (pair // 2) * 128
            small_ref[top : top + 64, left : left + 128] = summed.astype(BF)
    fine_acc[...] += dot(draw_ref[...], fine_patches(fine_in, step), NT)
    coarse_acc[...] += dot(small_ref[...], coarse_patches(coarse_in, step), NT)

    @pl.when(step == GROUPS - 1)
    def finish():
        total = jnp.zeros((168, 64), F32)
        for block in range(8):
            total = total + dot(
                sel_fine[block].astype(F32), fine_acc[block * 64 : (block + 1) * 64, :], NT, HIGH
            )
        packed[0:168, 0:64] = total
        packed[0:168, 64:128] = jnp.zeros((168, 64), F32)
        for duo in range(6):
            piece = jnp.zeros((56, 128), F32)
            for up in range(4):
                stacked = jnp.concatenate(
                    [
                        coarse_acc[up * 64 : (up + 1) * 64, chan * 128 : (chan + 1) * 128]
                        for chan in (2 * duo, 2 * duo + 1)
                    ],
                    axis=0,
                )
                piece = piece + dot(sel_coarse[up].astype(F32), stacked, NT, HIGH)
            packed[168 + duo * 56 : 224 + duo * 56, :] = piece
        packed[504:512, :] = jnp.zeros((8, 128), F32)


def whole(*dims):
    return pl.BlockSpec(dims, lambda step, *rest: (0,) * len(dims))


def group_block():
    return pl.BlockSpec((1, 512, 512), lambda step: (step, 0, 0))


def stem_first(frames, stem_weight, stem_diff_weight, tables, after):
    pool, fine_tab, coarse_tab, sel_fine, sel_coarse, lanes = tables
    weight = stem_weight.transpose(1, 2, 3, 0)
    diff_weight = stem_diff_weight.transpose(1, 2, 3, 0)
    return pl.pallas_call(
        stem_forward,
        grid=(GROUPS,),
        in_specs=[
            whole(2, 5, 3, SIDE, SIDE),
            whole(3, 7, 7, STEMC),
            whole(12, 7, 7, STEMC),
            whole(SIDE, 128),
            whole(2, SIDE, 1152),
            whole(256, 896),
            whole(8, 168, 432),
            whole(4, 56, 128),
            whole(8, 128),
            whole(2, MID),
        ],
        out_specs=[
            group_block(),
            whole(3, 232, 1152),
            whole(12, 120, 896),
            whole(8, 128),
        ],
        out_shape=[
            shape((GROUPS, 512, 512)),
            shape((3, 232, 1152)),
            shape((12, 120, 896)),
            shape((8, 128)),
        ],
        scratch_shapes=[
            pltpu.VMEM((SIDE, 128), F32),
            pltpu.VMEM((12, SIDE // 2, 256), BF),
            pltpu.VMEM((512, 432), BF),
            pltpu.VMEM((256, 1536), BF),
            pltpu.VMEM((128, 128), F32),
            pltpu.VMEM((168 + 672, STEMC), F32),
        ],
        compiler_params=params(),
        cost_estimate=cost(8e9, 2e7),
        name="stem_forward",
    )(frames, weight, diff_weight, pool, fine_tab, coarse_tab, sel_fine, sel_coarse, lanes, after)


def stem_second(raw, stem_cotangent, totals, stem_gain, stem_bias, lanes, count):
    gain = jnp.broadcast_to(stem_gain[:, None], (STEMC, 128))
    bias = jnp.broadcast_to(stem_bias[:, None], (STEMC, 128))
    cot = stem_cotangent.transpose(0, 2, 3, 1)
    return pl.pallas_call(
        functools.partial(stem_middle, count=count),
        grid=(GROUPS,),
        in_specs=[
            group_block(),
            whole(2, 56, 56, 64),
            whole(8, 128),
            whole(STEMC, 128),
            whole(STEMC, 128),
            whole(8, 128),
        ],
        out_specs=[group_block(), whole(8, 128)],
        out_shape=[shape((GROUPS, 512, 512)), shape((8, 128))],
        scratch_shapes=[
            pltpu.VMEM((8, 128), F32),
            pltpu.VMEM((2, 64, 128), F32),
            pltpu.VMEM((128, 128), F32),
        ],
        compiler_params=params(),
        cost_estimate=cost(8e9, 1.5e7),
        name="stem_middle",
    )(raw, cot, totals, gain, bias, lanes)


def stem_third(raw, back, fine, coarse, totals, back_totals, stem_gain, tables, count):
    pool, fine_tab, coarse_tab, sel_fine, sel_coarse, lanes = tables
    gain = jnp.broadcast_to(stem_gain[:, None], (STEMC, 128))
    return pl.pallas_call(
        functools.partial(stem_backward, count=count),
        grid=(GROUPS,),
        in_specs=[
            group_block(),
            group_block(),
            whole(3, 232, 1152),
            whole(12, 120, 896),
            whole(8, 128),
            whole(8, 128),
            whole(STEMC, 128),
            whole(8, 168, 432),
            whole(4, 56, 128),
            whole(8, 128),
        ],
        out_specs=whole(512, 128),
        out_shape=shape((512, 128)),
        scratch_shapes=[
            pltpu.VMEM((3, 64, 128), F32),
            pltpu.VMEM((512, 512), BF),
            pltpu.VMEM((256, 256), BF),
            pltpu.VMEM((512, 432), F32),
            pltpu.VMEM((256, 1536), F32),
        ],
        compiler_params=params(),
        cost_estimate=cost(8e9, 2.5e7),
        name="stem_backward",
    )(raw, back, fine, coarse, totals, back_totals, gain, sel_fine, sel_coarse, lanes)


def put_moments(out_ref, values):
    out_ref[0:1, :] = jnp.sum(values, axis=0, keepdims=True)
    out_ref[1:2, :] = jnp.sum(values * values, axis=0, keepdims=True)


def moments(totals, count):
    average = totals[0:1] * (1.0 / count)
    square = totals[1:2] * (1.0 / count)
    return average, lax.rsqrt(square - average * average + EPS)


def affine_of(totals, count, gain, bias=None):
    average, scale = moments(totals, count)
    slope = gain * scale
    shift = -average * slope
    return slope, shift if bias is None else shift + bias


def back_affine(totals, sums, count, gain):
    average, scale = moments(totals, count)
    first = sums[0:1] * (1.0 / count)
    second = sums[1:2] * (1.0 / count)
    on_grad = gain * scale
    on_value = -on_grad * scale * second
    return on_grad, on_value, -on_grad * first - on_value * average


def back_values(grad, value, totals, sums, gain, count):
    on_grad, on_value, constant = back_affine(totals, sums, count, gain)
    return (grad * on_grad + value * on_value + constant).astype(BF)


def silu_slope(values):
    sigma = sigmoid(values)
    return sigma * (1.0 + values * (1.0 - sigma))


def put_grad_moments(out_ref, grad, value, totals, count):
    average, scale = moments(totals, count)
    out_ref[0:1, :] = jnp.sum(grad, axis=0, keepdims=True)
    out_ref[1:2, :] = jnp.sum(grad * (value - average), axis=0, keepdims=True) * scale


def activation_back(grad, value, totals, gain, bias, count):
    slope, shift = affine_of(totals, count, gain, bias)
    return grad * silu_slope(value * slope + shift)


def first_matmuls(features, reduce_w, motion_w, reduce_out, motion_out, reduce_sum, motion_sum):
    value = dot(features[...], reduce_w[...])
    reduce_out[...] = value
    put_moments(reduce_sum, value)
    value = dot(features[...], motion_w[...])
    motion_out[...] = value
    put_moments(motion_sum, value)


def tap_mask(places, row_off, col_off):
    kept = None
    for off, base in ((row_off, 0), (col_off, 256)):
        if off:
            at = base + (128 if off > 0 else 0)
            good = places[:, at : at + 128]
            kept = good if kept is None else kept * good
    return kept


def tap_source(buffer, places, row_off, col_off, sign):
    move = sign * (7 * row_off + col_off)
    mask = tap_mask(places, sign * row_off, sign * col_off)
    value = buffer[8 + move : 8 + move + ROWS, :]
    if mask is not None:
        value = value * jnp.concatenate([mask] * (value.shape[1] // 128), axis=1)
    return value


def clear_ends(buffer):
    blank = jnp.zeros((8, buffer.shape[1]), F32)
    buffer[0:8, :] = blank
    buffer[8 + ROWS : 16 + ROWS, :] = blank


def spatial_forward(
    pre_reduce, totals, gain, bias, places, weight, hidden_out, pre_out, sums_out, buffer, *, count
):
    clear_ends(buffer)
    slope, shift = affine_of(totals[...], count, gain[...], bias[...])
    value = pre_reduce[...] * slope + shift
    hidden = (value * sigmoid(value)).astype(BF)
    hidden_out[...] = hidden
    buffer[8 : 8 + ROWS, :] = hidden.astype(F32)
    for tap in range(9):
        row_off, col_off = tap // 3 - 1, tap % 3 - 1
        source = tap_source(buffer, places, row_off, col_off, 1).astype(BF)
        value = dot(source, weight[tap * MID : (tap + 1) * MID, :])
        if tap == 0:
            pre_out[...] = value
        else:
            pre_out[...] += value
    put_moments(sums_out, pre_out[...])


def expand_forward(pre_spatial, totals, gain, bias, weight, hidden_out, pre_out, sums_out, *, count):
    @pl.when(pl.program_id(0) == 0)
    def prepare():
        slope, shift = affine_of(totals[...], count, gain[...], bias[...])
        value = pre_spatial[...] * slope + shift
        hidden_out[...] = (value * sigmoid(value)).astype(BF)

    value = dot(hidden_out[...], weight[...])
    pre_out[...] = value
    put_moments(sums_out, value)


def shifted(buffer, move):
    return buffer[64 + move : 64 + move + ROWS, :]


def fill(buffer, value):
    buffer[64 : 64 + ROWS, :] = value


def column_shifts(buffer, places):
    left = shifted(buffer, -1) * tap_mask(places, 0, -1)
    right = shifted(buffer, 1) * tap_mask(places, 0, 1)
    return left, shifted(buffer, 0), right


def box_of(value, buffer, places):
    fill(buffer, value)
    left, middle, right = column_shifts(buffer, places)
    fill(buffer, left + middle + right)
    return (
        shifted(buffer, -7) * tap_mask(places, -1, 0)
        + shifted(buffer, 0)
        + shifted(buffer, 7) * tap_mask(places, 1, 0)
    ) * (1.0 / 9.0)


def change_of(pre_motion, slope, keep, buffer, cols):
    fill(buffer, pre_motion[:, cols] * slope)
    return (shifted(buffer, 49) - shifted(buffer, 0)) * keep[...]


def clear_margins(buffer):
    buffer[0:64, :] = jnp.zeros((64, 128), F32)
    buffer[64 + ROWS : 128 + ROWS, :] = jnp.zeros((64, 128), F32)


def motion_forward(
    pre_motion, totals, gain, keep, places, depth, weight, mixed_out, pre_out, sums_out, buffer, *, count
):
    @pl.when(pl.program_id(0) == 0)
    def prepare():
        clear_margins(buffer)

        @pl.loop(0, MID // 128)
        def one(tile):
            cols = pl.ds(pl.multiple_of(tile * 128, 128), 128)
            slope, shift = affine_of(totals[:, cols], count, gain[:, cols])
            change = change_of(pre_motion, slope, keep, buffer, cols)
            fill(buffer, change)
            near = column_shifts(buffer, places)
            average = box_of(change, buffer, places)
            fill(buffer, average)
            wide = column_shifts(buffer, places)
            lines = []
            for row in range(3):
                line = None
                for col in range(3):
                    for scale, source in ((0, near), (1, wide)):
                        at = scale * 9 + row * 3 + col
                        term = source[col] * depth[at : at + 1, cols]
                        line = term if line is None else line + term
                lines.append(line)
            fill(buffer, lines[0])
            value = lines[1] + shifted(buffer, -7) * tap_mask(places, -1, 0)
            fill(buffer, lines[2])
            value = value + shifted(buffer, 7) * tap_mask(places, 1, 0)
            mixed_out[:, cols] = value.astype(BF)

    value = dot(mixed_out[...], weight[...])
    pre_out[...] = value
    put_moments(sums_out, value)


def gate_kernel(
    own, pre_expand, pre_excite, features, cotangent, expand_tot, excite_tot,
    expand_gain, expand_bias, excite_gain, excite_bias,
    mine_out, other_out, direct_out, comb_out, gate_out, sums_out, *, count
):
    step = pl.program_id(0)
    e_mean, e_scale = moments(expand_tot[...], count)
    x_mean, x_scale = moments(excite_tot[...], count)
    e_slope = expand_gain[...] * e_scale
    e_shift = expand_bias[...] - e_mean * e_slope
    x_slope = excite_gain[...] * x_scale
    x_shift = excite_bias[...] - x_mean * x_slope
    sums = [jnp.zeros((8, TILE), F32)] * 4
    for top, size in PIECES:
        rows = slice(top, top + size)
        feats = features[rows, :].astype(F32)
        seed = cotangent[rows, :].astype(F32)
        pre_e = pre_expand[rows, :]
        pre_x = pre_excite[rows, :]
        branch = (pre_e * e_slope + e_shift).astype(BF).astype(F32)
        gate = sigmoid(pre_x * x_slope + x_shift)
        lifted = feats * gate
        combined = branch + lifted
        sigma = sigmoid(combined)
        output = combined * sigma
        grad = seed * (sigma + output * (1.0 - sigma))
        rounded = grad.astype(BF)
        comb_out[rows, :] = rounded
        rounded = rounded.astype(F32)
        grad_gate = grad * lifted * (1.0 - gate)
        gate_out[rows, :] = grad_gate

        @pl.when(step < 2)
        def store_mine():
            mine_out[rows, :] = output.astype(BF)

        @pl.when((step >= 2) & (step < 4))
        def store_other():
            other_out[rows, :] = output.astype(BF)

        @pl.when(step < 4)
        def store_direct():
            direct_out[rows, :] = grad * gate

        for spot, value in enumerate(
            (
                rounded,
                rounded * (pre_e - e_mean),
                grad_gate,
                grad_gate * (pre_x - x_mean),
            )
        ):
            sums[spot] = sums[spot] + jnp.sum(value.reshape(size // 8, 8, TILE), axis=0)
    finals = [jnp.sum(value, axis=0, keepdims=True) for value in sums]
    sums_out[0:1, :] = finals[0]
    sums_out[1:2, :] = finals[1] * e_scale
    sums_out[2:3, :] = finals[2]
    sums_out[3:4, :] = finals[3] * x_scale


def add_up(acc, part):
    step = pl.program_id(0)

    @pl.when(step == 0)
    def begin():
        acc[...] = part

    @pl.when(step > 0)
    def add():
        acc[...] += part


def expand_backward(
    own, grad, pre_expand, totals, sums, gain, weight, pre_spatial, s_totals, s_gain, s_bias,
    own_out, grad_out, sums_out, acc, *, count
):
    step = pl.program_id(0)
    value = back_values(
        grad[...].astype(F32), pre_expand[...], totals[...], sums[0:2, :], gain[...], count
    )

    @pl.when(step < 4)
    def store_own():
        own_out[...] = value

    add_up(acc, dot(value, weight[...], NT))

    @pl.when(step == C // TILE - 1)
    def finish():
        hidden = acc[...].astype(BF).astype(F32)
        back = activation_back(hidden, pre_spatial[...], s_totals[...], s_gain[...], s_bias[...], count)
        grad_out[...] = back
        put_grad_moments(sums_out, back, pre_spatial[...], s_totals[...], count)


def excite_backward(
    own, grad, pre_excite, totals, sums, gain, weight, pre_motion, m_totals, m_gain, keep, places, depth,
    own_out, grad_out, sums_out, depth_out, acc, buffer, *, count
):
    step = pl.program_id(0)
    value = back_values(grad[...], pre_excite[...], totals[...], sums[2:4, :], gain[...], count)

    @pl.when(step < 4)
    def store_own():
        own_out[...] = value

    add_up(acc, dot(value, weight[...], NT))

    @pl.when(step == C // TILE - 1)
    def finish():
        clear_margins(buffer)

        @pl.loop(0, MID // 128)
        def one(tile):
            cols = pl.ds(pl.multiple_of(tile * 128, 128), 128)
            slope, shift = affine_of(m_totals[:, cols], count, m_gain[:, cols])
            change = change_of(pre_motion, slope, keep, buffer, cols)
            fill(buffer, change)
            near = column_shifts(buffer, places)
            average = box_of(change, buffer, places)
            fill(buffer, average)
            wide = column_shifts(buffer, places)
            grad_mixed = acc[:, cols]
            fill(buffer, grad_mixed)
            lines = (
                shifted(buffer, 7) * tap_mask(places, 1, 0),
                grad_mixed,
                shifted(buffer, -7) * tap_mask(places, -1, 0),
            )
            pulled = []
            for scale, source in ((0, near), (1, wide)):
                terms = []
                for col in range(3):
                    term = None
                    for row in range(3):
                        at = scale * 9 + row * 3 + col
                        piece = lines[row] * depth[at : at + 1, cols]
                        term = piece if term is None else term + piece
                        depth_out[at : at + 1, cols] = jnp.sum(
                            lines[row] * source[col], axis=0, keepdims=True
                        )
                    terms.append(term)
                fill(buffer, terms[0])
                total = terms[1] + shifted(buffer, 1) * tap_mask(places, 0, 1)
                fill(buffer, terms[2])
                pulled.append(total + shifted(buffer, -1) * tap_mask(places, 0, -1))
            grad_change = (pulled[0] + box_of(pulled[1], buffer, places)) * keep[...]
            fill(buffer, grad_change)
            grad_out[:, cols] = shifted(buffer, -49) - grad_change

        put_grad_moments(sums_out, grad_out[...], pre_motion[...], m_totals[...], count)


def spatial_backward(
    own, grad, pre_spatial, totals, sums, gain, places, weight, pre_reduce, r_totals, r_gain, r_bias,
    taps_out, grad_out, sums_out, buffer, source_ref, acc, *, count
):
    clear_ends(buffer)
    buffer[8 : 8 + ROWS, :] = back_values(
        grad[...], pre_spatial[...], totals[...], sums[...], gain[...], count
    ).astype(F32)
    mine = pl.ds(pl.multiple_of((own[0] // 2) * 256, 256), 256)
    for tap in range(9):
        row_off, col_off = tap // 3 - 1, tap % 3 - 1
        source_ref[...] = tap_source(buffer, places, row_off, col_off, -1).astype(BF)
        taps_out[:, tap * 256 : (tap + 1) * 256] = source_ref[:, mine]
        value = dot(source_ref[...], weight[tap * MID : (tap + 1) * MID, :], NT)
        if tap == 0:
            acc[...] = value
        else:
            acc[...] += value
    hidden = acc[...].astype(BF).astype(F32)
    back = activation_back(hidden, pre_reduce[...], r_totals[...], r_gain[...], r_bias[...], count)
    grad_out[...] = back
    put_grad_moments(sums_out, back, pre_reduce[...], r_totals[...], count)


def motion_backward(
    own, grad, pre_motion, totals, sums, gain, mine_w, other_w, direct, own_out, mine_out, other_out,
    value_ref, *, count
):
    value_ref[...] = back_values(
        grad[...], pre_motion[...], totals[...], sums[...], gain[...], count
    )
    own_out[...] = value_ref[:, pl.ds(pl.multiple_of((own[0] // 2) * 256, 256), 256)]
    mine_out[...] = direct[:, :MID] + dot(value_ref[...], mine_w[...], NT)
    other_out[...] = direct[:, MID:] + dot(value_ref[...], other_w[...], NT)


def reduce_backward(
    own, grad, pre_reduce, totals, sums, gain, mine_w, other_w, mine_part, other_part,
    own_out, mine_out, other_out, value_ref, *, count
):
    value_ref[...] = back_values(
        grad[...], pre_reduce[...], totals[...], sums[...], gain[...], count
    )
    own_out[...] = value_ref[:, pl.ds(pl.multiple_of((own[0] // 2) * 256, 256), 256)]
    other_out[...] = (other_part[...] + dot(value_ref[...], other_w[...], NT)).astype(BF)
    mine_out[...] = (mine_part[...] + dot(value_ref[...], mine_w[...], NT)).astype(BF)


def spatial_weight_kernel(hidden, taps, out, turned_ref):
    turned_ref[...] = jnp.transpose(hidden[...].astype(F32)).astype(BF)
    for tap in range(9):
        value = dot(turned_ref[...], taps[:, tap * 256 : (tap + 1) * 256])
        out[tap * MID : (tap + 1) * MID, :] = value.astype(BF)


def join_kernel(own, mine, got, out):
    first = jnp.where(own[0] % 2 == 0, mine[...].astype(F32), got[...].astype(F32))
    second = jnp.where(own[0] % 2 == 0, got[...].astype(F32), mine[...].astype(F32))
    out[...] = jnp.concatenate([first, second], axis=0).astype(BF)


def unpack_kernel(
    own, rest_0, rest_1, rest_2, rest_3, early_0, early_1, early_2, early_3, stem, mine, got,
    reduce_out, spatial_out, expand_out, motion_out, excite_out, fine_out, coarse_out, grad_out,
    packed_ref, *, clips
):
    join_kernel(own, mine, got, grad_out)
    cuts = (9 * MID // clips, (9 * MID + C) // clips, (9 * MID + 2 * C) // clips)
    half = own[0] // 2
    for side, left, right in ((half, rest_0, rest_1), (1 - half, rest_2, rest_3)):
        value = left[...].astype(F32) + right[...].astype(F32)
        cols = pl.ds(pl.multiple_of(side * 256, 256), 256)
        spatial_out[:, cols] = value[: cuts[0]]
        motion_out[:, cols] = value[cuts[0] : cuts[1]]
        reduce_out[:, cols] = value[cuts[1] : cuts[2]]
    for flip, left, right in (
        (0, (early_0, 0), (early_1, 1)),
        (1, (early_0, 1), (early_1, 0)),
        (2, (early_2, 0), (early_3, 1)),
        (3, (early_2, 1), (early_3, 0)),
    ):
        cols = pl.ds(pl.multiple_of((own[0] ^ flip) * MID, MID), MID)
        for base, out in ((0, expand_out), (2, excite_out)):
            value = None
            for ref, spot in (left, right):
                at = (base + spot) * MID
                part = ref[:, at : at + MID].astype(F32)
                value = part if value is None else value + part
            out[:, cols] = value
    for owner in range(clips):
        total = (stem[owner, 0] + stem[owner, 1]) + (stem[owner, 2] + stem[owner, 3])
        packed_ref[owner * 16 : (owner + 1) * 16, :] = total
    for chan in range(3):
        for row in range(7):
            at = chan * 56 + row * 8
            fine_out[chan, row] = packed_ref[at : at + 7, 0:64]
    for chan in range(12):
        side = (chan % 2) * 64
        for row in range(7):
            at = 168 + (chan // 2) * 56 + row * 8
            coarse_out[chan, row] = packed_ref[at : at + 7, side : side + 64]


def with_own(kernel, own, grid, in_specs, out_specs, out_shape, scratch, args, flops, nbytes, name, mib=50):
    return pl.pallas_call(
        kernel,
        grid_spec=pltpu.PrefetchScalarGridSpec(
            num_scalar_prefetch=1,
            grid=grid,
            in_specs=in_specs,
            out_specs=out_specs,
            scratch_shapes=scratch,
        ),
        out_shape=out_shape,
        compiler_params=params(mib),
        cost_estimate=cost(flops, nbytes),
        name=name,
    )(own, *args)


def place_table():
    rows = np.arange(ROWS)
    down = (rows % 49) // 7
    right = rows % 7
    kept = [down >= 1, down <= FEAT - 2, right >= 1, right <= FEAT - 2]
    return jnp.asarray(np.concatenate([np.repeat(k[:, None], 128, 1) for k in kept], axis=1), F32)


def keep_pairs(valid_rows, video_rows):
    valid_float = valid_rows.astype(F32)
    same_video = (video_rows[:, 1:] == video_rows[:, :-1]).astype(F32)
    pair_keep = valid_float[:, 1:] * valid_float[:, :-1] * same_video
    return jnp.concatenate([pair_keep, jnp.zeros_like(pair_keep[:, :1])], axis=1)


def on_device(
    features,
    out_cotangent,
    seg_valid,
    seg_video,
    frames,
    stem_cotangent,
    stem_weight,
    stem_diff_weight,
    stem_gain,
    stem_bias,
    reduce_weight,
    reduce_gain,
    reduce_bias,
    spatial_weight,
    spatial_gain,
    spatial_bias,
    expand_weight,
    expand_gain,
    expand_bias,
    motion_weight,
    motion_gain,
    depth_weight,
    excite_weight,
    excite_gain,
    excite_bias,
):
    clips = lax.axis_size("z") * lax.axis_size("y") * lax.axis_size("c")
    count = float(clips * ROWS)
    stem_count = float(clips * lax.axis_size("x") * (SIDE // 2) ** 2)
    here = lax.axis_index("x")
    micro = here % 2
    own = jnp.reshape(here, (1,)).astype(jnp.int32)
    places = place_table()

    def of_micro(rows):
        return lax.dynamic_index_in_dim(
            rows.reshape(MICRO, rows.shape[0] // MICRO, rows.shape[1]), micro, 0, False
        )

    feats = of_micro(features)
    seeds = of_micro(out_cotangent)
    keep = jnp.broadcast_to(
        jnp.repeat(of_micro(keep_pairs(seg_valid, seg_video)).reshape(-1), FEAT * FEAT)[:, None],
        (ROWS, 128),
    )
    line = lambda vector: vector.reshape(1, -1)
    reduce_gain, reduce_bias = line(reduce_gain), line(reduce_bias)
    spatial_gain, spatial_bias = line(spatial_gain), line(spatial_bias)
    expand_gain, expand_bias = line(expand_gain), line(expand_bias)
    excite_gain, excite_bias = line(excite_gain), line(excite_bias)
    motion_gain = line(motion_gain)
    depth = jnp.pad(depth_weight.reshape(18, MID), ((0, 6), (0, 0)))

    tables = stem_tables()
    lanes = tables[-1]
    column = lambda rows, width: pl.BlockSpec((rows, width), lambda step, *rest: (0, step))
    pre_reduce, pre_motion, reduce_sum, motion_sum = pl.pallas_call(
        first_matmuls,
        grid=(2,),
        in_specs=[whole(ROWS, C), column(C, 256), column(C, 256)],
        out_specs=[column(ROWS, 256), column(ROWS, 256), column(2, 256), column(2, 256)],
        out_shape=[shape((ROWS, MID)), shape((ROWS, MID)), shape((2, MID)), shape((2, MID))],
        compiler_params=params(),
        cost_estimate=cost(1.7e9, 1e7),
        name="first_matmuls",
    )(feats, reduce_weight, motion_weight)
    raw, fine, coarse, stem_sum = stem_first(
        frames, stem_weight, stem_diff_weight, tables, reduce_sum
    )
    stem_sum = ring_sum(stem_sum[:2], "x")

    reduce_tot, motion_tot, stem_tot = merge_sum(reduce_sum, motion_sum, stem_sum)
    stem_tot = jnp.pad(stem_tot, ((0, 6), (0, 0)))
    back, back_sum = stem_second(
        raw, stem_cotangent, stem_tot, stem_gain, stem_bias, lanes, stem_count
    )
    back_sum = ring_sum(back_sum[:2], "x")

    hidden_one, pre_spatial, spatial_sum = pl.pallas_call(
        functools.partial(spatial_forward, count=count),
        in_specs=[VMEM] * 6,
        out_specs=[VMEM] * 3,
        out_shape=[shape((ROWS, MID), BF), shape((ROWS, MID)), shape((2, MID))],
        scratch_shapes=[pltpu.VMEM((ROWS + 16, MID), F32)],
        compiler_params=params(),
        cost_estimate=cost(1.9e9, 8e6),
        name="spatial_forward",
    )(pre_reduce, reduce_tot, reduce_gain, reduce_bias, places, spatial_weight)

    mixed, pre_excite, excite_sum = pl.pallas_call(
        functools.partial(motion_forward, count=count),
        grid=(4,),
        in_specs=[
            whole(ROWS, MID), whole(2, MID), whole(1, MID), whole(ROWS, 128), whole(ROWS, 512),
            whole(24, MID), column(MID, 512),
        ],
        out_specs=[whole(ROWS, MID), column(ROWS, 512), column(2, 512)],
        out_shape=[shape((ROWS, MID), BF), shape((ROWS, C)), shape((2, C))],
        scratch_shapes=[pltpu.VMEM((ROWS + 128, 128), F32)],
        compiler_params=params(),
        cost_estimate=cost(2e9, 1.2e7),
        name="motion_forward",
    )(pre_motion, motion_tot, motion_gain, keep, places, depth, excite_weight)
    spatial_tot, excite_tot, back_tot = merge_sum(spatial_sum, excite_sum, back_sum)
    back_tot = jnp.pad(back_tot, ((0, 6), (0, 0)))
    stem_packed = stem_third(
        raw, back, fine, coarse, stem_tot, back_tot, stem_gain, tables, stem_count
    )
    stem_packed = lax.all_gather(scatter_dp(stem_packed), ("z", "y", "c", "x"))
    back_both = back_tot[0] + back_tot[1]
    stem_gain_grad, stem_bias_grad = back_both[64:], back_both[:64]

    hidden_two, pre_expand, expand_sum = pl.pallas_call(
        functools.partial(expand_forward, count=count),
        grid=(4,),
        in_specs=[
            whole(ROWS, MID), whole(2, MID), whole(1, MID), whole(1, MID), column(MID, 512),
        ],
        out_specs=[whole(ROWS, MID), column(ROWS, 512), column(2, 512)],
        out_shape=[shape((ROWS, MID), BF), shape((ROWS, C)), shape((2, C))],
        compiler_params=params(),
        cost_estimate=cost(1e9, 1e7),
        name="expand_forward",
    )(pre_spatial, spatial_tot, spatial_gain, spatial_bias, expand_weight)
    expand_tot = sum_dp(expand_sum)

    def turned(rows):
        return pl.BlockSpec((rows, TILE), lambda step, own_ref: (0, step ^ (2 * own_ref[0])))

    def kept(first, last):
        return pl.BlockSpec(
            (ROWS, TILE), lambda step, own_ref: (0, jnp.clip(step - first, 0, last - first))
        )

    mine, other, direct, grad_comb, grad_gate, gate_sum = with_own(
        functools.partial(gate_kernel, count=count),
        own,
        (C // TILE,),
        [turned(ROWS)] * 4 + [turned(2)] * 2 + [turned(1)] * 4,
        [kept(0, 1), kept(2, 3), kept(0, 3), turned(ROWS), turned(ROWS), turned(4)],
        [
            shape((ROWS, MID), BF), shape((ROWS, MID), BF), shape((ROWS, 2 * MID)),
            shape((ROWS, C), BF), shape((ROWS, C)), shape((4, C)),
        ],
        [],
        (
            pre_expand, pre_excite, feats, seeds, expand_tot, excite_tot,
            expand_gain, expand_bias, excite_gain, excite_bias,
        ),
        2e9,
        2e7,
        "gate",
    )
    gate_tot = sum_dp(gate_sum)

    result = with_own(
        join_kernel,
        own,
        (1,),
        [whole(ROWS, MID), whole(ROWS, MID)],
        whole(2 * ROWS, MID),
        shape((2 * ROWS, MID), BF),
        [],
        (mine, from_peer(other, 1)),
        1e5,
        2e6,
        "join_result",
    )

    expand_own, grad_spatial, spatial_back = with_own(
        functools.partial(expand_backward, count=count),
        own,
        (C // TILE,),
        [
            turned(ROWS), turned(ROWS), turned(2), turned(4), turned(1), turned(MID),
            whole(ROWS, MID), whole(2, MID), whole(1, MID), whole(1, MID),
        ],
        [kept(0, 3), whole(ROWS, MID), whole(2, MID)],
        [shape((ROWS, 2 * MID), BF), shape((ROWS, MID)), shape((2, MID))],
        [pltpu.VMEM((ROWS, MID), F32)],
        (
            grad_comb, pre_expand, expand_tot, gate_tot, expand_gain, expand_weight,
            pre_spatial, spatial_tot, spatial_gain, spatial_bias,
        ),
        1e9,
        1e7,
        "expand_backward",
    )

    excite_own, grad_reduced, motion_back, depth_part = with_own(
        functools.partial(excite_backward, count=count),
        own,
        (C // TILE,),
        [
            turned(ROWS), turned(ROWS), turned(2), turned(4), turned(1), turned(MID),
            whole(ROWS, MID), whole(2, MID), whole(1, MID), whole(ROWS, 128), whole(ROWS, 512),
            whole(24, MID),
        ],
        [kept(0, 3), whole(ROWS, MID), whole(2, MID), whole(18, MID)],
        [shape((ROWS, 2 * MID), BF), shape((ROWS, MID)), shape((2, MID)), shape((18, MID))],
        [pltpu.VMEM((ROWS, MID), F32), pltpu.VMEM((ROWS + 128, 128), F32)],
        (
            grad_gate, pre_excite, excite_tot, gate_tot, excite_gain, excite_weight,
            pre_motion, motion_tot, motion_gain, keep, places, depth,
        ),
        2e9,
        1e7,
        "excite_backward",
    )
    back_all = sum_dp(jnp.concatenate([motion_back, spatial_back, depth_part], axis=0))
    motion_back_tot, spatial_back_tot = back_all[:2], back_all[2:4]

    taps, grad_reduce, reduce_back = with_own(
        functools.partial(spatial_backward, count=count),
        own,
        (1,),
        [
            whole(ROWS, MID), whole(ROWS, MID), whole(2, MID), whole(2, MID), whole(1, MID),
            whole(ROWS, 512), whole(9 * MID, MID), whole(ROWS, MID), whole(2, MID),
            whole(1, MID), whole(1, MID),
        ],
        [whole(ROWS, 9 * 256), whole(ROWS, MID), whole(2, MID)],
        [shape((ROWS, 9 * 256), BF), shape((ROWS, MID)), shape((2, MID))],
        [
            pltpu.VMEM((ROWS + 16, MID), F32),
            pltpu.VMEM((ROWS, MID), BF),
            pltpu.VMEM((ROWS, MID), F32),
        ],
        (
            grad_spatial, pre_spatial, spatial_tot, spatial_back_tot, spatial_gain, places,
            spatial_weight, pre_reduce, reduce_tot, reduce_gain, reduce_bias,
        ),
        2e9,
        1e7,
        "spatial_backward",
    )
    reduce_back_tot = sum_dp(reduce_back)

    across = lambda left, right: dot(left, right, TN).astype(BF)
    early = lax.psum_scatter(
        jnp.concatenate([across(hidden_two, expand_own), across(mixed, excite_own)], axis=1),
        ("z", "y", "c"),
        scatter_dimension=0,
        tiled=True,
    )

    mine_rows = pl.BlockSpec((MID, MID), lambda step, own_ref: (own_ref[0], 0))
    other_rows = pl.BlockSpec((MID, MID), lambda step, own_ref: (own_ref[0] ^ 1, 0))
    motion_own, mine_part, other_part = with_own(
        functools.partial(motion_backward, count=count),
        own,
        (1,),
        [
            whole(ROWS, MID), whole(ROWS, MID), whole(2, MID), whole(2, MID), whole(1, MID),
            mine_rows, other_rows, whole(ROWS, 2 * MID),
        ],
        [whole(ROWS, 256), whole(ROWS, MID), whole(ROWS, MID)],
        [shape((ROWS, 256), BF), shape((ROWS, MID)), shape((ROWS, MID))],
        [pltpu.VMEM((ROWS, MID), BF)],
        (
            grad_reduced, pre_motion, motion_tot, motion_back_tot, motion_gain,
            motion_weight, motion_weight, direct,
        ),
        5e8,
        8e6,
        "motion_backward",
    )
    spatial_part = pl.pallas_call(
        spatial_weight_kernel,
        in_specs=[VMEM] * 2,
        out_specs=VMEM,
        out_shape=shape((9 * MID, 256), BF),
        scratch_shapes=[pltpu.VMEM((MID, ROWS), BF)],
        compiler_params=params(),
        cost_estimate=cost(1e9, 5e6),
        name="spatial_weight",
    )(hidden_one, taps)
    middle = jnp.concatenate(
        [scatter_dp(spatial_part), scatter_dp(across(feats, motion_own))], axis=0
    )
    reduce_own, mine_grad, other_grad = with_own(
        functools.partial(reduce_backward, count=count),
        own,
        (1,),
        [
            whole(ROWS, MID), whole(ROWS, MID), whole(2, MID), whole(2, MID), whole(1, MID),
            mine_rows, other_rows, whole(ROWS, MID), whole(ROWS, MID),
        ],
        [whole(ROWS, 256), whole(ROWS, MID), whole(ROWS, MID)],
        [shape((ROWS, 256), BF), shape((ROWS, MID), BF), shape((ROWS, MID), BF)],
        [pltpu.VMEM((ROWS, MID), BF)],
        (
            grad_reduce, pre_reduce, reduce_tot, reduce_back_tot, reduce_gain,
            reduce_weight, reduce_weight, mine_part, other_part,
        ),
        5e8,
        8e6,
        "reduce_backward",
    )
    got_grad = from_peer(other_grad, 1)
    late = scatter_dp(across(feats, reduce_own))
    early = gather_x(early)
    rest = gather_x(jnp.concatenate([middle, late], axis=0))
    packed_shape = (clips, lax.axis_size("x"), 512 // clips, 128)
    (
        reduce_grad, spatial_grad, expand_grad, motion_grad, excite_grad,
        stem_weight_grad, stem_diff_grad, features_grad,
    ) = with_own(
        functools.partial(unpack_kernel, clips=clips),
        own,
        (1,),
        [whole(*part.shape) for part in rest]
        + [whole(*part.shape) for part in early]
        + [whole(*packed_shape), whole(ROWS, MID), whole(ROWS, MID)],
        [
            whole(C // clips, MID), whole(9 * MID // clips, MID), whole(MID // clips, C),
            whole(C // clips, MID), whole(MID // clips, C),
            whole(3, 7, 7, STEMC), whole(12, 7, 7, STEMC), whole(2 * ROWS, MID),
        ],
        [
            shape((C // clips, MID)), shape((9 * MID // clips, MID)), shape((MID // clips, C)),
            shape((C // clips, MID)), shape((MID // clips, C)),
            shape((3, 7, 7, STEMC)), shape((12, 7, 7, STEMC)), shape((2 * ROWS, MID), BF),
        ],
        [pltpu.VMEM((512, 128), F32)],
        (*rest, *early, stem_packed.reshape(packed_shape), mine_grad, got_grad),
        1e6,
        6e6,
        "unpack",
    )
    stem_weight_grad = stem_weight_grad.transpose(3, 0, 1, 2)
    stem_diff_grad = stem_diff_grad.transpose(3, 0, 1, 2)

    small = jnp.concatenate([gate_tot.reshape(16, MID), back_all], axis=0)
    small = small + from_peer(small, 1)
    gate_both = small[:16].reshape(4, C)
    depth_grad = small[20:38].reshape(2, 3, 3, MID)
    reduce_both = reduce_back_tot + from_peer(reduce_back_tot, 1)
    return (
        result,
        features_grad,
        stem_weight_grad,
        stem_diff_grad,
        stem_gain_grad,
        stem_bias_grad,
        reduce_grad,
        reduce_both[1],
        reduce_both[0],
        spatial_grad,
        small[19],
        small[18],
        expand_grad,
        gate_both[1],
        gate_both[0],
        motion_grad,
        small[17],
        depth_grad,
        excite_grad,
        gate_both[3],
        gate_both[2],
    )


def solution(mesh):
    grid = Mesh(mesh.devices.reshape(4, 4, 2, 4), ("z", "y", "c", "x"))
    clips = ("z", "y", "c")
    everyone = ("z", "y", "c", "x")
    split = P(clips, None)
    copied = P()
    return jax.shard_map(
        on_device,
        mesh=grid,
        in_specs=(split,) * 4
        + (P(everyone, None, None, None, None), P(everyone, None, None, None))
        + (copied,) * 19,
        out_specs=(P(clips, "x"), P(clips, "x"))
        + (copied,) * 4
        + (split, copied, copied) * 3
        + (split, copied, copied)
        + (split, copied, copied),
        check_vma=False,
    )
```

```python
import functools

import jax
import jax.numpy as jnp
import numpy as np
from jax import lax
from jax.experimental import pallas as pl
from jax.experimental.pallas import tpu as pltpu
from jax.sharding import Mesh
from jax.sharding import PartitionSpec as P

C = 2048
MID = 512
STEMC = 64
SIDE = 224
FEAT = 7
SEG = 8
MICRO = 2
ROWS = SEG * FEAT * FEAT
EPS = 1e-05
BF = jnp.bfloat16
F32 = jnp.float32
HIGH = lax.Precision.HIGHEST
NN = (((1,), (0,)), ((), ()))
NT = (((1,), (1,)), ((), ()))
TN = (((0,), (0,)), ((), ()))
GROUPS = 7
TILE = 512
VMEM = pl.BlockSpec(memory_space=pltpu.VMEM)
PIECES = [slice(top, min(top + 16, ROWS)) for top in range(0, ROWS, 16)]
EIGHTS = [slice(top, top + 8) for top in range(0, ROWS, 8)]


def sigmoid(values):
    return 0.5 + 0.5 * jnp.tanh(0.5 * values)


def dot(left, right, dims=NN, precision=None):
    return lax.dot_general(left, right, dims, precision=precision, preferred_element_type=F32)


LIMITS = {}


def params(name):
    return pltpu.CompilerParams(vmem_limit_bytes=LIMITS.get(name, 20) * 2**20)


def cost(flops, nbytes):
    return pl.CostEstimate(flops=int(flops), bytes_accessed=int(nbytes), transcendentals=0)


def shape(dims, dtype=F32):
    return jax.ShapeDtypeStruct(dims, dtype)


def ring_sum(values, axis):
    size = lax.axis_size(axis)
    if size == 1:
        return values
    got = [
        lax.ppermute(values, axis, [(i, (i + step) % size) for i in range(size)])
        for step in range(1, size)
    ]
    if size == 2:
        return values + got[0]
    return (values + got[1]) + (got[0] + got[2])


def core_sum(values):
    pair = lax.all_gather(values, "c")
    return pair[0] + pair[1]


def sum_dp(values):
    return ring_sum(ring_sum(core_sum(values), "y"), "z")


def shift_by(values, axis, step):
    size = lax.axis_size(axis)
    return lax.ppermute(values, axis, [(i, (i + step) % size) for i in range(size)])


def scatter_lead(blocks, axis, kind=BF):
    size = lax.axis_size(axis)
    me = lax.axis_index(axis)
    pick = lambda at: lax.dynamic_index_in_dim(blocks, at % size, 0, False)
    total = pick(me).astype(F32)
    for step in range(1, size):
        total = total + shift_by(pick(me + step), axis, step).astype(F32)
    return total.astype(kind)


def scatter_start(blocks, axis):
    me = lax.axis_index(axis)
    half = blocks.shape[1] // 2
    far = lax.dynamic_index_in_dim(blocks, (me + 2) % 4, 0, False)
    return shift_by(far[:half], axis, 1), shift_by(far[half:], axis, -1)


def scatter_finish(blocks, axis, upward, downward):
    me = lax.axis_index(axis)
    pick = lambda at: lax.dynamic_index_in_dim(blocks, at % 4, 0, False).astype(F32)
    half = blocks.shape[1] // 2
    up, down = pick(me + 1), pick(me + 3)
    up = jnp.concatenate([up[:half] + upward.astype(F32), up[half:]], axis=0).astype(BF)
    down = jnp.concatenate([down[:half], down[half:] + downward.astype(F32)], axis=0).astype(BF)
    up, down = shift_by(up, axis, 1), shift_by(down, axis, -1)
    return (pick(me) + up.astype(F32) + down.astype(F32)).astype(BF)


def tie(*values):
    return lax.optimization_barrier(values)


def from_peer(values, flip):
    size = lax.axis_size("x")
    return lax.ppermute(values, "x", [(i, i ^ flip) for i in range(size)])


def gather_x(block):
    return [block] + [from_peer(block, flip) for flip in (1, 2, 3)]


def merge_sum(*pieces):
    wide = jnp.concatenate(pieces, axis=1)
    total = sum_dp(wide)
    ends = np.cumsum([piece.shape[1] for piece in pieces])
    return [total[:, end - piece.shape[1] : end] for end, piece in zip(ends, pieces)]


def stem_tables():
    half, quarter = SIDE // 2, SIDE // 4
    pool = np.zeros((SIDE, 128), np.float32)
    for column in range(SIDE):
        pool[column, column // 2] = 0.25
    fine = np.zeros((2, SIDE, 9 * 128), np.float32)
    coarse = np.zeros((2 * 128, 7 * 128), np.float32)
    for seg in range(2):
        for spot in range(quarter):
            for tap in range(9):
                column = 4 * spot + tap - 3
                if 0 <= column < SIDE:
                    fine[seg, column, tap * 128 + seg * 64 + spot] = 1
            for tap in range(7):
                column = 2 * spot + tap - 3
                if 0 <= column < half:
                    coarse[seg * 128 + column, tap * 128 + seg * 64 + spot] = 1
    sel_fine = np.zeros((8, 168, 432), np.float32)
    for up in range(2):
        for row in range(2):
            for col in range(2):
                for chan in range(3):
                    for dy in range(7):
                        for dx in range(7):
                            sel_fine[
                                up * 4 + row * 2 + col,
                                chan * 56 + dy * 8 + dx,
                                chan * 144 + (2 * col + dx) * 16 + 4 * up + 2 * row + dy,
                            ] = 1
    sel_coarse = np.zeros((4, 56, 128), np.float32)
    for up in range(4):
        for dy in range(7):
            for dx in range(7):
                sel_coarse[up, dy * 8 + dx, dx * 16 + 2 * up + dy] = 1
    lanes = np.zeros((8, 128), np.float32)
    lanes[0, :64] = 1
    lanes[1, 64:] = 1
    usable = np.zeros((8, 128), np.float32)
    usable[0, :56] = 1
    usable[1, 64:120] = 1
    return [
        jnp.asarray(table, dtype)
        for table, dtype in (
            (pool, BF),
            (fine, BF),
            (coarse, BF),
            (sel_fine, BF),
            (sel_coarse, BF),
            (lanes, F32),
            (usable, F32),
        )
    ]


def fine_patches(tall):
    parts = []
    for pair in range(4):
        rows = slice(8 * pair, 8 * pair + 16)
        parts.append(
            jnp.concatenate(
                [
                    tall[chan][rows, tap * 128 : (tap + 1) * 128]
                    for chan in range(3)
                    for tap in range(9)
                ],
                axis=0,
            ).astype(BF)
        )
    return jnp.concatenate(parts, axis=1)


def coarse_patches(tall):
    blank = jnp.zeros((16, 128), F32)
    parts = [[], []]
    for chan in range(12):
        for quad in range(2):
            rows = slice(8 * quad, 8 * quad + 16)
            for tap in range(7):
                parts[quad].append(tall[chan][rows, tap * 128 : (tap + 1) * 128])
            parts[quad].append(blank)
    return jnp.concatenate(
        [jnp.concatenate(pieces, axis=0).astype(BF) for pieces in parts], axis=1
    )


def stem_forward(
    frames, weight, diff_weight, pool, fine_tab, coarse_tab, sel_fine, sel_coarse, lanes, usable, after,
    raw_out, fine_out, coarse_out, sums_out, centre_out,
    planes_ref, pooled_ref, moved_ref, fine_ref, coarse_ref, wide_fine, wide_coarse, acc_ref, flat_ref,
):
    step = pl.program_id(0)

    @pl.when(step == 0)
    def prepare():
        pooled_ref[...] = jnp.zeros_like(pooled_ref)
        moved_ref[...] = jnp.zeros_like(moved_ref)
        for seg in range(2):
            planes_ref[...] = dot(frames[seg], pool[...])
            for chan in range(3):
                lines = []
                for k in range(5):
                    at = (k * 3 + chan) * SIDE
                    lines.append(
                        planes_ref[pl.ds(at, SIDE // 2, 2), :]
                        + planes_ref[pl.ds(at + 1, SIDE // 2, 2), :]
                    )
                for k in range(4):
                    at = (k * 3 + chan) * 128 + 3
                    pooled_ref[at : at + 112, seg * 128 : (seg + 1) * 128] = lines[k + 1] - lines[k]
                at = (6 + chan) * SIDE
                moved_ref[seg, chan * 256 + 3 : chan * 256 + 227, :] = frames[
                    seg, at : at + SIDE, :
                ].astype(F32)
        small = pooled_ref[...].astype(BF)
        for left in range(0, 896, 256):
            right = min(left + 256, 896)
            coarse_ref[:, :, left:right] = (
                dot(small, coarse_tab[:, left:right]).astype(BF).reshape(12, 128, right - left)
            )
        first, second = moved_ref[0].astype(BF), moved_ref[1].astype(BF)
        for left in range(0, 1152, 256):
            right = min(left + 256, 1152)
            value = dot(first, fine_tab[0, :, left:right]) + dot(second, fine_tab[1, :, left:right])
            fine_ref[:, :, left:right] = value.astype(BF).reshape(3, 256, right - left)

        flat_ref[...] = jnp.zeros_like(flat_ref)
        for chan in range(3):
            for row in range(7):
                at = chan * 56 + row * 8
                flat_ref[at : at + 7, :] = weight[chan, row].astype(F32)
        for chan in range(12):
            for row in range(7):
                at = 168 + chan * 56 + row * 8
                flat_ref[at : at + 7, :] = diff_weight[chan, row].astype(F32)
        narrow = jnp.transpose(flat_ref[0:168, :]).astype(BF)
        for block in range(8):
            wide_fine[block * 64 : (block + 1) * 64, :] = dot(narrow, sel_fine[block]).astype(BF)
        tall = jnp.concatenate(
            [jnp.transpose(flat_ref[168 + chan * 56 : 224 + chan * 56, :]) for chan in range(12)], axis=0
        ).astype(BF)
        for up in range(4):
            spread = dot(tall, sel_coarse[up]).astype(BF)
            for chan in range(12):
                wide_coarse[up * 64 : (up + 1) * 64, chan * 128 : (chan + 1) * 128] = spread[
                    chan * 64 : (chan + 1) * 64
                ]
        acc_ref[...] = jnp.zeros_like(acc_ref)

    @pl.when(step < 4)
    def store():
        fine_out[...] = fine_ref[:, pl.ds(pl.multiple_of(step * 64, 64), 64), :]
        coarse_out[...] = coarse_ref[:, pl.ds(pl.multiple_of(step * 32, 32), 32), :]

    start = pl.multiple_of(32 * step, 32)
    fine_sum = dot(
        wide_fine[...],
        fine_patches([fine_ref[chan, pl.ds(start, 48), :].astype(F32) for chan in range(3)]),
    )
    start = pl.multiple_of(16 * step, 16)
    coarse_sum = dot(
        wide_coarse[...],
        coarse_patches([coarse_ref[chan, pl.ds(start, 32), :].astype(F32) for chan in range(12)]),
    )

    def value_at(pair, up, spot, top):
        row = (up * 4 + spot) * 64 + top
        lift = (2 * (pair % 2) + up) * 64 + top
        left = (pair // 2) * 128
        return (
            fine_sum[row : row + 16, pair * 128 : (pair + 1) * 128]
            + coarse_sum[lift : lift + 16, left : left + 128]
        )

    @pl.when(step == 0)
    def find_centre():
        for top in range(0, 64, 16):
            total = jnp.zeros((16, 128), F32)
            for pair in range(4):
                for up in range(2):
                    for spot in range(4):
                        total = total + value_at(pair, up, spot, top)
            centre_out[top : top + 16, :] = total
        spread = dot(usable[...], usable[...], TN) * (1.0 / (32 * 56))
        centre_out[...] = dot(centre_out[...], spread)

    for top in range(0, 64, 16):
        centre = centre_out[top : top + 16, :]
        plain = acc_ref[top : top + 16, :]
        square = acc_ref[64 + top : 80 + top, :]
        for pair in range(4):
            for up in range(2):
                for spot in range(4):
                    value = value_at(pair, up, spot, top)
                    row = (up * 4 + spot) * 64 + top
                    raw_out[0, row : row + 16, pair * 128 : (pair + 1) * 128] = (value - centre).astype(BF)
                    plain = plain + value
                    square = square + value * value
        acc_ref[top : top + 16, :] = plain
        acc_ref[64 + top : 80 + top, :] = square

    @pl.when(step == GROUPS - 1)
    def finish():
        sums_out[...] = dot(lanes[...], acc_ref[...], NT, HIGH)


def stem_scales(totals, lanes, count):
    spread = dot(totals, lanes, TN, HIGH) * (1.0 / count)
    return spread[0:64, :], spread[64:128, :]


def stem_middle(
    raw, cotangent, totals, gain, bias, lanes, centre, back_out, sums_out,
    seed_ref, coef_ref, scale_ref, acc_ref, *, count
):
    step = pl.program_id(0)

    @pl.when(step == 0)
    def prepare():
        average, square = stem_scales(totals[...], lanes[...], count)
        scale = lax.rsqrt(square - average * average + EPS)
        scale_ref[...] = scale
        coef_ref[0] = average - centre[...]
        coef_ref[1] = scale * gain[...]
        coef_ref[2] = bias[...] - coef_ref[0] * coef_ref[1]
        acc_ref[...] = jnp.zeros_like(acc_ref)

    blank = jnp.zeros((8, 64), F32)
    for spot in range(8):
        line = 8 * step + spot
        tall = jnp.concatenate(
            [cotangent[0, line].astype(F32), blank, cotangent[1, line].astype(F32), blank], axis=0
        )
        seed_ref[spot] = jnp.transpose(tall) * 0.25
    for top in range(0, 64, 16):
        chans = slice(top, top + 16)
        average, slope, shift = coef_ref[0, chans], coef_ref[1, chans], coef_ref[2, chans]
        plain, cross = acc_ref[0, chans], acc_ref[1, chans]
        for pair in range(4):
            cols = slice(pair * 128, (pair + 1) * 128)
            for up in range(2):
                seed = seed_ref[2 * pair + up, chans]
                for spot in range(4):
                    row = (up * 4 + spot) * 64 + top
                    value = raw[0, row : row + 16, cols].astype(F32)
                    act = value * slope + shift
                    sigma = sigmoid(act)
                    grad = seed * (sigma * (1.0 + act * (1.0 - sigma)))
                    back_out[0, row : row + 16, cols] = grad.astype(BF)
                    plain = plain + grad
                    cross = cross + grad * (value - average)
        acc_ref[0, chans] = plain
        acc_ref[1, chans] = cross

    @pl.when(step == GROUPS - 1)
    def finish():
        acc_ref[1] = acc_ref[1] * scale_ref[...]
        sums_out[...] = dot(lanes[...], acc_ref[...].reshape(128, 128), NT, HIGH)


def stem_backward(
    raw, back, fine_now, fine_next, coarse_now, coarse_next, totals, back_totals, gain, sel_fine, sel_coarse, lanes, centre,
    packed_out,
    coef_ref, packed, draw_ref, small_ref, fine_acc, coarse_acc, *, count
):
    step = pl.program_id(0)

    @pl.when(step == 0)
    def prepare():
        average, square = stem_scales(totals[...], lanes[...], count)
        scale = lax.rsqrt(square - average * average + EPS)
        first, second = stem_scales(back_totals[...], lanes[...], count)
        coef_ref[0] = gain[...] * scale
        coef_ref[1] = -gain[...] * scale * scale * second
        coef_ref[2] = gain[...] * scale * ((average - centre[...]) * scale * second - first)
        fine_acc[...] = jnp.zeros_like(fine_acc)
        coarse_acc[...] = jnp.zeros_like(coarse_acc)

    for top in range(0, 64, 16):
        on_back, on_raw, constant = (coef_ref[k, top : top + 16] for k in range(3))
        for pair in range(4):
            cols = slice(pair * 128, (pair + 1) * 128)
            for up in range(2):
                summed = None
                for spot in range(4):
                    row = (up * 4 + spot) * 64 + top
                    draw = (
                        back[0, row : row + 16, cols].astype(F32) * on_back
                        + raw[0, row : row + 16, cols].astype(F32) * on_raw
                        + constant
                    ).astype(BF)
                    draw_ref[row : row + 16, cols] = draw
                    wide = draw.astype(F32)
                    summed = wide if summed is None else summed + wide
                lift = (2 * (pair % 2) + up) * 64 + top
                left = (pair // 2) * 128
                small_ref[lift : lift + 16, left : left + 128] = summed.astype(BF)
    both = lambda now, later, chan: jnp.concatenate(
        [now[chan].astype(F32), later[chan].astype(F32)], axis=0
    )
    patches = fine_patches([both(fine_now, fine_next, chan) for chan in range(3)])
    fine_acc[...] += dot(draw_ref[...], patches, NT)
    patches = coarse_patches([both(coarse_now, coarse_next, chan) for chan in range(12)])
    coarse_acc[...] += dot(small_ref[...], patches, NT)

    @pl.when(step == GROUPS - 1)
    def finish():
        total = jnp.zeros((168, 64), F32)
        for block in range(8):
            total = total + dot(
                sel_fine[block].astype(F32), fine_acc[block * 64 : (block + 1) * 64, :], NT, HIGH
            )
        packed[0:168, 0:64] = total
        packed[0:168, 64:128] = jnp.zeros((168, 64), F32)
        for duo in range(6):
            piece = jnp.zeros((56, 128), F32)
            for up in range(4):
                stacked = jnp.concatenate(
                    [
                        coarse_acc[up * 64 : (up + 1) * 64, chan * 128 : (chan + 1) * 128]
                        for chan in (2 * duo, 2 * duo + 1)
                    ],
                    axis=0,
                )
                piece = piece + dot(sel_coarse[up].astype(F32), stacked, NT, HIGH)
            packed[168 + duo * 56 : 224 + duo * 56, :] = piece
        packed[504:512, :] = jnp.zeros((8, 128), F32)
        for quarter in range(4):
            for block in range(4):
                top = quarter * 128 + block * 32
                packed_out[quarter, :, block * 128 : (block + 1) * 128] = packed[top : top + 32, :]


def whole(*dims):
    return pl.BlockSpec(
        dims, lambda step, *rest: (0,) * len(dims), pipeline_mode=pl.Buffered(1)
    )


def group_block():
    return pl.BlockSpec((1, 512, 512), lambda step: (step, 0, 0))


def stem_first(frames, stem_weight, stem_diff_weight, tables, after):
    pool, fine_tab, coarse_tab, sel_fine, sel_coarse, lanes, usable = tables
    weight = stem_weight.transpose(1, 2, 3, 0)
    diff_weight = stem_diff_weight.transpose(1, 2, 3, 0)
    return pl.pallas_call(
        stem_forward,
        grid=(GROUPS,),
        in_specs=[
            whole(2, 15 * SIDE, SIDE),
            whole(3, 7, 7, STEMC),
            whole(12, 7, 7, STEMC),
            whole(SIDE, 128),
            whole(2, SIDE, 1152),
            whole(256, 896),
            whole(8, 168, 432),
            whole(4, 56, 128),
            whole(8, 128),
            whole(8, 128),
            whole(2, MID),
        ],
        out_specs=[
            group_block(),
            pl.BlockSpec((3, 64, 1152), lambda step: (0, jnp.minimum(step, 3), 0)),
            pl.BlockSpec((12, 32, 896), lambda step: (0, jnp.minimum(step, 3), 0)),
            whole(8, 128),
            whole(STEMC, 128),
        ],
        out_shape=[
            shape((GROUPS, 512, 512), BF),
            shape((3, 256, 1152), BF),
            shape((12, 128, 896), BF),
            shape((8, 128)),
            shape((STEMC, 128)),
        ],
        scratch_shapes=[
            pltpu.VMEM((15 * SIDE, 128), F32),
            pltpu.VMEM((12 * 128, 256), F32),
            pltpu.VMEM((2, 768, SIDE), F32),
            pltpu.VMEM((3, 256, 1152), BF),
            pltpu.VMEM((12, 128, 896), BF),
            pltpu.VMEM((512, 432), BF),
            pltpu.VMEM((256, 1536), BF),
            pltpu.VMEM((128, 128), F32),
            pltpu.VMEM((168 + 672, STEMC), F32),
        ],
        compiler_params=params("stem_forward"),
        cost_estimate=cost(8e9, 2e7),
        name="stem_forward",
    )(frames.reshape(2, 15 * SIDE, SIDE), weight, diff_weight, pool, fine_tab, coarse_tab, sel_fine, sel_coarse, lanes, usable, after)


def stem_second(raw, centre, stem_cotangent, totals, stem_gain, stem_bias, lanes, count):
    gain = jnp.broadcast_to(stem_gain[:, None], (STEMC, 128))
    bias = jnp.broadcast_to(stem_bias[:, None], (STEMC, 128))
    cot = stem_cotangent.transpose(0, 2, 3, 1)
    return pl.pallas_call(
        functools.partial(stem_middle, count=count),
        grid=(GROUPS,),
        in_specs=[
            group_block(),
            whole(2, 56, 56, 64),
            whole(8, 128),
            whole(STEMC, 128),
            whole(STEMC, 128),
            whole(8, 128),
            whole(STEMC, 128),
        ],
        out_specs=[group_block(), whole(8, 128)],
        out_shape=[shape((GROUPS, 512, 512), BF), shape((8, 128))],
        scratch_shapes=[
            pltpu.VMEM((8, 64, 128), F32),
            pltpu.VMEM((3, 64, 128), F32),
            pltpu.VMEM((64, 128), F32),
            pltpu.VMEM((2, 64, 128), F32),
        ],
        compiler_params=params("stem_middle"),
        cost_estimate=cost(8e9, 1.5e7),
        name="stem_middle",
    )(raw, cot, totals, gain, bias, lanes, centre)


def stem_third(raw, centre, back, fine, coarse, totals, back_totals, stem_gain, tables, count):
    pool, fine_tab, coarse_tab, sel_fine, sel_coarse, lanes, usable = tables
    gain = jnp.broadcast_to(stem_gain[:, None], (STEMC, 128))
    return pl.pallas_call(
        functools.partial(stem_backward, count=count),
        grid=(GROUPS,),
        in_specs=[
            group_block(),
            group_block(),
            pl.BlockSpec((3, 32, 1152), lambda step: (0, step, 0)),
            pl.BlockSpec((3, 32, 1152), lambda step: (0, step + 1, 0)),
            pl.BlockSpec((12, 16, 896), lambda step: (0, step, 0)),
            pl.BlockSpec((12, 16, 896), lambda step: (0, step + 1, 0)),
            whole(8, 128),
            whole(8, 128),
            whole(STEMC, 128),
            whole(8, 168, 432),
            whole(4, 56, 128),
            whole(8, 128),
            whole(STEMC, 128),
        ],
        out_specs=whole(4, 32, 512),
        out_shape=shape((4, 32, 512)),
        scratch_shapes=[
            pltpu.VMEM((3, 64, 128), F32),
            pltpu.VMEM((512, 128), F32),
            pltpu.VMEM((512, 512), BF),
            pltpu.VMEM((256, 256), BF),
            pltpu.VMEM((512, 432), F32),
            pltpu.VMEM((256, 1536), F32),
        ],
        compiler_params=params("stem_backward"),
        cost_estimate=cost(8e9, 2.5e7),
        name="stem_backward",
    )(raw, back, fine, fine, coarse, coarse, totals, back_totals, gain, sel_fine, sel_coarse, lanes, centre)


def put_moments(out_ref, values):
    out_ref[0:1, :] = jnp.sum(values, axis=0, keepdims=True)
    out_ref[1:2, :] = jnp.sum(values * values, axis=0, keepdims=True)


def moments(totals, count):
    average = totals[0:1] * (1.0 / count)
    square = totals[1:2] * (1.0 / count)
    return average, lax.rsqrt(square - average * average + EPS)


def affine_of(totals, count, gain, bias):
    average, scale = moments(totals, count)
    slope = gain * scale
    return slope, bias - average * slope


def back_affine(totals, sums, count, gain, middle=0.0):
    average, scale = moments(totals, count)
    first = sums[0:1] * (1.0 / count)
    second = sums[1:2] * (1.0 / count)
    on_grad = gain * scale
    on_value = -on_grad * scale * second
    return on_grad, on_value, -on_grad * first - on_value * (average - middle)


def each_piece(width, pieces):
    for left in range(0, width, 128):
        for rows in pieces:
            yield rows, slice(left, left + 128)


def put_back(out_ref, grad, value, coefs):
    on_grad, on_value, constant = coefs
    for rows, cols in each_piece(out_ref.shape[1], PIECES):
        out_ref[rows, cols] = (
            grad[rows, cols].astype(F32) * on_grad[:, cols]
            + value[rows, cols].astype(F32) * on_value[:, cols]
            + constant[:, cols]
        ).astype(BF)


def put_activation_back(out_ref, sums_out, grad, value, totals, gain, bias, count):
    average, scale = moments(totals, count)
    slope = gain * scale
    shift = bias - average * slope
    for left in range(0, MID, 128):
        cols = slice(left, left + 128)
        plain = jnp.zeros((8, 128), F32)
        cross = jnp.zeros((8, 128), F32)
        for rows in EIGHTS:
            pre = value[rows, cols]
            act = pre * slope[:, cols] + shift[:, cols]
            sigma = sigmoid(act)
            hidden = grad[rows, cols].astype(BF).astype(F32)
            back = hidden * (sigma * (1.0 + act * (1.0 - sigma)))
            out_ref[rows, cols] = back
            plain = plain + back
            cross = cross + back * (pre - average[:, cols])
        sums_out[0:1, cols] = jnp.sum(plain, axis=0, keepdims=True)
        sums_out[1:2, cols] = jnp.sum(cross, axis=0, keepdims=True) * scale[:, cols]


def first_matmuls(features, reduce_w, motion_w, reduce_out, motion_out, reduce_sum, motion_sum):
    value = dot(features[...], reduce_w[...])
    reduce_out[...] = value
    put_moments(reduce_sum, value)
    value = dot(features[...], motion_w[...])
    motion_out[...] = value
    put_moments(motion_sum, value)


def tap_mask(places, row_off, col_off):
    kept = None
    for off, base in ((row_off, 0), (col_off, 256)):
        if off:
            at = base + (128 if off > 0 else 0)
            good = places[:, at : at + 128]
            kept = good if kept is None else kept * good
    return kept


def tap_source(buffer, places, row_off, col_off, sign):
    move = sign * (7 * row_off + col_off)
    mask = tap_mask(places, sign * row_off, sign * col_off)
    value = buffer[8 + move : 8 + move + ROWS, :]
    if mask is not None:
        value = value * jnp.concatenate([mask] * (value.shape[1] // 128), axis=1)
    return value


def clear_ends(buffer):
    blank = jnp.zeros((8, buffer.shape[1]), F32)
    buffer[0:8, :] = blank
    buffer[8 + ROWS : 16 + ROWS, :] = blank


def spatial_forward(
    pre_reduce, totals, gain, bias, places, weight, hidden_out, pre_out, sums_out, buffer, *, count
):
    clear_ends(buffer)
    slope, shift = affine_of(totals[...], count, gain[...], bias[...])
    for rows, cols in each_piece(MID, PIECES):
        value = pre_reduce[rows, cols] * slope[:, cols] + shift[:, cols]
        hidden = (value * sigmoid(value)).astype(BF)
        hidden_out[rows, cols] = hidden
        buffer[8 + rows.start : 8 + rows.stop, cols] = hidden.astype(F32)
    for tap in range(9):
        row_off, col_off = tap // 3 - 1, tap % 3 - 1
        source = tap_source(buffer, places, row_off, col_off, 1).astype(BF)
        value = dot(source, weight[tap * MID : (tap + 1) * MID, :])
        if tap == 0:
            pre_out[...] = value
        else:
            pre_out[...] += value
    put_moments(sums_out, pre_out[...])


def put_centred(value, pre_out, sums_out, mid_out):
    put_moments(sums_out, value)
    middle = sums_out[0:1, :] * (1.0 / ROWS)
    mid_out[...] = middle
    pre_out[...] = (value - middle).astype(BF)


def expand_forward(
    pre_spatial, totals, gain, bias, weight, hidden_out, pre_out, sums_out, mid_out, *, count
):
    @pl.when(pl.program_id(0) == 0)
    def prepare():
        slope, shift = affine_of(totals[...], count, gain[...], bias[...])
        for rows, cols in each_piece(MID, PIECES):
            value = pre_spatial[rows, cols] * slope[:, cols] + shift[:, cols]
            hidden_out[rows, cols] = (value * sigmoid(value)).astype(BF)

    put_centred(dot(hidden_out[...], weight[...]), pre_out, sums_out, mid_out)


def at(buffer, rows, move=0):
    return buffer[64 + rows.start + move : 64 + rows.stop + move, :]


def put(buffer, rows, value):
    buffer[64 + rows.start : 64 + rows.stop, :] = value


def clear_margins(buffers):
    for buffer in buffers:
        buffer[0:64, :] = jnp.zeros((64, 128), F32)
        buffer[64 + ROWS : 128 + ROWS, :] = jnp.zeros((64, 128), F32)


def mask_of(places, rows, which):
    return places[rows, which * 128 : (which + 1) * 128]


UP, DOWN, LEFT, RIGHT = range(4)


def three(buffer, places, rows, move, before, after):
    return (
        at(buffer, rows, -move) * mask_of(places, rows, before),
        at(buffer, rows),
        at(buffer, rows, move) * mask_of(places, rows, after),
    )


def box_rows(buffer, places, out):
    for rows in EIGHTS:
        first, second, third = three(buffer, places, rows, 1, LEFT, RIGHT)
        put(out, rows, first + second + third)


def box_columns(buffer, places, rows):
    first, second, third = three(buffer, places, rows, 7, UP, DOWN)
    return (first + second + third) * (1.0 / 9.0)


def change_and_average(pre_motion, slope, keep, places, cols, spare, change, average):
    for rows in EIGHTS:
        put(spare, rows, pre_motion[rows, cols] * slope)
    for rows in EIGHTS:
        put(change, rows, (at(spare, rows, 49) - at(spare, rows)) * keep[rows, :])
    box_rows(change, places, spare)
    for rows in EIGHTS:
        put(average, rows, box_columns(spare, places, rows))


def motion_forward(
    pre_motion, totals, gain, keep, places, depth, weight, mixed_out, pre_out, sums_out, mid_out,
    spare, change, average, lines_a, lines_b, lines_c, *, count
):
    @pl.when(pl.program_id(0) == 0)
    def prepare():
        clear_margins((spare, change, average, lines_a, lines_b, lines_c))

        @pl.loop(0, MID // 128)
        def one(tile):
            cols = pl.ds(pl.multiple_of(tile * 128, 128), 128)
            scale = moments(totals[:, cols], count)[1]
            change_and_average(
                pre_motion, gain[:, cols] * scale, keep, places, cols, spare, change, average
            )
            for rows in EIGHTS:
                near = three(change, places, rows, 1, LEFT, RIGHT)
                wide = three(average, places, rows, 1, LEFT, RIGHT)
                for row, out in enumerate((lines_a, lines_b, lines_c)):
                    line = None
                    for col in range(3):
                        for scale_at, source in ((0, near), (9, wide)):
                            spot = scale_at + row * 3 + col
                            term = source[col] * depth[spot : spot + 1, cols]
                            line = term if line is None else line + term
                    put(out, rows, line)
            for rows in PIECES:
                value = (
                    at(lines_b, rows)
                    + at(lines_a, rows, -7) * mask_of(places, rows, UP)
                    + at(lines_c, rows, 7) * mask_of(places, rows, DOWN)
                )
                mixed_out[rows, cols] = value.astype(BF)

    put_centred(dot(mixed_out[...], weight[...]), pre_out, sums_out, mid_out)


def gate_kernel(
    own, pre_expand, pre_excite, features, cotangent, expand_tot, excite_tot, expand_mid, excite_mid,
    expand_gain, expand_bias, excite_gain, excite_bias,
    mine_out, other_out, direct_out, comb_out, gate_out, sums_out, output_ref, direct_ref, *, count
):
    step = pl.program_id(0)
    e_mean, e_scale = moments(expand_tot[...], count)
    x_mean, x_scale = moments(excite_tot[...], count)
    e_mean = e_mean - expand_mid[...]
    x_mean = x_mean - excite_mid[...]
    e_slope = expand_gain[...] * e_scale
    e_shift = expand_bias[...] - e_mean * e_slope
    x_slope = excite_gain[...] * x_scale
    x_shift = excite_bias[...] - x_mean * x_slope
    for left in range(0, TILE, 128):
        cols = slice(left, left + 128)
        sums = [jnp.zeros((8, 128), F32)] * 4
        for rows in PIECES:
            feats = features[rows, cols].astype(F32)
            seed = cotangent[rows, cols].astype(F32)
            pre_e = pre_expand[rows, cols].astype(F32)
            pre_x = pre_excite[rows, cols].astype(F32)
            branch = (pre_e * e_slope[:, cols] + e_shift[:, cols]).astype(BF).astype(F32)
            gate = sigmoid(pre_x * x_slope[:, cols] + x_shift[:, cols])
            lifted = feats * gate
            combined = branch + lifted
            sigma = sigmoid(combined)
            output = combined * sigma
            output_ref[rows, cols] = output.astype(BF)
            grad = seed * (sigma + output * (1.0 - sigma))
            direct_ref[rows, cols] = (grad * gate).astype(BF)
            rounded = grad.astype(BF)
            comb_out[rows, cols] = rounded
            rounded = rounded.astype(F32)
            grad_gate = grad * lifted * (1.0 - gate)
            gate_out[rows, cols] = grad_gate.astype(BF)
            terms = (
                rounded,
                rounded * (pre_e - e_mean[:, cols]),
                grad_gate,
                grad_gate * (pre_x - x_mean[:, cols]),
            )
            for spot, value in enumerate(terms):
                for up in range(0, value.shape[0], 8):
                    sums[spot] = sums[spot] + value[up : up + 8]
        finals = [jnp.sum(value, axis=0, keepdims=True) for value in sums]
        sums_out[0:1, cols] = finals[0]
        sums_out[1:2, cols] = finals[1] * e_scale[:, cols]
        sums_out[2:3, cols] = finals[2]
        sums_out[3:4, cols] = finals[3] * x_scale[:, cols]

    @pl.when(step == 0)
    def store_mine():
        mine_out[...] = output_ref[...]

    @pl.when(step == 1)
    def store_other():
        other_out[...] = output_ref[...]

    @pl.when(step < 2)
    def store_direct():
        direct_out[...] = direct_ref[...]


def pull_back(grad, value, totals, sums, gain, middle, weight, own_out, value_ref, acc, count):
    step = pl.program_id(0)
    put_back(value_ref, grad, value, back_affine(totals[...], sums, count, gain[...], middle[...]))

    @pl.when(step < 2)
    def store_own():
        own_out[...] = value_ref[...]

    part = dot(value_ref[...], weight[...], NT)

    @pl.when(step == 0)
    def begin():
        acc[...] = part

    @pl.when(step > 0)
    def add():
        acc[...] += part


def expand_backward(
    own, grad, pre_expand, totals, sums, gain, middle, weight, pre_spatial, s_totals, s_gain, s_bias,
    own_out, grad_out, sums_out, value_ref, acc, *, count
):
    pull_back(
        grad, pre_expand, totals, sums[0:2, :], gain, middle, weight, own_out, value_ref, acc, count
    )

    @pl.when(pl.program_id(0) == C // TILE - 1)
    def finish():
        put_activation_back(
            grad_out, sums_out, acc, pre_spatial, s_totals[...], s_gain[...], s_bias[...], count
        )


def excite_backward(
    own, grad, pre_excite, totals, sums, gain, middle, weight, pre_motion, m_totals, m_gain, keep,
    places, depth, own_out, grad_out, sums_out, depth_out, value_ref, acc,
    spare, change, average, seed, pull_a, pull_b, pull_c, near_out, wide_out, *, count
):
    pull_back(
        grad, pre_excite, totals, sums[2:4, :], gain, middle, weight, own_out, value_ref, acc, count
    )

    @pl.when(pl.program_id(0) == C // TILE - 1)
    def finish():
        clear_margins((spare, change, average, seed, pull_a, pull_b, pull_c, near_out, wide_out))

        @pl.loop(0, MID // 128)
        def one(tile):
            cols = pl.ds(pl.multiple_of(tile * 128, 128), 128)
            mean, scale = moments(m_totals[:, cols], count)
            change_and_average(
                pre_motion, m_gain[:, cols] * scale, keep, places, cols, spare, change, average
            )
            for rows in EIGHTS:
                put(seed, rows, acc[rows, cols])
            for base, source, out in ((0, change, near_out), (9, average, wide_out)):
                totals_of = [jnp.zeros((8, 128), F32)] * 9
                for rows in EIGHTS:
                    later, now, before = three(seed, places, rows, -7, DOWN, UP)
                    taps = three(source, places, rows, 1, LEFT, RIGHT)
                    for col, pull in enumerate((pull_a, pull_b, pull_c)):
                        total = None
                        for row, line in enumerate((later, now, before)):
                            spot = row * 3 + col
                            term = line * depth[base + spot : base + spot + 1, cols]
                            total = term if total is None else total + term
                            totals_of[spot] = totals_of[spot] + line * taps[col]
                        put(pull, rows, total)
                for spot in range(9):
                    depth_out[base + spot : base + spot + 1, cols] = jnp.sum(
                        totals_of[spot], axis=0, keepdims=True
                    )
                for rows in EIGHTS:
                    put(
                        out,
                        rows,
                        at(pull_b, rows)
                        + at(pull_a, rows, 1) * mask_of(places, rows, RIGHT)
                        + at(pull_c, rows, -1) * mask_of(places, rows, LEFT),
                    )
            box_rows(wide_out, places, spare)
            for rows in EIGHTS:
                value = at(near_out, rows) + box_columns(spare, places, rows)
                put(change, rows, value * keep[rows, :])
            plain = jnp.zeros((8, 128), F32)
            cross = jnp.zeros((8, 128), F32)
            for rows in EIGHTS:
                value = at(change, rows, -49) - at(change, rows)
                grad_out[rows, cols] = value
                plain = plain + value
                cross = cross + value * (pre_motion[rows, cols] - mean)
            sums_out[0:1, cols] = jnp.sum(plain, axis=0, keepdims=True)
            sums_out[1:2, cols] = jnp.sum(cross, axis=0, keepdims=True) * scale


def spatial_backward(
    own, grad, pre_spatial, totals, sums, gain, places, weight, pre_reduce, r_totals, r_gain, r_bias,
    m_grad, pre_motion, m_totals, m_sums, m_gain,
    taps_out, grad_out, sums_out, motion_out, motion_own, buffer, source_ref, acc, *, count
):
    clear_ends(buffer)
    on_grad, on_value, constant = back_affine(totals[...], sums[...], count, gain[...])
    for rows, cols in each_piece(MID, EIGHTS):
        buffer[8 + rows.start : 8 + rows.stop, cols] = (
            (
                grad[rows, cols] * on_grad[:, cols]
                + pre_spatial[rows, cols] * on_value[:, cols]
                + constant[:, cols]
            )
            .astype(BF)
            .astype(F32)
        )
    mine = pl.ds(pl.multiple_of((own[0] // 2) * 256, 256), 256)
    for tap in range(9):
        row_off, col_off = tap // 3 - 1, tap % 3 - 1
        source_ref[...] = tap_source(buffer, places, row_off, col_off, -1).astype(BF)
        taps_out[:, tap * 256 : (tap + 1) * 256] = source_ref[:, mine]
        value = dot(source_ref[...], weight[tap * MID : (tap + 1) * MID, :], NT)
        if tap == 0:
            acc[...] = value
        else:
            acc[...] += value
    put_activation_back(
        grad_out, sums_out, acc, pre_reduce, r_totals[...], r_gain[...], r_bias[...], count
    )
    put_back(
        motion_out, m_grad, pre_motion, back_affine(m_totals[...], m_sums[...], count, m_gain[...])
    )
    motion_own[...] = motion_out[:, mine]


def reduce_backward(
    own, grad, pre_reduce, totals, sums, gain, mine_w, other_w, motion, mine_m, other_m, direct,
    own_out, mine_out, other_out, value_ref, *, count
):
    put_back(value_ref, grad, pre_reduce, back_affine(totals[...], sums[...], count, gain[...]))
    own_out[...] = value_ref[:, pl.ds(pl.multiple_of((own[0] // 2) * 256, 256), 256)]
    for out, reduce_w, motion_w, left in (
        (other_out, other_w, other_m, MID),
        (mine_out, mine_w, mine_m, 0),
    ):
        value = dot(value_ref[...], reduce_w[...], NT) + dot(motion[...], motion_w[...], NT)
        out[...] = (value + direct[:, left : left + MID].astype(F32)).astype(BF)


def owners(sizes):
    for z in range(sizes[0]):
        for y in range(sizes[1]):
            for c in range(sizes[2]):
                yield (z * sizes[1] + y) * sizes[2] + c, (c, y, z)


def spatial_weight_kernel(hidden, taps, motion, out, turned_ref, *, sizes):
    turned_ref[...] = jnp.transpose(hidden[...].astype(F32)).astype(BF)
    clips = sizes[0] * sizes[1] * sizes[2]
    spots = dict(owners(sizes))
    share = 9 * MID // clips
    for tap in range(9):
        value = dot(turned_ref[...], taps[:, tap * 256 : (tap + 1) * 256]).astype(BF)
        for top in range(0, MID, 16):
            row = tap * MID + top
            out[*spots[row // share], row % share : row % share + 16, :] = value[top : top + 16]
    for owner, spot in owners(sizes):
        out[*spot, share:, :] = motion[owner * (C // clips) : (owner + 1) * (C // clips), :]


def early_weight_kernel(hidden, expand, mixed, excite, out, turned_ref, *, sizes):
    rows = MID // (sizes[0] * sizes[1] * sizes[2])
    for base, left, right in ((0, hidden, expand), (4, mixed, excite)):
        turned_ref[...] = jnp.transpose(left[...].astype(F32)).astype(BF)
        for block in range(4):
            value = dot(turned_ref[...], right[:, block * 256 : (block + 1) * 256]).astype(BF)
            for owner, spot in owners(sizes):
                out[*spot, (base + block) * rows : (base + block + 1) * rows, :] = value[
                    owner * rows : (owner + 1) * rows
                ]


def join_kernel(own, mine, got, out):
    first = jnp.where(own[0] % 2 == 0, mine[...].astype(F32), got[...].astype(F32))
    second = jnp.where(own[0] % 2 == 0, got[...].astype(F32), mine[...].astype(F32))
    out[...] = jnp.concatenate([first, second], axis=0).astype(BF)


def unpack_kernel(
    own, rest_0, rest_1, rest_2, rest_3, early_0, early_1, early_2, early_3,
    mine, got,
    reduce_out, spatial_out, expand_out, motion_out, excite_out, fine_out, coarse_out, grad_out,
    packed_ref, *, clips
):
    join_kernel(own, mine, got, grad_out)
    cuts = (9 * MID // clips, (9 * MID + C) // clips, (9 * MID + 2 * C) // clips)
    half = own[0] // 2
    for side, left, right in ((half, rest_0, rest_1), (1 - half, rest_2, rest_3)):
        value = left[...].astype(F32) + right[...].astype(F32)
        cols = pl.ds(pl.multiple_of(side * 256, 256), 256)
        spatial_out[:, cols] = value[: cuts[0]]
        motion_out[:, cols] = value[cuts[0] : cuts[1]]
        reduce_out[:, cols] = value[cuts[1] : cuts[2]]
    rows = MID // clips
    for flip, left, right in (
        (0, (early_0, 0), (early_1, 1)),
        (1, (early_0, 1), (early_1, 0)),
        (2, (early_2, 0), (early_3, 1)),
        (3, (early_2, 1), (early_3, 0)),
    ):
        for base, out in ((0, expand_out), (4, excite_out)):
            for block in range(2):
                value = None
                for ref, spot in (left, right):
                    top = (base + 2 * spot + block) * rows
                    part = ref[top : top + rows, :].astype(F32)
                    value = part if value is None else value + part
                out[:, pl.ds(pl.multiple_of((own[0] ^ flip) * MID + block * 256, 256), 256)] = value
    base = 8 * rows
    for flip, ref in enumerate((early_0, early_1, early_2, early_3)):
        for block in range(4):
            top, left = base + (block // 2) * 32, (block % 2) * 128
            high = ref[top : top + 32, left : left + 128].astype(F32)
            low = ref[top + 64 : top + 96, left : left + 128].astype(F32)
            at = pl.multiple_of((own[0] ^ flip) * 128 + block * 32, 32)
            packed_ref[pl.ds(at, 32), :] = high + low
    for chan in range(3):
        for row in range(7):
            at = chan * 56 + row * 8
            fine_out[chan, row] = packed_ref[at : at + 7, 0:64]
    for chan in range(12):
        side = (chan % 2) * 64
        for row in range(7):
            at = 168 + (chan // 2) * 56 + row * 8
            coarse_out[chan, row] = packed_ref[at : at + 7, side : side + 64]


def with_own(kernel, own, grid, in_specs, out_specs, out_shape, scratch, args, flops, nbytes, name):
    return pl.pallas_call(
        kernel,
        grid_spec=pltpu.PrefetchScalarGridSpec(
            num_scalar_prefetch=1,
            grid=grid,
            in_specs=in_specs,
            out_specs=out_specs,
            scratch_shapes=scratch,
        ),
        out_shape=out_shape,
        compiler_params=params(name),
        cost_estimate=cost(flops, nbytes),
        name=name,
    )(own, *args)


def place_table():
    rows = np.arange(ROWS)
    down = (rows % 49) // 7
    right = rows % 7
    kept = [down >= 1, down <= FEAT - 2, right >= 1, right <= FEAT - 2]
    return jnp.asarray(np.concatenate([np.repeat(k[:, None], 128, 1) for k in kept], axis=1), F32)


def keep_pairs(valid_rows, video_rows):
    valid_float = valid_rows.astype(F32)
    same_video = (video_rows[:, 1:] == video_rows[:, :-1]).astype(F32)
    pair_keep = valid_float[:, 1:] * valid_float[:, :-1] * same_video
    return jnp.concatenate([pair_keep, jnp.zeros_like(pair_keep[:, :1])], axis=1)


def on_device(
    features,
    out_cotangent,
    seg_valid,
    seg_video,
    frames,
    stem_cotangent,
    stem_weight,
    stem_diff_weight,
    stem_gain,
    stem_bias,
    reduce_weight,
    reduce_gain,
    reduce_bias,
    spatial_weight,
    spatial_gain,
    spatial_bias,
    expand_weight,
    expand_gain,
    expand_bias,
    motion_weight,
    motion_gain,
    depth_weight,
    excite_weight,
    excite_gain,
    excite_bias,
):
    clips = lax.axis_size("z") * lax.axis_size("y") * lax.axis_size("c")
    count = float(clips * ROWS)
    stem_count = float(clips * lax.axis_size("x") * (SIDE // 2) ** 2)
    here = lax.axis_index("x")
    micro = here % 2
    own = jnp.reshape(here, (1,)).astype(jnp.int32)
    places = place_table()

    def of_micro(rows):
        return lax.dynamic_index_in_dim(
            rows.reshape(MICRO, rows.shape[0] // MICRO, rows.shape[1]), micro, 0, False
        )

    feats = of_micro(features)
    seeds = of_micro(out_cotangent)
    keep = jnp.broadcast_to(
        jnp.repeat(of_micro(keep_pairs(seg_valid, seg_video)).reshape(-1), FEAT * FEAT)[:, None],
        (ROWS, 128),
    )
    line = lambda vector: vector.reshape(1, -1)
    reduce_gain, reduce_bias = line(reduce_gain), line(reduce_bias)
    spatial_gain, spatial_bias = line(spatial_gain), line(spatial_bias)
    expand_gain, expand_bias = line(expand_gain), line(expand_bias)
    excite_gain, excite_bias = line(excite_gain), line(excite_bias)
    motion_gain = line(motion_gain)
    depth = jnp.pad(depth_weight.reshape(18, MID), ((0, 6), (0, 0)))

    tables = stem_tables()
    lanes = tables[5]
    column = lambda rows, width: pl.BlockSpec((rows, width), lambda step, *rest: (0, step))
    pre_reduce, pre_motion, reduce_sum, motion_sum = pl.pallas_call(
        first_matmuls,
        grid=(2,),
        in_specs=[whole(ROWS, C), column(C, 256), column(C, 256)],
        out_specs=[column(ROWS, 256), column(ROWS, 256), column(2, 256), column(2, 256)],
        out_shape=[shape((ROWS, MID)), shape((ROWS, MID)), shape((2, MID)), shape((2, MID))],
        compiler_params=params("first_matmuls"),
        cost_estimate=cost(1.7e9, 1e7),
        name="first_matmuls",
    )(feats, reduce_weight, motion_weight)
    raw, fine, coarse, stem_sum, centre = stem_first(
        frames, stem_weight, stem_diff_weight, tables, reduce_sum
    )
    stem_sum = ring_sum(stem_sum[:2], "x")

    reduce_tot, motion_tot, stem_tot = merge_sum(reduce_sum, motion_sum, stem_sum)
    stem_tot = jnp.pad(stem_tot, ((0, 6), (0, 0)))
    back, back_sum = stem_second(
        raw, centre, stem_cotangent, stem_tot, stem_gain, stem_bias, lanes, stem_count
    )
    back_sum = ring_sum(back_sum[:2], "x")

    hidden_one, pre_spatial, spatial_sum = pl.pallas_call(
        functools.partial(spatial_forward, count=count),
        in_specs=[VMEM] * 6,
        out_specs=[VMEM] * 3,
        out_shape=[shape((ROWS, MID), BF), shape((ROWS, MID)), shape((2, MID))],
        scratch_shapes=[pltpu.VMEM((ROWS + 16, MID), F32)],
        compiler_params=params("spatial_forward"),
        cost_estimate=cost(1.9e9, 8e6),
        name="spatial_forward",
    )(pre_reduce, reduce_tot, reduce_gain, reduce_bias, places, spatial_weight)

    mixed, pre_excite, excite_sum, excite_mid = pl.pallas_call(
        functools.partial(motion_forward, count=count),
        grid=(4,),
        in_specs=[
            whole(ROWS, MID), whole(2, MID), whole(1, MID), whole(ROWS, 128), whole(ROWS, 512),
            whole(24, MID), column(MID, 512),
        ],
        out_specs=[whole(ROWS, MID), column(ROWS, 512), column(2, 512), column(1, 512)],
        out_shape=[shape((ROWS, MID), BF), shape((ROWS, C), BF), shape((2, C)), shape((1, C))],
        scratch_shapes=[pltpu.VMEM((ROWS + 128, 128), F32)] * 6,
        compiler_params=params("motion_forward"),
        cost_estimate=cost(2e9, 1.2e7),
        name="motion_forward",
    )(pre_motion, motion_tot, motion_gain, keep, places, depth, excite_weight)
    spatial_tot, excite_tot, back_tot = merge_sum(spatial_sum, excite_sum, back_sum)
    back_tot = jnp.pad(back_tot, ((0, 6), (0, 0)))
    stem_packed = stem_third(
        raw, centre, back, fine, coarse, stem_tot, back_tot, stem_gain, tables, stem_count
    )
    back_both = back_tot[0] + back_tot[1]
    stem_gain_grad, stem_bias_grad = back_both[64:], back_both[:64]

    hidden_two, pre_expand, expand_sum, expand_mid = pl.pallas_call(
        functools.partial(expand_forward, count=count),
        grid=(4,),
        in_specs=[
            whole(ROWS, MID), whole(2, MID), whole(1, MID), whole(1, MID), column(MID, 512),
        ],
        out_specs=[whole(ROWS, MID), column(ROWS, 512), column(2, 512), column(1, 512)],
        out_shape=[shape((ROWS, MID), BF), shape((ROWS, C), BF), shape((2, C)), shape((1, C))],
        compiler_params=params("expand_forward"),
        cost_estimate=cost(1e9, 1e7),
        name="expand_forward",
    )(pre_spatial, spatial_tot, spatial_gain, spatial_bias, expand_weight)
    expand_tot = sum_dp(expand_sum)

    def turned(rows):
        return pl.BlockSpec((rows, TILE), lambda step, own_ref: (0, step ^ own_ref[0]))

    def kept(first, last):
        return pl.BlockSpec(
            (ROWS, TILE), lambda step, own_ref: (0, jnp.clip(step - first, 0, last - first))
        )

    mine, other, direct, grad_comb, grad_gate, gate_sum = with_own(
        functools.partial(gate_kernel, count=count),
        own,
        (C // TILE,),
        [turned(ROWS)] * 4 + [turned(2)] * 2 + [turned(1)] * 6,
        [
            whole(ROWS, MID), whole(ROWS, MID), kept(0, 1), turned(ROWS), turned(ROWS), turned(4),
        ],
        [
            shape((ROWS, MID), BF), shape((ROWS, MID), BF), shape((ROWS, 2 * MID), BF),
            shape((ROWS, C), BF), shape((ROWS, C), BF), shape((4, C)),
        ],
        [pltpu.VMEM((ROWS, TILE), BF)] * 2,
        (
            pre_expand, pre_excite, feats, seeds, expand_tot, excite_tot, expand_mid, excite_mid,
            expand_gain, expand_bias, excite_gain, excite_bias,
        ),
        2e9,
        2e7,
        "gate",
    )
    gate_tot = sum_dp(gate_sum)

    got_result = from_peer(other, 1)

    expand_own, grad_spatial, spatial_back = with_own(
        functools.partial(expand_backward, count=count),
        own,
        (C // TILE,),
        [
            turned(ROWS), turned(ROWS), turned(2), turned(4), turned(1), turned(1), turned(MID),
            whole(ROWS, MID), whole(2, MID), whole(1, MID), whole(1, MID),
        ],
        [kept(0, 1), whole(ROWS, MID), whole(2, MID)],
        [shape((ROWS, 2 * MID), BF), shape((ROWS, MID)), shape((2, MID))],
        [pltpu.VMEM((ROWS, TILE), BF), pltpu.VMEM((ROWS, MID), F32)],
        (
            grad_comb, pre_expand, expand_tot, gate_tot, expand_gain, expand_mid, expand_weight,
            pre_spatial, spatial_tot, spatial_gain, spatial_bias,
        ),
        1e9,
        1e7,
        "expand_backward",
    )

    excite_own, grad_reduced, motion_back, depth_part = with_own(
        functools.partial(excite_backward, count=count),
        own,
        (C // TILE,),
        [
            turned(ROWS), turned(ROWS), turned(2), turned(4), turned(1), turned(1), turned(MID),
            whole(ROWS, MID), whole(2, MID), whole(1, MID), whole(ROWS, 128), whole(ROWS, 512),
            whole(24, MID),
        ],
        [kept(0, 1), whole(ROWS, MID), whole(2, MID), whole(18, MID)],
        [shape((ROWS, 2 * MID), BF), shape((ROWS, MID)), shape((2, MID)), shape((18, MID))],
        [pltpu.VMEM((ROWS, TILE), BF), pltpu.VMEM((ROWS, MID), F32)]
        + [pltpu.VMEM((ROWS + 128, 128), F32)] * 9,
        (
            grad_gate, pre_excite, excite_tot, gate_tot, excite_gain, excite_mid, excite_weight,
            pre_motion, motion_tot, motion_gain, keep, places, depth,
        ),
        2e9,
        1e7,
        "excite_backward",
    )
    across = lambda left, right: dot(left, right, TN).astype(BF)
    sizes = [lax.axis_size(axis) for axis in ("z", "y", "c")]
    early = pl.pallas_call(
        functools.partial(early_weight_kernel, sizes=sizes),
        in_specs=[VMEM] * 4,
        out_specs=VMEM,
        out_shape=shape((*sizes[::-1], 8 * (MID // clips), 256), BF),
        scratch_shapes=[pltpu.VMEM((MID, ROWS), BF)],
        compiler_params=params("early_weight"),
        cost_estimate=cost(1e9, 5e6),
        name="early_weight",
    )(hidden_two, expand_own, mixed, excite_own)
    stem_quarter = scatter_lead(stem_packed, "x", F32)
    back_all = core_sum(jnp.concatenate([motion_back, spatial_back, stem_quarter], axis=0))
    back_all, early = tie(back_all, early)
    early = scatter_lead(early, "c")
    back_all = ring_sum(back_all, "y")
    back_all, early = tie(back_all, early)
    early = scatter_lead(early, "y")
    back_all = ring_sum(back_all, "z")
    motion_back_tot, spatial_back_tot = back_all[:2], back_all[2:4]

    taps, grad_reduce, reduce_back, motion_full, motion_own = with_own(
        functools.partial(spatial_backward, count=count),
        own,
        (1,),
        [
            whole(ROWS, MID), whole(ROWS, MID), whole(2, MID), whole(2, MID), whole(1, MID),
            whole(ROWS, 512), whole(9 * MID, MID), whole(ROWS, MID), whole(2, MID),
            whole(1, MID), whole(1, MID),
            whole(ROWS, MID), whole(ROWS, MID), whole(2, MID), whole(2, MID), whole(1, MID),
        ],
        [
            whole(ROWS, 9 * 256), whole(ROWS, MID), whole(2, MID), whole(ROWS, MID), whole(ROWS, 256),
        ],
        [
            shape((ROWS, 9 * 256), BF), shape((ROWS, MID)), shape((2, MID)),
            shape((ROWS, MID), BF), shape((ROWS, 256), BF),
        ],
        [
            pltpu.VMEM((ROWS + 16, MID), F32),
            pltpu.VMEM((ROWS, MID), BF),
            pltpu.VMEM((ROWS, MID), F32),
        ],
        (
            grad_spatial, pre_spatial, spatial_tot, spatial_back_tot, spatial_gain, places,
            spatial_weight, pre_reduce, reduce_tot, reduce_gain, reduce_bias,
            grad_reduced, pre_motion, motion_tot, motion_back_tot, motion_gain,
        ),
        2e9,
        1e7,
        "spatial_backward",
    )
    mine_rows = pl.BlockSpec((MID, MID), lambda step, own_ref: (own_ref[0], 0))
    other_rows = pl.BlockSpec((MID, MID), lambda step, own_ref: (own_ref[0] ^ 1, 0))
    middle = pl.pallas_call(
        functools.partial(spatial_weight_kernel, sizes=sizes),
        in_specs=[VMEM] * 3,
        out_specs=VMEM,
        out_shape=shape((*sizes[::-1], (9 * MID + C) // clips, 256), BF),
        scratch_shapes=[pltpu.VMEM((MID, ROWS), BF)],
        compiler_params=params("spatial_weight"),
        cost_estimate=cost(1e9, 5e6),
        name="spatial_weight",
    )(hidden_one, taps, across(feats, motion_own))

    reduce_back = core_sum(jnp.concatenate([reduce_back, depth_part], axis=0))
    reduce_back, middle, early, got_result = tie(reduce_back, middle, early, got_result)
    early = scatter_lead(early, "z")
    middle = scatter_lead(middle, "c")
    reduce_back = ring_sum(reduce_back, "y")
    reduce_back, middle, early = tie(reduce_back, middle, early)
    stem_quarter = back_all[4:]
    stem_high = stem_quarter.astype(BF)
    stem_low = (stem_quarter - stem_high.astype(F32)).astype(BF)
    halves = [part[:, left : left + 256] for part in (stem_high, stem_low) for left in (0, 256)]
    early = gather_x(jnp.concatenate([early, *halves], axis=0))
    upward, downward = scatter_start(middle, "y")
    reduce_back = ring_sum(reduce_back, "z")
    reduce_back, upward, downward = tie(reduce_back, upward, downward)
    reduce_back_tot = reduce_back[:2]
    middle = scatter_finish(middle, "y", upward, downward)

    reduce_own, mine_grad, other_grad = with_own(
        functools.partial(reduce_backward, count=count),
        own,
        (1,),
        [
            whole(ROWS, MID), whole(ROWS, MID), whole(2, MID), whole(2, MID), whole(1, MID),
            mine_rows, other_rows, whole(ROWS, MID), mine_rows, other_rows, whole(ROWS, 2 * MID),
        ],
        [whole(ROWS, 256), whole(ROWS, MID), whole(ROWS, MID)],
        [shape((ROWS, 256), BF), shape((ROWS, MID), BF), shape((ROWS, MID), BF)],
        [pltpu.VMEM((ROWS, MID), BF)],
        (
            grad_reduce, pre_reduce, reduce_tot, reduce_back_tot, reduce_gain,
            reduce_weight, reduce_weight, motion_full, motion_weight, motion_weight, direct,
        ),
        5e8,
        8e6,
        "reduce_backward",
    )
    got_grad = from_peer(other_grad, 1)
    late = across(feats, reduce_own).reshape(*sizes, C // clips, 256).transpose(2, 1, 0, 3, 4)
    late = scatter_lead(late, "c")
    late, middle, *early = tie(late, middle, *early)
    late = scatter_lead(late, "y")
    late, got_grad = tie(late, got_grad)
    rest = scatter_lead(jnp.concatenate([middle, late], axis=1), "z")
    rest = gather_x(rest)
    result = with_own(
        join_kernel,
        own,
        (1,),
        [whole(ROWS, MID), whole(ROWS, MID)],
        whole(2 * ROWS, MID),
        shape((2 * ROWS, MID), BF),
        [],
        (mine, got_result),
        1e5,
        2e6,
        "join_result",
    )

    (
        reduce_grad, spatial_grad, expand_grad, motion_grad, excite_grad,
        stem_weight_grad, stem_diff_grad, features_grad,
    ) = with_own(
        functools.partial(unpack_kernel, clips=clips),
        own,
        (1,),
        [whole(*part.shape) for part in rest]
        + [whole(*part.shape) for part in early]
        + [whole(ROWS, MID), whole(ROWS, MID)],
        [
            whole(C // clips, MID), whole(9 * MID // clips, MID), whole(MID // clips, C),
            whole(C // clips, MID), whole(MID // clips, C),
            whole(3, 7, 7, STEMC), whole(12, 7, 7, STEMC), whole(2 * ROWS, MID),
        ],
        [
            shape((C // clips, MID)), shape((9 * MID // clips, MID)), shape((MID // clips, C)),
            shape((C // clips, MID)), shape((MID // clips, C)),
            shape((3, 7, 7, STEMC)), shape((12, 7, 7, STEMC)), shape((2 * ROWS, MID), BF),
        ],
        [pltpu.VMEM((512, 128), F32)],
        (*rest, *early, mine_grad, got_grad),
        1e6,
        6e6,
        "unpack",
    )
    stem_weight_grad = stem_weight_grad.transpose(3, 0, 1, 2)
    stem_diff_grad = stem_diff_grad.transpose(3, 0, 1, 2)

    small = jnp.concatenate([gate_tot.reshape(16, MID), back_all[:4], reduce_back], axis=0)
    small = small + from_peer(small, 1)
    gate_both = small[:16].reshape(4, C)
    depth_grad = small[22:40].reshape(2, 3, 3, MID)
    reduce_both = small[20:22]
    return (
        result,
        features_grad,
        stem_weight_grad,
        stem_diff_grad,
        stem_gain_grad,
        stem_bias_grad,
        reduce_grad,
        reduce_both[1],
        reduce_both[0],
        spatial_grad,
        small[19],
        small[18],
        expand_grad,
        gate_both[1],
        gate_both[0],
        motion_grad,
        small[17],
        depth_grad,
        excite_grad,
        gate_both[3],
        gate_both[2],
    )


def solution(mesh):
    grid = Mesh(mesh.devices.reshape(4, 4, 2, 4), ("z", "y", "c", "x"))
    clips = ("z", "y", "c")
    everyone = ("z", "y", "c", "x")
    split = P(clips, None)
    copied = P()
    return jax.shard_map(
        on_device,
        mesh=grid,
        in_specs=(split,) * 4
        + (P(everyone, None, None, None, None), P(everyone, None, None, None))
        + (copied,) * 19,
        out_specs=(P(clips, "x"), P(clips, "x"))
        + (copied,) * 4
        + (split, copied, copied) * 3
        + (split, copied, copied)
        + (split, copied, copied),
        check_vma=False,
    )
```

```python
import functools

import jax
import jax.numpy as jnp
import numpy as np
from jax import lax
from jax.experimental import pallas as pl
from jax.experimental.pallas import tpu as pltpu
from jax.sharding import Mesh
from jax.sharding import PartitionSpec as P

C = 2048
MID = 512
STEMC = 64
SIDE = 224
FEAT = 7
SEG = 8
MICRO = 2
ROWS = SEG * FEAT * FEAT
EPS = 1e-05
BF = jnp.bfloat16
F32 = jnp.float32
HIGH = lax.Precision.HIGHEST
NN = (((1,), (0,)), ((), ()))
NT = (((1,), (1,)), ((), ()))
TN = (((0,), (0,)), ((), ()))
GROUPS = 7
TILE = 512
VMEM = pl.BlockSpec(memory_space=pltpu.VMEM)
SMEM = pl.BlockSpec(memory_space=pltpu.SMEM)
PIECES = [slice(top, min(top + 16, ROWS)) for top in range(0, ROWS, 16)]
EIGHTS = [slice(top, top + 8) for top in range(0, ROWS, 8)]


def sigmoid(values):
    return 0.5 + 0.5 * jnp.tanh(0.5 * values)


def dot(left, right, dims=NN, precision=None):
    return lax.dot_general(left, right, dims, precision=precision, preferred_element_type=F32)


LIMITS = {}


def params(name):
    return pltpu.CompilerParams(vmem_limit_bytes=LIMITS.get(name, 20) * 2**20)


def held(dims, dtype=F32):
    return pltpu.VMEM(dims, dtype)


def in_vmem(*values):
    return [pltpu.with_memory_space_constraint(value, pltpu.VMEM) for value in values]


def cost(flops, nbytes):
    return pl.CostEstimate(flops=int(flops), bytes_accessed=int(nbytes), transcendentals=0)


def shape(dims, dtype=F32):
    return jax.ShapeDtypeStruct(dims, dtype)


def ring_sum(values, axis):
    size = lax.axis_size(axis)
    if size == 1:
        return values
    got = [
        lax.ppermute(values, axis, [(i, (i + step) % size) for i in range(size)])
        for step in range(1, size)
    ]
    if size == 2:
        return values + got[0]
    return (values + got[1]) + (got[0] + got[2])


def core_sum(values):
    pair = lax.all_gather(values, "c")
    return pair[0] + pair[1]


def sum_dp(values):
    return ring_sum(ring_sum(core_sum(values), "y"), "z")


def shift_by(values, axis, step):
    size = lax.axis_size(axis)
    return lax.ppermute(values, axis, [(i, (i + step) % size) for i in range(size)])


def scatter_lead(blocks, axis, kind=BF):
    total = blocks[0].astype(F32)
    for step in range(1, blocks.shape[0]):
        total = total + shift_by(blocks[step], axis, step).astype(F32)
    return total.astype(kind)


def scatter_start(blocks, axis):
    half = blocks.shape[1] // 2
    return shift_by(blocks[2, :half], axis, 1), shift_by(blocks[2, half:], axis, -1)


def scatter_finish(blocks, axis, upward, downward):
    half = blocks.shape[1] // 2
    up, down = blocks[1].astype(F32), blocks[3].astype(F32)
    up = jnp.concatenate([up[:half] + upward.astype(F32), up[half:]], axis=0).astype(BF)
    down = jnp.concatenate([down[:half], down[half:] + downward.astype(F32)], axis=0).astype(BF)
    up, down = shift_by(up, axis, 1), shift_by(down, axis, -1)
    return (blocks[0].astype(F32) + up.astype(F32) + down.astype(F32)).astype(BF)


def tie(*values):
    return lax.optimization_barrier(values)


def from_peer(values, flip):
    size = lax.axis_size("x")
    return lax.ppermute(values, "x", [(i, i ^ flip) for i in range(size)])


def gather_x(block):
    return [block] + [from_peer(block, flip) for flip in (1, 2, 3)]


def merge_sum(*pieces):
    wide = jnp.concatenate(pieces, axis=1)
    total = sum_dp(wide)
    ends = np.cumsum([piece.shape[1] for piece in pieces])
    return [total[:, end - piece.shape[1] : end] for end, piece in zip(ends, pieces)]


def stem_tables():
    half, quarter = SIDE // 2, SIDE // 4
    pool = np.zeros((SIDE, 128), np.float32)
    for column in range(SIDE):
        pool[column, column // 2] = 0.25
    fine = np.zeros((2, SIDE, 9 * 128), np.float32)
    coarse = np.zeros((2 * 128, 7 * 128), np.float32)
    for seg in range(2):
        for spot in range(quarter):
            for tap in range(9):
                column = 4 * spot + tap - 3
                if 0 <= column < SIDE:
                    fine[seg, column, tap * 128 + seg * 64 + spot] = 1
            for tap in range(7):
                column = 2 * spot + tap - 3
                if 0 <= column < half:
                    coarse[seg * 128 + column, tap * 128 + seg * 64 + spot] = 1
    sel_fine = np.zeros((8, 168, 432), np.float32)
    for up in range(2):
        for row in range(2):
            for col in range(2):
                for chan in range(3):
                    for dy in range(7):
                        for dx in range(7):
                            sel_fine[
                                up * 4 + row * 2 + col,
                                chan * 56 + dy * 8 + dx,
                                chan * 144 + (2 * col + dx) * 16 + 4 * up + 2 * row + dy,
                            ] = 1
    sel_coarse = np.zeros((4, 56, 128), np.float32)
    for up in range(4):
        for dy in range(7):
            for dx in range(7):
                sel_coarse[up, dy * 8 + dx, dx * 16 + 2 * up + dy] = 1
    lanes = np.zeros((8, 128), np.float32)
    lanes[0, :64] = 1
    lanes[1, 64:] = 1
    usable = np.zeros((8, 128), np.float32)
    usable[0, :56] = 1
    usable[1, 64:120] = 1
    return [
        jnp.asarray(table, dtype)
        for table, dtype in (
            (pool, BF),
            (fine, BF),
            (coarse, BF),
            (sel_fine, BF),
            (sel_coarse, BF),
            (lanes, F32),
            (usable, F32),
        )
    ]


def fine_patches(tall):
    parts = []
    for pair in range(4):
        rows = slice(8 * pair, 8 * pair + 16)
        parts.append(
            jnp.concatenate(
                [
                    tall[chan][rows, tap * 128 : (tap + 1) * 128]
                    for chan in range(3)
                    for tap in range(9)
                ],
                axis=0,
            ).astype(BF)
        )
    return jnp.concatenate(parts, axis=1)


def coarse_patches(tall):
    blank = jnp.zeros((16, 128), F32)
    parts = [[], []]
    for chan in range(12):
        for quad in range(2):
            rows = slice(8 * quad, 8 * quad + 16)
            for tap in range(7):
                parts[quad].append(tall[chan][rows, tap * 128 : (tap + 1) * 128])
            parts[quad].append(blank)
    return jnp.concatenate(
        [jnp.concatenate(pieces, axis=0).astype(BF) for pieces in parts], axis=1
    )


def stem_forward(
    frames, weight, diff_weight, pool, fine_tab, coarse_tab, sel_fine, sel_coarse, lanes, usable, after,
    raw_out, fine_out, coarse_out, sums_out, centre_out,
    planes_ref, pooled_ref, moved_ref, fine_ref, coarse_ref, wide_fine, wide_coarse, acc_ref, flat_ref,
):
    step = pl.program_id(0)

    @pl.when(step == 0)
    def prepare():
        pooled_ref[...] = jnp.zeros_like(pooled_ref)
        moved_ref[...] = jnp.zeros_like(moved_ref)
        for seg in range(2):
            planes_ref[...] = dot(frames[seg], pool[...])
            for chan in range(3):
                lines = []
                for k in range(5):
                    at = (k * 3 + chan) * SIDE
                    lines.append(
                        planes_ref[pl.ds(at, SIDE // 2, 2), :]
                        + planes_ref[pl.ds(at + 1, SIDE // 2, 2), :]
                    )
                for k in range(4):
                    at = (k * 3 + chan) * 128 + 3
                    pooled_ref[at : at + 112, seg * 128 : (seg + 1) * 128] = lines[k + 1] - lines[k]
                at = (6 + chan) * SIDE
                moved_ref[seg, chan * 256 + 3 : chan * 256 + 227, :] = frames[
                    seg, at : at + SIDE, :
                ].astype(F32)
        small = pooled_ref[...].astype(BF)
        for left in range(0, 896, 256):
            right = min(left + 256, 896)
            coarse_ref[:, :, left:right] = (
                dot(small, coarse_tab[:, left:right]).astype(BF).reshape(12, 128, right - left)
            )
        first, second = moved_ref[0].astype(BF), moved_ref[1].astype(BF)
        for left in range(0, 1152, 256):
            right = min(left + 256, 1152)
            value = dot(first, fine_tab[0, :, left:right]) + dot(second, fine_tab[1, :, left:right])
            fine_ref[:, :, left:right] = value.astype(BF).reshape(3, 256, right - left)

        flat_ref[...] = jnp.zeros_like(flat_ref)
        for chan in range(3):
            for row in range(7):
                at = chan * 56 + row * 8
                flat_ref[at : at + 7, :] = weight[chan, row].astype(F32)
        for chan in range(12):
            for row in range(7):
                at = 168 + chan * 56 + row * 8
                flat_ref[at : at + 7, :] = diff_weight[chan, row].astype(F32)
        narrow = jnp.transpose(flat_ref[0:168, :]).astype(BF)
        for block in range(8):
            wide_fine[block * 64 : (block + 1) * 64, :] = dot(narrow, sel_fine[block]).astype(BF)
        tall = jnp.concatenate(
            [jnp.transpose(flat_ref[168 + chan * 56 : 224 + chan * 56, :]) for chan in range(12)], axis=0
        ).astype(BF)
        for up in range(4):
            spread = dot(tall, sel_coarse[up]).astype(BF)
            for chan in range(12):
                wide_coarse[up * 64 : (up + 1) * 64, chan * 128 : (chan + 1) * 128] = spread[
                    chan * 64 : (chan + 1) * 64
                ]
        acc_ref[...] = jnp.zeros_like(acc_ref)

    @pl.when(step < 4)
    def store():
        fine_out[...] = fine_ref[:, pl.ds(pl.multiple_of(step * 64, 64), 64), :]
        coarse_out[...] = coarse_ref[:, pl.ds(pl.multiple_of(step * 32, 32), 32), :]

    start = pl.multiple_of(32 * step, 32)
    fine_sum = dot(
        wide_fine[...],
        fine_patches([fine_ref[chan, pl.ds(start, 48), :].astype(F32) for chan in range(3)]),
    )
    start = pl.multiple_of(16 * step, 16)
    coarse_sum = dot(
        wide_coarse[...],
        coarse_patches([coarse_ref[chan, pl.ds(start, 32), :].astype(F32) for chan in range(12)]),
    )

    def value_at(pair, up, spot, top):
        row = (up * 4 + spot) * 64 + top
        lift = (2 * (pair % 2) + up) * 64 + top
        left = (pair // 2) * 128
        return (
            fine_sum[row : row + 16, pair * 128 : (pair + 1) * 128]
            + coarse_sum[lift : lift + 16, left : left + 128]
        )

    @pl.when(step == 0)
    def find_centre():
        for top in range(0, 64, 16):
            total = jnp.zeros((16, 128), F32)
            for pair in range(4):
                for up in range(2):
                    for spot in range(4):
                        total = total + value_at(pair, up, spot, top)
            centre_out[top : top + 16, :] = total
        spread = dot(usable[...], usable[...], TN) * (1.0 / (32 * 56))
        centre_out[...] = dot(centre_out[...], spread)

    for top in range(0, 64, 16):
        centre = centre_out[top : top + 16, :]
        plain = acc_ref[top : top + 16, :]
        square = acc_ref[64 + top : 80 + top, :]
        for pair in range(4):
            for up in range(2):
                for spot in range(4):
                    value = value_at(pair, up, spot, top)
                    row = (up * 4 + spot) * 64 + top
                    raw_out[0, row : row + 16, pair * 128 : (pair + 1) * 128] = (value - centre).astype(BF)
                    plain = plain + value
                    square = square + value * value
        acc_ref[top : top + 16, :] = plain
        acc_ref[64 + top : 80 + top, :] = square

    @pl.when(step == GROUPS - 1)
    def finish():
        sums_out[...] = dot(lanes[...], acc_ref[...], NT, HIGH)


def over_lanes(vector):
    return dot(vector, jnp.ones((1, 128), F32), TN, HIGH)


def stem_scales(totals, lanes, count):
    spread = dot(totals, lanes, TN, HIGH) * (1.0 / count)
    return spread[0:64, :], spread[64:128, :]


def stem_middle(
    raw, cotangent, totals, gain, bias, lanes, centre, back_out, sums_out,
    seed_ref, coef_ref, scale_ref, acc_ref, *, count
):
    step = pl.program_id(0)

    @pl.when(step == 0)
    def prepare():
        average, square = stem_scales(totals[...], lanes[...], count)
        scale = lax.rsqrt(square - average * average + EPS)
        scale_ref[...] = scale
        coef_ref[0] = average - centre[...]
        coef_ref[1] = scale * over_lanes(gain[...])
        coef_ref[2] = over_lanes(bias[...]) - coef_ref[0] * coef_ref[1]
        acc_ref[...] = jnp.zeros_like(acc_ref)

    blank = jnp.zeros((8, 64), F32)
    for spot in range(8):
        line = 8 * step + spot
        tall = jnp.concatenate(
            [cotangent[0, line].astype(F32), blank, cotangent[1, line].astype(F32), blank], axis=0
        )
        seed_ref[spot] = jnp.transpose(tall) * 0.25
    for top in range(0, 64, 16):
        chans = slice(top, top + 16)
        average, slope, shift = coef_ref[0, chans], coef_ref[1, chans], coef_ref[2, chans]
        plain, cross = acc_ref[0, chans], acc_ref[1, chans]
        for pair in range(4):
            cols = slice(pair * 128, (pair + 1) * 128)
            for up in range(2):
                seed = seed_ref[2 * pair + up, chans]
                for spot in range(4):
                    row = (up * 4 + spot) * 64 + top
                    value = raw[0, row : row + 16, cols].astype(F32)
                    act = value * slope + shift
                    sigma = sigmoid(act)
                    grad = seed * (sigma * (1.0 + act * (1.0 - sigma)))
                    back_out[0, row : row + 16, cols] = grad.astype(BF)
                    plain = plain + grad
                    cross = cross + grad * (value - average)
        acc_ref[0, chans] = plain
        acc_ref[1, chans] = cross

    @pl.when(step == GROUPS - 1)
    def finish():
        acc_ref[1] = acc_ref[1] * scale_ref[...]
        sums_out[...] = dot(lanes[...], acc_ref[...].reshape(128, 128), NT, HIGH)


def stem_backward(
    place, raw, back, fine_now, fine_next, coarse_now, coarse_next, totals, back_totals, gain, sel_fine, sel_coarse, lanes, centre,
    packed_out,
    coef_ref, packed, draw_ref, small_ref, fine_acc, coarse_acc, *, count
):
    step = pl.program_id(0)

    @pl.when(step == 0)
    def prepare():
        average, square = stem_scales(totals[...], lanes[...], count)
        scale = lax.rsqrt(square - average * average + EPS)
        first, second = stem_scales(back_totals[...], lanes[...], count)
        slope = over_lanes(gain[...]) * scale
        coef_ref[0] = slope
        coef_ref[1] = -slope * scale * second
        coef_ref[2] = slope * ((average - centre[...]) * scale * second - first)
        fine_acc[...] = jnp.zeros_like(fine_acc)
        coarse_acc[...] = jnp.zeros_like(coarse_acc)

    for top in range(0, 64, 16):
        on_back, on_raw, constant = (coef_ref[k, top : top + 16] for k in range(3))
        for pair in range(4):
            cols = slice(pair * 128, (pair + 1) * 128)
            for up in range(2):
                summed = None
                for spot in range(4):
                    row = (up * 4 + spot) * 64 + top
                    draw = (
                        back[0, row : row + 16, cols].astype(F32) * on_back
                        + raw[0, row : row + 16, cols].astype(F32) * on_raw
                        + constant
                    ).astype(BF)
                    draw_ref[row : row + 16, cols] = draw
                    wide = draw.astype(F32)
                    summed = wide if summed is None else summed + wide
                lift = (2 * (pair % 2) + up) * 64 + top
                left = (pair // 2) * 128
                small_ref[lift : lift + 16, left : left + 128] = summed.astype(BF)
    both = lambda now, later, chan: jnp.concatenate(
        [now[chan].astype(F32), later[chan].astype(F32)], axis=0
    )
    patches = fine_patches([both(fine_now, fine_next, chan) for chan in range(3)])
    fine_acc[...] += dot(draw_ref[...], patches, NT)
    patches = coarse_patches([both(coarse_now, coarse_next, chan) for chan in range(12)])
    coarse_acc[...] += dot(small_ref[...], patches, NT)

    @pl.when(step == GROUPS - 1)
    def finish():
        total = jnp.zeros((168, 64), F32)
        for block in range(8):
            total = total + dot(
                sel_fine[block].astype(F32), fine_acc[block * 64 : (block + 1) * 64, :], NT, HIGH
            )
        packed[0:168, 0:64] = total
        packed[0:168, 64:128] = jnp.zeros((168, 64), F32)
        for duo in range(6):
            piece = jnp.zeros((56, 128), F32)
            for up in range(4):
                stacked = jnp.concatenate(
                    [
                        coarse_acc[up * 64 : (up + 1) * 64, chan * 128 : (chan + 1) * 128]
                        for chan in (2 * duo, 2 * duo + 1)
                    ],
                    axis=0,
                )
                piece = piece + dot(sel_coarse[up].astype(F32), stacked, NT, HIGH)
            packed[168 + duo * 56 : 224 + duo * 56, :] = piece
        packed[504:512, :] = jnp.zeros((8, 128), F32)
        for quarter in range(4):
            for block in range(4):
                top = quarter * 128 + block * 32
                packed_out[lax.rem(quarter + 4 - place[0], 4), :, block * 128 : (block + 1) * 128] = packed[top : top + 32, :]


def whole(*dims):
    return pl.BlockSpec(
        dims, lambda step, *rest: (0,) * len(dims), pipeline_mode=pl.Buffered(1)
    )


def group_block():
    return pl.BlockSpec((1, 512, 512), lambda step: (step, 0, 0))


def stem_first(frames, stem_weight, stem_diff_weight, tables, after):
    pool, fine_tab, coarse_tab, sel_fine, sel_coarse, lanes, usable = tables
    weight = stem_weight.transpose(1, 2, 3, 0)
    diff_weight = stem_diff_weight.transpose(1, 2, 3, 0)
    return pl.pallas_call(
        stem_forward,
        grid=(GROUPS,),
        in_specs=[
            whole(2, 15 * SIDE, SIDE),
            whole(3, 7, 7, STEMC),
            whole(12, 7, 7, STEMC),
            whole(SIDE, 128),
            whole(2, SIDE, 1152),
            whole(256, 896),
            whole(8, 168, 432),
            whole(4, 56, 128),
            whole(8, 128),
            whole(8, 128),
            whole(2, MID),
        ],
        out_specs=[
            group_block(),
            pl.BlockSpec((3, 64, 1152), lambda step: (0, jnp.minimum(step, 3), 0)),
            pl.BlockSpec((12, 32, 896), lambda step: (0, jnp.minimum(step, 3), 0)),
            whole(8, 128),
            whole(STEMC, 128),
        ],
        out_shape=[
            pltpu.VMEM((GROUPS, 512, 512), BF),
            pltpu.VMEM((3, 256, 1152), BF),
            pltpu.VMEM((12, 128, 896), BF),
            shape((8, 128)),
            shape((STEMC, 128)),
        ],
        scratch_shapes=[
            pltpu.VMEM((15 * SIDE, 128), F32),
            pltpu.VMEM((12 * 128, 256), F32),
            pltpu.VMEM((2, 768, SIDE), F32),
            pltpu.VMEM((3, 256, 1152), BF),
            pltpu.VMEM((12, 128, 896), BF),
            pltpu.VMEM((512, 432), BF),
            pltpu.VMEM((256, 1536), BF),
            pltpu.VMEM((128, 128), F32),
            pltpu.VMEM((168 + 672, STEMC), F32),
        ],
        compiler_params=params("stem_forward"),
        cost_estimate=cost(8e9, 2e7),
        name="stem_forward",
    )(frames.reshape(2, 15 * SIDE, SIDE), weight, diff_weight, pool, fine_tab, coarse_tab, sel_fine, sel_coarse, lanes, usable, after)


def stem_second(raw, centre, stem_cotangent, totals, stem_gain, stem_bias, lanes, count):
    gain = stem_gain.reshape(1, STEMC)
    bias = stem_bias.reshape(1, STEMC)
    cot = stem_cotangent.transpose(0, 2, 3, 1)
    return pl.pallas_call(
        functools.partial(stem_middle, count=count),
        grid=(GROUPS,),
        in_specs=[
            group_block(),
            whole(2, 56, 56, 64),
            whole(8, 128),
            whole(1, STEMC),
            whole(1, STEMC),
            whole(8, 128),
            whole(STEMC, 128),
        ],
        out_specs=[group_block(), whole(8, 128)],
        out_shape=[pltpu.VMEM((GROUPS, 512, 512), BF), shape((8, 128))],
        scratch_shapes=[
            pltpu.VMEM((8, 64, 128), F32),
            pltpu.VMEM((3, 64, 128), F32),
            pltpu.VMEM((64, 128), F32),
            pltpu.VMEM((2, 64, 128), F32),
        ],
        compiler_params=params("stem_middle"),
        cost_estimate=cost(8e9, 1.5e7),
        name="stem_middle",
    )(*in_vmem(raw), cot, totals, gain, bias, lanes, centre)


def stem_third(place, raw, centre, back, fine, coarse, totals, back_totals, stem_gain, tables, count):
    pool, fine_tab, coarse_tab, sel_fine, sel_coarse, lanes, usable = tables
    gain = stem_gain.reshape(1, STEMC)
    return pl.pallas_call(
        functools.partial(stem_backward, count=count),
        grid=(GROUPS,),
        in_specs=[
            SMEM,
            group_block(),
            group_block(),
            pl.BlockSpec((3, 32, 1152), lambda step: (0, step, 0)),
            pl.BlockSpec((3, 32, 1152), lambda step: (0, step + 1, 0)),
            pl.BlockSpec((12, 16, 896), lambda step: (0, step, 0)),
            pl.BlockSpec((12, 16, 896), lambda step: (0, step + 1, 0)),
            whole(8, 128),
            whole(8, 128),
            whole(1, STEMC),
            whole(8, 168, 432),
            whole(4, 56, 128),
            whole(8, 128),
            whole(STEMC, 128),
        ],
        out_specs=whole(4, 32, 512),
        out_shape=shape((4, 32, 512)),
        scratch_shapes=[
            pltpu.VMEM((3, 64, 128), F32),
            pltpu.VMEM((512, 128), F32),
            pltpu.VMEM((512, 512), BF),
            pltpu.VMEM((256, 256), BF),
            pltpu.VMEM((512, 432), F32),
            pltpu.VMEM((256, 1536), F32),
        ],
        compiler_params=params("stem_backward"),
        cost_estimate=cost(8e9, 2.5e7),
        name="stem_backward",
    )(place, *in_vmem(raw, back, fine, fine, coarse, coarse), totals, back_totals, gain, sel_fine, sel_coarse, lanes, centre)


def put_moments(out_ref, values):
    out_ref[0:1, :] = jnp.sum(values, axis=0, keepdims=True)
    out_ref[1:2, :] = jnp.sum(values * values, axis=0, keepdims=True)


def moments(totals, count):
    average = totals[0:1] * (1.0 / count)
    square = totals[1:2] * (1.0 / count)
    return average, lax.rsqrt(square - average * average + EPS)


def affine_of(totals, count, gain, bias):
    average, scale = moments(totals, count)
    slope = gain * scale
    return slope, bias - average * slope


def back_affine(totals, sums, count, gain, middle=0.0):
    average, scale = moments(totals, count)
    first = sums[0:1] * (1.0 / count)
    second = sums[1:2] * (1.0 / count)
    on_grad = gain * scale
    on_value = -on_grad * scale * second
    return on_grad, on_value, -on_grad * first - on_value * (average - middle)


def each_piece(width, pieces):
    for left in range(0, width, 128):
        for rows in pieces:
            yield rows, slice(left, left + 128)


def put_back(out_ref, grad, value, coefs):
    on_grad, on_value, constant = coefs
    for rows, cols in each_piece(out_ref.shape[1], PIECES):
        out_ref[rows, cols] = (
            grad[rows, cols].astype(F32) * on_grad[:, cols]
            + value[rows, cols].astype(F32) * on_value[:, cols]
            + constant[:, cols]
        ).astype(BF)


def put_activation_back(out_ref, sums_out, grad, value, totals, gain, bias, count):
    average, scale = moments(totals, count)
    slope = gain * scale
    shift = bias - average * slope
    for left in range(0, MID, 128):
        cols = slice(left, left + 128)
        plain = jnp.zeros((8, 128), F32)
        cross = jnp.zeros((8, 128), F32)
        for rows in EIGHTS:
            pre = value[rows, cols]
            act = pre * slope[:, cols] + shift[:, cols]
            sigma = sigmoid(act)
            hidden = grad[rows, cols].astype(BF).astype(F32)
            back = hidden * (sigma * (1.0 + act * (1.0 - sigma)))
            out_ref[rows, cols] = back
            plain = plain + back
            cross = cross + back * (pre - average[:, cols])
        sums_out[0:1, cols] = jnp.sum(plain, axis=0, keepdims=True)
        sums_out[1:2, cols] = jnp.sum(cross, axis=0, keepdims=True) * scale[:, cols]


def first_matmuls(place, features, reduce_w, motion_w, reduce_out, motion_out, reduce_sum, motion_sum):
    value = dot(features[...], reduce_w[...])
    reduce_out[...] = value
    put_moments(reduce_sum, value)
    value = dot(features[...], motion_w[...])
    motion_out[...] = value
    put_moments(motion_sum, value)


def tap_mask(places, row_off, col_off):
    kept = None
    for off, base in ((row_off, 0), (col_off, 256)):
        if off:
            at = base + (128 if off > 0 else 0)
            good = places[:, at : at + 128]
            kept = good if kept is None else kept * good
    return kept


def tap_source(buffer, places, row_off, col_off, sign):
    move = sign * (7 * row_off + col_off)
    mask = tap_mask(places, sign * row_off, sign * col_off)
    value = buffer[8 + move : 8 + move + ROWS, :]
    if mask is not None:
        value = value * jnp.concatenate([mask] * (value.shape[1] // 128), axis=1)
    return value


def clear_ends(buffer):
    blank = jnp.zeros((8, buffer.shape[1]), F32)
    buffer[0:8, :] = blank
    buffer[8 + ROWS : 16 + ROWS, :] = blank


def spatial_forward(
    pre_reduce, totals, gain, bias, places, weight, hidden_out, pre_out, sums_out, buffer, *, count
):
    clear_ends(buffer)
    slope, shift = affine_of(totals[...], count, gain[...], bias[...])
    for rows, cols in each_piece(MID, PIECES):
        value = pre_reduce[rows, cols] * slope[:, cols] + shift[:, cols]
        hidden = (value * sigmoid(value)).astype(BF)
        hidden_out[rows, cols] = hidden
        buffer[8 + rows.start : 8 + rows.stop, cols] = hidden.astype(F32)
    for tap in range(9):
        row_off, col_off = tap // 3 - 1, tap % 3 - 1
        source = tap_source(buffer, places, row_off, col_off, 1).astype(BF)
        value = dot(source, weight[tap * MID : (tap + 1) * MID, :])
        if tap == 0:
            pre_out[...] = value
        else:
            pre_out[...] += value
    put_moments(sums_out, pre_out[...])


def put_centred(value, pre_out, sums_out, mid_out):
    put_moments(sums_out, value)
    middle = sums_out[0:1, :] * (1.0 / ROWS)
    mid_out[...] = middle
    pre_out[...] = (value - middle).astype(BF)


def expand_forward(
    pre_spatial, totals, gain, bias, weight, hidden_out, pre_out, sums_out, mid_out, *, count
):
    @pl.when(pl.program_id(0) == 0)
    def prepare():
        slope, shift = affine_of(totals[...], count, gain[...], bias[...])
        for rows, cols in each_piece(MID, PIECES):
            value = pre_spatial[rows, cols] * slope[:, cols] + shift[:, cols]
            hidden_out[rows, cols] = (value * sigmoid(value)).astype(BF)

    put_centred(dot(hidden_out[...], weight[...]), pre_out, sums_out, mid_out)


def at(buffer, rows, move=0):
    return buffer[64 + rows.start + move : 64 + rows.stop + move, :]


def put(buffer, rows, value):
    buffer[64 + rows.start : 64 + rows.stop, :] = value


def clear_margins(buffers):
    for buffer in buffers:
        buffer[0:64, :] = jnp.zeros((64, 128), F32)
        buffer[64 + ROWS : 128 + ROWS, :] = jnp.zeros((64, 128), F32)


def mask_of(places, rows, which):
    return places[rows, which * 128 : (which + 1) * 128]


UP, DOWN, LEFT, RIGHT = range(4)


def three(buffer, places, rows, move, before, after):
    return (
        at(buffer, rows, -move) * mask_of(places, rows, before),
        at(buffer, rows),
        at(buffer, rows, move) * mask_of(places, rows, after),
    )


def box_rows(buffer, places, out):
    for rows in EIGHTS:
        first, second, third = three(buffer, places, rows, 1, LEFT, RIGHT)
        put(out, rows, first + second + third)


def box_columns(buffer, places, rows):
    first, second, third = three(buffer, places, rows, 7, UP, DOWN)
    return (first + second + third) * (1.0 / 9.0)


def kept(value, rows, keep):
    first, last = rows.start // 49, (rows.stop - 1) // 49
    if first == last:
        return value * keep[0, first]
    lines = lax.broadcasted_iota(jnp.int32, value.shape, 0)
    return value * jnp.where(lines < last * 49 - rows.start, keep[0, first], keep[0, last])


def change_and_average(pre_motion, slope, keep, places, cols, spare, change, average):
    for rows in EIGHTS:
        put(spare, rows, pre_motion[rows, cols] * slope)
    for rows in EIGHTS:
        put(change, rows, kept(at(spare, rows, 49) - at(spare, rows), rows, keep))
    box_rows(change, places, spare)
    for rows in EIGHTS:
        put(average, rows, box_columns(spare, places, rows))


def motion_forward(
    pre_motion, totals, gain, keep, places, depth, weight, mixed_out, pre_out, sums_out, mid_out,
    spare, change, average, lines_a, lines_b, lines_c, *, count
):
    @pl.when(pl.program_id(0) == 0)
    def prepare():
        clear_margins((spare, change, average, lines_a, lines_b, lines_c))

        @pl.loop(0, MID // 128)
        def one(tile):
            cols = pl.ds(pl.multiple_of(tile * 128, 128), 128)
            scale = moments(totals[:, cols], count)[1]
            change_and_average(
                pre_motion, gain[:, cols] * scale, keep, places, cols, spare, change, average
            )
            for rows in EIGHTS:
                near = three(change, places, rows, 1, LEFT, RIGHT)
                wide = three(average, places, rows, 1, LEFT, RIGHT)
                for row, out in enumerate((lines_a, lines_b, lines_c)):
                    line = None
                    for col in range(3):
                        for scale_at, source in enumerate((near, wide)):
                            term = source[col] * depth[scale_at, row, col : col + 1, cols]
                            line = term if line is None else line + term
                    put(out, rows, line)
            for rows in PIECES:
                value = (
                    at(lines_b, rows)
                    + at(lines_a, rows, -7) * mask_of(places, rows, UP)
                    + at(lines_c, rows, 7) * mask_of(places, rows, DOWN)
                )
                mixed_out[rows, cols] = value.astype(BF)

    put_centred(dot(mixed_out[...], weight[...]), pre_out, sums_out, mid_out)


def gate_kernel(
    own, pre_expand, pre_excite, features, cotangent, expand_tot, excite_tot, expand_mid, excite_mid,
    expand_gain, expand_bias, excite_gain, excite_bias,
    mine_out, other_out, direct_out, comb_out, gate_out, sums_out, output_ref, direct_ref, *, count
):
    step = pl.program_id(0)
    e_mean, e_scale = moments(expand_tot[...], count)
    x_mean, x_scale = moments(excite_tot[...], count)
    e_mean = e_mean - expand_mid[...]
    x_mean = x_mean - excite_mid[...]
    e_slope = expand_gain[...] * e_scale
    e_shift = expand_bias[...] - e_mean * e_slope
    x_slope = excite_gain[...] * x_scale
    x_shift = excite_bias[...] - x_mean * x_slope
    for left in range(0, TILE, 128):
        cols = slice(left, left + 128)
        sums = [jnp.zeros((8, 128), F32)] * 4
        for rows in PIECES:
            feats = features[rows, cols].astype(F32)
            seed = cotangent[rows, cols].astype(F32)
            pre_e = pre_expand[rows, cols].astype(F32)
            pre_x = pre_excite[rows, cols].astype(F32)
            branch = (pre_e * e_slope[:, cols] + e_shift[:, cols]).astype(BF).astype(F32)
            gate = sigmoid(pre_x * x_slope[:, cols] + x_shift[:, cols])
            lifted = feats * gate
            combined = branch + lifted
            sigma = sigmoid(combined)
            output = combined * sigma
            output_ref[rows, cols] = output.astype(BF)
            grad = seed * (sigma + output * (1.0 - sigma))
            direct_ref[rows, cols] = (grad * gate).astype(BF)
            rounded = grad.astype(BF)
            comb_out[rows, cols] = rounded
            rounded = rounded.astype(F32)
            grad_gate = grad * lifted * (1.0 - gate)
            gate_out[rows, cols] = grad_gate.astype(BF)
            terms = (
                rounded,
                rounded * (pre_e - e_mean[:, cols]),
                grad_gate,
                grad_gate * (pre_x - x_mean[:, cols]),
            )
            for spot, value in enumerate(terms):
                for up in range(0, value.shape[0], 8):
                    sums[spot] = sums[spot] + value[up : up + 8]
        finals = [jnp.sum(value, axis=0, keepdims=True) for value in sums]
        sums_out[0:1, cols] = finals[0]
        sums_out[1:2, cols] = finals[1] * e_scale[:, cols]
        sums_out[2:3, cols] = finals[2]
        sums_out[3:4, cols] = finals[3] * x_scale[:, cols]

    @pl.when(step == 0)
    def store_mine():
        mine_out[...] = output_ref[...]

    @pl.when(step == 1)
    def store_other():
        other_out[...] = output_ref[...]

    @pl.when(step < 2)
    def store_direct():
        direct_out[...] = direct_ref[...]


def pull_back(grad, value, totals, sums, gain, middle, weight, own_out, value_ref, acc, count):
    step = pl.program_id(0)
    put_back(value_ref, grad, value, back_affine(totals[...], sums, count, gain[...], middle[...]))

    @pl.when(step < 2)
    def store_own():
        own_out[...] = value_ref[...]

    part = dot(value_ref[...], weight[...], NT)

    @pl.when(step == 0)
    def begin():
        acc[...] = part

    @pl.when(step > 0)
    def add():
        acc[...] += part


def expand_backward(
    own, grad, pre_expand, totals, sums, gain, middle, weight, pre_spatial, s_totals, s_gain, s_bias,
    own_out, grad_out, sums_out, value_ref, acc, *, count
):
    pull_back(
        grad, pre_expand, totals, sums[0:2, :], gain, middle, weight, own_out, value_ref, acc, count
    )

    @pl.when(pl.program_id(0) == C // TILE - 1)
    def finish():
        put_activation_back(
            grad_out, sums_out, acc, pre_spatial, s_totals[...], s_gain[...], s_bias[...], count
        )


def excite_backward(
    own, grad, pre_excite, totals, sums, gain, middle, weight, pre_motion, m_totals, m_gain, keep,
    places, depth, own_out, grad_out, sums_out, depth_out, value_ref, acc,
    spare, change, average, seed, pull_a, pull_b, pull_c, near_out, wide_out, *, count
):
    pull_back(
        grad, pre_excite, totals, sums[2:4, :], gain, middle, weight, own_out, value_ref, acc, count
    )

    @pl.when(pl.program_id(0) == C // TILE - 1)
    def finish():
        clear_margins((spare, change, average, seed, pull_a, pull_b, pull_c, near_out, wide_out))

        @pl.loop(0, MID // 128)
        def one(tile):
            cols = pl.ds(pl.multiple_of(tile * 128, 128), 128)
            mean, scale = moments(m_totals[:, cols], count)
            change_and_average(
                pre_motion, m_gain[:, cols] * scale, keep, places, cols, spare, change, average
            )
            for rows in EIGHTS:
                put(seed, rows, acc[rows, cols])
            for base, source, out in ((0, change, near_out), (9, average, wide_out)):
                totals_of = [jnp.zeros((8, 128), F32)] * 9
                for rows in EIGHTS:
                    later, now, before = three(seed, places, rows, -7, DOWN, UP)
                    taps = three(source, places, rows, 1, LEFT, RIGHT)
                    for col, pull in enumerate((pull_a, pull_b, pull_c)):
                        total = None
                        for row, line in enumerate((later, now, before)):
                            spot = row * 3 + col
                            term = line * depth[base // 9, row, col : col + 1, cols]
                            total = term if total is None else total + term
                            totals_of[spot] = totals_of[spot] + line * taps[col]
                        put(pull, rows, total)
                for spot in range(9):
                    depth_out[base + spot : base + spot + 1, cols] = jnp.sum(
                        totals_of[spot], axis=0, keepdims=True
                    )
                for rows in EIGHTS:
                    put(
                        out,
                        rows,
                        at(pull_b, rows)
                        + at(pull_a, rows, 1) * mask_of(places, rows, RIGHT)
                        + at(pull_c, rows, -1) * mask_of(places, rows, LEFT),
                    )
            box_rows(wide_out, places, spare)
            for rows in EIGHTS:
                value = at(near_out, rows) + box_columns(spare, places, rows)
                put(change, rows, kept(value, rows, keep))
            plain = jnp.zeros((8, 128), F32)
            cross = jnp.zeros((8, 128), F32)
            for rows in EIGHTS:
                value = at(change, rows, -49) - at(change, rows)
                grad_out[rows, cols] = value
                plain = plain + value
                cross = cross + value * (pre_motion[rows, cols] - mean)
            sums_out[0:1, cols] = jnp.sum(plain, axis=0, keepdims=True)
            sums_out[1:2, cols] = jnp.sum(cross, axis=0, keepdims=True) * scale


def spatial_backward(
    own, grad, pre_spatial, totals, sums, gain, places, weight, pre_reduce, r_totals, r_gain, r_bias,
    m_grad, pre_motion, m_totals, m_sums, m_gain,
    taps_out, grad_out, sums_out, motion_out, motion_own, buffer, source_ref, acc, *, count
):
    clear_ends(buffer)
    on_grad, on_value, constant = back_affine(totals[...], sums[...], count, gain[...])
    for rows, cols in each_piece(MID, EIGHTS):
        buffer[8 + rows.start : 8 + rows.stop, cols] = (
            (
                grad[rows, cols] * on_grad[:, cols]
                + pre_spatial[rows, cols] * on_value[:, cols]
                + constant[:, cols]
            )
            .astype(BF)
            .astype(F32)
        )
    mine = pl.ds(pl.multiple_of((own[0] // 2) * 256, 256), 256)
    for tap in range(9):
        row_off, col_off = tap // 3 - 1, tap % 3 - 1
        source_ref[...] = tap_source(buffer, places, row_off, col_off, -1).astype(BF)
        taps_out[:, tap * 256 : (tap + 1) * 256] = source_ref[:, mine]
        value = dot(source_ref[...], weight[tap * MID : (tap + 1) * MID, :], NT)
        if tap == 0:
            acc[...] = value
        else:
            acc[...] += value
    put_activation_back(
        grad_out, sums_out, acc, pre_reduce, r_totals[...], r_gain[...], r_bias[...], count
    )
    put_back(
        motion_out, m_grad, pre_motion, back_affine(m_totals[...], m_sums[...], count, m_gain[...])
    )
    motion_own[...] = motion_out[:, mine]


def reduce_backward(
    own, grad, pre_reduce, totals, sums, gain, mine_w, other_w, motion, mine_m, other_m, direct,
    own_out, mine_out, other_out, value_ref, *, count
):
    put_back(value_ref, grad, pre_reduce, back_affine(totals[...], sums[...], count, gain[...]))
    own_out[...] = value_ref[:, pl.ds(pl.multiple_of((own[0] // 2) * 256, 256), 256)]
    for out, reduce_w, motion_w, left in (
        (other_out, other_w, other_m, MID),
        (mine_out, mine_w, mine_m, 0),
    ):
        value = dot(value_ref[...], reduce_w[...], NT) + dot(motion[...], motion_w[...], NT)
        out[...] = (value + direct[:, left : left + MID].astype(F32)).astype(BF)


def owners(place, sizes):
    away = lambda at, axis, size: lax.rem(at + size - place[axis], size)
    for z in range(sizes[0]):
        for y in range(sizes[1]):
            for c in range(sizes[2]):
                owner = (z * sizes[1] + y) * sizes[2] + c
                yield owner, (away(c, 1, sizes[2]), away(y, 2, sizes[1]), away(z, 3, sizes[0]))


def spatial_weight_kernel(place, hidden, taps, motion, out, turned_ref, *, sizes):
    turned_ref[...] = jnp.transpose(hidden[...].astype(F32)).astype(BF)
    clips = sizes[0] * sizes[1] * sizes[2]
    spots = dict(owners(place, sizes))
    share = 9 * MID // clips
    for tap in range(9):
        value = dot(turned_ref[...], taps[:, tap * 256 : (tap + 1) * 256]).astype(BF)
        for top in range(0, MID, 16):
            row = tap * MID + top
            out[*spots[row // share], row % share : row % share + 16, :] = value[top : top + 16]
    for owner, spot in spots.items():
        out[*spot, share:, :] = motion[owner * (C // clips) : (owner + 1) * (C // clips), :]


def early_weight_kernel(place, hidden, expand, mixed, excite, out, turned_ref, *, sizes):
    rows = MID // (sizes[0] * sizes[1] * sizes[2])
    spots = dict(owners(place, sizes))
    for base, left, right in ((0, hidden, expand), (4, mixed, excite)):
        turned_ref[...] = jnp.transpose(left[...].astype(F32)).astype(BF)
        for block in range(4):
            value = dot(turned_ref[...], right[:, block * 256 : (block + 1) * 256]).astype(BF)
            for owner, spot in spots.items():
                out[*spot, (base + block) * rows : (base + block + 1) * rows, :] = value[
                    owner * rows : (owner + 1) * rows
                ]


def late_weight_kernel(place, values, out, *, sizes):
    rows = out.shape[3]
    for owner, spot in owners(place, sizes):
        out[*spot] = values[owner * rows : (owner + 1) * rows, :]


def join_kernel(own, mine, got, out):
    first = jnp.where(own[0] % 2 == 0, mine[...].astype(F32), got[...].astype(F32))
    second = jnp.where(own[0] % 2 == 0, got[...].astype(F32), mine[...].astype(F32))
    out[...] = jnp.concatenate([first, second], axis=0).astype(BF)


def unpack_kernel(
    own, rest_0, rest_1, rest_2, rest_3, early_0, early_1, early_2, early_3,
    mine, got, gate, got_gate, tail, got_tail,
    reduce_out, spatial_out, expand_out, motion_out, excite_out, fine_out, coarse_out, grad_out,
    depth_out, e_bias, e_gain, x_bias, x_gain, m_gain, s_bias, s_gain, r_bias, r_gain,
    packed_ref, *, clips
):
    join_kernel(own, mine, got, grad_out)
    both = tail[...] + got_tail[...]
    for spot in range(18):
        depth_out[spot // 9, spot // 3 % 3, spot % 3 : spot % 3 + 1, :] = both[6 + spot : 7 + spot]
    wide = gate[...] + got_gate[...]
    for row, out in enumerate((e_bias, e_gain, x_bias, x_gain)):
        out[...] = wide[row]
    for row, out in ((1, m_gain), (2, s_bias), (3, s_gain), (4, r_bias), (5, r_gain)):
        out[...] = both[row]
    cuts = (9 * MID // clips, (9 * MID + C) // clips, (9 * MID + 2 * C) // clips)
    half = own[0] // 2
    for side, left, right in ((half, rest_0, rest_1), (1 - half, rest_2, rest_3)):
        value = left[...].astype(F32) + right[...].astype(F32)
        cols = pl.ds(pl.multiple_of(side * 256, 256), 256)
        spatial_out[:, cols] = value[: cuts[0]]
        motion_out[:, cols] = value[cuts[0] : cuts[1]]
        reduce_out[:, cols] = value[cuts[1] : cuts[2]]
    rows = MID // clips
    for flip, left, right in (
        (0, (early_0, 0), (early_1, 1)),
        (1, (early_0, 1), (early_1, 0)),
        (2, (early_2, 0), (early_3, 1)),
        (3, (early_2, 1), (early_3, 0)),
    ):
        for base, out in ((0, expand_out), (4, excite_out)):
            for block in range(2):
                value = None
                for ref, spot in (left, right):
                    top = (base + 2 * spot + block) * rows
                    part = ref[top : top + rows, :].astype(F32)
                    value = part if value is None else value + part
                out[:, pl.ds(pl.multiple_of((own[0] ^ flip) * MID + block * 256, 256), 256)] = value
    base = 8 * rows
    for flip, ref in enumerate((early_0, early_1, early_2, early_3)):
        for block in range(4):
            top, left = base + (block // 2) * 32, (block % 2) * 128
            high = ref[top : top + 32, left : left + 128].astype(F32)
            low = ref[top + 64 : top + 96, left : left + 128].astype(F32)
            at = pl.multiple_of((own[0] ^ flip) * 128 + block * 32, 32)
            packed_ref[pl.ds(at, 32), :] = high + low
    for chan in range(3):
        for row in range(7):
            at = chan * 56 + row * 8
            fine_out[chan, row] = packed_ref[at : at + 7, 0:64]
    for chan in range(12):
        side = (chan % 2) * 64
        for row in range(7):
            at = 168 + (chan // 2) * 56 + row * 8
            coarse_out[chan, row] = packed_ref[at : at + 7, side : side + 64]


def with_own(kernel, own, grid, in_specs, out_specs, out_shape, scratch, args, flops, nbytes, name):
    return pl.pallas_call(
        kernel,
        grid_spec=pltpu.PrefetchScalarGridSpec(
            num_scalar_prefetch=1,
            grid=grid,
            in_specs=in_specs,
            out_specs=out_specs,
            scratch_shapes=scratch,
        ),
        out_shape=out_shape,
        compiler_params=params(name),
        cost_estimate=cost(flops, nbytes),
        name=name,
    )(own, *args)


def place_table():
    rows = np.arange(ROWS)
    down = (rows % 49) // 7
    right = rows % 7
    kept = [down >= 1, down <= FEAT - 2, right >= 1, right <= FEAT - 2]
    return jnp.asarray(np.concatenate([np.repeat(k[:, None], 128, 1) for k in kept], axis=1), F32)


def keep_pairs(valid_rows, video_rows):
    valid_float = valid_rows.astype(F32)
    same_video = (video_rows[:, 1:] == video_rows[:, :-1]).astype(F32)
    pair_keep = valid_float[:, 1:] * valid_float[:, :-1] * same_video
    return jnp.concatenate([pair_keep, jnp.zeros_like(pair_keep[:, :1])], axis=1)


def on_device(
    features,
    out_cotangent,
    seg_valid,
    seg_video,
    frames,
    stem_cotangent,
    stem_weight,
    stem_diff_weight,
    stem_gain,
    stem_bias,
    reduce_weight,
    reduce_gain,
    reduce_bias,
    spatial_weight,
    spatial_gain,
    spatial_bias,
    expand_weight,
    expand_gain,
    expand_bias,
    motion_weight,
    motion_gain,
    depth_weight,
    excite_weight,
    excite_gain,
    excite_bias,
):
    clips = lax.axis_size("z") * lax.axis_size("y") * lax.axis_size("c")
    count = float(clips * ROWS)
    stem_count = float(clips * lax.axis_size("x") * (SIDE // 2) ** 2)
    here = lax.axis_index("x")
    micro = here % 2
    own = jnp.stack([here] + [lax.axis_index(axis) for axis in ("c", "y", "z")]).astype(jnp.int32)
    places = place_table()

    def of_micro(rows):
        return lax.dynamic_index_in_dim(
            rows.reshape(MICRO, rows.shape[0] // MICRO, rows.shape[1]), micro, 0, False
        )

    feats = of_micro(features)
    seeds = of_micro(out_cotangent)
    keep = of_micro(keep_pairs(seg_valid, seg_video))
    line = lambda vector: vector.reshape(1, -1)
    reduce_gain, reduce_bias = line(reduce_gain), line(reduce_bias)
    spatial_gain, spatial_bias = line(spatial_gain), line(spatial_bias)
    expand_gain, expand_bias = line(expand_gain), line(expand_bias)
    excite_gain, excite_bias = line(excite_gain), line(excite_bias)
    motion_gain = line(motion_gain)

    tables = stem_tables()
    lanes = tables[5]
    column = lambda rows, width: pl.BlockSpec((rows, width), lambda step, *rest: (0, step))
    pre_reduce, pre_motion, reduce_sum, motion_sum = pl.pallas_call(
        first_matmuls,
        grid=(2,),
        in_specs=[SMEM, whole(ROWS, C), column(C, 256), column(C, 256)],
        out_specs=[column(ROWS, 256), column(ROWS, 256), column(2, 256), column(2, 256)],
        out_shape=[held((ROWS, MID)), held((ROWS, MID)), shape((2, MID)), shape((2, MID))],
        compiler_params=params("first_matmuls"),
        cost_estimate=cost(1.7e9, 1e7),
        name="first_matmuls",
    )(own, *in_vmem(feats), reduce_weight, motion_weight)
    raw, fine, coarse, stem_sum, centre = stem_first(
        frames, stem_weight, stem_diff_weight, tables, reduce_sum
    )
    stem_sum = ring_sum(stem_sum[:2], "x")

    reduce_tot, motion_tot, stem_tot = merge_sum(reduce_sum, motion_sum, stem_sum)
    stem_tot = jnp.pad(stem_tot, ((0, 6), (0, 0)))
    back, back_sum = stem_second(
        raw, centre, stem_cotangent, stem_tot, stem_gain, stem_bias, lanes, stem_count
    )
    back_sum = ring_sum(back_sum[:2], "x")

    hidden_one, pre_spatial, spatial_sum = pl.pallas_call(
        functools.partial(spatial_forward, count=count),
        in_specs=[VMEM] * 6,
        out_specs=[VMEM] * 3,
        out_shape=[held((ROWS, MID), BF), held((ROWS, MID)), shape((2, MID))],
        scratch_shapes=[pltpu.VMEM((ROWS + 16, MID), F32)],
        compiler_params=params("spatial_forward"),
        cost_estimate=cost(1.9e9, 8e6),
        name="spatial_forward",
    )(*in_vmem(pre_reduce), reduce_tot, reduce_gain, reduce_bias, places, spatial_weight)

    mixed, pre_excite, excite_sum, excite_mid = pl.pallas_call(
        functools.partial(motion_forward, count=count),
        grid=(4,),
        in_specs=[
            whole(ROWS, MID), whole(2, MID), whole(1, MID), SMEM, whole(ROWS, 512),
            whole(2, 3, 3, MID), column(MID, 512),
        ],
        out_specs=[whole(ROWS, MID), column(ROWS, 512), column(2, 512), column(1, 512)],
        out_shape=[held((ROWS, MID), BF), held((ROWS, C), BF), shape((2, C)), shape((1, C))],
        scratch_shapes=[pltpu.VMEM((ROWS + 128, 128), F32)] * 6,
        compiler_params=params("motion_forward"),
        cost_estimate=cost(2e9, 1.2e7),
        name="motion_forward",
    )(*in_vmem(pre_motion), motion_tot, motion_gain, keep, places, depth_weight, excite_weight)
    spatial_tot, excite_tot, back_tot = merge_sum(spatial_sum, excite_sum, back_sum)
    back_tot = jnp.pad(back_tot, ((0, 6), (0, 0)))
    stem_packed = stem_third(
        own, raw, centre, back, fine, coarse, stem_tot, back_tot, stem_gain, tables, stem_count
    )
    back_both = back_tot[0] + back_tot[1]
    stem_gain_grad, stem_bias_grad = back_both[64:], back_both[:64]

    hidden_two, pre_expand, expand_sum, expand_mid = pl.pallas_call(
        functools.partial(expand_forward, count=count),
        grid=(4,),
        in_specs=[
            whole(ROWS, MID), whole(2, MID), whole(1, MID), whole(1, MID), column(MID, 512),
        ],
        out_specs=[whole(ROWS, MID), column(ROWS, 512), column(2, 512), column(1, 512)],
        out_shape=[held((ROWS, MID), BF), held((ROWS, C), BF), shape((2, C)), shape((1, C))],
        compiler_params=params("expand_forward"),
        cost_estimate=cost(1e9, 1e7),
        name="expand_forward",
    )(*in_vmem(pre_spatial), spatial_tot, spatial_gain, spatial_bias, expand_weight)
    expand_tot = sum_dp(expand_sum)

    def turned(rows):
        return pl.BlockSpec((rows, TILE), lambda step, own_ref: (0, step ^ own_ref[0]))

    def within(first, last):
        return pl.BlockSpec(
            (ROWS, TILE), lambda step, own_ref: (0, jnp.clip(step - first, 0, last - first))
        )

    mine, other, direct, grad_comb, grad_gate, gate_sum = with_own(
        functools.partial(gate_kernel, count=count),
        own,
        (C // TILE,),
        [turned(ROWS)] * 4 + [turned(2)] * 2 + [turned(1)] * 6,
        [
            whole(ROWS, MID), whole(ROWS, MID), within(0, 1), turned(ROWS), turned(ROWS), turned(4),
        ],
        [
            shape((ROWS, MID), BF), shape((ROWS, MID), BF), held((ROWS, 2 * MID), BF),
            held((ROWS, C), BF), held((ROWS, C), BF), shape((4, C)),
        ],
        [pltpu.VMEM((ROWS, TILE), BF)] * 2,
        (
            *in_vmem(pre_expand, pre_excite, feats, seeds), expand_tot, excite_tot, expand_mid, excite_mid,
            expand_gain, expand_bias, excite_gain, excite_bias,
        ),
        2e9,
        2e7,
        "gate",
    )
    gate_tot = sum_dp(gate_sum)

    got_result = from_peer(other, 1)

    expand_own, grad_spatial, spatial_back = with_own(
        functools.partial(expand_backward, count=count),
        own,
        (C // TILE,),
        [
            turned(ROWS), turned(ROWS), turned(2), turned(4), turned(1), turned(1), turned(MID),
            whole(ROWS, MID), whole(2, MID), whole(1, MID), whole(1, MID),
        ],
        [within(0, 1), whole(ROWS, MID), whole(2, MID)],
        [held((ROWS, 2 * MID), BF), held((ROWS, MID)), shape((2, MID))],
        [pltpu.VMEM((ROWS, TILE), BF), pltpu.VMEM((ROWS, MID), F32)],
        (
            *in_vmem(grad_comb, pre_expand), expand_tot, gate_tot, expand_gain, expand_mid, expand_weight,
            *in_vmem(pre_spatial), spatial_tot, spatial_gain, spatial_bias,
        ),
        1e9,
        1e7,
        "expand_backward",
    )

    excite_own, grad_reduced, motion_back, depth_part = with_own(
        functools.partial(excite_backward, count=count),
        own,
        (C // TILE,),
        [
            turned(ROWS), turned(ROWS), turned(2), turned(4), turned(1), turned(1), turned(MID),
            whole(ROWS, MID), whole(2, MID), whole(1, MID), SMEM, whole(ROWS, 512),
            whole(2, 3, 3, MID),
        ],
        [within(0, 1), whole(ROWS, MID), whole(2, MID), whole(18, MID)],
        [held((ROWS, 2 * MID), BF), held((ROWS, MID)), shape((2, MID)), shape((18, MID))],
        [pltpu.VMEM((ROWS, TILE), BF), pltpu.VMEM((ROWS, MID), F32)]
        + [pltpu.VMEM((ROWS + 128, 128), F32)] * 9,
        (
            *in_vmem(grad_gate, pre_excite), excite_tot, gate_tot, excite_gain, excite_mid, excite_weight,
            *in_vmem(pre_motion), motion_tot, motion_gain, keep, places, depth_weight,
        ),
        2e9,
        1e7,
        "excite_backward",
    )
    across = lambda left, right: dot(left, right, TN).astype(BF)
    sizes = [lax.axis_size(axis) for axis in ("z", "y", "c")]
    early = pl.pallas_call(
        functools.partial(early_weight_kernel, sizes=sizes),
        in_specs=[SMEM] + [VMEM] * 4,
        out_specs=VMEM,
        out_shape=shape((*sizes[::-1], 8 * (MID // clips), 256), BF),
        scratch_shapes=[pltpu.VMEM((MID, ROWS), BF)],
        compiler_params=params("early_weight"),
        cost_estimate=cost(1e9, 5e6),
        name="early_weight",
    )(own, *in_vmem(hidden_two, expand_own, mixed, excite_own))
    stem_quarter = scatter_lead(stem_packed, "x", F32)
    back_all = core_sum(jnp.concatenate([motion_back, spatial_back, stem_quarter], axis=0))
    back_all, early = tie(back_all, early)
    early = scatter_lead(early, "c")
    back_all = ring_sum(back_all, "y")
    back_all, early = tie(back_all, early)
    early = scatter_lead(early, "y")
    back_all = ring_sum(back_all, "z")
    motion_back_tot, spatial_back_tot = back_all[:2], back_all[2:4]

    taps, grad_reduce, reduce_back, motion_full, motion_own = with_own(
        functools.partial(spatial_backward, count=count),
        own,
        (1,),
        [
            whole(ROWS, MID), whole(ROWS, MID), whole(2, MID), whole(2, MID), whole(1, MID),
            whole(ROWS, 512), whole(9 * MID, MID), whole(ROWS, MID), whole(2, MID),
            whole(1, MID), whole(1, MID),
            whole(ROWS, MID), whole(ROWS, MID), whole(2, MID), whole(2, MID), whole(1, MID),
        ],
        [
            whole(ROWS, 9 * 256), whole(ROWS, MID), whole(2, MID), whole(ROWS, MID), whole(ROWS, 256),
        ],
        [
            held((ROWS, 9 * 256), BF), held((ROWS, MID)), shape((2, MID)),
            held((ROWS, MID), BF), shape((ROWS, 256), BF),
        ],
        [
            pltpu.VMEM((ROWS + 16, MID), F32),
            pltpu.VMEM((ROWS, MID), BF),
            pltpu.VMEM((ROWS, MID), F32),
        ],
        (
            *in_vmem(grad_spatial, pre_spatial), spatial_tot, spatial_back_tot, spatial_gain, places,
            spatial_weight, *in_vmem(pre_reduce), reduce_tot, reduce_gain, reduce_bias,
            *in_vmem(grad_reduced, pre_motion), motion_tot, motion_back_tot, motion_gain,
        ),
        2e9,
        1e7,
        "spatial_backward",
    )
    mine_rows = pl.BlockSpec((MID, MID), lambda step, own_ref: (own_ref[0], 0))
    other_rows = pl.BlockSpec((MID, MID), lambda step, own_ref: (own_ref[0] ^ 1, 0))
    middle = pl.pallas_call(
        functools.partial(spatial_weight_kernel, sizes=sizes),
        in_specs=[SMEM] + [VMEM] * 3,
        out_specs=VMEM,
        out_shape=shape((*sizes[::-1], (9 * MID + C) // clips, 256), BF),
        scratch_shapes=[pltpu.VMEM((MID, ROWS), BF)],
        compiler_params=params("spatial_weight"),
        cost_estimate=cost(1e9, 5e6),
        name="spatial_weight",
    )(own, *in_vmem(hidden_one, taps), across(feats, motion_own))

    reduce_back = core_sum(jnp.concatenate([reduce_back, depth_part], axis=0))
    reduce_back, middle, early, got_result = tie(reduce_back, middle, early, got_result)
    early = scatter_lead(early, "z")
    middle = scatter_lead(middle, "c")
    reduce_back = ring_sum(reduce_back, "y")
    reduce_back, middle, early = tie(reduce_back, middle, early)
    stem_quarter = back_all[4:]
    stem_high = stem_quarter.astype(BF)
    stem_low = (stem_quarter - stem_high.astype(F32)).astype(BF)
    halves = [part[:, left : left + 256] for part in (stem_high, stem_low) for left in (0, 256)]
    early = gather_x(jnp.concatenate([early, *halves], axis=0))
    upward, downward = scatter_start(middle, "y")
    reduce_back = ring_sum(reduce_back, "z")
    reduce_back, upward, downward = tie(reduce_back, upward, downward)
    reduce_back_tot = reduce_back[:2]
    got_gate = from_peer(gate_tot, 1)
    tail = jnp.concatenate([back_all[:4], reduce_back], axis=0)
    got_tail = from_peer(tail, 1)
    middle = scatter_finish(middle, "y", upward, downward)

    reduce_own, mine_grad, other_grad = with_own(
        functools.partial(reduce_backward, count=count),
        own,
        (1,),
        [
            whole(ROWS, MID), whole(ROWS, MID), whole(2, MID), whole(2, MID), whole(1, MID),
            mine_rows, other_rows, whole(ROWS, MID), mine_rows, other_rows, whole(ROWS, 2 * MID),
        ],
        [whole(ROWS, 256), whole(ROWS, MID), whole(ROWS, MID)],
        [shape((ROWS, 256), BF), shape((ROWS, MID), BF), shape((ROWS, MID), BF)],
        [pltpu.VMEM((ROWS, MID), BF)],
        (
            *in_vmem(grad_reduce, pre_reduce), reduce_tot, reduce_back_tot, reduce_gain,
            reduce_weight, reduce_weight, *in_vmem(motion_full), motion_weight, motion_weight,
            *in_vmem(direct),
        ),
        5e8,
        8e6,
        "reduce_backward",
    )
    got_grad = from_peer(other_grad, 1)
    late = pl.pallas_call(
        functools.partial(late_weight_kernel, sizes=sizes),
        in_specs=[SMEM, VMEM],
        out_specs=VMEM,
        out_shape=shape((*sizes[::-1], C // clips, 256), BF),
        compiler_params=params("late_weight"),
        cost_estimate=cost(1e5, 2e6),
        name="late_weight",
    )(own, across(feats, reduce_own))
    late = scatter_lead(late, "c")
    late, middle, *early = tie(late, middle, *early)
    late = scatter_lead(late, "y")
    late, got_grad, got_gate, got_tail = tie(late, got_grad, got_gate, got_tail)
    rest = scatter_lead(jnp.concatenate([middle, late], axis=1), "z")
    rest = gather_x(rest)
    result = with_own(
        join_kernel,
        own,
        (1,),
        [whole(ROWS, MID), whole(ROWS, MID)],
        whole(2 * ROWS, MID),
        shape((2 * ROWS, MID), BF),
        [],
        (mine, got_result),
        1e5,
        2e6,
        "join_result",
    )

    (
        reduce_grad, spatial_grad, expand_grad, motion_grad, excite_grad,
        stem_weight_grad, stem_diff_grad, features_grad, depth_grad, *vectors,
    ) = with_own(
        functools.partial(unpack_kernel, clips=clips),
        own,
        (1,),
        [whole(*part.shape) for part in rest]
        + [whole(*part.shape) for part in early]
        + [
            whole(ROWS, MID), whole(ROWS, MID), whole(4, C), whole(4, C), whole(24, MID), whole(24, MID),
        ],
        [
            whole(C // clips, MID), whole(9 * MID // clips, MID), whole(MID // clips, C),
            whole(C // clips, MID), whole(MID // clips, C),
            whole(3, 7, 7, STEMC), whole(12, 7, 7, STEMC), whole(2 * ROWS, MID),
            whole(2, 3, 3, MID), *[whole(C)] * 4, *[whole(MID)] * 5,
        ],
        [
            shape((C // clips, MID)), shape((9 * MID // clips, MID)), shape((MID // clips, C)),
            shape((C // clips, MID)), shape((MID // clips, C)),
            shape((3, 7, 7, STEMC)), shape((12, 7, 7, STEMC)), shape((2 * ROWS, MID), BF),
            shape((2, 3, 3, MID)), *[shape((C,))] * 4, *[shape((MID,))] * 5,
        ],
        [pltpu.VMEM((512, 128), F32)],
        (*rest, *early, mine_grad, got_grad, gate_tot, got_gate, tail, got_tail),
        1e6,
        6e6,
        "unpack",
    )
    stem_weight_grad = stem_weight_grad.transpose(3, 0, 1, 2)
    stem_diff_grad = stem_diff_grad.transpose(3, 0, 1, 2)

    return (
        result,
        features_grad,
        stem_weight_grad,
        stem_diff_grad,
        stem_gain_grad,
        stem_bias_grad,
        reduce_grad,
        vectors[8],
        vectors[7],
        spatial_grad,
        vectors[6],
        vectors[5],
        expand_grad,
        vectors[1],
        vectors[0],
        motion_grad,
        vectors[4],
        depth_grad,
        excite_grad,
        vectors[3],
        vectors[2],
    )


def solution(mesh):
    grid = Mesh(mesh.devices.reshape(4, 4, 2, 4), ("z", "y", "c", "x"))
    clips = ("z", "y", "c")
    everyone = ("z", "y", "c", "x")
    split = P(clips, None)
    copied = P()
    return jax.shard_map(
        on_device,
        mesh=grid,
        in_specs=(split,) * 4
        + (P(everyone, None, None, None, None), P(everyone, None, None, None))
        + (copied,) * 19,
        out_specs=(P(clips, "x"), P(clips, "x"))
        + (copied,) * 4
        + (split, copied, copied) * 3
        + (split, copied, copied)
        + (split, copied, copied),
        check_vma=False,
    )
```

```python
import functools

import jax
import jax.numpy as jnp
import numpy as np
from jax import lax
from jax.experimental import pallas as pl
from jax.experimental.pallas import tpu as pltpu
from jax.sharding import Mesh
from jax.sharding import PartitionSpec as P

C = 2048
MID = 512
STEMC = 64
SIDE = 224
FEAT = 7
SEG = 8
MICRO = 2
ROWS = SEG * FEAT * FEAT
EPS = 1e-05
BF = jnp.bfloat16
F32 = jnp.float32
HIGH = lax.Precision.HIGHEST
NN = (((1,), (0,)), ((), ()))
NT = (((1,), (1,)), ((), ()))
TN = (((0,), (0,)), ((), ()))
GROUPS = 7
TILE = 512
VMEM = pl.BlockSpec(memory_space=pltpu.VMEM)
SMEM = pl.BlockSpec(memory_space=pltpu.SMEM)
PIECES = [slice(top, min(top + 16, ROWS)) for top in range(0, ROWS, 16)]
EIGHTS = [slice(top, top + 8) for top in range(0, ROWS, 8)]


def sigmoid(values):
    return 0.5 + 0.5 * jnp.tanh(0.5 * values)


def dot(left, right, dims=NN, precision=None):
    return lax.dot_general(left, right, dims, precision=precision, preferred_element_type=F32)


LIMITS = {}


def params(name):
    return pltpu.CompilerParams(vmem_limit_bytes=LIMITS.get(name, 20) * 2**20)


def held(dims, dtype=F32):
    return pltpu.VMEM(dims, dtype)


def in_vmem(*values):
    return [pltpu.with_memory_space_constraint(value, pltpu.VMEM) for value in values]


def cost(flops, nbytes):
    return pl.CostEstimate(flops=int(flops), bytes_accessed=int(nbytes), transcendentals=0)


def shape(dims, dtype=F32):
    return jax.ShapeDtypeStruct(dims, dtype)


def ring_sum(values, axis):
    size = lax.axis_size(axis)
    if size == 1:
        return values
    got = [
        lax.ppermute(values, axis, [(i, (i + step) % size) for i in range(size)])
        for step in range(1, size)
    ]
    if size == 2:
        return values + got[0]
    return (values + got[1]) + (got[0] + got[2])


def core_sum(values):
    pair = lax.all_gather(values, "c")
    return pair[0] + pair[1]


def sum_dp(values):
    return ring_sum(ring_sum(core_sum(values), "y"), "z")


def shift_by(values, axis, step):
    size = lax.axis_size(axis)
    return lax.ppermute(values, axis, [(i, (i + step) % size) for i in range(size)])


def scatter_lead(blocks, axis, kind=BF):
    total = blocks[0].astype(F32)
    for step in range(1, blocks.shape[0]):
        total = total + shift_by(blocks[step], axis, step).astype(F32)
    return total.astype(kind)


def scatter_start(blocks, axis):
    half = blocks.shape[1] // 2
    return shift_by(blocks[2, :half], axis, 1), shift_by(blocks[2, half:], axis, -1)


def scatter_finish(blocks, axis, upward, downward):
    half = blocks.shape[1] // 2
    up, down = blocks[1].astype(F32), blocks[3].astype(F32)
    up = jnp.concatenate([up[:half] + upward.astype(F32), up[half:]], axis=0).astype(BF)
    down = jnp.concatenate([down[:half], down[half:] + downward.astype(F32)], axis=0).astype(BF)
    up, down = shift_by(up, axis, 1), shift_by(down, axis, -1)
    return (blocks[0].astype(F32) + up.astype(F32) + down.astype(F32)).astype(BF)


def tie(*values):
    return lax.optimization_barrier(values)


def from_peer(values, flip):
    size = lax.axis_size("x")
    return lax.ppermute(values, "x", [(i, i ^ flip) for i in range(size)])


def gather_x(block):
    return [block] + [from_peer(block, flip) for flip in (1, 2, 3)]


def stem_tables():
    half, quarter = SIDE // 2, SIDE // 4
    pool = np.zeros((SIDE, 128), np.float32)
    for column in range(SIDE):
        pool[column, column // 2] = 0.25
    fine = np.zeros((2, SIDE, 9 * 128), np.float32)
    coarse = np.zeros((2 * 128, 7 * 128), np.float32)
    for seg in range(2):
        for spot in range(quarter):
            for tap in range(9):
                column = 4 * spot + tap - 3
                if 0 <= column < SIDE:
                    fine[seg, column, tap * 128 + seg * 64 + spot] = 1
            for tap in range(7):
                column = 2 * spot + tap - 3
                if 0 <= column < half:
                    coarse[seg * 128 + column, tap * 128 + seg * 64 + spot] = 1
    sel_fine = np.zeros((8, 168, 432), np.float32)
    for up in range(2):
        for row in range(2):
            for col in range(2):
                for chan in range(3):
                    for dy in range(7):
                        for dx in range(7):
                            sel_fine[
                                up * 4 + row * 2 + col,
                                chan * 56 + dy * 8 + dx,
                                chan * 144 + (2 * col + dx) * 16 + 4 * up + 2 * row + dy,
                            ] = 1
    sel_coarse = np.zeros((4, 56, 128), np.float32)
    for up in range(4):
        for dy in range(7):
            for dx in range(7):
                sel_coarse[up, dy * 8 + dx, dx * 16 + 2 * up + dy] = 1
    lanes = np.zeros((8, 128), np.float32)
    lanes[0, :64] = 1
    lanes[1, 64:] = 1
    usable = np.zeros((8, 128), np.float32)
    usable[0, :56] = 1
    usable[1, 64:120] = 1
    return [
        jnp.asarray(table, dtype)
        for table, dtype in (
            (pool, BF),
            (fine, BF),
            (coarse, BF),
            (sel_fine, BF),
            (sel_coarse, BF),
            (lanes, F32),
            (usable, F32),
        )
    ]


def fine_patches(tall):
    parts = []
    for pair in range(4):
        rows = slice(8 * pair, 8 * pair + 16)
        parts.append(
            jnp.concatenate(
                [
                    tall[chan][rows, tap * 128 : (tap + 1) * 128]
                    for chan in range(3)
                    for tap in range(9)
                ],
                axis=0,
            ).astype(BF)
        )
    return jnp.concatenate(parts, axis=1)


def coarse_patches(tall):
    blank = jnp.zeros((16, 128), F32)
    parts = [[], []]
    for chan in range(12):
        for quad in range(2):
            rows = slice(8 * quad, 8 * quad + 16)
            for tap in range(7):
                parts[quad].append(tall[chan][rows, tap * 128 : (tap + 1) * 128])
            parts[quad].append(blank)
    return jnp.concatenate(
        [jnp.concatenate(pieces, axis=0).astype(BF) for pieces in parts], axis=1
    )


def stem_spread(
    frames, weight, diff_weight, pool, fine_tab, coarse_tab, sel_fine, sel_coarse, after,
    fine_out, coarse_out, wide_fine, wide_coarse,
    planes_ref, pooled_ref, moved_ref, flat_ref,
):
    pooled_ref[...] = jnp.zeros_like(pooled_ref)
    moved_ref[...] = jnp.zeros_like(moved_ref)
    for seg in range(2):
        planes_ref[...] = dot(frames[seg], pool[...])
        for chan in range(3):
            lines = []
            for k in range(5):
                at = (k * 3 + chan) * SIDE
                lines.append(
                    planes_ref[pl.ds(at, SIDE // 2, 2), :]
                    + planes_ref[pl.ds(at + 1, SIDE // 2, 2), :]
                )
            for k in range(4):
                at = (k * 3 + chan) * 128 + 3
                pooled_ref[at : at + 112, seg * 128 : (seg + 1) * 128] = lines[k + 1] - lines[k]
            at = (6 + chan) * SIDE
            moved_ref[seg, chan * 256 + 3 : chan * 256 + 227, :] = frames[
                seg, at : at + SIDE, :
            ].astype(F32)
    small = pooled_ref[...].astype(BF)
    for left in range(0, 896, 256):
        right = min(left + 256, 896)
        coarse_out[:, :, left:right] = (
            dot(small, coarse_tab[:, left:right]).astype(BF).reshape(12, 128, right - left)
        )
    first, second = moved_ref[0].astype(BF), moved_ref[1].astype(BF)
    for left in range(0, 1152, 256):
        right = min(left + 256, 1152)
        value = dot(first, fine_tab[0, :, left:right]) + dot(second, fine_tab[1, :, left:right])
        fine_out[:, :, left:right] = value.astype(BF).reshape(3, 256, right - left)

    flat_ref[...] = jnp.zeros_like(flat_ref)
    for chan in range(3):
        for row in range(7):
            at = chan * 56 + row * 8
            flat_ref[at : at + 7, :] = weight[chan, row].astype(F32)
    for chan in range(12):
        for row in range(7):
            at = 168 + chan * 56 + row * 8
            flat_ref[at : at + 7, :] = diff_weight[chan, row].astype(F32)
    narrow = jnp.transpose(flat_ref[0:168, :]).astype(BF)
    for block in range(8):
        wide_fine[block * 64 : (block + 1) * 64, :] = dot(narrow, sel_fine[block]).astype(BF)
    tall = jnp.concatenate(
        [jnp.transpose(flat_ref[168 + chan * 56 : 224 + chan * 56, :]) for chan in range(12)], axis=0
    ).astype(BF)
    for up in range(4):
        spread = dot(tall, sel_coarse[up]).astype(BF)
        for chan in range(12):
            wide_coarse[up * 64 : (up + 1) * 64, chan * 128 : (chan + 1) * 128] = spread[
                chan * 64 : (chan + 1) * 64
            ]


def fine_rows(fine, group):
    start = pl.multiple_of(32 * group, 16)
    return [fine[chan, pl.ds(start, 48), :].astype(F32) for chan in range(3)]


def coarse_rows(coarse, group):
    start = pl.multiple_of(16 * group, 16)
    return [coarse[chan, pl.ds(start, 32), :].astype(F32) for chan in range(12)]


def stem_forward(
    fine, coarse, wide_fine, wide_coarse, lanes, usable, after,
    raw_out, sums_out, centre_out, acc_ref,
):
    acc_ref[...] = jnp.zeros_like(acc_ref)

    @pl.loop(0, GROUPS)
    def group(step):
        fine_sum = dot(
            wide_fine[...], fine_patches(fine_rows(fine, step))
        )
        coarse_sum = dot(
            wide_coarse[...],
            coarse_patches(coarse_rows(coarse, step)),
        )

        def value_at(pair, up, spot, top):
            row = (up * 4 + spot) * 64 + top
            lift = (2 * (pair % 2) + up) * 64 + top
            left = (pair // 2) * 128
            return (
                fine_sum[row : row + 16, pair * 128 : (pair + 1) * 128]
                + coarse_sum[lift : lift + 16, left : left + 128]
            )

        @pl.when(step == 0)
        def find_centre():
            for top in range(0, 64, 16):
                total = jnp.zeros((16, 128), F32)
                for pair in range(4):
                    for up in range(2):
                        for spot in range(4):
                            total = total + value_at(pair, up, spot, top)
                centre_out[top : top + 16, :] = total
            spread = dot(usable[...], usable[...], TN) * (1.0 / (32 * 56))
            centre_out[...] = dot(centre_out[...], spread)

        for top in range(0, 64, 16):
            centre = centre_out[top : top + 16, :]
            plain = acc_ref[top : top + 16, :]
            square = acc_ref[64 + top : 80 + top, :]
            for pair in range(4):
                for up in range(2):
                    for spot in range(4):
                        value = value_at(pair, up, spot, top)
                        row = (up * 4 + spot) * 64 + top
                        raw_out[step, row : row + 16, pair * 128 : (pair + 1) * 128] = (value - centre).astype(BF)
                        plain = plain + value
                        square = square + value * value
            acc_ref[top : top + 16, :] = plain
            acc_ref[64 + top : 80 + top, :] = square

    sums_out[...] = dot(lanes[...], acc_ref[...], NT, HIGH)


def dot_exact(select, values):
    total = None
    for _ in range(3):
        part = values.astype(BF)
        values = values - part.astype(F32)
        term = dot(select, part, NT)
        total = term if total is None else total + term
    return total


def over_lanes(vector):
    return dot(vector, jnp.ones((1, 128), F32), TN, HIGH)


def stem_scales(totals, lanes, count):
    spread = dot(totals, lanes, TN, HIGH) * (1.0 / count)
    return spread[0:64, :], spread[64:128, :]


def stem_middle(
    raw, cotangent, totals, gain, bias, lanes, centre, after, back_out, sums_out,
    seed_ref, coef_ref, scale_ref, acc_ref, *, count
):
    average, square = stem_scales(totals[...], lanes[...], count)
    scale = lax.rsqrt(square - average * average + EPS)
    scale_ref[...] = scale
    coef_ref[0] = average - centre[...]
    coef_ref[1] = scale * over_lanes(gain[...])
    coef_ref[2] = over_lanes(bias[...]) - coef_ref[0] * coef_ref[1]
    acc_ref[...] = jnp.zeros_like(acc_ref)

    @pl.loop(0, GROUPS)
    def group(step):
        blank = jnp.zeros((8, 64), F32)
        for spot in range(8):
            line = 8 * step + spot
            tall = jnp.concatenate(
                [cotangent[0, line].astype(F32), blank, cotangent[1, line].astype(F32), blank], axis=0
            )
            seed_ref[spot] = jnp.transpose(tall) * 0.25
        for top in range(0, 64, 16):
            chans = slice(top, top + 16)
            average, slope, shift = coef_ref[0, chans], coef_ref[1, chans], coef_ref[2, chans]
            plain, cross = acc_ref[0, chans], acc_ref[1, chans]
            for pair in range(4):
                cols = slice(pair * 128, (pair + 1) * 128)
                for up in range(2):
                    seed = seed_ref[2 * pair + up, chans]
                    for spot in range(4):
                        row = (up * 4 + spot) * 64 + top
                        value = raw[step, row : row + 16, cols].astype(F32)
                        act = value * slope + shift
                        sigma = sigmoid(act)
                        grad = seed * (sigma * (1.0 + act * (1.0 - sigma)))
                        back_out[step, row : row + 16, cols] = grad.astype(BF)
                        plain = plain + grad
                        cross = cross + grad * (value - average)
            acc_ref[0, chans] = plain
            acc_ref[1, chans] = cross

    acc_ref[1] = acc_ref[1] * scale_ref[...]
    sums_out[...] = dot(lanes[...], acc_ref[...].reshape(128, 128), NT, HIGH)


def stem_backward(
    place, raw, back, fine, coarse, totals, back_totals, gain, sel_fine, sel_coarse, lanes, centre, after,
    packed_out,
    coef_ref, packed, draw_ref, small_ref, fine_acc, coarse_acc, *, count
):
    average, square = stem_scales(totals[...], lanes[...], count)
    scale = lax.rsqrt(square - average * average + EPS)
    first, second = stem_scales(back_totals[...], lanes[...], count)
    slope = over_lanes(gain[...]) * scale
    coef_ref[0] = slope
    coef_ref[1] = -slope * scale * second
    coef_ref[2] = slope * ((average - centre[...]) * scale * second - first)
    fine_acc[...] = jnp.zeros_like(fine_acc)
    coarse_acc[...] = jnp.zeros_like(coarse_acc)

    @pl.loop(0, GROUPS)
    def group(step):
        for top in range(0, 64, 16):
            on_back, on_raw, constant = (coef_ref[k, top : top + 16] for k in range(3))
            for pair in range(4):
                cols = slice(pair * 128, (pair + 1) * 128)
                for up in range(2):
                    summed = None
                    for spot in range(4):
                        row = (up * 4 + spot) * 64 + top
                        draw = (
                            back[step, row : row + 16, cols].astype(F32) * on_back
                            + raw[step, row : row + 16, cols].astype(F32) * on_raw
                            + constant
                        ).astype(BF)
                        draw_ref[row : row + 16, cols] = draw
                        wide = draw.astype(F32)
                        summed = wide if summed is None else summed + wide
                    lift = (2 * (pair % 2) + up) * 64 + top
                    left = (pair // 2) * 128
                    small_ref[lift : lift + 16, left : left + 128] = summed.astype(BF)
        patches = fine_patches(fine_rows(fine, step))
        fine_acc[...] += dot(draw_ref[...], patches, NT)
        patches = coarse_patches(coarse_rows(coarse, step))
        coarse_acc[...] += dot(small_ref[...], patches, NT)

    total = jnp.zeros((168, 64), F32)
    for block in range(8):
        total = total + dot_exact(sel_fine[block], fine_acc[block * 64 : (block + 1) * 64, :])
    packed[0:168, 0:64] = total
    packed[0:168, 64:128] = jnp.zeros((168, 64), F32)
    for duo in range(6):
        piece = jnp.zeros((56, 128), F32)
        for up in range(4):
            stacked = jnp.concatenate(
                [
                    coarse_acc[up * 64 : (up + 1) * 64, chan * 128 : (chan + 1) * 128]
                    for chan in (2 * duo, 2 * duo + 1)
                ],
                axis=0,
            )
            piece = piece + dot_exact(sel_coarse[up], stacked)
        packed[168 + duo * 56 : 224 + duo * 56, :] = piece
    packed[504:512, :] = jnp.zeros((8, 128), F32)
    for quarter in range(4):
        for block in range(4):
            top = quarter * 128 + block * 32
            packed_out[lax.rem(quarter + 4 - place[0], 4), :, block * 128 : (block + 1) * 128] = packed[top : top + 32, :]


def whole(*dims):
    return pl.BlockSpec(
        dims, lambda step, *rest: (0,) * len(dims), pipeline_mode=pl.Buffered(1)
    )


def stem_planes(frames, stem_weight, stem_diff_weight, tables, after):
    pool, fine_tab, coarse_tab, sel_fine, sel_coarse, lanes, usable = tables
    return pl.pallas_call(
        stem_spread,
        in_specs=[VMEM] * 9,
        out_specs=[VMEM] * 4,
        out_shape=[
            held((3, 256, 1152), BF),
            held((12, 128, 896), BF),
            held((512, 432), BF),
            held((256, 1536), BF),
        ],
        scratch_shapes=[
            pltpu.VMEM((15 * SIDE, 128), F32),
            pltpu.VMEM((12 * 128, 256), F32),
            pltpu.VMEM((2, 768, SIDE), F32),
            pltpu.VMEM((168 + 672, STEMC), F32),
        ],
        compiler_params=params("stem_spread"),
        cost_estimate=cost(4e9, 1e7),
        name="stem_spread",
    )(
        frames.reshape(2, 15 * SIDE, SIDE),
        stem_weight.transpose(1, 2, 3, 0),
        stem_diff_weight.transpose(1, 2, 3, 0),
        pool, fine_tab, coarse_tab, sel_fine, sel_coarse, after,
    )


def stem_first(fine, coarse, wide_fine, wide_coarse, tables, after):
    lanes, usable = tables[5:]
    return pl.pallas_call(
        stem_forward,
        in_specs=[VMEM] * 7,
        out_specs=[VMEM] * 3,
        out_shape=[held((GROUPS, 512, 512), BF), shape((8, 128)), shape((STEMC, 128))],
        scratch_shapes=[pltpu.VMEM((128, 128), F32)],
        compiler_params=params("stem_forward"),
        cost_estimate=cost(4e9, 1e7),
        name="stem_forward",
    )(*in_vmem(fine, coarse, wide_fine, wide_coarse), lanes, usable, after)


def stem_second(raw, centre, stem_cotangent, totals, stem_gain, stem_bias, lanes, count, after):
    gain = stem_gain.reshape(1, STEMC)
    bias = stem_bias.reshape(1, STEMC)
    cot = stem_cotangent.transpose(0, 2, 3, 1)
    return pl.pallas_call(
        functools.partial(stem_middle, count=count),
        in_specs=[VMEM] * 8,
        out_specs=[VMEM] * 2,
        out_shape=[pltpu.VMEM((GROUPS, 512, 512), BF), shape((8, 128))],
        scratch_shapes=[
            pltpu.VMEM((8, 64, 128), F32),
            pltpu.VMEM((3, 64, 128), F32),
            pltpu.VMEM((64, 128), F32),
            pltpu.VMEM((2, 64, 128), F32),
        ],
        compiler_params=params("stem_middle"),
        cost_estimate=cost(8e9, 1.5e7),
        name="stem_middle",
    )(*in_vmem(raw), cot, totals, gain, bias, lanes, centre, after)


def stem_third(
    place, raw, centre, back, fine, coarse, totals, back_totals, stem_gain, tables, count, after
):
    pool, fine_tab, coarse_tab, sel_fine, sel_coarse, lanes, usable = tables
    gain = stem_gain.reshape(1, STEMC)
    return pl.pallas_call(
        functools.partial(stem_backward, count=count),
        in_specs=[SMEM] + [VMEM] * 12,
        out_specs=VMEM,
        out_shape=shape((4, 32, 512)),
        scratch_shapes=[
            pltpu.VMEM((3, 64, 128), F32),
            pltpu.VMEM((512, 128), F32),
            pltpu.VMEM((512, 512), BF),
            pltpu.VMEM((256, 256), BF),
            pltpu.VMEM((512, 432), F32),
            pltpu.VMEM((256, 1536), F32),
        ],
        compiler_params=params("stem_backward"),
        cost_estimate=cost(8e9, 2.5e7),
        name="stem_backward",
    )(place, *in_vmem(raw, back, fine, coarse), totals, back_totals, gain, sel_fine, sel_coarse, lanes, centre, after)


def put_moments(out_ref, values):
    out_ref[0:1, :] = jnp.sum(values, axis=0, keepdims=True)
    out_ref[1:2, :] = jnp.sum(values * values, axis=0, keepdims=True)


def moments(totals, count):
    average = totals[0:1] * (1.0 / count)
    square = totals[1:2] * (1.0 / count)
    return average, lax.rsqrt(square - average * average + EPS)


def affine_of(totals, count, gain, bias):
    average, scale = moments(totals, count)
    slope = gain * scale
    return slope, bias - average * slope


def back_affine(totals, sums, count, gain, middle=0.0):
    average, scale = moments(totals, count)
    first = sums[0:1] * (1.0 / count)
    second = sums[1:2] * (1.0 / count)
    on_grad = gain * scale
    on_value = -on_grad * scale * second
    return on_grad, on_value, -on_grad * first - on_value * (average - middle)


def each_piece(width, pieces):
    for left in range(0, width, 128):
        for rows in pieces:
            yield rows, slice(left, left + 128)


def lane_tile(tile, width=128):
    return pl.ds(pl.multiple_of(tile * width, width), width)


def put_wide_back(out_ref, grad, value, totals, sums, first, gain, middle, count):
    @pl.loop(0, C // 128)
    def one(tile):
        cols = lane_tile(tile)
        on_grad, on_value, constant = back_affine(
            totals[:, cols], sums[first : first + 2, cols], count, gain[:, cols], middle[:, cols]
        )
        for rows in PIECES:
            out_ref[rows, cols] = (
                grad[rows, cols].astype(F32) * on_grad + value[rows, cols].astype(F32) * on_value + constant
            ).astype(BF)


def put_back(out_ref, grad, value, coefs):
    on_grad, on_value, constant = coefs
    for rows, cols in each_piece(out_ref.shape[1], PIECES):
        out_ref[rows, cols] = (
            grad[rows, cols].astype(F32) * on_grad[:, cols]
            + value[rows, cols].astype(F32) * on_value[:, cols]
            + constant[:, cols]
        ).astype(BF)


def put_activation_back(out_ref, sums_out, grad, value, totals, gain, bias, count):
    average, scale = moments(totals, count)
    slope = gain * scale
    shift = bias - average * slope
    for left in range(0, MID, 128):
        cols = slice(left, left + 128)
        plain = jnp.zeros((8, 128), F32)
        cross = jnp.zeros((8, 128), F32)
        for rows in EIGHTS:
            pre = value[rows, cols]
            act = pre * slope[:, cols] + shift[:, cols]
            sigma = sigmoid(act)
            hidden = grad[rows, cols].astype(BF).astype(F32)
            back = hidden * (sigma * (1.0 + act * (1.0 - sigma)))
            out_ref[rows, cols] = back
            plain = plain + back
            cross = cross + back * (pre - average[:, cols])
        sums_out[0:1, cols] = jnp.sum(plain, axis=0, keepdims=True)
        sums_out[1:2, cols] = jnp.sum(cross, axis=0, keepdims=True) * scale[:, cols]


def first_matmuls(place, features, reduce_w, motion_w, reduce_out, motion_out, reduce_sum, motion_sum):
    value = dot(features[...], reduce_w[...])
    reduce_out[...] = value
    put_moments(reduce_sum, value)
    value = dot(features[...], motion_w[...])
    motion_out[...] = value
    put_moments(motion_sum, value)


def tap_mask(places, row_off, col_off):
    kept = None
    for off, base in ((row_off, 0), (col_off, 256)):
        if off:
            at = base + (128 if off > 0 else 0)
            good = places[:, at : at + 128]
            kept = good if kept is None else kept * good
    return kept


def tap_source(buffer, places, row_off, col_off, sign):
    move = sign * (7 * row_off + col_off)
    mask = tap_mask(places, sign * row_off, sign * col_off)
    value = buffer[8 + move : 8 + move + ROWS, :]
    if mask is not None:
        value = value * jnp.concatenate([mask] * (value.shape[1] // 128), axis=1)
    return value


def clear_ends(buffer):
    blank = jnp.zeros((8, buffer.shape[1]), F32)
    buffer[0:8, :] = blank
    buffer[8 + ROWS : 16 + ROWS, :] = blank


def spatial_forward(
    pre_reduce, totals, gain, bias, places, weight, hidden_out, pre_out, sums_out, buffer, *, count
):
    clear_ends(buffer)
    slope, shift = affine_of(totals[...], count, gain[...], bias[...])
    for rows, cols in each_piece(MID, PIECES):
        value = pre_reduce[rows, cols] * slope[:, cols] + shift[:, cols]
        hidden = (value * sigmoid(value)).astype(BF)
        hidden_out[rows, cols] = hidden
        buffer[8 + rows.start : 8 + rows.stop, cols] = hidden.astype(F32)
    for tap in range(9):
        row_off, col_off = tap // 3 - 1, tap % 3 - 1
        source = tap_source(buffer, places, row_off, col_off, 1).astype(BF)
        value = dot(source, weight[tap * MID : (tap + 1) * MID, :])
        if tap == 0:
            pre_out[...] = value
        else:
            pre_out[...] += value
    put_moments(sums_out, pre_out[...])


def wide_product(hidden, weight, pre_out, sums_out, mid_out):
    @pl.loop(0, C // TILE)
    def one(tile):
        cols = lane_tile(tile, TILE)
        value = dot(hidden[...], weight[:, cols])
        total = jnp.sum(value, axis=0, keepdims=True)
        sums_out[0:1, cols] = total
        sums_out[1:2, cols] = jnp.sum(value * value, axis=0, keepdims=True)
        middle = total * (1.0 / ROWS)
        mid_out[:, cols] = middle
        pre_out[:, cols] = (value - middle).astype(BF)


def expand_forward(
    pre_spatial, totals, gain, bias, weight, hidden_out, pre_out, sums_out, mid_out, *, count
):
    slope, shift = affine_of(totals[...], count, gain[...], bias[...])
    for rows, cols in each_piece(MID, PIECES):
        value = pre_spatial[rows, cols] * slope[:, cols] + shift[:, cols]
        hidden_out[rows, cols] = (value * sigmoid(value)).astype(BF)
    wide_product(hidden_out, weight, pre_out, sums_out, mid_out)


def at(buffer, rows, move=0):
    return buffer[64 + rows.start + move : 64 + rows.stop + move, :]


def put(buffer, rows, value):
    buffer[64 + rows.start : 64 + rows.stop, :] = value


def clear_margins(buffers):
    for buffer in buffers:
        buffer[0:64, :] = jnp.zeros((64, 128), F32)
        buffer[64 + ROWS : 128 + ROWS, :] = jnp.zeros((64, 128), F32)


def mask_of(places, rows, which):
    return places[rows, which * 128 : (which + 1) * 128]


UP, DOWN, LEFT, RIGHT = range(4)


def three(buffer, places, rows, move, before, after):
    return (
        at(buffer, rows, -move) * mask_of(places, rows, before),
        at(buffer, rows),
        at(buffer, rows, move) * mask_of(places, rows, after),
    )


def box_rows(buffer, places, out):
    for rows in EIGHTS:
        first, second, third = three(buffer, places, rows, 1, LEFT, RIGHT)
        put(out, rows, first + second + third)


def box_columns(buffer, places, rows):
    first, second, third = three(buffer, places, rows, 7, UP, DOWN)
    return (first + second + third) * (1.0 / 9.0)


def kept(value, rows, keep):
    first, last = rows.start // 49, (rows.stop - 1) // 49
    if first == last:
        return value * keep[0, first]
    lines = lax.broadcasted_iota(jnp.int32, value.shape, 0)
    return value * jnp.where(lines < last * 49 - rows.start, keep[0, first], keep[0, last])


def change_and_average(pre_motion, slope, keep, places, cols, spare, change, average):
    for rows in EIGHTS:
        put(spare, rows, pre_motion[rows, cols] * slope)
    for rows in EIGHTS:
        put(change, rows, kept(at(spare, rows, 49) - at(spare, rows), rows, keep))
    box_rows(change, places, spare)
    for rows in EIGHTS:
        put(average, rows, box_columns(spare, places, rows))


def motion_forward(
    pre_motion, totals, gain, keep, places, depth, weight, after, mixed_out, pre_out, sums_out, mid_out,
    spare, change, average, lines_a, lines_b, lines_c, *, count
):
    clear_margins((spare, change, average, lines_a, lines_b, lines_c))

    @pl.loop(0, MID // 128)
    def one(tile):
        cols = pl.ds(pl.multiple_of(tile * 128, 128), 128)
        scale = moments(totals[:, cols], count)[1]
        change_and_average(
            pre_motion, gain[:, cols] * scale, keep, places, cols, spare, change, average
        )
        for rows in EIGHTS:
            near = three(change, places, rows, 1, LEFT, RIGHT)
            wide = three(average, places, rows, 1, LEFT, RIGHT)
            for row, out in enumerate((lines_a, lines_b, lines_c)):
                line = None
                for col in range(3):
                    for scale_at, source in enumerate((near, wide)):
                        term = source[col] * depth[scale_at, row, col : col + 1, cols]
                        line = term if line is None else line + term
                put(out, rows, line)
        for rows in PIECES:
            value = (
                at(lines_b, rows)
                + at(lines_a, rows, -7) * mask_of(places, rows, UP)
                + at(lines_c, rows, 7) * mask_of(places, rows, DOWN)
            )
            mixed_out[rows, cols] = value.astype(BF)

    wide_product(mixed_out, weight, pre_out, sums_out, mid_out)


def gate_kernel(
    own, pre_expand, pre_excite, features, cotangent, expand_tot, excite_tot, expand_mid, excite_mid,
    expand_gain, expand_bias, excite_gain, excite_bias,
    mine_out, other_out, direct_out, comb_out, gate_out, sums_out, output_ref, direct_ref, *, count
):
    @pl.loop(0, C // 128)
    def one(tile):
        cols = lane_tile(tile)
        e_mean, e_scale = moments(expand_tot[:, cols], count)
        x_mean, x_scale = moments(excite_tot[:, cols], count)
        e_mean = e_mean - expand_mid[:, cols]
        x_mean = x_mean - excite_mid[:, cols]
        e_slope = expand_gain[:, cols] * e_scale
        e_shift = expand_bias[:, cols] - e_mean * e_slope
        x_slope = excite_gain[:, cols] * x_scale
        x_shift = excite_bias[:, cols] - x_mean * x_slope
        sums = [jnp.zeros((8, 128), F32)] * 4
        for rows in PIECES:
            feats = features[rows, cols].astype(F32)
            seed = cotangent[rows, cols].astype(F32)
            pre_e = pre_expand[rows, cols].astype(F32)
            pre_x = pre_excite[rows, cols].astype(F32)
            branch = (pre_e * e_slope + e_shift).astype(BF).astype(F32)
            gate = sigmoid(pre_x * x_slope + x_shift)
            lifted = feats * gate
            combined = branch + lifted
            sigma = sigmoid(combined)
            output = combined * sigma
            output_ref[rows, cols] = output.astype(BF)
            grad = seed * (sigma + output * (1.0 - sigma))
            direct_ref[rows, cols] = (grad * gate).astype(BF)
            rounded = grad.astype(BF)
            comb_out[rows, cols] = rounded
            rounded = rounded.astype(F32)
            grad_gate = grad * lifted * (1.0 - gate)
            gate_out[rows, cols] = grad_gate.astype(BF)
            terms = (
                rounded,
                rounded * (pre_e - e_mean),
                grad_gate,
                grad_gate * (pre_x - x_mean),
            )
            for spot, value in enumerate(terms):
                for up in range(0, value.shape[0], 8):
                    sums[spot] = sums[spot] + value[up : up + 8]
        finals = [jnp.sum(value, axis=0, keepdims=True) for value in sums]
        sums_out[0:1, cols] = finals[0]
        sums_out[1:2, cols] = finals[1] * e_scale
        sums_out[2:3, cols] = finals[2]
        sums_out[3:4, cols] = finals[3] * x_scale

    mine, other = lane_tile(own[0], MID), lane_tile(own[0] ^ 1, MID)
    mine_out[...] = output_ref[:, mine]
    other_out[...] = output_ref[:, other]
    direct_out[:, :MID] = direct_ref[:, mine]
    direct_out[:, MID:] = direct_ref[:, other]


def expand_backward(
    own, grad, pre_expand, totals, sums, gain, middle, weight, pre_spatial, s_totals, s_gain, s_bias,
    own_out, grad_out, sums_out, value_ref, acc, *, count
):
    put_wide_back(value_ref, grad, pre_expand, totals, sums, 0, gain, middle, count)
    own_out[:, :MID] = value_ref[:, lane_tile(own[0], MID)]
    own_out[:, MID:] = value_ref[:, lane_tile(own[0] ^ 1, MID)]
    acc[...] = dot(value_ref[...], weight[...], NT)
    put_activation_back(
        grad_out, sums_out, acc, pre_spatial, s_totals[...], s_gain[...], s_bias[...], count
    )


def excite_backward(
    own, grad, pre_excite, totals, sums, gain, middle, weight, pre_motion, m_totals, m_gain, keep,
    places, depth, own_out, grad_out, sums_out, depth_out, value_ref, acc,
    spare, change, average, seed, pull_a, pull_b, pull_c, near_out, wide_out, *, count
):
    put_wide_back(value_ref, grad, pre_excite, totals, sums, 2, gain, middle, count)
    own_out[:, :MID] = value_ref[:, lane_tile(own[0], MID)]
    own_out[:, MID:] = value_ref[:, lane_tile(own[0] ^ 1, MID)]
    acc[...] = dot(value_ref[...], weight[...], NT)
    clear_margins((spare, change, average, seed, pull_a, pull_b, pull_c, near_out, wide_out))

    @pl.loop(0, MID // 128)
    def one(tile):
        cols = pl.ds(pl.multiple_of(tile * 128, 128), 128)
        mean, scale = moments(m_totals[:, cols], count)
        change_and_average(
            pre_motion, m_gain[:, cols] * scale, keep, places, cols, spare, change, average
        )
        for rows in EIGHTS:
            put(seed, rows, acc[rows, cols])
        for base, source, out in ((0, change, near_out), (9, average, wide_out)):
            totals_of = [jnp.zeros((8, 128), F32)] * 9
            for rows in EIGHTS:
                later, now, before = three(seed, places, rows, -7, DOWN, UP)
                taps = three(source, places, rows, 1, LEFT, RIGHT)
                for col, pull in enumerate((pull_a, pull_b, pull_c)):
                    total = None
                    for row, line in enumerate((later, now, before)):
                        spot = row * 3 + col
                        term = line * depth[base // 9, row, col : col + 1, cols]
                        total = term if total is None else total + term
                        totals_of[spot] = totals_of[spot] + line * taps[col]
                    put(pull, rows, total)
            for spot in range(9):
                depth_out[base + spot : base + spot + 1, cols] = jnp.sum(
                    totals_of[spot], axis=0, keepdims=True
                )
            for rows in EIGHTS:
                put(
                    out,
                    rows,
                    at(pull_b, rows)
                    + at(pull_a, rows, 1) * mask_of(places, rows, RIGHT)
                    + at(pull_c, rows, -1) * mask_of(places, rows, LEFT),
                )
        box_rows(wide_out, places, spare)
        for rows in EIGHTS:
            value = at(near_out, rows) + box_columns(spare, places, rows)
            put(change, rows, kept(value, rows, keep))
        plain = jnp.zeros((8, 128), F32)
        cross = jnp.zeros((8, 128), F32)
        for rows in EIGHTS:
            value = at(change, rows, -49) - at(change, rows)
            grad_out[rows, cols] = value
            plain = plain + value
            cross = cross + value * (pre_motion[rows, cols] - mean)
        sums_out[0:1, cols] = jnp.sum(plain, axis=0, keepdims=True)
        sums_out[1:2, cols] = jnp.sum(cross, axis=0, keepdims=True) * scale


def spatial_backward(
    own, grad, pre_spatial, totals, sums, gain, places, weight, pre_reduce, r_totals, r_gain, r_bias,
    m_grad, pre_motion, m_totals, m_sums, m_gain,
    taps_out, grad_out, sums_out, motion_out, motion_own, buffer, source_ref, acc, *, count
):
    clear_ends(buffer)
    on_grad, on_value, constant = back_affine(totals[...], sums[...], count, gain[...])
    for rows, cols in each_piece(MID, EIGHTS):
        buffer[8 + rows.start : 8 + rows.stop, cols] = (
            (
                grad[rows, cols] * on_grad[:, cols]
                + pre_spatial[rows, cols] * on_value[:, cols]
                + constant[:, cols]
            )
            .astype(BF)
            .astype(F32)
        )
    mine = pl.ds(pl.multiple_of((own[0] // 2) * 256, 256), 256)
    for tap in range(9):
        row_off, col_off = tap // 3 - 1, tap % 3 - 1
        source_ref[...] = tap_source(buffer, places, row_off, col_off, -1).astype(BF)
        taps_out[:, tap * 256 : (tap + 1) * 256] = source_ref[:, mine]
        value = dot(source_ref[...], weight[tap * MID : (tap + 1) * MID, :], NT)
        if tap == 0:
            acc[...] = value
        else:
            acc[...] += value
    put_activation_back(
        grad_out, sums_out, acc, pre_reduce, r_totals[...], r_gain[...], r_bias[...], count
    )
    put_back(
        motion_out, m_grad, pre_motion, back_affine(m_totals[...], m_sums[...], count, m_gain[...])
    )
    motion_own[...] = motion_out[:, mine]


def reduce_backward(
    own, grad, pre_reduce, totals, sums, gain, mine_w, other_w, motion, mine_m, other_m, direct,
    own_out, mine_out, other_out, value_ref, *, count
):
    put_back(value_ref, grad, pre_reduce, back_affine(totals[...], sums[...], count, gain[...]))
    own_out[...] = value_ref[:, pl.ds(pl.multiple_of((own[0] // 2) * 256, 256), 256)]
    for out, reduce_w, motion_w, left in (
        (other_out, other_w, other_m, MID),
        (mine_out, mine_w, mine_m, 0),
    ):
        value = dot(value_ref[...], reduce_w[...], NT) + dot(motion[...], motion_w[...], NT)
        out[...] = (value + direct[:, left : left + MID].astype(F32)).astype(BF)


def owners(place, sizes):
    away = lambda at, axis, size: lax.rem(at + size - place[axis], size)
    for z in range(sizes[0]):
        for y in range(sizes[1]):
            for c in range(sizes[2]):
                owner = (z * sizes[1] + y) * sizes[2] + c
                yield owner, (away(c, 1, sizes[2]), away(y, 2, sizes[1]), away(z, 3, sizes[0]))


def spatial_weight_kernel(place, hidden, taps, motion, out, turned_ref, *, sizes):
    turned_ref[...] = jnp.transpose(hidden[...].astype(F32)).astype(BF)
    clips = sizes[0] * sizes[1] * sizes[2]
    spots = dict(owners(place, sizes))
    share = 9 * MID // clips
    for tap in range(9):
        value = dot(turned_ref[...], taps[:, tap * 256 : (tap + 1) * 256]).astype(BF)
        for top in range(0, MID, 16):
            row = tap * MID + top
            out[*spots[row // share], row % share : row % share + 16, :] = value[top : top + 16]
    for owner, spot in spots.items():
        out[*spot, share:, :] = motion[owner * (C // clips) : (owner + 1) * (C // clips), :]


def early_weight_kernel(place, hidden, expand, mixed, excite, out, turned_ref, *, sizes):
    rows = MID // (sizes[0] * sizes[1] * sizes[2])
    spots = dict(owners(place, sizes))
    for base, left, right in ((0, hidden, expand), (4, mixed, excite)):
        turned_ref[...] = jnp.transpose(left[...].astype(F32)).astype(BF)
        for block in range(4):
            value = dot(turned_ref[...], right[:, block * 256 : (block + 1) * 256]).astype(BF)
            for owner, spot in spots.items():
                out[*spot, (base + block) * rows : (base + block + 1) * rows, :] = value[
                    owner * rows : (owner + 1) * rows
                ]


def late_weight_kernel(place, values, out, *, sizes):
    rows = out.shape[3]
    for owner, spot in owners(place, sizes):
        out[*spot] = values[owner * rows : (owner + 1) * rows, :]


def join_kernel(own, mine, got, out):
    first = jnp.where(own[0] % 2 == 0, mine[...].astype(F32), got[...].astype(F32))
    second = jnp.where(own[0] % 2 == 0, got[...].astype(F32), mine[...].astype(F32))
    out[...] = jnp.concatenate([first, second], axis=0).astype(BF)


def unpack_kernel(
    own, rest_0, rest_1, rest_2, rest_3, early_0, early_1, early_2, early_3,
    mine, got, gate, got_gate, tail, got_tail,
    reduce_out, spatial_out, expand_out, motion_out, excite_out, fine_out, coarse_out, grad_out,
    depth_out, e_bias, e_gain, x_bias, x_gain, m_gain, s_bias, s_gain, r_bias, r_gain,
    packed_ref, *, clips
):
    join_kernel(own, mine, got, grad_out)
    both = tail[...] + got_tail[...]
    for spot in range(18):
        depth_out[spot // 9, spot // 3 % 3, spot % 3 : spot % 3 + 1, :] = both[6 + spot : 7 + spot]
    wide = gate[...] + got_gate[...]
    for row, out in enumerate((e_bias, e_gain, x_bias, x_gain)):
        out[...] = wide[row]
    for row, out in ((1, m_gain), (2, s_bias), (3, s_gain), (4, r_bias), (5, r_gain)):
        out[...] = both[row]
    cuts = (9 * MID // clips, (9 * MID + C) // clips, (9 * MID + 2 * C) // clips)
    half = own[0] // 2
    for side, left, right in ((half, rest_0, rest_1), (1 - half, rest_2, rest_3)):
        value = left[...].astype(F32) + right[...].astype(F32)
        cols = pl.ds(pl.multiple_of(side * 256, 256), 256)
        spatial_out[:, cols] = value[: cuts[0]]
        motion_out[:, cols] = value[cuts[0] : cuts[1]]
        reduce_out[:, cols] = value[cuts[1] : cuts[2]]
    rows = MID // clips
    for flip, left, right in (
        (0, (early_0, 0), (early_1, 1)),
        (1, (early_0, 1), (early_1, 0)),
        (2, (early_2, 0), (early_3, 1)),
        (3, (early_2, 1), (early_3, 0)),
    ):
        for base, out in ((0, expand_out), (4, excite_out)):
            for block in range(2):
                value = None
                for ref, spot in (left, right):
                    top = (base + 2 * spot + block) * rows
                    part = ref[top : top + rows, :].astype(F32)
                    value = part if value is None else value + part
                out[:, pl.ds(pl.multiple_of((own[0] ^ flip) * MID + block * 256, 256), 256)] = value
    base = 8 * rows
    for flip, ref in enumerate((early_0, early_1, early_2, early_3)):
        for block in range(4):
            top, left = base + (block // 2) * 32, (block % 2) * 128
            high = ref[top : top + 32, left : left + 128].astype(F32)
            low = ref[top + 64 : top + 96, left : left + 128].astype(F32)
            at = pl.multiple_of((own[0] ^ flip) * 128 + block * 32, 32)
            packed_ref[pl.ds(at, 32), :] = high + low
    for chan in range(3):
        for row in range(7):
            at = chan * 56 + row * 8
            fine_out[chan, row] = packed_ref[at : at + 7, 0:64]
    for chan in range(12):
        side = (chan % 2) * 64
        for row in range(7):
            at = 168 + (chan // 2) * 56 + row * 8
            coarse_out[chan, row] = packed_ref[at : at + 7, side : side + 64]


def with_own(kernel, own, grid, in_specs, out_specs, out_shape, scratch, args, flops, nbytes, name):
    if not grid:
        return pl.pallas_call(
            kernel,
            in_specs=[SMEM] + in_specs,
            out_specs=out_specs,
            out_shape=out_shape,
            scratch_shapes=scratch,
            compiler_params=params(name),
            cost_estimate=cost(flops, nbytes),
            name=name,
        )(own, *args)
    return pl.pallas_call(
        kernel,
        grid_spec=pltpu.PrefetchScalarGridSpec(
            num_scalar_prefetch=1,
            grid=grid,
            in_specs=in_specs,
            out_specs=out_specs,
            scratch_shapes=scratch,
        ),
        out_shape=out_shape,
        compiler_params=params(name),
        cost_estimate=cost(flops, nbytes),
        name=name,
    )(own, *args)


def place_table():
    rows = np.arange(ROWS)
    down = (rows % 49) // 7
    right = rows % 7
    kept = [down >= 1, down <= FEAT - 2, right >= 1, right <= FEAT - 2]
    return jnp.asarray(np.concatenate([np.repeat(k[:, None], 128, 1) for k in kept], axis=1), F32)


def keep_pairs(valid_rows, video_rows):
    valid_float = valid_rows.astype(F32)
    same_video = (video_rows[:, 1:] == video_rows[:, :-1]).astype(F32)
    pair_keep = valid_float[:, 1:] * valid_float[:, :-1] * same_video
    return jnp.concatenate([pair_keep, jnp.zeros_like(pair_keep[:, :1])], axis=1)


def on_device(
    features,
    out_cotangent,
    seg_valid,
    seg_video,
    frames,
    stem_cotangent,
    stem_weight,
    stem_diff_weight,
    stem_gain,
    stem_bias,
    reduce_weight,
    reduce_gain,
    reduce_bias,
    spatial_weight,
    spatial_gain,
    spatial_bias,
    expand_weight,
    expand_gain,
    expand_bias,
    motion_weight,
    motion_gain,
    depth_weight,
    excite_weight,
    excite_gain,
    excite_bias,
):
    clips = lax.axis_size("z") * lax.axis_size("y") * lax.axis_size("c")
    count = float(clips * ROWS)
    stem_count = float(clips * lax.axis_size("x") * (SIDE // 2) ** 2)
    here = lax.axis_index("x")
    micro = here % 2
    own = jnp.stack([here] + [lax.axis_index(axis) for axis in ("c", "y", "z")]).astype(jnp.int32)
    places = place_table()

    def of_micro(rows):
        return lax.dynamic_index_in_dim(
            rows.reshape(MICRO, rows.shape[0] // MICRO, rows.shape[1]), micro, 0, False
        )

    feats = of_micro(features)
    seeds = of_micro(out_cotangent)
    keep = of_micro(keep_pairs(seg_valid, seg_video))
    line = lambda vector: vector.reshape(1, -1)
    reduce_gain, reduce_bias = line(reduce_gain), line(reduce_bias)
    spatial_gain, spatial_bias = line(spatial_gain), line(spatial_bias)
    expand_gain, expand_bias = line(expand_gain), line(expand_bias)
    excite_gain, excite_bias = line(excite_gain), line(excite_bias)
    motion_gain = line(motion_gain)

    tables = stem_tables()
    lanes = tables[5]
    column = lambda rows, width: pl.BlockSpec((rows, width), lambda step, *rest: (0, step))
    pre_reduce, pre_motion, reduce_sum, motion_sum = pl.pallas_call(
        first_matmuls,
        grid=(2,),
        in_specs=[SMEM, whole(ROWS, C), column(C, 256), column(C, 256)],
        out_specs=[column(ROWS, 256), column(ROWS, 256), column(2, 256), column(2, 256)],
        out_shape=[held((ROWS, MID)), held((ROWS, MID)), shape((2, MID)), shape((2, MID))],
        compiler_params=params("first_matmuls"),
        cost_estimate=cost(1.7e9, 1e7),
        name="first_matmuls",
    )(own, *in_vmem(feats), reduce_weight, motion_weight)
    first_wide = core_sum(jnp.concatenate([reduce_sum, motion_sum], axis=1))
    fine, coarse, wide_fine, wide_coarse = stem_planes(
        frames, stem_weight, stem_diff_weight, tables, first_wide
    )
    first_wide = ring_sum(first_wide, "y")
    raw, stem_sum, centre = stem_first(fine, coarse, wide_fine, wide_coarse, tables, first_wide)
    first_tot = ring_sum(first_wide, "z")
    reduce_tot, motion_tot = first_tot[:, :MID], first_tot[:, MID:]
    stem_sum = ring_sum(stem_sum[:2], "x")

    hidden_one, pre_spatial, spatial_sum = pl.pallas_call(
        functools.partial(spatial_forward, count=count),
        in_specs=[VMEM] * 6,
        out_specs=[VMEM] * 3,
        out_shape=[held((ROWS, MID), BF), held((ROWS, MID)), shape((2, MID))],
        scratch_shapes=[pltpu.VMEM((ROWS + 16, MID), F32)],
        compiler_params=params("spatial_forward"),
        cost_estimate=cost(1.9e9, 8e6),
        name="spatial_forward",
    )(*in_vmem(pre_reduce), reduce_tot, reduce_gain, reduce_bias, places, spatial_weight)

    spatial_wide = core_sum(jnp.concatenate([spatial_sum, stem_sum], axis=1))
    mixed, pre_excite, excite_sum, excite_mid = pl.pallas_call(
        functools.partial(motion_forward, count=count),
        in_specs=[VMEM] * 3 + [SMEM] + [VMEM] * 4,
        out_specs=[VMEM] * 4,
        out_shape=[held((ROWS, MID), BF), held((ROWS, C), BF), shape((2, C)), shape((1, C))],
        scratch_shapes=[pltpu.VMEM((ROWS + 128, 128), F32)] * 6,
        compiler_params=params("motion_forward"),
        cost_estimate=cost(2e9, 1.2e7),
        name="motion_forward",
    )(*in_vmem(pre_motion), motion_tot, motion_gain, keep, places, depth_weight, excite_weight, spatial_wide)
    spatial_wide = ring_sum(ring_sum(spatial_wide, "y"), "z")
    spatial_tot, stem_tot = spatial_wide[:, :MID], spatial_wide[:, MID:]
    stem_tot = jnp.pad(stem_tot, ((0, 6), (0, 0)))

    hidden_two, pre_expand, expand_sum, expand_mid = pl.pallas_call(
        functools.partial(expand_forward, count=count),
        in_specs=[VMEM] * 5,
        out_specs=[VMEM] * 4,
        out_shape=[held((ROWS, MID), BF), held((ROWS, C), BF), shape((2, C)), shape((1, C))],
        compiler_params=params("expand_forward"),
        cost_estimate=cost(1e9, 1e7),
        name="expand_forward",
    )(*in_vmem(pre_spatial), spatial_tot, spatial_gain, spatial_bias, expand_weight)
    expand_wide = core_sum(jnp.concatenate([expand_sum, excite_sum], axis=1))
    back, back_sum = stem_second(
        raw, centre, stem_cotangent, stem_tot, stem_gain, stem_bias, lanes, stem_count, expand_wide
    )
    expand_wide = ring_sum(ring_sum(expand_wide, "y"), "z")
    expand_tot, excite_tot = expand_wide[:, :C], expand_wide[:, C:]
    back_sum = ring_sum(back_sum[:2], "x")

    mine, other, direct, grad_comb, grad_gate, gate_sum = with_own(
        functools.partial(gate_kernel, count=count),
        own,
        (),
        [VMEM] * 12,
        [VMEM] * 6,
        [
            shape((ROWS, MID), BF), shape((ROWS, MID), BF), held((ROWS, 2 * MID), BF),
            held((ROWS, C), BF), held((ROWS, C), BF), shape((4, C)),
        ],
        [pltpu.VMEM((ROWS, C), BF)] * 2,
        (
            *in_vmem(pre_expand, pre_excite, feats, seeds), expand_tot, excite_tot, expand_mid, excite_mid,
            expand_gain, expand_bias, excite_gain, excite_bias,
        ),
        2e9,
        2e7,
        "gate",
    )
    gate_wide = sum_dp(
        jnp.concatenate([gate_sum, jnp.pad(back_sum, ((0, 2), (0, 0)))], axis=1)
    )
    gate_tot, back_tot = gate_wide[:, :C], gate_wide[:2, C:]
    back_tot = jnp.pad(back_tot, ((0, 6), (0, 0)))
    back_both = back_tot[0] + back_tot[1]
    stem_gain_grad, stem_bias_grad = back_both[64:], back_both[:64]

    got_result = from_peer(other, 1)

    expand_own, grad_spatial, spatial_back = with_own(
        functools.partial(expand_backward, count=count),
        own,
        (),
        [VMEM] * 11,
        [VMEM] * 3,
        [held((ROWS, 2 * MID), BF), held((ROWS, MID)), shape((2, MID))],
        [pltpu.VMEM((ROWS, C), BF), pltpu.VMEM((ROWS, MID), F32)],
        (
            *in_vmem(grad_comb, pre_expand), expand_tot, gate_tot, expand_gain, expand_mid, expand_weight,
            *in_vmem(pre_spatial), spatial_tot, spatial_gain, spatial_bias,
        ),
        1e9,
        1e7,
        "expand_backward",
    )

    excite_own, grad_reduced, motion_back, depth_part = with_own(
        functools.partial(excite_backward, count=count),
        own,
        (),
        [VMEM] * 10 + [SMEM] + [VMEM] * 2,
        [VMEM] * 4,
        [held((ROWS, 2 * MID), BF), held((ROWS, MID)), shape((2, MID)), shape((18, MID))],
        [pltpu.VMEM((ROWS, C), BF), pltpu.VMEM((ROWS, MID), F32)]
        + [pltpu.VMEM((ROWS + 128, 128), F32)] * 9,
        (
            *in_vmem(grad_gate, pre_excite), excite_tot, gate_tot, excite_gain, excite_mid, excite_weight,
            *in_vmem(pre_motion), motion_tot, motion_gain, keep, places, depth_weight,
        ),
        2e9,
        1e7,
        "excite_backward",
    )
    across = lambda left, right: dot(left, right, TN).astype(BF)
    sizes = [lax.axis_size(axis) for axis in ("z", "y", "c")]
    early = pl.pallas_call(
        functools.partial(early_weight_kernel, sizes=sizes),
        in_specs=[SMEM] + [VMEM] * 4,
        out_specs=VMEM,
        out_shape=shape((*sizes[::-1], 8 * (MID // clips), 256), BF),
        scratch_shapes=[pltpu.VMEM((MID, ROWS), BF)],
        compiler_params=params("early_weight"),
        cost_estimate=cost(1e9, 5e6),
        name="early_weight",
    )(own, *in_vmem(hidden_two, expand_own, mixed, excite_own))
    back_all = core_sum(jnp.concatenate([motion_back, spatial_back, depth_part], axis=0))
    stem_packed = stem_third(
        own, raw, centre, back, fine, coarse, stem_tot, back_tot, stem_gain, tables, stem_count,
        back_all,
    )
    back_all, early = tie(back_all, early)
    early = scatter_lead(early, "c")
    back_all = ring_sum(back_all, "y")
    back_all, early = tie(back_all, early)
    early = scatter_lead(early, "y")
    back_all = ring_sum(back_all, "z")
    stem_quarter = scatter_lead(stem_packed, "x", F32)
    motion_back_tot, spatial_back_tot = back_all[:2], back_all[2:4]

    taps, grad_reduce, reduce_back, motion_full, motion_own = with_own(
        functools.partial(spatial_backward, count=count),
        own,
        (1,),
        [
            whole(ROWS, MID), whole(ROWS, MID), whole(2, MID), whole(2, MID), whole(1, MID),
            whole(ROWS, 512), whole(9 * MID, MID), whole(ROWS, MID), whole(2, MID),
            whole(1, MID), whole(1, MID),
            whole(ROWS, MID), whole(ROWS, MID), whole(2, MID), whole(2, MID), whole(1, MID),
        ],
        [
            whole(ROWS, 9 * 256), whole(ROWS, MID), whole(2, MID), whole(ROWS, MID), whole(ROWS, 256),
        ],
        [
            held((ROWS, 9 * 256), BF), held((ROWS, MID)), shape((2, MID)),
            held((ROWS, MID), BF), shape((ROWS, 256), BF),
        ],
        [
            pltpu.VMEM((ROWS + 16, MID), F32),
            pltpu.VMEM((ROWS, MID), BF),
            pltpu.VMEM((ROWS, MID), F32),
        ],
        (
            *in_vmem(grad_spatial, pre_spatial), spatial_tot, spatial_back_tot, spatial_gain, places,
            spatial_weight, *in_vmem(pre_reduce), reduce_tot, reduce_gain, reduce_bias,
            *in_vmem(grad_reduced, pre_motion), motion_tot, motion_back_tot, motion_gain,
        ),
        2e9,
        1e7,
        "spatial_backward",
    )
    mine_rows = pl.BlockSpec((MID, MID), lambda step, own_ref: (own_ref[0], 0))
    other_rows = pl.BlockSpec((MID, MID), lambda step, own_ref: (own_ref[0] ^ 1, 0))
    middle = pl.pallas_call(
        functools.partial(spatial_weight_kernel, sizes=sizes),
        in_specs=[SMEM] + [VMEM] * 3,
        out_specs=VMEM,
        out_shape=shape((*sizes[::-1], (9 * MID + C) // clips, 256), BF),
        scratch_shapes=[pltpu.VMEM((MID, ROWS), BF)],
        compiler_params=params("spatial_weight"),
        cost_estimate=cost(1e9, 5e6),
        name="spatial_weight",
    )(own, *in_vmem(hidden_one, taps), across(feats, motion_own))

    reduce_back = core_sum(jnp.concatenate([reduce_back, stem_quarter], axis=0))
    reduce_back, middle, early, got_result = tie(reduce_back, middle, early, got_result)
    early = scatter_lead(early, "z")
    middle = scatter_lead(middle, "c")
    reduce_back = ring_sum(reduce_back, "y")
    reduce_back, middle, early = tie(reduce_back, middle, early)
    upward, downward = scatter_start(middle, "y")
    reduce_back = ring_sum(reduce_back, "z")
    reduce_back, upward, downward = tie(reduce_back, upward, downward)
    reduce_back_tot = reduce_back[:2]
    stem_quarter = reduce_back[2:]
    stem_high = stem_quarter.astype(BF)
    stem_low = (stem_quarter - stem_high.astype(F32)).astype(BF)
    halves = [part[:, left : left + 256] for part in (stem_high, stem_low) for left in (0, 256)]
    early = gather_x(jnp.concatenate([early, *halves], axis=0))
    got_gate = from_peer(gate_tot, 1)
    tail = jnp.concatenate([back_all[:4], reduce_back_tot, back_all[4:]], axis=0)
    got_tail = from_peer(tail, 1)
    middle = scatter_finish(middle, "y", upward, downward)

    reduce_own, mine_grad, other_grad = with_own(
        functools.partial(reduce_backward, count=count),
        own,
        (1,),
        [
            whole(ROWS, MID), whole(ROWS, MID), whole(2, MID), whole(2, MID), whole(1, MID),
            mine_rows, other_rows, whole(ROWS, MID), mine_rows, other_rows, whole(ROWS, 2 * MID),
        ],
        [whole(ROWS, 256), whole(ROWS, MID), whole(ROWS, MID)],
        [shape((ROWS, 256), BF), shape((ROWS, MID), BF), shape((ROWS, MID), BF)],
        [pltpu.VMEM((ROWS, MID), BF)],
        (
            *in_vmem(grad_reduce, pre_reduce), reduce_tot, reduce_back_tot, reduce_gain,
            reduce_weight, reduce_weight, *in_vmem(motion_full), motion_weight, motion_weight,
            *in_vmem(direct),
        ),
        5e8,
        8e6,
        "reduce_backward",
    )
    got_grad = from_peer(other_grad, 1)
    late = pl.pallas_call(
        functools.partial(late_weight_kernel, sizes=sizes),
        in_specs=[SMEM, VMEM],
        out_specs=VMEM,
        out_shape=shape((*sizes[::-1], C // clips, 256), BF),
        compiler_params=params("late_weight"),
        cost_estimate=cost(1e5, 2e6),
        name="late_weight",
    )(own, across(feats, reduce_own))
    late = scatter_lead(late, "c")
    late, middle, *early = tie(late, middle, *early)
    late = scatter_lead(late, "y")
    late, got_grad, got_gate, got_tail = tie(late, got_grad, got_gate, got_tail)
    rest = scatter_lead(jnp.concatenate([middle, late], axis=1), "z")
    rest = gather_x(rest)
    result = with_own(
        join_kernel,
        own,
        (1,),
        [whole(ROWS, MID), whole(ROWS, MID)],
        whole(2 * ROWS, MID),
        shape((2 * ROWS, MID), BF),
        [],
        (mine, got_result),
        1e5,
        2e6,
        "join_result",
    )

    (
        reduce_grad, spatial_grad, expand_grad, motion_grad, excite_grad,
        stem_weight_grad, stem_diff_grad, features_grad, depth_grad, *vectors,
    ) = with_own(
        functools.partial(unpack_kernel, clips=clips),
        own,
        (1,),
        [whole(*part.shape) for part in rest]
        + [whole(*part.shape) for part in early]
        + [
            whole(ROWS, MID), whole(ROWS, MID), whole(4, C), whole(4, C), whole(24, MID), whole(24, MID),
        ],
        [
            whole(C // clips, MID), whole(9 * MID // clips, MID), whole(MID // clips, C),
            whole(C // clips, MID), whole(MID // clips, C),
            whole(3, 7, 7, STEMC), whole(12, 7, 7, STEMC), whole(2 * ROWS, MID),
            whole(2, 3, 3, MID), *[whole(C)] * 4, *[whole(MID)] * 5,
        ],
        [
            shape((C // clips, MID)), shape((9 * MID // clips, MID)), shape((MID // clips, C)),
            shape((C // clips, MID)), shape((MID // clips, C)),
            shape((3, 7, 7, STEMC)), shape((12, 7, 7, STEMC)), shape((2 * ROWS, MID), BF),
            shape((2, 3, 3, MID)), *[shape((C,))] * 4, *[shape((MID,))] * 5,
        ],
        [pltpu.VMEM((512, 128), F32)],
        (*rest, *early, mine_grad, got_grad, gate_tot, got_gate, tail, got_tail),
        1e6,
        6e6,
        "unpack",
    )
    stem_weight_grad = stem_weight_grad.transpose(3, 0, 1, 2)
    stem_diff_grad = stem_diff_grad.transpose(3, 0, 1, 2)

    return (
        result,
        features_grad,
        stem_weight_grad,
        stem_diff_grad,
        stem_gain_grad,
        stem_bias_grad,
        reduce_grad,
        vectors[8],
        vectors[7],
        spatial_grad,
        vectors[6],
        vectors[5],
        expand_grad,
        vectors[1],
        vectors[0],
        motion_grad,
        vectors[4],
        depth_grad,
        excite_grad,
        vectors[3],
        vectors[2],
    )


def solution(mesh):
    grid = Mesh(mesh.devices.reshape(4, 4, 2, 4), ("z", "y", "c", "x"))
    clips = ("z", "y", "c")
    everyone = ("z", "y", "c", "x")
    split = P(clips, None)
    copied = P()
    return jax.shard_map(
        on_device,
        mesh=grid,
        in_specs=(split,) * 4
        + (P(everyone, None, None, None, None), P(everyone, None, None, None))
        + (copied,) * 19,
        out_specs=(P(clips, "x"), P(clips, "x"))
        + (copied,) * 4
        + (split, copied, copied) * 3
        + (split, copied, copied)
        + (split, copied, copied),
        check_vma=False,
    )
```

```python
import functools

import jax
import jax.numpy as jnp
import numpy as np
from jax import lax
from jax.experimental import pallas as pl
from jax.experimental.pallas import tpu as pltpu
from jax.sharding import Mesh
from jax.sharding import PartitionSpec as P

C = 2048
MID = 512
STEMC = 64
SIDE = 224
FEAT = 7
SEG = 8
MICRO = 2
ROWS = SEG * FEAT * FEAT
EPS = 1e-05
BF = jnp.bfloat16
F32 = jnp.float32
HIGH = lax.Precision.HIGHEST
NN = (((1,), (0,)), ((), ()))
NT = (((1,), (1,)), ((), ()))
TN = (((0,), (0,)), ((), ()))
GROUPS = 7
TILE = 512
VMEM = pl.BlockSpec(memory_space=pltpu.VMEM)
SMEM = pl.BlockSpec(memory_space=pltpu.SMEM)
PIECES = [slice(top, min(top + 16, ROWS)) for top in range(0, ROWS, 16)]
EIGHTS = [slice(top, top + 8) for top in range(0, ROWS, 8)]


def sigmoid(values):
    return 0.5 + 0.5 * jnp.tanh(0.5 * values)


def dot(left, right, dims=NN, precision=None):
    return lax.dot_general(left, right, dims, precision=precision, preferred_element_type=F32)


LIMITS = {"stem_spread": 20, "first_matmuls": 14, "spatial_backward": 14, "unpack": 14}


def params(name):
    return pltpu.CompilerParams(vmem_limit_bytes=LIMITS.get(name, 10) * 2**20)


def held(dims, dtype=F32):
    return pltpu.VMEM(dims, dtype)


def in_vmem(*values):
    return [pltpu.with_memory_space_constraint(value, pltpu.VMEM) for value in values]


def cost(flops, nbytes):
    return pl.CostEstimate(flops=int(flops), bytes_accessed=int(nbytes), transcendentals=0)


def shape(dims, dtype=F32):
    return jax.ShapeDtypeStruct(dims, dtype)


def ring_sum(values, axis):
    size = lax.axis_size(axis)
    if size == 1:
        return values
    got = [
        lax.ppermute(values, axis, [(i, (i + step) % size) for i in range(size)])
        for step in range(1, size)
    ]
    if size == 2:
        return values + got[0]
    return (values + got[1]) + (got[0] + got[2])


def core_sum(values):
    pair = lax.all_gather(values, "c")
    return pair[0] + pair[1]


def sum_dp(values):
    return ring_sum(ring_sum(core_sum(values), "y"), "z")


def shift_by(values, axis, step):
    size = lax.axis_size(axis)
    return lax.ppermute(values, axis, [(i, (i + step) % size) for i in range(size)])


def scatter_lead(blocks, axis, kind=BF):
    total = blocks[0].astype(F32)
    for step in range(1, blocks.shape[0]):
        total = total + shift_by(blocks[step], axis, step).astype(F32)
    return total.astype(kind)


def scatter_start(blocks, axis):
    half = blocks.shape[1] // 2
    return shift_by(blocks[2, :half], axis, 1), shift_by(blocks[2, half:], axis, -1)


def scatter_finish(blocks, axis, upward, downward):
    half = blocks.shape[1] // 2
    up, down = blocks[1].astype(F32), blocks[3].astype(F32)
    up = jnp.concatenate([up[:half] + upward.astype(F32), up[half:]], axis=0).astype(BF)
    down = jnp.concatenate([down[:half], down[half:] + downward.astype(F32)], axis=0).astype(BF)
    up, down = shift_by(up, axis, 1), shift_by(down, axis, -1)
    return (blocks[0].astype(F32) + up.astype(F32) + down.astype(F32)).astype(BF)


def tie(*values):
    return lax.optimization_barrier(values)


def from_peer(values, flip):
    size = lax.axis_size("x")
    return lax.ppermute(values, "x", [(i, i ^ flip) for i in range(size)])


def gather_x(block):
    return [block] + [from_peer(block, flip) for flip in (1, 2, 3)]


def stem_tables():
    half, quarter = SIDE // 2, SIDE // 4
    pool = np.zeros((SIDE, 128), np.float32)
    for column in range(SIDE):
        pool[column, column // 2] = 0.25
    fine = np.zeros((2, SIDE, 9 * 128), np.float32)
    coarse = np.zeros((2 * 128, 7 * 128), np.float32)
    for seg in range(2):
        for spot in range(quarter):
            for tap in range(9):
                column = 4 * spot + tap - 3
                if 0 <= column < SIDE:
                    fine[seg, column, tap * 128 + seg * 64 + spot] = 1
            for tap in range(7):
                column = 2 * spot + tap - 3
                if 0 <= column < half:
                    coarse[seg * 128 + column, tap * 128 + seg * 64 + spot] = 1
    sel_fine = np.zeros((8, 168, 432), np.float32)
    for up in range(2):
        for row in range(2):
            for col in range(2):
                for chan in range(3):
                    for dy in range(7):
                        for dx in range(7):
                            sel_fine[
                                up * 4 + row * 2 + col,
                                chan * 56 + dy * 8 + dx,
                                chan * 144 + (2 * col + dx) * 16 + 4 * up + 2 * row + dy,
                            ] = 1
    sel_coarse = np.zeros((4, 56, 128), np.float32)
    for up in range(4):
        for dy in range(7):
            for dx in range(7):
                sel_coarse[up, dy * 8 + dx, dx * 16 + 2 * up + dy] = 1
    lanes = np.zeros((8, 128), np.float32)
    lanes[0, :64] = 1
    lanes[1, 64:] = 1
    usable = np.zeros((8, 128), np.float32)
    usable[0, :56] = 1
    usable[1, 64:120] = 1
    return [
        jnp.asarray(table, dtype)
        for table, dtype in (
            (pool, BF),
            (fine, BF),
            (coarse, BF),
            (sel_fine, BF),
            (sel_coarse, BF),
            (lanes, F32),
            (usable, F32),
        )
    ]


def fine_patches(tall):
    parts = []
    for pair in range(4):
        rows = slice(8 * pair, 8 * pair + 16)
        parts.append(
            jnp.concatenate(
                [
                    tall[chan][rows, tap * 128 : (tap + 1) * 128]
                    for chan in range(3)
                    for tap in range(9)
                ],
                axis=0,
            ).astype(BF)
        )
    return jnp.concatenate(parts, axis=1)


def coarse_patches(tall):
    blank = jnp.zeros((16, 128), F32)
    parts = [[], []]
    for chan in range(12):
        for quad in range(2):
            rows = slice(8 * quad, 8 * quad + 16)
            for tap in range(7):
                parts[quad].append(tall[chan][rows, tap * 128 : (tap + 1) * 128])
            parts[quad].append(blank)
    return jnp.concatenate(
        [jnp.concatenate(pieces, axis=0).astype(BF) for pieces in parts], axis=1
    )


def stem_spread(
    frames, weight, diff_weight, pool, fine_tab, coarse_tab, sel_fine, sel_coarse, after,
    fine_out, coarse_out, wide_fine, wide_coarse,
    planes_ref, pooled_ref, moved_ref, flat_ref,
):
    pooled_ref[...] = jnp.zeros_like(pooled_ref)
    moved_ref[...] = jnp.zeros_like(moved_ref)
    for seg in range(2):
        planes_ref[...] = dot(frames[seg], pool[...])
        for chan in range(3):
            lines = []
            for k in range(5):
                at = (k * 3 + chan) * SIDE
                lines.append(
                    planes_ref[pl.ds(at, SIDE // 2, 2), :]
                    + planes_ref[pl.ds(at + 1, SIDE // 2, 2), :]
                )
            for k in range(4):
                at = (k * 3 + chan) * 128 + 3
                pooled_ref[at : at + 112, seg * 128 : (seg + 1) * 128] = lines[k + 1] - lines[k]
            at = (6 + chan) * SIDE
            moved_ref[seg, chan * 256 + 3 : chan * 256 + 227, :] = frames[
                seg, at : at + SIDE, :
            ].astype(F32)
    small = pooled_ref[...].astype(BF)
    for left in range(0, 896, 256):
        right = min(left + 256, 896)
        coarse_out[:, :, left:right] = (
            dot(small, coarse_tab[:, left:right]).astype(BF).reshape(12, 128, right - left)
        )
    first, second = moved_ref[0].astype(BF), moved_ref[1].astype(BF)
    for left in range(0, 1152, 256):
        right = min(left + 256, 1152)
        value = dot(first, fine_tab[0, :, left:right]) + dot(second, fine_tab[1, :, left:right])
        fine_out[:, :, left:right] = value.astype(BF).reshape(3, 256, right - left)

    flat_ref[...] = jnp.zeros_like(flat_ref)
    for chan in range(3):
        for row in range(7):
            at = chan * 56 + row * 8
            flat_ref[at : at + 7, :] = weight[chan, row].astype(F32)
    for chan in range(12):
        for row in range(7):
            at = 168 + chan * 56 + row * 8
            flat_ref[at : at + 7, :] = diff_weight[chan, row].astype(F32)
    narrow = jnp.transpose(flat_ref[0:168, :]).astype(BF)
    for block in range(8):
        wide_fine[block * 64 : (block + 1) * 64, :] = dot(narrow, sel_fine[block]).astype(BF)
    tall = jnp.concatenate(
        [jnp.transpose(flat_ref[168 + chan * 56 : 224 + chan * 56, :]) for chan in range(12)], axis=0
    ).astype(BF)
    for up in range(4):
        spread = dot(tall, sel_coarse[up]).astype(BF)
        for chan in range(12):
            wide_coarse[up * 64 : (up + 1) * 64, chan * 128 : (chan + 1) * 128] = spread[
                chan * 64 : (chan + 1) * 64
            ]


def fine_rows(fine, group):
    start = pl.multiple_of(32 * group, 16)
    return [fine[chan, pl.ds(start, 48), :].astype(F32) for chan in range(3)]


def coarse_rows(coarse, group):
    start = pl.multiple_of(16 * group, 16)
    return [coarse[chan, pl.ds(start, 32), :].astype(F32) for chan in range(12)]


def stem_forward(
    fine, coarse, wide_fine, wide_coarse, lanes, usable, after,
    raw_out, sums_out, centre_out, acc_ref,
):
    acc_ref[...] = jnp.zeros_like(acc_ref)

    @pl.loop(0, GROUPS)
    def group(step):
        fine_sum = dot(
            wide_fine[...], fine_patches(fine_rows(fine, step))
        )
        coarse_sum = dot(
            wide_coarse[...],
            coarse_patches(coarse_rows(coarse, step)),
        )

        def value_at(pair, up, spot, top):
            row = (up * 4 + spot) * 64 + top
            lift = (2 * (pair % 2) + up) * 64 + top
            left = (pair // 2) * 128
            return (
                fine_sum[row : row + 16, pair * 128 : (pair + 1) * 128]
                + coarse_sum[lift : lift + 16, left : left + 128]
            )

        @pl.when(step == 0)
        def find_centre():
            for top in range(0, 64, 16):
                total = jnp.zeros((16, 128), F32)
                for pair in range(4):
                    for up in range(2):
                        for spot in range(4):
                            total = total + value_at(pair, up, spot, top)
                centre_out[top : top + 16, :] = total
            spread = dot(usable[...], usable[...], TN) * (1.0 / (32 * 56))
            centre_out[...] = dot(centre_out[...], spread)

        for top in range(0, 64, 16):
            centre = centre_out[top : top + 16, :]
            plain = acc_ref[top : top + 16, :]
            square = acc_ref[64 + top : 80 + top, :]
            for pair in range(4):
                for up in range(2):
                    for spot in range(4):
                        value = value_at(pair, up, spot, top)
                        row = (up * 4 + spot) * 64 + top
                        raw_out[step, row : row + 16, pair * 128 : (pair + 1) * 128] = (value - centre).astype(BF)
                        plain = plain + value
                        square = square + value * value
            acc_ref[top : top + 16, :] = plain
            acc_ref[64 + top : 80 + top, :] = square

    sums_out[...] = dot(lanes[...], acc_ref[...], NT, HIGH)


def dot_exact(select, values):
    total = None
    for _ in range(3):
        part = values.astype(BF)
        values = values - part.astype(F32)
        term = dot(select, part, NT)
        total = term if total is None else total + term
    return total


def over_lanes(vector):
    return dot(vector, jnp.ones((1, 128), F32), TN, HIGH)


def stem_scales(totals, lanes, count):
    spread = dot(totals, lanes, TN, HIGH) * (1.0 / count)
    return spread[0:64, :], spread[64:128, :]


def stem_middle(
    raw, cotangent, totals, gain, bias, lanes, centre, after, back_out, sums_out,
    seed_ref, coef_ref, scale_ref, acc_ref, *, count
):
    average, square = stem_scales(totals[...], lanes[...], count)
    scale = lax.rsqrt(square - average * average + EPS)
    scale_ref[...] = scale
    coef_ref[0] = average - centre[...]
    coef_ref[1] = scale * over_lanes(gain[...])
    coef_ref[2] = over_lanes(bias[...]) - coef_ref[0] * coef_ref[1]
    acc_ref[...] = jnp.zeros_like(acc_ref)

    @pl.loop(0, GROUPS)
    def group(step):
        blank = jnp.zeros((8, 64), F32)
        for spot in range(8):
            line = 8 * step + spot
            tall = jnp.concatenate(
                [cotangent[0, line].astype(F32), blank, cotangent[1, line].astype(F32), blank], axis=0
            )
            seed_ref[spot] = jnp.transpose(tall) * 0.25
        for top in range(0, 64, 16):
            chans = slice(top, top + 16)
            average, slope, shift = coef_ref[0, chans], coef_ref[1, chans], coef_ref[2, chans]
            plain, cross = acc_ref[0, chans], acc_ref[1, chans]
            for pair in range(4):
                cols = slice(pair * 128, (pair + 1) * 128)
                for up in range(2):
                    seed = seed_ref[2 * pair + up, chans]
                    for spot in range(4):
                        row = (up * 4 + spot) * 64 + top
                        value = raw[step, row : row + 16, cols].astype(F32)
                        act = value * slope + shift
                        sigma = sigmoid(act)
                        grad = seed * (sigma * (1.0 + act * (1.0 - sigma)))
                        back_out[step, row : row + 16, cols] = grad.astype(BF)
                        plain = plain + grad
                        cross = cross + grad * (value - average)
            acc_ref[0, chans] = plain
            acc_ref[1, chans] = cross

    acc_ref[1] = acc_ref[1] * scale_ref[...]
    sums_out[...] = dot(lanes[...], acc_ref[...].reshape(128, 128), NT, HIGH)


def stem_backward(
    place, raw, back, fine, coarse, totals, back_totals, gain, sel_fine, sel_coarse, lanes, centre, after,
    packed_out,
    coef_ref, packed, draw_ref, small_ref, fine_acc, coarse_acc, *, count
):
    average, square = stem_scales(totals[...], lanes[...], count)
    scale = lax.rsqrt(square - average * average + EPS)
    first, second = stem_scales(back_totals[...], lanes[...], count)
    slope = over_lanes(gain[...]) * scale
    coef_ref[0] = slope
    coef_ref[1] = -slope * scale * second
    coef_ref[2] = slope * ((average - centre[...]) * scale * second - first)
    fine_acc[...] = jnp.zeros_like(fine_acc)
    coarse_acc[...] = jnp.zeros_like(coarse_acc)

    @pl.loop(0, GROUPS)
    def group(step):
        for top in range(0, 64, 16):
            on_back, on_raw, constant = (coef_ref[k, top : top + 16] for k in range(3))
            for pair in range(4):
                cols = slice(pair * 128, (pair + 1) * 128)
                for up in range(2):
                    summed = None
                    for spot in range(4):
                        row = (up * 4 + spot) * 64 + top
                        draw = (
                            back[step, row : row + 16, cols].astype(F32) * on_back
                            + raw[step, row : row + 16, cols].astype(F32) * on_raw
                            + constant
                        ).astype(BF)
                        draw_ref[row : row + 16, cols] = draw
                        wide = draw.astype(F32)
                        summed = wide if summed is None else summed + wide
                    lift = (2 * (pair % 2) + up) * 64 + top
                    left = (pair // 2) * 128
                    small_ref[lift : lift + 16, left : left + 128] = summed.astype(BF)
        patches = fine_patches(fine_rows(fine, step))
        fine_acc[...] += dot(draw_ref[...], patches, NT)
        patches = coarse_patches(coarse_rows(coarse, step))
        coarse_acc[...] += dot(small_ref[...], patches, NT)

    total = jnp.zeros((168, 64), F32)
    for block in range(8):
        total = total + dot_exact(sel_fine[block], fine_acc[block * 64 : (block + 1) * 64, :])
    packed[0:168, 0:64] = total
    packed[0:168, 64:128] = jnp.zeros((168, 64), F32)
    for duo in range(6):
        piece = jnp.zeros((56, 128), F32)
        for up in range(4):
            stacked = jnp.concatenate(
                [
                    coarse_acc[up * 64 : (up + 1) * 64, chan * 128 : (chan + 1) * 128]
                    for chan in (2 * duo, 2 * duo + 1)
                ],
                axis=0,
            )
            piece = piece + dot_exact(sel_coarse[up], stacked)
        packed[168 + duo * 56 : 224 + duo * 56, :] = piece
    packed[504:512, :] = jnp.zeros((8, 128), F32)
    for quarter in range(4):
        for block in range(4):
            top = quarter * 128 + block * 32
            packed_out[lax.rem(quarter + 4 - place[0], 4), :, block * 128 : (block + 1) * 128] = packed[top : top + 32, :]


def whole(*dims):
    return pl.BlockSpec(
        dims, lambda step, *rest: (0,) * len(dims), pipeline_mode=pl.Buffered(1)
    )


def stem_planes(frames, stem_weight, stem_diff_weight, tables, after):
    pool, fine_tab, coarse_tab, sel_fine, sel_coarse, lanes, usable = tables
    return pl.pallas_call(
        stem_spread,
        in_specs=[VMEM] * 9,
        out_specs=[VMEM] * 4,
        out_shape=[
            held((3, 256, 1152), BF),
            held((12, 128, 896), BF),
            held((512, 432), BF),
            held((256, 1536), BF),
        ],
        scratch_shapes=[
            pltpu.VMEM((15 * SIDE, 128), F32),
            pltpu.VMEM((12 * 128, 256), F32),
            pltpu.VMEM((2, 768, SIDE), F32),
            pltpu.VMEM((168 + 672, STEMC), F32),
        ],
        compiler_params=params("stem_spread"),
        cost_estimate=cost(4e9, 1e7),
        name="stem_spread",
    )(
        frames.reshape(2, 15 * SIDE, SIDE),
        stem_weight.transpose(1, 2, 3, 0),
        stem_diff_weight.transpose(1, 2, 3, 0),
        pool, fine_tab, coarse_tab, sel_fine, sel_coarse, after,
    )


def stem_first(fine, coarse, wide_fine, wide_coarse, tables, after):
    lanes, usable = tables[5:]
    return pl.pallas_call(
        stem_forward,
        in_specs=[VMEM] * 7,
        out_specs=[VMEM] * 3,
        out_shape=[held((GROUPS, 512, 512), BF), shape((8, 128)), shape((STEMC, 128))],
        scratch_shapes=[pltpu.VMEM((128, 128), F32)],
        compiler_params=params("stem_forward"),
        cost_estimate=cost(4e9, 1e7),
        name="stem_forward",
    )(*in_vmem(fine, coarse, wide_fine, wide_coarse), lanes, usable, after)


def stem_second(raw, centre, stem_cotangent, totals, stem_gain, stem_bias, lanes, count, after):
    gain = stem_gain.reshape(1, STEMC)
    bias = stem_bias.reshape(1, STEMC)
    cot = stem_cotangent.transpose(0, 2, 3, 1)
    return pl.pallas_call(
        functools.partial(stem_middle, count=count),
        in_specs=[VMEM] * 8,
        out_specs=[VMEM] * 2,
        out_shape=[pltpu.VMEM((GROUPS, 512, 512), BF), shape((8, 128))],
        scratch_shapes=[
            pltpu.VMEM((8, 64, 128), F32),
            pltpu.VMEM((3, 64, 128), F32),
            pltpu.VMEM((64, 128), F32),
            pltpu.VMEM((2, 64, 128), F32),
        ],
        compiler_params=params("stem_middle"),
        cost_estimate=cost(8e9, 1.5e7),
        name="stem_middle",
    )(*in_vmem(raw), cot, totals, gain, bias, lanes, centre, after)


def stem_third(
    place, raw, centre, back, fine, coarse, totals, back_totals, stem_gain, tables, count, after
):
    pool, fine_tab, coarse_tab, sel_fine, sel_coarse, lanes, usable = tables
    gain = stem_gain.reshape(1, STEMC)
    return pl.pallas_call(
        functools.partial(stem_backward, count=count),
        in_specs=[SMEM] + [VMEM] * 12,
        out_specs=VMEM,
        out_shape=shape((4, 32, 512)),
        scratch_shapes=[
            pltpu.VMEM((3, 64, 128), F32),
            pltpu.VMEM((512, 128), F32),
            pltpu.VMEM((512, 512), BF),
            pltpu.VMEM((256, 256), BF),
            pltpu.VMEM((512, 432), F32),
            pltpu.VMEM((256, 1536), F32),
        ],
        compiler_params=params("stem_backward"),
        cost_estimate=cost(8e9, 2.5e7),
        name="stem_backward",
    )(place, *in_vmem(raw, back, fine, coarse), totals, back_totals, gain, sel_fine, sel_coarse, lanes, centre, after)


def put_moments(out_ref, values):
    out_ref[0:1, :] = jnp.sum(values, axis=0, keepdims=True)
    out_ref[1:2, :] = jnp.sum(values * values, axis=0, keepdims=True)


def moments(totals, count):
    average = totals[0:1] * (1.0 / count)
    square = totals[1:2] * (1.0 / count)
    return average, lax.rsqrt(square - average * average + EPS)


def affine_of(totals, count, gain, bias):
    average, scale = moments(totals, count)
    slope = gain * scale
    return slope, bias - average * slope


def back_affine(totals, sums, count, gain, middle=0.0):
    average, scale = moments(totals, count)
    first = sums[0:1] * (1.0 / count)
    second = sums[1:2] * (1.0 / count)
    on_grad = gain * scale
    on_value = -on_grad * scale * second
    return on_grad, on_value, -on_grad * first - on_value * (average - middle)


def each_piece(width, pieces):
    for left in range(0, width, 128):
        for rows in pieces:
            yield rows, slice(left, left + 128)


def lane_tile(tile, width=128):
    return pl.ds(pl.multiple_of(tile * width, width), width)


def put_wide_back(out_ref, grad, value, totals, sums, first, gain, middle, count):
    @pl.loop(0, C // 128)
    def one(tile):
        cols = lane_tile(tile)
        on_grad, on_value, constant = back_affine(
            totals[:, cols], sums[first : first + 2, cols], count, gain[:, cols], middle[:, cols]
        )
        for rows in PIECES:
            out_ref[rows, cols] = (
                grad[rows, cols].astype(F32) * on_grad + value[rows, cols].astype(F32) * on_value + constant
            ).astype(BF)


def put_back(out_ref, grad, value, coefs):
    on_grad, on_value, constant = coefs
    for rows, cols in each_piece(out_ref.shape[1], PIECES):
        out_ref[rows, cols] = (
            grad[rows, cols].astype(F32) * on_grad[:, cols]
            + value[rows, cols].astype(F32) * on_value[:, cols]
            + constant[:, cols]
        ).astype(BF)


def put_activation_back(out_ref, sums_out, grad, value, totals, gain, bias, count):
    average, scale = moments(totals, count)
    slope = gain * scale
    shift = bias - average * slope
    for left in range(0, MID, 128):
        cols = slice(left, left + 128)
        plain = jnp.zeros((8, 128), F32)
        cross = jnp.zeros((8, 128), F32)
        for rows in EIGHTS:
            pre = value[rows, cols]
            act = pre * slope[:, cols] + shift[:, cols]
            sigma = sigmoid(act)
            hidden = grad[rows, cols].astype(BF).astype(F32)
            back = hidden * (sigma * (1.0 + act * (1.0 - sigma)))
            out_ref[rows, cols] = back
            plain = plain + back
            cross = cross + back * (pre - average[:, cols])
        sums_out[0:1, cols] = jnp.sum(plain, axis=0, keepdims=True)
        sums_out[1:2, cols] = jnp.sum(cross, axis=0, keepdims=True) * scale[:, cols]


def first_matmuls(place, features, reduce_w, motion_w, reduce_out, motion_out, reduce_sum, motion_sum):
    value = dot(features[...], reduce_w[...])
    reduce_out[...] = value
    put_moments(reduce_sum, value)
    value = dot(features[...], motion_w[...])
    motion_out[...] = value
    put_moments(motion_sum, value)


def tap_mask(places, row_off, col_off):
    kept = None
    for off, base in ((row_off, 0), (col_off, 256)):
        if off:
            at = base + (128 if off > 0 else 0)
            good = places[:, at : at + 128]
            kept = good if kept is None else kept * good
    return kept


def tap_source(buffer, places, row_off, col_off, sign):
    move = sign * (7 * row_off + col_off)
    mask = tap_mask(places, sign * row_off, sign * col_off)
    value = buffer[8 + move : 8 + move + ROWS, :]
    if mask is not None:
        value = value * jnp.concatenate([mask] * (value.shape[1] // 128), axis=1)
    return value


def clear_ends(buffer):
    blank = jnp.zeros((8, buffer.shape[1]), F32)
    buffer[0:8, :] = blank
    buffer[8 + ROWS : 16 + ROWS, :] = blank


def spatial_forward(
    pre_reduce, totals, gain, bias, places, weight, hidden_out, pre_out, sums_out, buffer, *, count
):
    clear_ends(buffer)
    slope, shift = affine_of(totals[...], count, gain[...], bias[...])
    for rows, cols in each_piece(MID, PIECES):
        value = pre_reduce[rows, cols] * slope[:, cols] + shift[:, cols]
        hidden = (value * sigmoid(value)).astype(BF)
        hidden_out[rows, cols] = hidden
        buffer[8 + rows.start : 8 + rows.stop, cols] = hidden.astype(F32)
    for tap in range(9):
        row_off, col_off = tap // 3 - 1, tap % 3 - 1
        source = tap_source(buffer, places, row_off, col_off, 1).astype(BF)
        value = dot(source, weight[tap * MID : (tap + 1) * MID, :])
        if tap == 0:
            pre_out[...] = value
        else:
            pre_out[...] += value
    put_moments(sums_out, pre_out[...])


def wide_product(hidden, weight, pre_out, sums_out, mid_out):
    @pl.loop(0, C // TILE)
    def one(tile):
        cols = lane_tile(tile, TILE)
        value = dot(hidden[...], weight[:, cols])
        total = jnp.sum(value, axis=0, keepdims=True)
        sums_out[0:1, cols] = total
        sums_out[1:2, cols] = jnp.sum(value * value, axis=0, keepdims=True)
        middle = total * (1.0 / ROWS)
        mid_out[:, cols] = middle
        pre_out[:, cols] = (value - middle).astype(BF)


def expand_forward(
    pre_spatial, totals, gain, bias, weight, hidden_out, pre_out, sums_out, mid_out, *, count
):
    slope, shift = affine_of(totals[...], count, gain[...], bias[...])
    for rows, cols in each_piece(MID, PIECES):
        value = pre_spatial[rows, cols] * slope[:, cols] + shift[:, cols]
        hidden_out[rows, cols] = (value * sigmoid(value)).astype(BF)
    wide_product(hidden_out, weight, pre_out, sums_out, mid_out)


def at(buffer, rows, move=0):
    return buffer[64 + rows.start + move : 64 + rows.stop + move, :]


def put(buffer, rows, value):
    buffer[64 + rows.start : 64 + rows.stop, :] = value


def clear_margins(buffers):
    for buffer in buffers:
        buffer[0:64, :] = jnp.zeros((64, 128), F32)
        buffer[64 + ROWS : 128 + ROWS, :] = jnp.zeros((64, 128), F32)


def mask_of(places, rows, which):
    return places[rows, which * 128 : (which + 1) * 128]


UP, DOWN, LEFT, RIGHT = range(4)


def three(buffer, places, rows, move, before, after):
    return (
        at(buffer, rows, -move) * mask_of(places, rows, before),
        at(buffer, rows),
        at(buffer, rows, move) * mask_of(places, rows, after),
    )


def box_rows(buffer, places, out):
    for rows in EIGHTS:
        first, second, third = three(buffer, places, rows, 1, LEFT, RIGHT)
        put(out, rows, first + second + third)


def box_columns(buffer, places, rows):
    first, second, third = three(buffer, places, rows, 7, UP, DOWN)
    return (first + second + third) * (1.0 / 9.0)


def kept(value, rows, keep):
    first, last = rows.start // 49, (rows.stop - 1) // 49
    if first == last:
        return value * keep[0, first]
    lines = lax.broadcasted_iota(jnp.int32, value.shape, 0)
    return value * jnp.where(lines < last * 49 - rows.start, keep[0, first], keep[0, last])


def change_and_average(pre_motion, slope, keep, places, cols, spare, change, average):
    for rows in EIGHTS:
        put(spare, rows, pre_motion[rows, cols] * slope)
    for rows in EIGHTS:
        put(change, rows, kept(at(spare, rows, 49) - at(spare, rows), rows, keep))
    box_rows(change, places, spare)
    for rows in EIGHTS:
        put(average, rows, box_columns(spare, places, rows))


def motion_forward(
    pre_motion, totals, gain, keep, places, depth, weight, after, mixed_out, pre_out, sums_out, mid_out,
    spare, change, average, lines_a, lines_b, lines_c, *, count
):
    clear_margins((spare, change, average, lines_a, lines_b, lines_c))

    @pl.loop(0, MID // 128)
    def one(tile):
        cols = pl.ds(pl.multiple_of(tile * 128, 128), 128)
        scale = moments(totals[:, cols], count)[1]
        change_and_average(
            pre_motion, gain[:, cols] * scale, keep, places, cols, spare, change, average
        )
        for rows in EIGHTS:
            near = three(change, places, rows, 1, LEFT, RIGHT)
            wide = three(average, places, rows, 1, LEFT, RIGHT)
            for row, out in enumerate((lines_a, lines_b, lines_c)):
                line = None
                for col in range(3):
                    for scale_at, source in enumerate((near, wide)):
                        term = source[col] * depth[scale_at, row, col : col + 1, cols]
                        line = term if line is None else line + term
                put(out, rows, line)
        for rows in PIECES:
            value = (
                at(lines_b, rows)
                + at(lines_a, rows, -7) * mask_of(places, rows, UP)
                + at(lines_c, rows, 7) * mask_of(places, rows, DOWN)
            )
            mixed_out[rows, cols] = value.astype(BF)

    wide_product(mixed_out, weight, pre_out, sums_out, mid_out)


def gate_kernel(
    own, pre_expand, pre_excite, features, cotangent, expand_tot, excite_tot, expand_mid, excite_mid,
    expand_gain, expand_bias, excite_gain, excite_bias,
    mine_out, other_out, direct_out, comb_out, gate_out, sums_out, output_ref, direct_ref, *, count
):
    @pl.loop(0, C // 128)
    def one(tile):
        cols = lane_tile(tile)
        e_mean, e_scale = moments(expand_tot[:, cols], count)
        x_mean, x_scale = moments(excite_tot[:, cols], count)
        e_mean = e_mean - expand_mid[:, cols]
        x_mean = x_mean - excite_mid[:, cols]
        e_slope = expand_gain[:, cols] * e_scale
        e_shift = expand_bias[:, cols] - e_mean * e_slope
        x_slope = excite_gain[:, cols] * x_scale
        x_shift = excite_bias[:, cols] - x_mean * x_slope
        sums = [jnp.zeros((8, 128), F32)] * 4
        for rows in PIECES:
            feats = features[rows, cols].astype(F32)
            seed = cotangent[rows, cols].astype(F32)
            pre_e = pre_expand[rows, cols].astype(F32)
            pre_x = pre_excite[rows, cols].astype(F32)
            branch = (pre_e * e_slope + e_shift).astype(BF).astype(F32)
            gate = sigmoid(pre_x * x_slope + x_shift)
            lifted = feats * gate
            combined = branch + lifted
            sigma = sigmoid(combined)
            output = combined * sigma
            output_ref[rows, cols] = output.astype(BF)
            grad = seed * (sigma + output * (1.0 - sigma))
            direct_ref[rows, cols] = (grad * gate).astype(BF)
            rounded = grad.astype(BF)
            comb_out[rows, cols] = rounded
            rounded = rounded.astype(F32)
            grad_gate = grad * lifted * (1.0 - gate)
            gate_out[rows, cols] = grad_gate.astype(BF)
            terms = (
                rounded,
                rounded * (pre_e - e_mean),
                grad_gate,
                grad_gate * (pre_x - x_mean),
            )
            for spot, value in enumerate(terms):
                for up in range(0, value.shape[0], 8):
                    sums[spot] = sums[spot] + value[up : up + 8]
        finals = [jnp.sum(value, axis=0, keepdims=True) for value in sums]
        sums_out[0:1, cols] = finals[0]
        sums_out[1:2, cols] = finals[1] * e_scale
        sums_out[2:3, cols] = finals[2]
        sums_out[3:4, cols] = finals[3] * x_scale

    mine, other = lane_tile(own[0], MID), lane_tile(own[0] ^ 1, MID)
    mine_out[...] = output_ref[:, mine]
    other_out[...] = output_ref[:, other]
    direct_out[:, :MID] = direct_ref[:, mine]
    direct_out[:, MID:] = direct_ref[:, other]


def expand_backward(
    own, grad, pre_expand, totals, sums, gain, middle, weight, pre_spatial, s_totals, s_gain, s_bias,
    own_out, grad_out, sums_out, value_ref, acc, *, count
):
    put_wide_back(value_ref, grad, pre_expand, totals, sums, 0, gain, middle, count)
    own_out[:, :MID] = value_ref[:, lane_tile(own[0], MID)]
    own_out[:, MID:] = value_ref[:, lane_tile(own[0] ^ 1, MID)]
    acc[...] = dot(value_ref[...], weight[...], NT)
    put_activation_back(
        grad_out, sums_out, acc, pre_spatial, s_totals[...], s_gain[...], s_bias[...], count
    )


def excite_backward(
    own, grad, pre_excite, totals, sums, gain, middle, weight, pre_motion, m_totals, m_gain, keep,
    places, depth, own_out, grad_out, sums_out, depth_out, value_ref, acc,
    spare, change, average, seed, pull_a, pull_b, pull_c, near_out, wide_out, *, count
):
    put_wide_back(value_ref, grad, pre_excite, totals, sums, 2, gain, middle, count)
    own_out[:, :MID] = value_ref[:, lane_tile(own[0], MID)]
    own_out[:, MID:] = value_ref[:, lane_tile(own[0] ^ 1, MID)]
    acc[...] = dot(value_ref[...], weight[...], NT)
    clear_margins((spare, change, average, seed, pull_a, pull_b, pull_c, near_out, wide_out))

    @pl.loop(0, MID // 128)
    def one(tile):
        cols = pl.ds(pl.multiple_of(tile * 128, 128), 128)
        mean, scale = moments(m_totals[:, cols], count)
        change_and_average(
            pre_motion, m_gain[:, cols] * scale, keep, places, cols, spare, change, average
        )
        for rows in EIGHTS:
            put(seed, rows, acc[rows, cols])
        for base, source, out in ((0, change, near_out), (9, average, wide_out)):
            totals_of = [jnp.zeros((8, 128), F32)] * 9
            for rows in EIGHTS:
                later, now, before = three(seed, places, rows, -7, DOWN, UP)
                taps = three(source, places, rows, 1, LEFT, RIGHT)
                for col, pull in enumerate((pull_a, pull_b, pull_c)):
                    total = None
                    for row, line in enumerate((later, now, before)):
                        spot = row * 3 + col
                        term = line * depth[base // 9, row, col : col + 1, cols]
                        total = term if total is None else total + term
                        totals_of[spot] = totals_of[spot] + line * taps[col]
                    put(pull, rows, total)
            for spot in range(9):
                depth_out[base + spot : base + spot + 1, cols] = jnp.sum(
                    totals_of[spot], axis=0, keepdims=True
                )
            for rows in EIGHTS:
                put(
                    out,
                    rows,
                    at(pull_b, rows)
                    + at(pull_a, rows, 1) * mask_of(places, rows, RIGHT)
                    + at(pull_c, rows, -1) * mask_of(places, rows, LEFT),
                )
        box_rows(wide_out, places, spare)
        for rows in EIGHTS:
            value = at(near_out, rows) + box_columns(spare, places, rows)
            put(change, rows, kept(value, rows, keep))
        plain = jnp.zeros((8, 128), F32)
        cross = jnp.zeros((8, 128), F32)
        for rows in EIGHTS:
            value = at(change, rows, -49) - at(change, rows)
            grad_out[rows, cols] = value
            plain = plain + value
            cross = cross + value * (pre_motion[rows, cols] - mean)
        sums_out[0:1, cols] = jnp.sum(plain, axis=0, keepdims=True)
        sums_out[1:2, cols] = jnp.sum(cross, axis=0, keepdims=True) * scale


def spatial_backward(
    own, grad, pre_spatial, totals, sums, gain, places, weight, pre_reduce, r_totals, r_gain, r_bias,
    m_grad, pre_motion, m_totals, m_sums, m_gain,
    taps_out, grad_out, sums_out, motion_out, motion_own, buffer, source_ref, acc, *, count
):
    clear_ends(buffer)
    on_grad, on_value, constant = back_affine(totals[...], sums[...], count, gain[...])
    for rows, cols in each_piece(MID, EIGHTS):
        buffer[8 + rows.start : 8 + rows.stop, cols] = (
            (
                grad[rows, cols] * on_grad[:, cols]
                + pre_spatial[rows, cols] * on_value[:, cols]
                + constant[:, cols]
            )
            .astype(BF)
            .astype(F32)
        )
    mine = pl.ds(pl.multiple_of((own[0] // 2) * 256, 256), 256)
    for tap in range(9):
        row_off, col_off = tap // 3 - 1, tap % 3 - 1
        source_ref[...] = tap_source(buffer, places, row_off, col_off, -1).astype(BF)
        taps_out[:, tap * 256 : (tap + 1) * 256] = source_ref[:, mine]
        value = dot(source_ref[...], weight[tap * MID : (tap + 1) * MID, :], NT)
        if tap == 0:
            acc[...] = value
        else:
            acc[...] += value
    put_activation_back(
        grad_out, sums_out, acc, pre_reduce, r_totals[...], r_gain[...], r_bias[...], count
    )
    put_back(
        motion_out, m_grad, pre_motion, back_affine(m_totals[...], m_sums[...], count, m_gain[...])
    )
    motion_own[...] = motion_out[:, mine]


def reduce_backward(
    own, grad, pre_reduce, totals, sums, gain, mine_w, other_w, motion, mine_m, other_m, direct, lines,
    own_out, mine_out, other_out, tail_out, value_ref, tail_ref, *, count
):
    put_back(value_ref, grad, pre_reduce, back_affine(totals[...], sums[...], count, gain[...]))
    tail_ref[...] = jnp.zeros_like(tail_ref)
    for row in range(6):
        ref, at = (lines, row) if row < 4 else (sums, row - 4)
        for side in range(2):
            tail_ref[2 * row + side : 2 * row + side + 1, :] = ref[
                at : at + 1, side * 256 : (side + 1) * 256
            ]
    tail_out[...] = tail_ref[...].astype(BF)
    own_out[...] = value_ref[:, pl.ds(pl.multiple_of((own[0] // 2) * 256, 256), 256)]
    for out, reduce_w, motion_w, left in (
        (other_out, other_w, other_m, MID),
        (mine_out, mine_w, mine_m, 0),
    ):
        value = dot(value_ref[...], reduce_w[...], NT) + dot(motion[...], motion_w[...], NT)
        out[...] = (value + direct[:, left : left + MID].astype(F32)).astype(BF)


def owners(place, sizes):
    away = lambda at, axis, size: lax.rem(at + size - place[axis], size)
    for z in range(sizes[0]):
        for y in range(sizes[1]):
            for c in range(sizes[2]):
                owner = (z * sizes[1] + y) * sizes[2] + c
                yield owner, (away(c, 1, sizes[2]), away(y, 2, sizes[1]), away(z, 3, sizes[0]))


def spatial_weight_kernel(place, hidden, taps, motion, out, turned_ref, *, sizes):
    turned_ref[...] = jnp.transpose(hidden[...].astype(F32)).astype(BF)
    clips = sizes[0] * sizes[1] * sizes[2]
    spots = dict(owners(place, sizes))
    share = 9 * MID // clips
    for tap in range(9):
        value = dot(turned_ref[...], taps[:, tap * 256 : (tap + 1) * 256]).astype(BF)
        for top in range(0, MID, 16):
            row = tap * MID + top
            out[*spots[row // share], row % share : row % share + 16, :] = value[top : top + 16]
    for owner, spot in spots.items():
        out[*spot, share:, :] = motion[owner * (C // clips) : (owner + 1) * (C // clips), :]


def early_weight_kernel(place, hidden, expand, mixed, excite, out, turned_ref, *, sizes):
    rows = MID // (sizes[0] * sizes[1] * sizes[2])
    spots = dict(owners(place, sizes))
    for base, left, right in ((0, hidden, expand), (4, mixed, excite)):
        turned_ref[...] = jnp.transpose(left[...].astype(F32)).astype(BF)
        for block in range(4):
            value = dot(turned_ref[...], right[:, block * 256 : (block + 1) * 256]).astype(BF)
            for owner, spot in spots.items():
                out[*spot, (base + block) * rows : (base + block + 1) * rows, :] = value[
                    owner * rows : (owner + 1) * rows
                ]


def pack_kernel(early, stem, gate, depth, out, buffer):
    buffer[...] = jnp.zeros_like(buffer)
    for side in range(2):
        cols = slice(side * 256, (side + 1) * 256)
        buffer[32 * side : 32 * side + 32, :] = stem[:, cols]
        buffer[96 + 18 * side : 114 + 18 * side, :] = depth[:, cols]
    for block in range(8):
        buffer[64 + 4 * block : 68 + 4 * block, :] = gate[:, block * 256 : (block + 1) * 256]
    out[0:128, :] = early[...]
    out[128:272, :] = buffer[...].astype(BF)


def late_weight_kernel(place, values, out, *, sizes):
    rows = out.shape[3]
    for owner, spot in owners(place, sizes):
        out[*spot] = values[owner * rows : (owner + 1) * rows, :]


def join_kernel(own, mine, got, out):
    first = jnp.where(own[0] % 2 == 0, mine[...].astype(F32), got[...].astype(F32))
    second = jnp.where(own[0] % 2 == 0, got[...].astype(F32), mine[...].astype(F32))
    out[...] = jnp.concatenate([first, second], axis=0).astype(BF)


def unpack_kernel(
    own, rest_0, rest_1, rest_2, rest_3, early_0, early_1, early_2, early_3,
    mine, got,
    reduce_out, spatial_out, expand_out, motion_out, excite_out, fine_out, coarse_out, grad_out,
    depth_out, e_bias, e_gain, x_bias, x_gain, m_gain, s_bias, s_gain, r_bias, r_gain,
    packed_ref, *, clips
):
    join_kernel(own, mine, got, grad_out)
    wide = early_0[192:224, :].astype(F32) + early_1[192:224, :].astype(F32)
    for row, out in enumerate((e_bias, e_gain, x_bias, x_gain)):
        for block in range(8):
            out[block * 256 : (block + 1) * 256] = wide[4 * block + row]
    both = early_0[224:272, :].astype(F32) + early_1[224:272, :].astype(F32)
    for spot in range(18):
        for side in range(2):
            at = 18 * side + spot
            depth_out[spot // 9, spot // 3 % 3, spot % 3 : spot % 3 + 1, side * 256 : (side + 1) * 256] = (
                both[at : at + 1]
            )
    last = rest_0.shape[0] - 16
    both = rest_0[last:, :].astype(F32) + rest_1[last:, :].astype(F32)
    for row, out in ((1, m_gain), (2, s_bias), (3, s_gain), (4, r_bias), (5, r_gain)):
        for side in range(2):
            out[side * 256 : (side + 1) * 256] = both[2 * row + side]
    cuts = (9 * MID // clips, (9 * MID + C) // clips, (9 * MID + 2 * C) // clips)
    half = own[0] // 2
    for side, left, right in ((half, rest_0, rest_1), (1 - half, rest_2, rest_3)):
        value = left[...].astype(F32) + right[...].astype(F32)
        cols = pl.ds(pl.multiple_of(side * 256, 256), 256)
        spatial_out[:, cols] = value[: cuts[0]]
        motion_out[:, cols] = value[cuts[0] : cuts[1]]
        reduce_out[:, cols] = value[cuts[1] : cuts[2]]
    rows = MID // clips
    for flip, left, right in (
        (0, (early_0, 0), (early_1, 1)),
        (1, (early_0, 1), (early_1, 0)),
        (2, (early_2, 0), (early_3, 1)),
        (3, (early_2, 1), (early_3, 0)),
    ):
        for base, out in ((0, expand_out), (4, excite_out)):
            for block in range(2):
                value = None
                for ref, spot in (left, right):
                    top = (base + 2 * spot + block) * rows
                    part = ref[top : top + rows, :].astype(F32)
                    value = part if value is None else value + part
                out[:, pl.ds(pl.multiple_of((own[0] ^ flip) * MID + block * 256, 256), 256)] = value
    base = 8 * rows
    for flip, ref in enumerate((early_0, early_1, early_2, early_3)):
        for block in range(4):
            top, left = base + (block // 2) * 32, (block % 2) * 128
            at = pl.multiple_of((own[0] ^ flip) * 128 + block * 32, 32)
            packed_ref[pl.ds(at, 32), :] = ref[top : top + 32, left : left + 128].astype(F32)
    for chan in range(3):
        for row in range(7):
            at = chan * 56 + row * 8
            fine_out[chan, row] = packed_ref[at : at + 7, 0:64]
    for chan in range(12):
        side = (chan % 2) * 64
        for row in range(7):
            at = 168 + (chan // 2) * 56 + row * 8
            coarse_out[chan, row] = packed_ref[at : at + 7, side : side + 64]


def with_own(kernel, own, grid, in_specs, out_specs, out_shape, scratch, args, flops, nbytes, name):
    if not grid:
        return pl.pallas_call(
            kernel,
            in_specs=[SMEM] + in_specs,
            out_specs=out_specs,
            out_shape=out_shape,
            scratch_shapes=scratch,
            compiler_params=params(name),
            cost_estimate=cost(flops, nbytes),
            name=name,
        )(own, *args)
    return pl.pallas_call(
        kernel,
        grid_spec=pltpu.PrefetchScalarGridSpec(
            num_scalar_prefetch=1,
            grid=grid,
            in_specs=in_specs,
            out_specs=out_specs,
            scratch_shapes=scratch,
        ),
        out_shape=out_shape,
        compiler_params=params(name),
        cost_estimate=cost(flops, nbytes),
        name=name,
    )(own, *args)


def place_table():
    rows = np.arange(ROWS)
    down = (rows % 49) // 7
    right = rows % 7
    kept = [down >= 1, down <= FEAT - 2, right >= 1, right <= FEAT - 2]
    return jnp.asarray(np.concatenate([np.repeat(k[:, None], 128, 1) for k in kept], axis=1), F32)


def keep_pairs(valid_rows, video_rows):
    valid_float = valid_rows.astype(F32)
    same_video = (video_rows[:, 1:] == video_rows[:, :-1]).astype(F32)
    pair_keep = valid_float[:, 1:] * valid_float[:, :-1] * same_video
    return jnp.concatenate([pair_keep, jnp.zeros_like(pair_keep[:, :1])], axis=1)


def on_device(
    features,
    out_cotangent,
    seg_valid,
    seg_video,
    frames,
    stem_cotangent,
    stem_weight,
    stem_diff_weight,
    stem_gain,
    stem_bias,
    reduce_weight,
    reduce_gain,
    reduce_bias,
    spatial_weight,
    spatial_gain,
    spatial_bias,
    expand_weight,
    expand_gain,
    expand_bias,
    motion_weight,
    motion_gain,
    depth_weight,
    excite_weight,
    excite_gain,
    excite_bias,
):
    clips = lax.axis_size("z") * lax.axis_size("y") * lax.axis_size("c")
    count = float(clips * ROWS)
    stem_count = float(clips * lax.axis_size("x") * (SIDE // 2) ** 2)
    here = lax.axis_index("x")
    micro = here % 2
    own = jnp.stack([here] + [lax.axis_index(axis) for axis in ("c", "y", "z")]).astype(jnp.int32)
    places = place_table()

    def of_micro(rows):
        return lax.dynamic_index_in_dim(
            rows.reshape(MICRO, rows.shape[0] // MICRO, rows.shape[1]), micro, 0, False
        )

    feats = of_micro(features)
    seeds = of_micro(out_cotangent)
    keep = of_micro(keep_pairs(seg_valid, seg_video))
    line = lambda vector: vector.reshape(1, -1)
    reduce_gain, reduce_bias = line(reduce_gain), line(reduce_bias)
    spatial_gain, spatial_bias = line(spatial_gain), line(spatial_bias)
    expand_gain, expand_bias = line(expand_gain), line(expand_bias)
    excite_gain, excite_bias = line(excite_gain), line(excite_bias)
    motion_gain = line(motion_gain)

    tables = stem_tables()
    lanes = tables[5]
    column = lambda rows, width: pl.BlockSpec((rows, width), lambda step, *rest: (0, step))
    pre_reduce, pre_motion, reduce_sum, motion_sum = pl.pallas_call(
        first_matmuls,
        grid=(2,),
        in_specs=[SMEM, whole(ROWS, C), column(C, 256), column(C, 256)],
        out_specs=[column(ROWS, 256), column(ROWS, 256), column(2, 256), column(2, 256)],
        out_shape=[held((ROWS, MID)), held((ROWS, MID)), shape((2, MID)), shape((2, MID))],
        compiler_params=params("first_matmuls"),
        cost_estimate=cost(1.7e9, 1e7),
        name="first_matmuls",
    )(own, *in_vmem(feats), reduce_weight, motion_weight)
    first_wide = core_sum(jnp.concatenate([reduce_sum, motion_sum], axis=1))
    fine, coarse, wide_fine, wide_coarse = stem_planes(
        frames, stem_weight, stem_diff_weight, tables, first_wide
    )
    first_wide = ring_sum(first_wide, "y")
    raw, stem_sum, centre = stem_first(fine, coarse, wide_fine, wide_coarse, tables, first_wide)
    first_tot = ring_sum(first_wide, "z")
    reduce_tot, motion_tot = first_tot[:, :MID], first_tot[:, MID:]
    stem_sum = ring_sum(stem_sum[:2], "x")

    hidden_one, pre_spatial, spatial_sum = pl.pallas_call(
        functools.partial(spatial_forward, count=count),
        in_specs=[VMEM] * 6,
        out_specs=[VMEM] * 3,
        out_shape=[held((ROWS, MID), BF), held((ROWS, MID)), shape((2, MID))],
        scratch_shapes=[pltpu.VMEM((ROWS + 16, MID), F32)],
        compiler_params=params("spatial_forward"),
        cost_estimate=cost(1.9e9, 8e6),
        name="spatial_forward",
    )(*in_vmem(pre_reduce), reduce_tot, reduce_gain, reduce_bias, places, spatial_weight)

    spatial_wide = core_sum(jnp.concatenate([spatial_sum, stem_sum], axis=1))
    mixed, pre_excite, excite_sum, excite_mid = pl.pallas_call(
        functools.partial(motion_forward, count=count),
        in_specs=[VMEM] * 3 + [SMEM] + [VMEM] * 4,
        out_specs=[VMEM] * 4,
        out_shape=[held((ROWS, MID), BF), held((ROWS, C), BF), shape((2, C)), shape((1, C))],
        scratch_shapes=[pltpu.VMEM((ROWS + 128, 128), F32)] * 6,
        compiler_params=params("motion_forward"),
        cost_estimate=cost(2e9, 1.2e7),
        name="motion_forward",
    )(*in_vmem(pre_motion), motion_tot, motion_gain, keep, places, depth_weight, excite_weight, spatial_wide)
    spatial_wide = ring_sum(ring_sum(spatial_wide, "y"), "z")
    spatial_tot, stem_tot = spatial_wide[:, :MID], spatial_wide[:, MID:]
    stem_tot = jnp.pad(stem_tot, ((0, 6), (0, 0)))

    hidden_two, pre_expand, expand_sum, expand_mid = pl.pallas_call(
        functools.partial(expand_forward, count=count),
        in_specs=[VMEM] * 5,
        out_specs=[VMEM] * 4,
        out_shape=[held((ROWS, MID), BF), held((ROWS, C), BF), shape((2, C)), shape((1, C))],
        compiler_params=params("expand_forward"),
        cost_estimate=cost(1e9, 1e7),
        name="expand_forward",
    )(*in_vmem(pre_spatial), spatial_tot, spatial_gain, spatial_bias, expand_weight)
    expand_wide = core_sum(jnp.concatenate([expand_sum, excite_sum], axis=1))
    back, back_sum = stem_second(
        raw, centre, stem_cotangent, stem_tot, stem_gain, stem_bias, lanes, stem_count, expand_wide
    )
    expand_wide = ring_sum(ring_sum(expand_wide, "y"), "z")
    expand_tot, excite_tot = expand_wide[:, :C], expand_wide[:, C:]
    back_sum = ring_sum(back_sum[:2], "x")

    mine, other, direct, grad_comb, grad_gate, gate_sum = with_own(
        functools.partial(gate_kernel, count=count),
        own,
        (),
        [VMEM] * 12,
        [VMEM] * 6,
        [
            shape((ROWS, MID), BF), shape((ROWS, MID), BF), held((ROWS, 2 * MID), BF),
            held((ROWS, C), BF), held((ROWS, C), BF), shape((4, C)),
        ],
        [pltpu.VMEM((ROWS, C), BF)] * 2,
        (
            *in_vmem(pre_expand, pre_excite, feats, seeds), expand_tot, excite_tot, expand_mid, excite_mid,
            expand_gain, expand_bias, excite_gain, excite_bias,
        ),
        2e9,
        2e7,
        "gate",
    )
    gate_wide = sum_dp(
        jnp.concatenate([gate_sum, jnp.pad(back_sum, ((0, 2), (0, 0)))], axis=1)
    )
    gate_tot, back_tot = gate_wide[:, :C], gate_wide[:2, C:]
    back_tot = jnp.pad(back_tot, ((0, 6), (0, 0)))
    back_both = back_tot[0] + back_tot[1]
    stem_gain_grad, stem_bias_grad = back_both[64:], back_both[:64]

    got_result = from_peer(other, 1)

    expand_own, grad_spatial, spatial_back = with_own(
        functools.partial(expand_backward, count=count),
        own,
        (),
        [VMEM] * 11,
        [VMEM] * 3,
        [held((ROWS, 2 * MID), BF), held((ROWS, MID)), shape((2, MID))],
        [pltpu.VMEM((ROWS, C), BF), pltpu.VMEM((ROWS, MID), F32)],
        (
            *in_vmem(grad_comb, pre_expand), expand_tot, gate_tot, expand_gain, expand_mid, expand_weight,
            *in_vmem(pre_spatial), spatial_tot, spatial_gain, spatial_bias,
        ),
        1e9,
        1e7,
        "expand_backward",
    )

    excite_own, grad_reduced, motion_back, depth_part = with_own(
        functools.partial(excite_backward, count=count),
        own,
        (),
        [VMEM] * 10 + [SMEM] + [VMEM] * 2,
        [VMEM] * 4,
        [held((ROWS, 2 * MID), BF), held((ROWS, MID)), shape((2, MID)), shape((18, MID))],
        [pltpu.VMEM((ROWS, C), BF), pltpu.VMEM((ROWS, MID), F32)]
        + [pltpu.VMEM((ROWS + 128, 128), F32)] * 9,
        (
            *in_vmem(grad_gate, pre_excite), excite_tot, gate_tot, excite_gain, excite_mid, excite_weight,
            *in_vmem(pre_motion), motion_tot, motion_gain, keep, places, depth_weight,
        ),
        2e9,
        1e7,
        "excite_backward",
    )
    across = lambda left, right: dot(left, right, TN).astype(BF)
    sizes = [lax.axis_size(axis) for axis in ("z", "y", "c")]
    early = pl.pallas_call(
        functools.partial(early_weight_kernel, sizes=sizes),
        in_specs=[SMEM] + [VMEM] * 4,
        out_specs=VMEM,
        out_shape=shape((*sizes[::-1], 8 * (MID // clips), 256), BF),
        scratch_shapes=[pltpu.VMEM((MID, ROWS), BF)],
        compiler_params=params("early_weight"),
        cost_estimate=cost(1e9, 5e6),
        name="early_weight",
    )(own, *in_vmem(hidden_two, expand_own, mixed, excite_own))
    back_all = core_sum(jnp.concatenate([motion_back, spatial_back, depth_part], axis=0))
    stem_packed = stem_third(
        own, raw, centre, back, fine, coarse, stem_tot, back_tot, stem_gain, tables, stem_count,
        back_all,
    )
    back_all, early = tie(back_all, early)
    early = scatter_lead(early, "c")
    back_all = ring_sum(back_all, "y")
    back_all, early = tie(back_all, early)
    early = scatter_lead(early, "y")
    back_all = ring_sum(back_all, "z")
    stem_quarter = scatter_lead(stem_packed, "x", F32)
    motion_back_tot, spatial_back_tot = back_all[:2], back_all[2:4]

    taps, grad_reduce, reduce_back, motion_full, motion_own = with_own(
        functools.partial(spatial_backward, count=count),
        own,
        (1,),
        [
            whole(ROWS, MID), whole(ROWS, MID), whole(2, MID), whole(2, MID), whole(1, MID),
            whole(ROWS, 512), whole(9 * MID, MID), whole(ROWS, MID), whole(2, MID),
            whole(1, MID), whole(1, MID),
            whole(ROWS, MID), whole(ROWS, MID), whole(2, MID), whole(2, MID), whole(1, MID),
        ],
        [
            whole(ROWS, 9 * 256), whole(ROWS, MID), whole(2, MID), whole(ROWS, MID), whole(ROWS, 256),
        ],
        [
            held((ROWS, 9 * 256), BF), held((ROWS, MID)), shape((2, MID)),
            held((ROWS, MID), BF), shape((ROWS, 256), BF),
        ],
        [
            pltpu.VMEM((ROWS + 16, MID), F32),
            pltpu.VMEM((ROWS, MID), BF),
            pltpu.VMEM((ROWS, MID), F32),
        ],
        (
            *in_vmem(grad_spatial, pre_spatial), spatial_tot, spatial_back_tot, spatial_gain, places,
            spatial_weight, *in_vmem(pre_reduce), reduce_tot, reduce_gain, reduce_bias,
            *in_vmem(grad_reduced, pre_motion), motion_tot, motion_back_tot, motion_gain,
        ),
        2e9,
        1e7,
        "spatial_backward",
    )
    mine_rows = pl.BlockSpec((MID, MID), lambda step, own_ref: (own_ref[0], 0))
    other_rows = pl.BlockSpec((MID, MID), lambda step, own_ref: (own_ref[0] ^ 1, 0))
    middle = pl.pallas_call(
        functools.partial(spatial_weight_kernel, sizes=sizes),
        in_specs=[SMEM] + [VMEM] * 3,
        out_specs=VMEM,
        out_shape=shape((*sizes[::-1], (9 * MID + C) // clips, 256), BF),
        scratch_shapes=[pltpu.VMEM((MID, ROWS), BF)],
        compiler_params=params("spatial_weight"),
        cost_estimate=cost(1e9, 5e6),
        name="spatial_weight",
    )(own, *in_vmem(hidden_one, taps), across(feats, motion_own))

    reduce_back = core_sum(jnp.concatenate([reduce_back, stem_quarter], axis=0))
    reduce_back, middle, early, got_result = tie(reduce_back, middle, early, got_result)
    early = scatter_lead(early, "z")
    middle = scatter_lead(middle, "c")
    reduce_back = ring_sum(reduce_back, "y")
    reduce_back, middle, early = tie(reduce_back, middle, early)
    upward, downward = scatter_start(middle, "y")
    reduce_back = ring_sum(reduce_back, "z")
    reduce_back, upward, downward = tie(reduce_back, upward, downward)
    reduce_back_tot = reduce_back[:2]
    early = gather_x(
        pl.pallas_call(
            pack_kernel,
            in_specs=[VMEM] * 4,
            out_specs=VMEM,
            out_shape=shape((272, 256), BF),
            scratch_shapes=[pltpu.VMEM((144, 256), F32)],
            compiler_params=params("pack"),
            cost_estimate=cost(1e5, 5e5),
            name="pack",
        )(early, reduce_back[2:], gate_tot, back_all[4:])
    )
    middle = scatter_finish(middle, "y", upward, downward)

    reduce_own, mine_grad, other_grad, tail = with_own(
        functools.partial(reduce_backward, count=count),
        own,
        (1,),
        [
            whole(ROWS, MID), whole(ROWS, MID), whole(2, MID), whole(2, MID), whole(1, MID),
            mine_rows, other_rows, whole(ROWS, MID), mine_rows, other_rows, whole(ROWS, 2 * MID),
            whole(22, MID),
        ],
        [whole(ROWS, 256), whole(ROWS, MID), whole(ROWS, MID), whole(16, 256)],
        [
            shape((ROWS, 256), BF), shape((ROWS, MID), BF), shape((ROWS, MID), BF), shape((16, 256), BF),
        ],
        [pltpu.VMEM((ROWS, MID), BF), pltpu.VMEM((16, 256), F32)],
        (
            *in_vmem(grad_reduce, pre_reduce), reduce_tot, reduce_back_tot, reduce_gain,
            reduce_weight, reduce_weight, *in_vmem(motion_full), motion_weight, motion_weight,
            *in_vmem(direct), back_all,
        ),
        5e8,
        8e6,
        "reduce_backward",
    )
    got_grad = from_peer(other_grad, 1)
    late = pl.pallas_call(
        functools.partial(late_weight_kernel, sizes=sizes),
        in_specs=[SMEM, VMEM],
        out_specs=VMEM,
        out_shape=shape((*sizes[::-1], C // clips, 256), BF),
        compiler_params=params("late_weight"),
        cost_estimate=cost(1e5, 2e6),
        name="late_weight",
    )(own, across(feats, reduce_own))
    late = scatter_lead(late, "c")
    late, middle, *early = tie(late, middle, *early)
    late = scatter_lead(late, "y")
    late, got_grad = tie(late, got_grad)
    rest = scatter_lead(jnp.concatenate([middle, late], axis=1), "z")
    rest = gather_x(jnp.concatenate([rest, tail], axis=0))
    result = with_own(
        join_kernel,
        own,
        (1,),
        [whole(ROWS, MID), whole(ROWS, MID)],
        whole(2 * ROWS, MID),
        shape((2 * ROWS, MID), BF),
        [],
        (mine, got_result),
        1e5,
        2e6,
        "join_result",
    )

    (
        reduce_grad, spatial_grad, expand_grad, motion_grad, excite_grad,
        stem_weight_grad, stem_diff_grad, features_grad, depth_grad, *vectors,
    ) = with_own(
        functools.partial(unpack_kernel, clips=clips),
        own,
        (1,),
        [whole(*part.shape) for part in rest]
        + [whole(*part.shape) for part in early]
        + [
            whole(ROWS, MID), whole(ROWS, MID),
        ],
        [
            whole(C // clips, MID), whole(9 * MID // clips, MID), whole(MID // clips, C),
            whole(C // clips, MID), whole(MID // clips, C),
            whole(3, 7, 7, STEMC), whole(12, 7, 7, STEMC), whole(2 * ROWS, MID),
            whole(2, 3, 3, MID), *[whole(C)] * 4, *[whole(MID)] * 5,
        ],
        [
            shape((C // clips, MID)), shape((9 * MID // clips, MID)), shape((MID // clips, C)),
            shape((C // clips, MID)), shape((MID // clips, C)),
            shape((3, 7, 7, STEMC)), shape((12, 7, 7, STEMC)), shape((2 * ROWS, MID), BF),
            shape((2, 3, 3, MID)), *[shape((C,))] * 4, *[shape((MID,))] * 5,
        ],
        [pltpu.VMEM((512, 128), F32)],
        (*rest, *early, mine_grad, got_grad),
        1e6,
        6e6,
        "unpack",
    )
    stem_weight_grad = stem_weight_grad.transpose(3, 0, 1, 2)
    stem_diff_grad = stem_diff_grad.transpose(3, 0, 1, 2)

    return (
        result,
        features_grad,
        stem_weight_grad,
        stem_diff_grad,
        stem_gain_grad,
        stem_bias_grad,
        reduce_grad,
        vectors[8],
        vectors[7],
        spatial_grad,
        vectors[6],
        vectors[5],
        expand_grad,
        vectors[1],
        vectors[0],
        motion_grad,
        vectors[4],
        depth_grad,
        excite_grad,
        vectors[3],
        vectors[2],
    )


def solution(mesh):
    grid = Mesh(mesh.devices.reshape(4, 4, 2, 4), ("z", "y", "c", "x"))
    clips = ("z", "y", "c")
    everyone = ("z", "y", "c", "x")
    split = P(clips, None)
    copied = P()
    return jax.shard_map(
        on_device,
        mesh=grid,
        in_specs=(split,) * 4
        + (P(everyone, None, None, None, None), P(everyone, None, None, None))
        + (copied,) * 19,
        out_specs=(P(clips, "x"), P(clips, "x"))
        + (copied,) * 4
        + (split, copied, copied) * 3
        + (split, copied, copied)
        + (split, copied, copied),
        check_vma=False,
    )
```

```python
import functools

import jax
import jax.numpy as jnp
import numpy as np
from jax import lax
from jax.experimental import pallas as pl
from jax.experimental.pallas import tpu as pltpu
from jax.sharding import Mesh
from jax.sharding import PartitionSpec as P

C = 2048
MID = 512
STEMC = 64
SIDE = 224
FEAT = 7
SEG = 8
MICRO = 2
ROWS = SEG * FEAT * FEAT
EPS = 1e-05
BF = jnp.bfloat16
F32 = jnp.float32
HIGH = lax.Precision.HIGHEST
NN = (((1,), (0,)), ((), ()))
NT = (((1,), (1,)), ((), ()))
TN = (((0,), (0,)), ((), ()))
GROUPS = 7
TILE = 512
VMEM = pl.BlockSpec(memory_space=pltpu.VMEM)
SMEM = pl.BlockSpec(memory_space=pltpu.SMEM)
PIECES = [slice(top, min(top + 16, ROWS)) for top in range(0, ROWS, 16)]
EIGHTS = [slice(top, top + 8) for top in range(0, ROWS, 8)]


def sigmoid(values):
    return 0.5 + 0.5 * jnp.tanh(0.5 * values)


def dot(left, right, dims=NN, precision=None):
    return lax.dot_general(left, right, dims, precision=precision, preferred_element_type=F32)


LIMITS = {"stem_spread": 20, "first_matmuls": 14, "spatial_backward": 14, "unpack": 14}


def params(name):
    return pltpu.CompilerParams(vmem_limit_bytes=LIMITS.get(name, 10) * 2**20)


def held(dims, dtype=F32):
    return pltpu.VMEM(dims, dtype)


def in_vmem(*values):
    return [pltpu.with_memory_space_constraint(value, pltpu.VMEM) for value in values]


def cost(flops, nbytes):
    return pl.CostEstimate(flops=int(flops), bytes_accessed=int(nbytes), transcendentals=0)


def shape(dims, dtype=F32):
    return jax.ShapeDtypeStruct(dims, dtype)


def ring_sum(values, axis):
    size = lax.axis_size(axis)
    if size == 1:
        return values
    got = [
        lax.ppermute(values, axis, [(i, (i + step) % size) for i in range(size)])
        for step in range(1, size)
    ]
    if size == 2:
        return values + got[0]
    return (values + got[1]) + (got[0] + got[2])


def core_sum(values):
    pair = lax.all_gather(values, "c")
    return pair[0] + pair[1]


def sum_dp(values):
    return ring_sum(ring_sum(core_sum(values), "y"), "z")


def shift_by(values, axis, step):
    size = lax.axis_size(axis)
    return lax.ppermute(values, axis, [(i, (i + step) % size) for i in range(size)])


def scatter_lead(blocks, axis, kind=BF):
    total = blocks[0].astype(F32)
    for step in range(1, blocks.shape[0]):
        total = total + shift_by(blocks[step], axis, step).astype(F32)
    return total.astype(kind)


def tie(*values):
    return lax.optimization_barrier(values)


def from_peer(values, flip):
    size = lax.axis_size("x")
    return lax.ppermute(values, "x", [(i, i ^ flip) for i in range(size)])


def gather_x(block):
    return [block] + [from_peer(block, flip) for flip in (1, 2, 3)]


def stem_tables():
    half, quarter = SIDE // 2, SIDE // 4
    pool = np.zeros((SIDE, 128), np.float32)
    for column in range(SIDE):
        pool[column, column // 2] = 0.25
    fine = np.zeros((2, SIDE, 9 * 128), np.float32)
    coarse = np.zeros((2 * 128, 7 * 128), np.float32)
    for seg in range(2):
        for spot in range(quarter):
            for tap in range(9):
                column = 4 * spot + tap - 3
                if 0 <= column < SIDE:
                    fine[seg, column, tap * 128 + seg * 64 + spot] = 1
            for tap in range(7):
                column = 2 * spot + tap - 3
                if 0 <= column < half:
                    coarse[seg * 128 + column, tap * 128 + seg * 64 + spot] = 1
    sel_fine = np.zeros((8, 168, 432), np.float32)
    for up in range(2):
        for row in range(2):
            for col in range(2):
                for chan in range(3):
                    for dy in range(7):
                        for dx in range(7):
                            sel_fine[
                                up * 4 + row * 2 + col,
                                chan * 56 + dy * 8 + dx,
                                chan * 144 + (2 * col + dx) * 16 + 4 * up + 2 * row + dy,
                            ] = 1
    sel_coarse = np.zeros((4, 56, 128), np.float32)
    for up in range(4):
        for dy in range(7):
            for dx in range(7):
                sel_coarse[up, dy * 8 + dx, dx * 16 + 2 * up + dy] = 1
    lanes = np.zeros((8, 128), np.float32)
    lanes[0, :64] = 1
    lanes[1, 64:] = 1
    usable = np.zeros((8, 128), np.float32)
    usable[0, :56] = 1
    usable[1, 64:120] = 1
    return [
        jnp.asarray(table, dtype)
        for table, dtype in (
            (pool, BF),
            (fine, BF),
            (coarse, BF),
            (sel_fine, BF),
            (sel_coarse, BF),
            (lanes, F32),
            (usable, F32),
        )
    ]


def fine_patches(tall):
    parts = []
    for pair in range(4):
        rows = slice(8 * pair, 8 * pair + 16)
        parts.append(
            jnp.concatenate(
                [
                    tall[chan][rows, tap * 128 : (tap + 1) * 128]
                    for chan in range(3)
                    for tap in range(9)
                ],
                axis=0,
            ).astype(BF)
        )
    return jnp.concatenate(parts, axis=1)


def coarse_patches(tall):
    blank = jnp.zeros((16, 128), F32)
    parts = [[], []]
    for chan in range(12):
        for quad in range(2):
            rows = slice(8 * quad, 8 * quad + 16)
            for tap in range(7):
                parts[quad].append(tall[chan][rows, tap * 128 : (tap + 1) * 128])
            parts[quad].append(blank)
    return jnp.concatenate(
        [jnp.concatenate(pieces, axis=0).astype(BF) for pieces in parts], axis=1
    )


def stem_spread(
    frames, weight, diff_weight, pool, fine_tab, coarse_tab, sel_fine, sel_coarse, after,
    fine_out, coarse_out, wide_fine, wide_coarse,
    planes_ref, pooled_ref, moved_ref, flat_ref,
):
    pooled_ref[...] = jnp.zeros_like(pooled_ref)
    moved_ref[...] = jnp.zeros_like(moved_ref)
    for seg in range(2):
        planes_ref[...] = dot(frames[seg], pool[...])
        for chan in range(3):
            lines = []
            for k in range(5):
                at = (k * 3 + chan) * SIDE
                lines.append(
                    planes_ref[pl.ds(at, SIDE // 2, 2), :]
                    + planes_ref[pl.ds(at + 1, SIDE // 2, 2), :]
                )
            for k in range(4):
                at = (k * 3 + chan) * 128 + 3
                pooled_ref[at : at + 112, seg * 128 : (seg + 1) * 128] = lines[k + 1] - lines[k]
            at = (6 + chan) * SIDE
            moved_ref[seg, chan * 256 + 3 : chan * 256 + 227, :] = frames[
                seg, at : at + SIDE, :
            ].astype(F32)
    small = pooled_ref[...].astype(BF)
    for left in range(0, 896, 256):
        right = min(left + 256, 896)
        coarse_out[:, :, left:right] = (
            dot(small, coarse_tab[:, left:right]).astype(BF).reshape(12, 128, right - left)
        )
    first, second = moved_ref[0].astype(BF), moved_ref[1].astype(BF)
    for left in range(0, 1152, 256):
        right = min(left + 256, 1152)
        value = dot(first, fine_tab[0, :, left:right]) + dot(second, fine_tab[1, :, left:right])
        fine_out[:, :, left:right] = value.astype(BF).reshape(3, 256, right - left)

    flat_ref[...] = jnp.zeros_like(flat_ref)
    for chan in range(3):
        for row in range(7):
            at = chan * 56 + row * 8
            flat_ref[at : at + 7, :] = weight[chan, row].astype(F32)
    for chan in range(12):
        for row in range(7):
            at = 168 + chan * 56 + row * 8
            flat_ref[at : at + 7, :] = diff_weight[chan, row].astype(F32)
    narrow = jnp.transpose(flat_ref[0:168, :]).astype(BF)
    for block in range(8):
        wide_fine[block * 64 : (block + 1) * 64, :] = dot(narrow, sel_fine[block]).astype(BF)
    tall = jnp.concatenate(
        [jnp.transpose(flat_ref[168 + chan * 56 : 224 + chan * 56, :]) for chan in range(12)], axis=0
    ).astype(BF)
    for up in range(4):
        spread = dot(tall, sel_coarse[up]).astype(BF)
        for chan in range(12):
            wide_coarse[up * 64 : (up + 1) * 64, chan * 128 : (chan + 1) * 128] = spread[
                chan * 64 : (chan + 1) * 64
            ]


def fine_rows(fine, group):
    start = pl.multiple_of(32 * group, 16)
    return [fine[chan, pl.ds(start, 48), :].astype(F32) for chan in range(3)]


def coarse_rows(coarse, group):
    start = pl.multiple_of(16 * group, 16)
    return [coarse[chan, pl.ds(start, 32), :].astype(F32) for chan in range(12)]


def stem_forward(
    fine, coarse, wide_fine, wide_coarse, lanes, usable, after,
    raw_out, sums_out, centre_out, acc_ref,
):
    acc_ref[...] = jnp.zeros_like(acc_ref)

    @pl.loop(0, GROUPS)
    def group(step):
        fine_sum = dot(
            wide_fine[...], fine_patches(fine_rows(fine, step))
        )
        coarse_sum = dot(
            wide_coarse[...],
            coarse_patches(coarse_rows(coarse, step)),
        )

        def value_at(pair, up, spot, top):
            row = (up * 4 + spot) * 64 + top
            lift = (2 * (pair % 2) + up) * 64 + top
            left = (pair // 2) * 128
            return (
                fine_sum[row : row + 16, pair * 128 : (pair + 1) * 128]
                + coarse_sum[lift : lift + 16, left : left + 128]
            )

        @pl.when(step == 0)
        def find_centre():
            for top in range(0, 64, 16):
                total = jnp.zeros((16, 128), F32)
                for pair in range(4):
                    for up in range(2):
                        for spot in range(4):
                            total = total + value_at(pair, up, spot, top)
                centre_out[top : top + 16, :] = total
            spread = dot(usable[...], usable[...], TN) * (1.0 / (32 * 56))
            centre_out[...] = dot(centre_out[...], spread)

        for top in range(0, 64, 16):
            centre = centre_out[top : top + 16, :]
            plain = acc_ref[top : top + 16, :]
            square = acc_ref[64 + top : 80 + top, :]
            for pair in range(4):
                for up in range(2):
                    for spot in range(4):
                        value = value_at(pair, up, spot, top)
                        row = (up * 4 + spot) * 64 + top
                        raw_out[step, row : row + 16, pair * 128 : (pair + 1) * 128] = (value - centre).astype(BF)
                        plain = plain + value
                        square = square + value * value
            acc_ref[top : top + 16, :] = plain
            acc_ref[64 + top : 80 + top, :] = square

    sums_out[...] = dot(lanes[...], acc_ref[...], NT, HIGH)


def dot_exact(select, values):
    total = None
    for _ in range(3):
        part = values.astype(BF)
        values = values - part.astype(F32)
        term = dot(select, part, NT)
        total = term if total is None else total + term
    return total


def over_lanes(vector):
    return dot(vector, jnp.ones((1, 128), F32), TN, HIGH)


def stem_scales(totals, lanes, count):
    spread = dot(totals, lanes, TN, HIGH) * (1.0 / count)
    return spread[0:64, :], spread[64:128, :]


def stem_middle(
    raw, cotangent, totals, gain, bias, lanes, centre, after, back_out, sums_out,
    seed_ref, coef_ref, scale_ref, acc_ref, *, count
):
    average, square = stem_scales(totals[...], lanes[...], count)
    scale = lax.rsqrt(square - average * average + EPS)
    scale_ref[...] = scale
    coef_ref[0] = average - centre[...]
    coef_ref[1] = scale * over_lanes(gain[...])
    coef_ref[2] = over_lanes(bias[...]) - coef_ref[0] * coef_ref[1]
    acc_ref[...] = jnp.zeros_like(acc_ref)

    @pl.loop(0, GROUPS)
    def group(step):
        blank = jnp.zeros((8, 64), F32)
        for spot in range(8):
            line = 8 * step + spot
            tall = jnp.concatenate(
                [cotangent[0, line].astype(F32), blank, cotangent[1, line].astype(F32), blank], axis=0
            )
            seed_ref[spot] = jnp.transpose(tall) * 0.25
        for top in range(0, 64, 16):
            chans = slice(top, top + 16)
            average, slope, shift = coef_ref[0, chans], coef_ref[1, chans], coef_ref[2, chans]
            plain, cross = acc_ref[0, chans], acc_ref[1, chans]
            for pair in range(4):
                cols = slice(pair * 128, (pair + 1) * 128)
                for up in range(2):
                    seed = seed_ref[2 * pair + up, chans]
                    for spot in range(4):
                        row = (up * 4 + spot) * 64 + top
                        value = raw[step, row : row + 16, cols].astype(F32)
                        act = value * slope + shift
                        sigma = sigmoid(act)
                        grad = seed * (sigma * (1.0 + act * (1.0 - sigma)))
                        back_out[step, row : row + 16, cols] = grad.astype(BF)
                        plain = plain + grad
                        cross = cross + grad * (value - average)
            acc_ref[0, chans] = plain
            acc_ref[1, chans] = cross

    acc_ref[1] = acc_ref[1] * scale_ref[...]
    sums_out[...] = dot(lanes[...], acc_ref[...].reshape(128, 128), NT, HIGH)


def stem_backward(
    place, raw, back, fine, coarse, totals, back_totals, gain, sel_fine, sel_coarse, lanes, centre, after,
    packed_out,
    coef_ref, packed, draw_ref, small_ref, fine_acc, coarse_acc, *, count
):
    average, square = stem_scales(totals[...], lanes[...], count)
    scale = lax.rsqrt(square - average * average + EPS)
    first, second = stem_scales(back_totals[...], lanes[...], count)
    slope = over_lanes(gain[...]) * scale
    coef_ref[0] = slope
    coef_ref[1] = -slope * scale * second
    coef_ref[2] = slope * ((average - centre[...]) * scale * second - first)
    fine_acc[...] = jnp.zeros_like(fine_acc)
    coarse_acc[...] = jnp.zeros_like(coarse_acc)

    @pl.loop(0, GROUPS)
    def group(step):
        for top in range(0, 64, 16):
            on_back, on_raw, constant = (coef_ref[k, top : top + 16] for k in range(3))
            for pair in range(4):
                cols = slice(pair * 128, (pair + 1) * 128)
                for up in range(2):
                    summed = None
                    for spot in range(4):
                        row = (up * 4 + spot) * 64 + top
                        draw = (
                            back[step, row : row + 16, cols].astype(F32) * on_back
                            + raw[step, row : row + 16, cols].astype(F32) * on_raw
                            + constant
                        ).astype(BF)
                        draw_ref[row : row + 16, cols] = draw
                        wide = draw.astype(F32)
                        summed = wide if summed is None else summed + wide
                    lift = (2 * (pair % 2) + up) * 64 + top
                    left = (pair // 2) * 128
                    small_ref[lift : lift + 16, left : left + 128] = summed.astype(BF)
        patches = fine_patches(fine_rows(fine, step))
        fine_acc[...] += dot(draw_ref[...], patches, NT)
        patches = coarse_patches(coarse_rows(coarse, step))
        coarse_acc[...] += dot(small_ref[...], patches, NT)

    total = jnp.zeros((168, 64), F32)
    for block in range(8):
        total = total + dot_exact(sel_fine[block], fine_acc[block * 64 : (block + 1) * 64, :])
    packed[0:168, 0:64] = total
    packed[0:168, 64:128] = jnp.zeros((168, 64), F32)
    for duo in range(6):
        piece = jnp.zeros((56, 128), F32)
        for up in range(4):
            stacked = jnp.concatenate(
                [
                    coarse_acc[up * 64 : (up + 1) * 64, chan * 128 : (chan + 1) * 128]
                    for chan in (2 * duo, 2 * duo + 1)
                ],
                axis=0,
            )
            piece = piece + dot_exact(sel_coarse[up], stacked)
        packed[168 + duo * 56 : 224 + duo * 56, :] = piece
    packed[504:512, :] = jnp.zeros((8, 128), F32)
    for quarter in range(4):
        for block in range(4):
            top = quarter * 128 + block * 32
            packed_out[lax.rem(quarter + 4 - place[0], 4), :, block * 128 : (block + 1) * 128] = packed[top : top + 32, :]


def whole(*dims):
    return pl.BlockSpec(
        dims, lambda step, *rest: (0,) * len(dims), pipeline_mode=pl.Buffered(1)
    )


def stem_planes(frames, stem_weight, stem_diff_weight, tables, after):
    pool, fine_tab, coarse_tab, sel_fine, sel_coarse, lanes, usable = tables
    return pl.pallas_call(
        stem_spread,
        in_specs=[VMEM] * 9,
        out_specs=[VMEM] * 4,
        out_shape=[
            held((3, 256, 1152), BF),
            held((12, 128, 896), BF),
            held((512, 432), BF),
            held((256, 1536), BF),
        ],
        scratch_shapes=[
            pltpu.VMEM((15 * SIDE, 128), F32),
            pltpu.VMEM((12 * 128, 256), F32),
            pltpu.VMEM((2, 768, SIDE), F32),
            pltpu.VMEM((168 + 672, STEMC), F32),
        ],
        compiler_params=params("stem_spread"),
        cost_estimate=cost(4e9, 1e7),
        name="stem_spread",
    )(
        frames.reshape(2, 15 * SIDE, SIDE),
        stem_weight.transpose(1, 2, 3, 0),
        stem_diff_weight.transpose(1, 2, 3, 0),
        pool, fine_tab, coarse_tab, sel_fine, sel_coarse, after,
    )


def stem_first(fine, coarse, wide_fine, wide_coarse, tables, after):
    lanes, usable = tables[5:]
    return pl.pallas_call(
        stem_forward,
        in_specs=[VMEM] * 7,
        out_specs=[VMEM] * 3,
        out_shape=[held((GROUPS, 512, 512), BF), shape((8, 128)), shape((STEMC, 128))],
        scratch_shapes=[pltpu.VMEM((128, 128), F32)],
        compiler_params=params("stem_forward"),
        cost_estimate=cost(4e9, 1e7),
        name="stem_forward",
    )(*in_vmem(fine, coarse, wide_fine, wide_coarse), lanes, usable, after)


def stem_second(raw, centre, stem_cotangent, totals, stem_gain, stem_bias, lanes, count, after):
    gain = stem_gain.reshape(1, STEMC)
    bias = stem_bias.reshape(1, STEMC)
    cot = stem_cotangent.transpose(0, 2, 3, 1)
    return pl.pallas_call(
        functools.partial(stem_middle, count=count),
        in_specs=[VMEM] * 8,
        out_specs=[VMEM] * 2,
        out_shape=[pltpu.VMEM((GROUPS, 512, 512), BF), shape((8, 128))],
        scratch_shapes=[
            pltpu.VMEM((8, 64, 128), F32),
            pltpu.VMEM((3, 64, 128), F32),
            pltpu.VMEM((64, 128), F32),
            pltpu.VMEM((2, 64, 128), F32),
        ],
        compiler_params=params("stem_middle"),
        cost_estimate=cost(8e9, 1.5e7),
        name="stem_middle",
    )(*in_vmem(raw), cot, totals, gain, bias, lanes, centre, after)


def stem_third(
    place, raw, centre, back, fine, coarse, totals, back_totals, stem_gain, tables, count, after
):
    pool, fine_tab, coarse_tab, sel_fine, sel_coarse, lanes, usable = tables
    gain = stem_gain.reshape(1, STEMC)
    return pl.pallas_call(
        functools.partial(stem_backward, count=count),
        in_specs=[SMEM] + [VMEM] * 12,
        out_specs=VMEM,
        out_shape=shape((4, 32, 512)),
        scratch_shapes=[
            pltpu.VMEM((3, 64, 128), F32),
            pltpu.VMEM((512, 128), F32),
            pltpu.VMEM((512, 512), BF),
            pltpu.VMEM((256, 256), BF),
            pltpu.VMEM((512, 432), F32),
            pltpu.VMEM((256, 1536), F32),
        ],
        compiler_params=params("stem_backward"),
        cost_estimate=cost(8e9, 2.5e7),
        name="stem_backward",
    )(place, *in_vmem(raw, back, fine, coarse), totals, back_totals, gain, sel_fine, sel_coarse, lanes, centre, after)


def put_moments(out_ref, values):
    out_ref[0:1, :] = jnp.sum(values, axis=0, keepdims=True)
    out_ref[1:2, :] = jnp.sum(values * values, axis=0, keepdims=True)


def moments(totals, count):
    average = totals[0:1] * (1.0 / count)
    square = totals[1:2] * (1.0 / count)
    return average, lax.rsqrt(square - average * average + EPS)


def affine_of(totals, count, gain, bias):
    average, scale = moments(totals, count)
    slope = gain * scale
    return slope, bias - average * slope


def back_affine(totals, sums, count, gain, middle=0.0):
    average, scale = moments(totals, count)
    first = sums[0:1] * (1.0 / count)
    second = sums[1:2] * (1.0 / count)
    on_grad = gain * scale
    on_value = -on_grad * scale * second
    return on_grad, on_value, -on_grad * first - on_value * (average - middle)


def each_piece(width, pieces):
    for left in range(0, width, 128):
        for rows in pieces:
            yield rows, slice(left, left + 128)


def lane_tile(tile, width=128):
    return pl.ds(pl.multiple_of(tile * width, width), width)


def put_wide_back(out_ref, grad, value, totals, sums, first, gain, middle, count):
    @pl.loop(0, C // 128)
    def one(tile):
        cols = lane_tile(tile)
        on_grad, on_value, constant = back_affine(
            totals[:, cols], sums[first : first + 2, cols], count, gain[:, cols], middle[:, cols]
        )
        for rows in PIECES:
            out_ref[rows, cols] = (
                grad[rows, cols].astype(F32) * on_grad + value[rows, cols].astype(F32) * on_value + constant
            ).astype(BF)


def put_back(out_ref, grad, value, coefs):
    on_grad, on_value, constant = coefs
    for rows, cols in each_piece(out_ref.shape[1], PIECES):
        out_ref[rows, cols] = (
            grad[rows, cols].astype(F32) * on_grad[:, cols]
            + value[rows, cols].astype(F32) * on_value[:, cols]
            + constant[:, cols]
        ).astype(BF)


def put_activation_back(out_ref, sums_out, grad, value, totals, gain, bias, count):
    average, scale = moments(totals, count)
    slope = gain * scale
    shift = bias - average * slope
    for left in range(0, MID, 128):
        cols = slice(left, left + 128)
        plain = jnp.zeros((8, 128), F32)
        cross = jnp.zeros((8, 128), F32)
        for rows in EIGHTS:
            pre = value[rows, cols]
            act = pre * slope[:, cols] + shift[:, cols]
            sigma = sigmoid(act)
            hidden = grad[rows, cols].astype(BF).astype(F32)
            back = hidden * (sigma * (1.0 + act * (1.0 - sigma)))
            out_ref[rows, cols] = back
            plain = plain + back
            cross = cross + back * (pre - average[:, cols])
        sums_out[0:1, cols] = jnp.sum(plain, axis=0, keepdims=True)
        sums_out[1:2, cols] = jnp.sum(cross, axis=0, keepdims=True) * scale[:, cols]


def first_matmuls(place, features, reduce_w, motion_w, reduce_out, motion_out, reduce_sum, motion_sum):
    value = dot(features[...], reduce_w[...])
    reduce_out[...] = value
    put_moments(reduce_sum, value)
    value = dot(features[...], motion_w[...])
    motion_out[...] = value
    put_moments(motion_sum, value)


def tap_mask(places, row_off, col_off):
    kept = None
    for off, base in ((row_off, 0), (col_off, 256)):
        if off:
            at = base + (128 if off > 0 else 0)
            good = places[:, at : at + 128]
            kept = good if kept is None else kept * good
    return kept


def tap_source(buffer, places, row_off, col_off, sign):
    move = sign * (7 * row_off + col_off)
    mask = tap_mask(places, sign * row_off, sign * col_off)
    value = buffer[8 + move : 8 + move + ROWS, :]
    if mask is not None:
        value = value * jnp.concatenate([mask] * (value.shape[1] // 128), axis=1)
    return value


def clear_ends(buffer):
    blank = jnp.zeros((8, buffer.shape[1]), F32)
    buffer[0:8, :] = blank
    buffer[8 + ROWS : 16 + ROWS, :] = blank


def spatial_forward(
    pre_reduce, totals, gain, bias, places, weight, hidden_out, pre_out, sums_out, buffer, *, count
):
    clear_ends(buffer)
    slope, shift = affine_of(totals[...], count, gain[...], bias[...])
    for rows, cols in each_piece(MID, PIECES):
        value = pre_reduce[rows, cols] * slope[:, cols] + shift[:, cols]
        hidden = (value * sigmoid(value)).astype(BF)
        hidden_out[rows, cols] = hidden
        buffer[8 + rows.start : 8 + rows.stop, cols] = hidden.astype(F32)
    for tap in range(9):
        row_off, col_off = tap // 3 - 1, tap % 3 - 1
        source = tap_source(buffer, places, row_off, col_off, 1).astype(BF)
        value = dot(source, weight[tap * MID : (tap + 1) * MID, :])
        if tap == 0:
            pre_out[...] = value
        else:
            pre_out[...] += value
    put_moments(sums_out, pre_out[...])


def wide_product(hidden, weight, pre_out, sums_out, mid_out):
    @pl.loop(0, C // TILE)
    def one(tile):
        cols = lane_tile(tile, TILE)
        value = dot(hidden[...], weight[:, cols])
        total = jnp.sum(value, axis=0, keepdims=True)
        sums_out[0:1, cols] = total
        sums_out[1:2, cols] = jnp.sum(value * value, axis=0, keepdims=True)
        middle = total * (1.0 / ROWS)
        mid_out[:, cols] = middle
        pre_out[:, cols] = (value - middle).astype(BF)


def expand_forward(
    pre_spatial, totals, gain, bias, weight, hidden_out, pre_out, sums_out, mid_out, *, count
):
    slope, shift = affine_of(totals[...], count, gain[...], bias[...])
    for rows, cols in each_piece(MID, PIECES):
        value = pre_spatial[rows, cols] * slope[:, cols] + shift[:, cols]
        hidden_out[rows, cols] = (value * sigmoid(value)).astype(BF)
    wide_product(hidden_out, weight, pre_out, sums_out, mid_out)


def at(buffer, rows, move=0):
    return buffer[64 + rows.start + move : 64 + rows.stop + move, :]


def put(buffer, rows, value):
    buffer[64 + rows.start : 64 + rows.stop, :] = value


def clear_margins(buffers):
    for buffer in buffers:
        buffer[0:64, :] = jnp.zeros((64, 128), F32)
        buffer[64 + ROWS : 128 + ROWS, :] = jnp.zeros((64, 128), F32)


def mask_of(places, rows, which):
    return places[rows, which * 128 : (which + 1) * 128]


UP, DOWN, LEFT, RIGHT = range(4)


def three(buffer, places, rows, move, before, after):
    return (
        at(buffer, rows, -move) * mask_of(places, rows, before),
        at(buffer, rows),
        at(buffer, rows, move) * mask_of(places, rows, after),
    )


def box_rows(buffer, places, out):
    for rows in EIGHTS:
        first, second, third = three(buffer, places, rows, 1, LEFT, RIGHT)
        put(out, rows, first + second + third)


def box_columns(buffer, places, rows):
    first, second, third = three(buffer, places, rows, 7, UP, DOWN)
    return (first + second + third) * (1.0 / 9.0)


def kept(value, rows, keep):
    first, last = rows.start // 49, (rows.stop - 1) // 49
    if first == last:
        return value * keep[0, first]
    lines = lax.broadcasted_iota(jnp.int32, value.shape, 0)
    return value * jnp.where(lines < last * 49 - rows.start, keep[0, first], keep[0, last])


def change_and_average(pre_motion, slope, keep, places, cols, spare, change, average):
    for rows in EIGHTS:
        put(spare, rows, pre_motion[rows, cols] * slope)
    for rows in EIGHTS:
        put(change, rows, kept(at(spare, rows, 49) - at(spare, rows), rows, keep))
    box_rows(change, places, spare)
    for rows in EIGHTS:
        put(average, rows, box_columns(spare, places, rows))


def motion_forward(
    pre_motion, totals, gain, keep, places, depth, weight, after, mixed_out, pre_out, sums_out, mid_out,
    spare, change, average, lines_a, lines_b, lines_c, *, count
):
    clear_margins((spare, change, average, lines_a, lines_b, lines_c))

    @pl.loop(0, MID // 128)
    def one(tile):
        cols = pl.ds(pl.multiple_of(tile * 128, 128), 128)
        scale = moments(totals[:, cols], count)[1]
        change_and_average(
            pre_motion, gain[:, cols] * scale, keep, places, cols, spare, change, average
        )
        for rows in EIGHTS:
            near = three(change, places, rows, 1, LEFT, RIGHT)
            wide = three(average, places, rows, 1, LEFT, RIGHT)
            for row, out in enumerate((lines_a, lines_b, lines_c)):
                line = None
                for col in range(3):
                    for scale_at, source in enumerate((near, wide)):
                        term = source[col] * depth[scale_at, row, col : col + 1, cols]
                        line = term if line is None else line + term
                put(out, rows, line)
        for rows in PIECES:
            value = (
                at(lines_b, rows)
                + at(lines_a, rows, -7) * mask_of(places, rows, UP)
                + at(lines_c, rows, 7) * mask_of(places, rows, DOWN)
            )
            mixed_out[rows, cols] = value.astype(BF)

    wide_product(mixed_out, weight, pre_out, sums_out, mid_out)


def gate_kernel(
    own, pre_expand, pre_excite, features, cotangent, expand_tot, excite_tot, expand_mid, excite_mid,
    expand_gain, expand_bias, excite_gain, excite_bias,
    mine_out, other_out, direct_out, comb_out, gate_out, sums_out, output_ref, direct_ref, *, count
):
    @pl.loop(0, C // 128)
    def one(tile):
        cols = lane_tile(tile)
        e_mean, e_scale = moments(expand_tot[:, cols], count)
        x_mean, x_scale = moments(excite_tot[:, cols], count)
        e_mean = e_mean - expand_mid[:, cols]
        x_mean = x_mean - excite_mid[:, cols]
        e_slope = expand_gain[:, cols] * e_scale
        e_shift = expand_bias[:, cols] - e_mean * e_slope
        x_slope = excite_gain[:, cols] * x_scale
        x_shift = excite_bias[:, cols] - x_mean * x_slope
        sums = [jnp.zeros((8, 128), F32)] * 4
        for rows in PIECES:
            feats = features[rows, cols].astype(F32)
            seed = cotangent[rows, cols].astype(F32)
            pre_e = pre_expand[rows, cols].astype(F32)
            pre_x = pre_excite[rows, cols].astype(F32)
            branch = (pre_e * e_slope + e_shift).astype(BF).astype(F32)
            gate = sigmoid(pre_x * x_slope + x_shift)
            lifted = feats * gate
            combined = branch + lifted
            sigma = sigmoid(combined)
            output = combined * sigma
            output_ref[rows, cols] = output.astype(BF)
            grad = seed * (sigma + output * (1.0 - sigma))
            direct_ref[rows, cols] = (grad * gate).astype(BF)
            rounded = grad.astype(BF)
            comb_out[rows, cols] = rounded
            rounded = rounded.astype(F32)
            grad_gate = grad * lifted * (1.0 - gate)
            gate_out[rows, cols] = grad_gate.astype(BF)
            terms = (
                rounded,
                rounded * (pre_e - e_mean),
                grad_gate,
                grad_gate * (pre_x - x_mean),
            )
            for spot, value in enumerate(terms):
                for up in range(0, value.shape[0], 8):
                    sums[spot] = sums[spot] + value[up : up + 8]
        finals = [jnp.sum(value, axis=0, keepdims=True) for value in sums]
        sums_out[0:1, cols] = finals[0]
        sums_out[1:2, cols] = finals[1] * e_scale
        sums_out[2:3, cols] = finals[2]
        sums_out[3:4, cols] = finals[3] * x_scale

    mine, other = lane_tile(own[0], MID), lane_tile(own[0] ^ 1, MID)
    mine_out[...] = output_ref[:, mine]
    other_out[...] = output_ref[:, other]
    direct_out[:, :MID] = direct_ref[:, mine]
    direct_out[:, MID:] = direct_ref[:, other]


def expand_backward(
    own, grad, pre_expand, totals, sums, gain, middle, weight, pre_spatial, s_totals, s_gain, s_bias,
    own_out, grad_out, sums_out, value_ref, acc, *, count
):
    put_wide_back(value_ref, grad, pre_expand, totals, sums, 0, gain, middle, count)
    own_out[:, :MID] = value_ref[:, lane_tile(own[0], MID)]
    own_out[:, MID:] = value_ref[:, lane_tile(own[0] ^ 1, MID)]
    acc[...] = dot(value_ref[...], weight[...], NT)
    put_activation_back(
        grad_out, sums_out, acc, pre_spatial, s_totals[...], s_gain[...], s_bias[...], count
    )


def excite_backward(
    own, grad, pre_excite, totals, sums, gain, middle, weight, pre_motion, m_totals, m_gain, keep,
    places, depth, own_out, grad_out, sums_out, depth_out, value_ref, acc,
    spare, change, average, seed, pull_a, pull_b, pull_c, near_out, wide_out, *, count
):
    put_wide_back(value_ref, grad, pre_excite, totals, sums, 2, gain, middle, count)
    own_out[:, :MID] = value_ref[:, lane_tile(own[0], MID)]
    own_out[:, MID:] = value_ref[:, lane_tile(own[0] ^ 1, MID)]
    acc[...] = dot(value_ref[...], weight[...], NT)
    clear_margins((spare, change, average, seed, pull_a, pull_b, pull_c, near_out, wide_out))

    @pl.loop(0, MID // 128)
    def one(tile):
        cols = pl.ds(pl.multiple_of(tile * 128, 128), 128)
        mean, scale = moments(m_totals[:, cols], count)
        change_and_average(
            pre_motion, m_gain[:, cols] * scale, keep, places, cols, spare, change, average
        )
        for rows in EIGHTS:
            put(seed, rows, acc[rows, cols])
        for base, source, out in ((0, change, near_out), (9, average, wide_out)):
            totals_of = [jnp.zeros((8, 128), F32)] * 9
            for rows in EIGHTS:
                later, now, before = three(seed, places, rows, -7, DOWN, UP)
                taps = three(source, places, rows, 1, LEFT, RIGHT)
                for col, pull in enumerate((pull_a, pull_b, pull_c)):
                    total = None
                    for row, line in enumerate((later, now, before)):
                        spot = row * 3 + col
                        term = line * depth[base // 9, row, col : col + 1, cols]
                        total = term if total is None else total + term
                        totals_of[spot] = totals_of[spot] + line * taps[col]
                    put(pull, rows, total)
            for spot in range(9):
                depth_out[base + spot : base + spot + 1, cols] = jnp.sum(
                    totals_of[spot], axis=0, keepdims=True
                )
            for rows in EIGHTS:
                put(
                    out,
                    rows,
                    at(pull_b, rows)
                    + at(pull_a, rows, 1) * mask_of(places, rows, RIGHT)
                    + at(pull_c, rows, -1) * mask_of(places, rows, LEFT),
                )
        box_rows(wide_out, places, spare)
        for rows in EIGHTS:
            value = at(near_out, rows) + box_columns(spare, places, rows)
            put(change, rows, kept(value, rows, keep))
        plain = jnp.zeros((8, 128), F32)
        cross = jnp.zeros((8, 128), F32)
        for rows in EIGHTS:
            value = at(change, rows, -49) - at(change, rows)
            grad_out[rows, cols] = value
            plain = plain + value
            cross = cross + value * (pre_motion[rows, cols] - mean)
        sums_out[0:1, cols] = jnp.sum(plain, axis=0, keepdims=True)
        sums_out[1:2, cols] = jnp.sum(cross, axis=0, keepdims=True) * scale


def spatial_backward(
    own, grad, pre_spatial, totals, sums, gain, places, weight, pre_reduce, r_totals, r_gain, r_bias,
    m_grad, pre_motion, m_totals, m_sums, m_gain,
    taps_out, grad_out, sums_out, motion_out, motion_own, buffer, source_ref, acc, *, count
):
    clear_ends(buffer)
    on_grad, on_value, constant = back_affine(totals[...], sums[...], count, gain[...])
    for rows, cols in each_piece(MID, EIGHTS):
        buffer[8 + rows.start : 8 + rows.stop, cols] = (
            (
                grad[rows, cols] * on_grad[:, cols]
                + pre_spatial[rows, cols] * on_value[:, cols]
                + constant[:, cols]
            )
            .astype(BF)
            .astype(F32)
        )
    mine = pl.ds(pl.multiple_of((own[0] // 2) * 256, 256), 256)
    for tap in range(9):
        row_off, col_off = tap // 3 - 1, tap % 3 - 1
        source_ref[...] = tap_source(buffer, places, row_off, col_off, -1).astype(BF)
        taps_out[:, tap * 256 : (tap + 1) * 256] = source_ref[:, mine]
        value = dot(source_ref[...], weight[tap * MID : (tap + 1) * MID, :], NT)
        if tap == 0:
            acc[...] = value
        else:
            acc[...] += value
    put_activation_back(
        grad_out, sums_out, acc, pre_reduce, r_totals[...], r_gain[...], r_bias[...], count
    )
    put_back(
        motion_out, m_grad, pre_motion, back_affine(m_totals[...], m_sums[...], count, m_gain[...])
    )
    motion_own[...] = motion_out[:, mine]


def reduce_backward(
    own, grad, pre_reduce, totals, sums, gain, mine_w, other_w, motion, mine_m, other_m, direct, lines,
    own_out, mine_out, other_out, tail_out, value_ref, tail_ref, *, count
):
    put_back(value_ref, grad, pre_reduce, back_affine(totals[...], sums[...], count, gain[...]))
    tail_ref[...] = jnp.zeros_like(tail_ref)
    for row in range(6):
        ref, at = (lines, row) if row < 4 else (sums, row - 4)
        for side in range(2):
            tail_ref[2 * row + side : 2 * row + side + 1, :] = ref[
                at : at + 1, side * 256 : (side + 1) * 256
            ]
    tail_out[...] = tail_ref[...].astype(BF)
    own_out[...] = value_ref[:, pl.ds(pl.multiple_of((own[0] // 2) * 256, 256), 256)]
    for out, reduce_w, motion_w, left in (
        (other_out, other_w, other_m, MID),
        (mine_out, mine_w, mine_m, 0),
    ):
        value = dot(value_ref[...], reduce_w[...], NT) + dot(motion[...], motion_w[...], NT)
        out[...] = (value + direct[:, left : left + MID].astype(F32)).astype(BF)


def owners(place, sizes):
    away = lambda at, axis, size: lax.rem(at + size - place[axis], size)
    for z in range(sizes[0]):
        for y in range(sizes[1]):
            for c in range(sizes[2]):
                owner = (z * sizes[1] + y) * sizes[2] + c
                yield owner, (away(c, 1, sizes[2]), away(y, 2, sizes[1]), away(z, 3, sizes[0]))


def spatial_weight_kernel(place, hidden, taps, motion, out, turned_ref, *, sizes):
    turned_ref[...] = jnp.transpose(hidden[...].astype(F32)).astype(BF)
    clips = sizes[0] * sizes[1] * sizes[2]
    spots = dict(owners(place, sizes))
    share = 9 * MID // clips
    for tap in range(9):
        value = dot(turned_ref[...], taps[:, tap * 256 : (tap + 1) * 256]).astype(BF)
        for top in range(0, MID, 16):
            row = tap * MID + top
            out[*spots[row // share], row % share : row % share + 16, :] = value[top : top + 16]
    for owner, spot in spots.items():
        out[*spot, share:, :] = motion[owner * (C // clips) : (owner + 1) * (C // clips), :]


def early_weight_kernel(place, hidden, expand, mixed, excite, out, turned_ref, *, sizes):
    rows = MID // (sizes[0] * sizes[1] * sizes[2])
    spots = dict(owners(place, sizes))
    for base, left, right in ((0, hidden, expand), (4, mixed, excite)):
        turned_ref[...] = jnp.transpose(left[...].astype(F32)).astype(BF)
        for block in range(4):
            value = dot(turned_ref[...], right[:, block * 256 : (block + 1) * 256]).astype(BF)
            for owner, spot in spots.items():
                out[*spot, (base + block) * rows : (base + block + 1) * rows, :] = value[
                    owner * rows : (owner + 1) * rows
                ]


def pack_kernel(early, stem, gate, depth, out, buffer):
    buffer[...] = jnp.zeros_like(buffer)
    for side in range(2):
        cols = slice(side * 256, (side + 1) * 256)
        buffer[32 * side : 32 * side + 32, :] = stem[:, cols]
        buffer[96 + 18 * side : 114 + 18 * side, :] = depth[:, cols]
    for block in range(8):
        buffer[64 + 4 * block : 68 + 4 * block, :] = gate[:, block * 256 : (block + 1) * 256]
    out[0:128, :] = early[...]
    out[128:272, :] = buffer[...].astype(BF)


def late_weight_kernel(place, values, out, *, sizes):
    rows = out.shape[3]
    for owner, spot in owners(place, sizes):
        out[*spot] = values[owner * rows : (owner + 1) * rows, :]


def join_kernel(own, mine, got, out):
    first = jnp.where(own[0] % 2 == 0, mine[...].astype(F32), got[...].astype(F32))
    second = jnp.where(own[0] % 2 == 0, got[...].astype(F32), mine[...].astype(F32))
    out[...] = jnp.concatenate([first, second], axis=0).astype(BF)


def unpack_kernel(
    own, rest_0, rest_1, rest_2, rest_3, early_0, early_1, early_2, early_3,
    mine, got,
    reduce_out, spatial_out, expand_out, motion_out, excite_out, fine_out, coarse_out, grad_out,
    depth_out, e_bias, e_gain, x_bias, x_gain, m_gain, s_bias, s_gain, r_bias, r_gain,
    packed_ref, *, clips
):
    join_kernel(own, mine, got, grad_out)
    wide = early_0[192:224, :].astype(F32) + early_1[192:224, :].astype(F32)
    for row, out in enumerate((e_bias, e_gain, x_bias, x_gain)):
        for block in range(8):
            out[block * 256 : (block + 1) * 256] = wide[4 * block + row]
    both = early_0[224:272, :].astype(F32) + early_1[224:272, :].astype(F32)
    for spot in range(18):
        for side in range(2):
            at = 18 * side + spot
            cols = slice(side * 256, (side + 1) * 256)
            depth_out[spot // 3 % 3, spot % 3, spot // 9 : spot // 9 + 1, cols] = both[at : at + 1]
    last = rest_0.shape[0] - 16
    both = rest_0[last:, :].astype(F32) + rest_1[last:, :].astype(F32)
    for row, out in ((1, m_gain), (2, s_bias), (3, s_gain), (4, r_bias), (5, r_gain)):
        for side in range(2):
            out[side * 256 : (side + 1) * 256] = both[2 * row + side]
    cuts = (9 * MID // clips, (9 * MID + C) // clips, (9 * MID + 2 * C) // clips)
    half = own[0] // 2
    for side, left, right in ((half, rest_0, rest_1), (1 - half, rest_2, rest_3)):
        value = left[...].astype(F32) + right[...].astype(F32)
        cols = pl.ds(pl.multiple_of(side * 256, 256), 256)
        spatial_out[:, cols] = value[: cuts[0]]
        motion_out[:, cols] = value[cuts[0] : cuts[1]]
        reduce_out[:, cols] = value[cuts[1] : cuts[2]]
    rows = MID // clips
    for flip, left, right in (
        (0, (early_0, 0), (early_1, 1)),
        (1, (early_0, 1), (early_1, 0)),
        (2, (early_2, 0), (early_3, 1)),
        (3, (early_2, 1), (early_3, 0)),
    ):
        for base, out in ((0, expand_out), (4, excite_out)):
            for block in range(2):
                value = None
                for ref, spot in (left, right):
                    top = (base + 2 * spot + block) * rows
                    part = ref[top : top + rows, :].astype(F32)
                    value = part if value is None else value + part
                out[:, pl.ds(pl.multiple_of((own[0] ^ flip) * MID + block * 256, 256), 256)] = value
    base = 8 * rows
    for flip, ref in enumerate((early_0, early_1, early_2, early_3)):
        for block in range(4):
            top, left = base + (block // 2) * 32, (block % 2) * 128
            at = pl.multiple_of((own[0] ^ flip) * 128 + block * 32, 32)
            packed_ref[pl.ds(at, 32), :] = ref[top : top + 32, left : left + 128].astype(F32)
    for chan in range(3):
        for row in range(7):
            at = chan * 56 + row * 8
            fine_out[chan, row] = packed_ref[at : at + 7, 0:64]
    for chan in range(12):
        side = (chan % 2) * 64
        for row in range(7):
            at = 168 + (chan // 2) * 56 + row * 8
            coarse_out[chan, row] = packed_ref[at : at + 7, side : side + 64]


def with_own(kernel, own, grid, in_specs, out_specs, out_shape, scratch, args, flops, nbytes, name):
    if not grid:
        return pl.pallas_call(
            kernel,
            in_specs=[SMEM] + in_specs,
            out_specs=out_specs,
            out_shape=out_shape,
            scratch_shapes=scratch,
            compiler_params=params(name),
            cost_estimate=cost(flops, nbytes),
            name=name,
        )(own, *args)
    return pl.pallas_call(
        kernel,
        grid_spec=pltpu.PrefetchScalarGridSpec(
            num_scalar_prefetch=1,
            grid=grid,
            in_specs=in_specs,
            out_specs=out_specs,
            scratch_shapes=scratch,
        ),
        out_shape=out_shape,
        compiler_params=params(name),
        cost_estimate=cost(flops, nbytes),
        name=name,
    )(own, *args)


def place_table():
    rows = np.arange(ROWS)
    down = (rows % 49) // 7
    right = rows % 7
    kept = [down >= 1, down <= FEAT - 2, right >= 1, right <= FEAT - 2]
    return jnp.asarray(np.concatenate([np.repeat(k[:, None], 128, 1) for k in kept], axis=1), F32)


def keep_pairs(valid_rows, video_rows):
    valid_float = valid_rows.astype(F32)
    same_video = (video_rows[:, 1:] == video_rows[:, :-1]).astype(F32)
    pair_keep = valid_float[:, 1:] * valid_float[:, :-1] * same_video
    return jnp.concatenate([pair_keep, jnp.zeros_like(pair_keep[:, :1])], axis=1)


def on_device(
    features,
    out_cotangent,
    seg_valid,
    seg_video,
    frames,
    stem_cotangent,
    stem_weight,
    stem_diff_weight,
    stem_gain,
    stem_bias,
    reduce_weight,
    reduce_gain,
    reduce_bias,
    spatial_weight,
    spatial_gain,
    spatial_bias,
    expand_weight,
    expand_gain,
    expand_bias,
    motion_weight,
    motion_gain,
    depth_weight,
    excite_weight,
    excite_gain,
    excite_bias,
):
    clips = lax.axis_size("z") * lax.axis_size("y") * lax.axis_size("c")
    count = float(clips * ROWS)
    stem_count = float(clips * lax.axis_size("x") * (SIDE // 2) ** 2)
    here = lax.axis_index("x")
    micro = here % 2
    own = jnp.stack([here] + [lax.axis_index(axis) for axis in ("c", "y", "z")]).astype(jnp.int32)
    places = place_table()

    def of_micro(rows):
        return lax.dynamic_index_in_dim(
            rows.reshape(MICRO, rows.shape[0] // MICRO, rows.shape[1]), micro, 0, False
        )

    feats = of_micro(features)
    seeds = of_micro(out_cotangent)
    keep = of_micro(keep_pairs(seg_valid, seg_video))
    line = lambda vector: vector.reshape(1, -1)
    reduce_gain, reduce_bias = line(reduce_gain), line(reduce_bias)
    spatial_gain, spatial_bias = line(spatial_gain), line(spatial_bias)
    expand_gain, expand_bias = line(expand_gain), line(expand_bias)
    excite_gain, excite_bias = line(excite_gain), line(excite_bias)
    motion_gain = line(motion_gain)

    tables = stem_tables()
    lanes = tables[5]
    column = lambda rows, width: pl.BlockSpec((rows, width), lambda step, *rest: (0, step))
    pre_reduce, pre_motion, reduce_sum, motion_sum = pl.pallas_call(
        first_matmuls,
        grid=(2,),
        in_specs=[SMEM, whole(ROWS, C), column(C, 256), column(C, 256)],
        out_specs=[column(ROWS, 256), column(ROWS, 256), column(2, 256), column(2, 256)],
        out_shape=[held((ROWS, MID)), held((ROWS, MID)), shape((2, MID)), shape((2, MID))],
        compiler_params=params("first_matmuls"),
        cost_estimate=cost(1.7e9, 1e7),
        name="first_matmuls",
    )(own, *in_vmem(feats), reduce_weight, motion_weight)
    first_wide = core_sum(jnp.concatenate([reduce_sum, motion_sum], axis=1))
    fine, coarse, wide_fine, wide_coarse = stem_planes(
        frames, stem_weight, stem_diff_weight, tables, first_wide
    )
    first_wide = ring_sum(first_wide, "y")
    raw, stem_sum, centre = stem_first(fine, coarse, wide_fine, wide_coarse, tables, first_wide)
    first_tot = ring_sum(first_wide, "z")
    reduce_tot, motion_tot = first_tot[:, :MID], first_tot[:, MID:]
    stem_sum = ring_sum(stem_sum[:2], "x")

    hidden_one, pre_spatial, spatial_sum = pl.pallas_call(
        functools.partial(spatial_forward, count=count),
        in_specs=[VMEM] * 6,
        out_specs=[VMEM] * 3,
        out_shape=[held((ROWS, MID), BF), held((ROWS, MID)), shape((2, MID))],
        scratch_shapes=[pltpu.VMEM((ROWS + 16, MID), F32)],
        compiler_params=params("spatial_forward"),
        cost_estimate=cost(1.9e9, 8e6),
        name="spatial_forward",
    )(*in_vmem(pre_reduce), reduce_tot, reduce_gain, reduce_bias, places, spatial_weight)

    spatial_wide = core_sum(jnp.concatenate([spatial_sum, stem_sum], axis=1))
    mixed, pre_excite, excite_sum, excite_mid = pl.pallas_call(
        functools.partial(motion_forward, count=count),
        in_specs=[VMEM] * 3 + [SMEM] + [VMEM] * 4,
        out_specs=[VMEM] * 4,
        out_shape=[held((ROWS, MID), BF), held((ROWS, C), BF), shape((2, C)), shape((1, C))],
        scratch_shapes=[pltpu.VMEM((ROWS + 128, 128), F32)] * 6,
        compiler_params=params("motion_forward"),
        cost_estimate=cost(2e9, 1.2e7),
        name="motion_forward",
    )(*in_vmem(pre_motion), motion_tot, motion_gain, keep, places, depth_weight, excite_weight, spatial_wide)
    spatial_wide = ring_sum(ring_sum(spatial_wide, "y"), "z")
    spatial_tot, stem_tot = spatial_wide[:, :MID], spatial_wide[:, MID:]
    stem_tot = jnp.pad(stem_tot, ((0, 6), (0, 0)))

    hidden_two, pre_expand, expand_sum, expand_mid = pl.pallas_call(
        functools.partial(expand_forward, count=count),
        in_specs=[VMEM] * 5,
        out_specs=[VMEM] * 4,
        out_shape=[held((ROWS, MID), BF), held((ROWS, C), BF), shape((2, C)), shape((1, C))],
        compiler_params=params("expand_forward"),
        cost_estimate=cost(1e9, 1e7),
        name="expand_forward",
    )(*in_vmem(pre_spatial), spatial_tot, spatial_gain, spatial_bias, expand_weight)
    expand_wide = core_sum(jnp.concatenate([expand_sum, excite_sum], axis=1))
    back, back_sum = stem_second(
        raw, centre, stem_cotangent, stem_tot, stem_gain, stem_bias, lanes, stem_count, expand_wide
    )
    expand_wide = ring_sum(ring_sum(expand_wide, "y"), "z")
    expand_tot, excite_tot = expand_wide[:, :C], expand_wide[:, C:]
    back_sum = ring_sum(back_sum[:2], "x")

    mine, other, direct, grad_comb, grad_gate, gate_sum = with_own(
        functools.partial(gate_kernel, count=count),
        own,
        (),
        [VMEM] * 12,
        [VMEM] * 6,
        [
            shape((ROWS, MID), BF), shape((ROWS, MID), BF), held((ROWS, 2 * MID), BF),
            held((ROWS, C), BF), held((ROWS, C), BF), shape((4, C)),
        ],
        [pltpu.VMEM((ROWS, C), BF)] * 2,
        (
            *in_vmem(pre_expand, pre_excite, feats, seeds), expand_tot, excite_tot, expand_mid, excite_mid,
            expand_gain, expand_bias, excite_gain, excite_bias,
        ),
        2e9,
        2e7,
        "gate",
    )
    gate_wide = sum_dp(
        jnp.concatenate([gate_sum, jnp.pad(back_sum, ((0, 2), (0, 0)))], axis=1)
    )
    gate_tot, back_tot = gate_wide[:, :C], gate_wide[:2, C:]
    back_tot = jnp.pad(back_tot, ((0, 6), (0, 0)))
    back_both = back_tot[0] + back_tot[1]
    stem_gain_grad, stem_bias_grad = back_both[64:], back_both[:64]

    got_result = from_peer(other, 1)

    expand_own, grad_spatial, spatial_back = with_own(
        functools.partial(expand_backward, count=count),
        own,
        (),
        [VMEM] * 11,
        [VMEM] * 3,
        [held((ROWS, 2 * MID), BF), held((ROWS, MID)), shape((2, MID))],
        [pltpu.VMEM((ROWS, C), BF), pltpu.VMEM((ROWS, MID), F32)],
        (
            *in_vmem(grad_comb, pre_expand), expand_tot, gate_tot, expand_gain, expand_mid, expand_weight,
            *in_vmem(pre_spatial), spatial_tot, spatial_gain, spatial_bias,
        ),
        1e9,
        1e7,
        "expand_backward",
    )

    excite_own, grad_reduced, motion_back, depth_part = with_own(
        functools.partial(excite_backward, count=count),
        own,
        (),
        [VMEM] * 10 + [SMEM] + [VMEM] * 2,
        [VMEM] * 4,
        [held((ROWS, 2 * MID), BF), held((ROWS, MID)), shape((2, MID)), shape((18, MID))],
        [pltpu.VMEM((ROWS, C), BF), pltpu.VMEM((ROWS, MID), F32)]
        + [pltpu.VMEM((ROWS + 128, 128), F32)] * 9,
        (
            *in_vmem(grad_gate, pre_excite), excite_tot, gate_tot, excite_gain, excite_mid, excite_weight,
            *in_vmem(pre_motion), motion_tot, motion_gain, keep, places, depth_weight,
        ),
        2e9,
        1e7,
        "excite_backward",
    )
    across = lambda left, right: dot(left, right, TN).astype(BF)
    sizes = [lax.axis_size(axis) for axis in ("z", "y", "c")]
    early = pl.pallas_call(
        functools.partial(early_weight_kernel, sizes=sizes),
        in_specs=[SMEM] + [VMEM] * 4,
        out_specs=VMEM,
        out_shape=shape((*sizes[::-1], 8 * (MID // clips), 256), BF),
        scratch_shapes=[pltpu.VMEM((MID, ROWS), BF)],
        compiler_params=params("early_weight"),
        cost_estimate=cost(1e9, 5e6),
        name="early_weight",
    )(own, *in_vmem(hidden_two, expand_own, mixed, excite_own))
    back_all = core_sum(jnp.concatenate([motion_back, spatial_back, depth_part], axis=0))
    stem_packed = stem_third(
        own, raw, centre, back, fine, coarse, stem_tot, back_tot, stem_gain, tables, stem_count,
        back_all,
    )
    back_all, early = tie(back_all, early)
    early = scatter_lead(early, "c")
    back_all = ring_sum(back_all, "y")
    back_all, early = tie(back_all, early)
    early = scatter_lead(early, "y")
    back_all = ring_sum(back_all, "z")
    stem_quarter = scatter_lead(stem_packed, "x", F32)
    motion_back_tot, spatial_back_tot = back_all[:2], back_all[2:4]

    taps, grad_reduce, reduce_back, motion_full, motion_own = with_own(
        functools.partial(spatial_backward, count=count),
        own,
        (1,),
        [
            whole(ROWS, MID), whole(ROWS, MID), whole(2, MID), whole(2, MID), whole(1, MID),
            whole(ROWS, 512), whole(9 * MID, MID), whole(ROWS, MID), whole(2, MID),
            whole(1, MID), whole(1, MID),
            whole(ROWS, MID), whole(ROWS, MID), whole(2, MID), whole(2, MID), whole(1, MID),
        ],
        [
            whole(ROWS, 9 * 256), whole(ROWS, MID), whole(2, MID), whole(ROWS, MID), whole(ROWS, 256),
        ],
        [
            held((ROWS, 9 * 256), BF), held((ROWS, MID)), shape((2, MID)),
            held((ROWS, MID), BF), shape((ROWS, 256), BF),
        ],
        [
            pltpu.VMEM((ROWS + 16, MID), F32),
            pltpu.VMEM((ROWS, MID), BF),
            pltpu.VMEM((ROWS, MID), F32),
        ],
        (
            *in_vmem(grad_spatial, pre_spatial), spatial_tot, spatial_back_tot, spatial_gain, places,
            spatial_weight, *in_vmem(pre_reduce), reduce_tot, reduce_gain, reduce_bias,
            *in_vmem(grad_reduced, pre_motion), motion_tot, motion_back_tot, motion_gain,
        ),
        2e9,
        1e7,
        "spatial_backward",
    )
    mine_rows = pl.BlockSpec((MID, MID), lambda step, own_ref: (own_ref[0], 0))
    other_rows = pl.BlockSpec((MID, MID), lambda step, own_ref: (own_ref[0] ^ 1, 0))
    middle = pl.pallas_call(
        functools.partial(spatial_weight_kernel, sizes=sizes),
        in_specs=[SMEM] + [VMEM] * 3,
        out_specs=VMEM,
        out_shape=shape((*sizes[::-1], (9 * MID + C) // clips, 256), BF),
        scratch_shapes=[pltpu.VMEM((MID, ROWS), BF)],
        compiler_params=params("spatial_weight"),
        cost_estimate=cost(1e9, 5e6),
        name="spatial_weight",
    )(own, *in_vmem(hidden_one, taps), across(feats, motion_own))

    reduce_back = core_sum(jnp.concatenate([reduce_back, stem_quarter], axis=0))
    reduce_back, middle, early, got_result = tie(reduce_back, middle, early, got_result)
    early = scatter_lead(early, "z")
    middle = scatter_lead(middle, "c")
    reduce_back = ring_sum(reduce_back, "y")
    reduce_back, middle, early = tie(reduce_back, middle, early)
    reduce_back = ring_sum(reduce_back, "z")
    middle = scatter_lead(middle, "y")
    reduce_back_tot = reduce_back[:2]
    early = gather_x(
        pl.pallas_call(
            pack_kernel,
            in_specs=[VMEM] * 4,
            out_specs=VMEM,
            out_shape=shape((272, 256), BF),
            scratch_shapes=[pltpu.VMEM((144, 256), F32)],
            compiler_params=params("pack"),
            cost_estimate=cost(1e5, 5e5),
            name="pack",
        )(early, reduce_back[2:], gate_tot, back_all[4:])
    )

    reduce_own, mine_grad, other_grad, tail = with_own(
        functools.partial(reduce_backward, count=count),
        own,
        (1,),
        [
            whole(ROWS, MID), whole(ROWS, MID), whole(2, MID), whole(2, MID), whole(1, MID),
            mine_rows, other_rows, whole(ROWS, MID), mine_rows, other_rows, whole(ROWS, 2 * MID),
            whole(22, MID),
        ],
        [whole(ROWS, 256), whole(ROWS, MID), whole(ROWS, MID), whole(16, 256)],
        [
            shape((ROWS, 256), BF), shape((ROWS, MID), BF), shape((ROWS, MID), BF), shape((16, 256), BF),
        ],
        [pltpu.VMEM((ROWS, MID), BF), pltpu.VMEM((16, 256), F32)],
        (
            *in_vmem(grad_reduce, pre_reduce), reduce_tot, reduce_back_tot, reduce_gain,
            reduce_weight, reduce_weight, *in_vmem(motion_full), motion_weight, motion_weight,
            *in_vmem(direct), back_all,
        ),
        5e8,
        8e6,
        "reduce_backward",
    )
    got_grad = from_peer(other_grad, 1)
    late = pl.pallas_call(
        functools.partial(late_weight_kernel, sizes=sizes),
        in_specs=[SMEM, VMEM],
        out_specs=VMEM,
        out_shape=shape((*sizes[::-1], C // clips, 256), BF),
        compiler_params=params("late_weight"),
        cost_estimate=cost(1e5, 2e6),
        name="late_weight",
    )(own, across(feats, reduce_own))
    late = scatter_lead(late, "c")
    late, middle, *early = tie(late, middle, *early)
    late = scatter_lead(late, "y")
    late, got_grad = tie(late, got_grad)
    rest = scatter_lead(jnp.concatenate([middle, late], axis=1), "z")
    rest = gather_x(jnp.concatenate([rest, tail], axis=0))
    result = with_own(
        join_kernel,
        own,
        (1,),
        [whole(ROWS, MID), whole(ROWS, MID)],
        whole(2 * ROWS, MID),
        shape((2 * ROWS, MID), BF),
        [],
        (mine, got_result),
        1e5,
        2e6,
        "join_result",
    )

    (
        reduce_grad, spatial_grad, expand_grad, motion_grad, excite_grad,
        stem_weight_grad, stem_diff_grad, features_grad, depth_grad, *vectors,
    ) = with_own(
        functools.partial(unpack_kernel, clips=clips),
        own,
        (1,),
        [whole(*part.shape) for part in rest]
        + [whole(*part.shape) for part in early]
        + [
            whole(ROWS, MID), whole(ROWS, MID),
        ],
        [
            whole(C // clips, MID), whole(9 * MID // clips, MID), whole(MID // clips, C),
            whole(C // clips, MID), whole(MID // clips, C),
            whole(3, 7, 7, STEMC), whole(12, 7, 7, STEMC), whole(2 * ROWS, MID),
            whole(3, 3, 2, MID), *[whole(C)] * 4, *[whole(MID)] * 5,
        ],
        [
            shape((C // clips, MID)), shape((9 * MID // clips, MID)), shape((MID // clips, C)),
            shape((C // clips, MID)), shape((MID // clips, C)),
            shape((3, 7, 7, STEMC)), shape((12, 7, 7, STEMC)), shape((2 * ROWS, MID), BF),
            shape((3, 3, 2, MID)), *[shape((C,))] * 4, *[shape((MID,))] * 5,
        ],
        [pltpu.VMEM((512, 128), F32)],
        (*rest, *early, mine_grad, got_grad),
        1e6,
        6e6,
        "unpack",
    )
    stem_weight_grad = stem_weight_grad.transpose(3, 0, 1, 2)
    stem_diff_grad = stem_diff_grad.transpose(3, 0, 1, 2)
    depth_grad = depth_grad.transpose(2, 0, 1, 3)

    return (
        result,
        features_grad,
        stem_weight_grad,
        stem_diff_grad,
        stem_gain_grad,
        stem_bias_grad,
        reduce_grad,
        vectors[8],
        vectors[7],
        spatial_grad,
        vectors[6],
        vectors[5],
        expand_grad,
        vectors[1],
        vectors[0],
        motion_grad,
        vectors[4],
        depth_grad,
        excite_grad,
        vectors[3],
        vectors[2],
    )


def solution(mesh):
    grid = Mesh(mesh.devices.reshape(4, 4, 2, 4), ("z", "y", "c", "x"))
    clips = ("z", "y", "c")
    everyone = ("z", "y", "c", "x")
    split = P(clips, None)
    copied = P()
    return jax.shard_map(
        on_device,
        mesh=grid,
        in_specs=(split,) * 4
        + (P(everyone, None, None, None, None), P(everyone, None, None, None))
        + (copied,) * 19,
        out_specs=(P(clips, "x"), P(clips, "x"))
        + (copied,) * 4
        + (split, copied, copied) * 3
        + (split, copied, copied)
        + (split, copied, copied),
        check_vma=False,
    )
```
